32 devices in a mesh: seq: 16 (over z, x, core), batch: 2 (over y).
Axes of the slice: x: 2, y: 2, z: 4, core: 2. Of those that a mesh axis runs over, the one named last changes fastest.
Arguments:
- tokens: bfloat16 [2, 2048, 1536], P('batch', 'seq'), may hold values from -6 to 6
- doc_ids: int32 [2, 2048], P('batch', 'seq'), may hold values from 0 to 3, never falling along the last dimension, each value on 1 to 1024 neighbouring positions
- norm_gain: float32 [1536], P(('seq', 'batch')), may hold values from 0.5 to 1.5
- query_weight: float32 [1536, 1536], P(('seq', 'batch')), may hold values from -0.15625 to 0.15625
- key_weight: float32 [1536, 1536], P(('seq', 'batch')), may hold values from -0.15625 to 0.15625
- value_weight: float32 [1536, 1536], P(('seq', 'batch')), may hold values from -0.15625 to 0.15625
- house_weight: float32 [1536, 1536], P(('seq', 'batch')), may hold values from -0.15625 to 0.15625
- beta_weight: float32 [1536, 12], P(('seq', 'batch')), may hold values from -0.3125 to 0.3125
- out_weight: float32 [1536, 1536], P(('seq', 'batch')), may hold values from -1.75 to 1.75
- ffn_gain: float32 [1536], P(('seq', 'batch')), may hold values from 0.5 to 1.5
- gate_weight: float32 [1536, 4096], P(('seq', 'batch')), may hold values from -0.15625 to 0.15625
- up_weight: float32 [1536, 4096], P(('seq', 'batch')), may hold values from -0.15625 to 0.15625
- down_weight: float32 [4096, 1536], P(('seq', 'batch')), may hold values from -0.09375 to 0.09375
- cotangent: bfloat16 [2, 2048, 1536], P('batch', 'seq'), may hold values from -6 to 6
Outputs:
- output: bfloat16 [2, 2048, 1536], P('batch', 'seq')
- grad_tokens: bfloat16 [2, 2048, 1536], P('batch', 'seq')
- grad_norm_gain: float32 [1536], P(('seq', 'batch'))
- grad_query_weight: float32 [1536, 1536], P(('seq', 'batch'))
- grad_key_weight: float32 [1536, 1536], P(('seq', 'batch'))
- grad_value_weight: float32 [1536, 1536], P(('seq', 'batch'))
- grad_house_weight: float32 [1536, 1536], P(('seq', 'batch'))
- grad_beta_weight: float32 [1536, 12], P(('seq', 'batch'))
- grad_out_weight: float32 [1536, 1536], P(('seq', 'batch'))
- grad_ffn_gain: float32 [1536], P(('seq', 'batch'))
- grad_gate_weight: float32 [1536, 4096], P(('seq', 'batch'))
- grad_up_weight: float32 [1536, 4096], P(('seq', 'batch'))
- grad_down_weight: float32 [4096, 1536], P(('seq', 'batch'))
The draws below stay inside these ranges and needn't reach their ends.
Inputs may be any that keep to these rules, and one draw needn't show every extreme that they name: `doc_ids`: documents cover consecutive positions of one sequence, numbered upward from 0; none holds more than 1024 positions and some holds exactly that many.
All inputs are finite; a program needn't handle non-finite values.
Results may differ from the reference program's by a relative error of at most 0.017.
The reference program's roundings to bfloat16 on the way count: a program that leaves them out, or rounds other values in their place, can miss the bound.
Values may be sent and summed in bfloat16 or wider, within the bound.
A program may use at most 448 MiB of HBM per device.

```python
import math
import jax
import jax.numpy as jnp
import numpy as np
from jax import lax

D = 1536
HEADS = 12
HEAD_DIM = 128
FF = 4096
TOK_DEV = 128
DOC_COUNT = 4
SEQS = 2
LENGTH = 2048


def level_of(key, shape, pieces, low, largest):
    loudness, own = 1.0, jax.random.fold_in(key, 6)
    for axis_at, blocks in pieces:
        draws = jnp.exp(jax.random.uniform(jax.random.fold_in(own, axis_at), (blocks,), jnp.float32, low / len(pieces), largest / len(pieces)))
        loudness = loudness * jnp.repeat(draws, shape[axis_at] // blocks).reshape([-1 if axis == axis_at else 1 for axis in range(len(shape))])
    return loudness


def split_up(amount, total, most, lean):
    loads = [(1 << 20) // math.isqrt(grade ** lean) + 1 for grade in range(2, amount + 1)]
    surplus, holding = total - most - (amount - 1), [1] * (amount - 1)
    while surplus > 0:
        free = [i for i in range(amount - 1) if holding[i] < most]
        mass, left = sum([loads[i] for i in free]), surplus
        for i in free:
            addition = min(most - holding[i], max(1, left * loads[i] // mass), surplus)
            holding[i] = holding[i] + addition
            surplus = surplus - addition
    return np.array([most] + holding)


def uneven_parts(own_key, number_of, total, most, slope):
    if number_of == 2:
        one = jax.random.randint(own_key, (), max(1, total - most), min(most, total - 1) + 1)
        return jnp.stack([one, total - one])
    tallies = jnp.asarray(split_up(number_of, total, most, slope), jnp.int32)
    pairs = (number_of - 1) // 2
    source_of, sink = tallies[1:1 + 2 * pairs:2], tallies[2:2 + 2 * pairs:2]
    slack = jnp.minimum(source_of - 1, most - sink)
    shifted = jax.random.randint(jax.random.fold_in(own_key, 1), (pairs,), 0, 1 << 20) % (slack + 1)
    tallies = tallies.at[1:1 + 2 * pairs:2].set(source_of - shifted).at[2:2 + 2 * pairs:2].set(sink + shifted)
    return tallies[jax.random.permutation(jax.random.fold_in(own_key, 2), number_of)]


def scatter_about(key, dims, scale, reach, cuts=(), kind=jnp.bfloat16):
    loudness = level_of(key, dims, cuts, -0.22, 0.18) if cuts else 1.0
    array = jax.random.normal(key, dims, jnp.float32) * scale * loudness
    return jnp.minimum(jnp.maximum(array, -reach), reach).astype(kind)


def setup_inputs(seed: int = 0) -> dict:
    splits = jax.random.split(jax.random.key(seed), 15)
    return {
        "tokens": scatter_about(splits[0], (SEQS, LENGTH, D), 1.0, 6.0, ((0, 2), (1, 16))),
        "doc_ids": jax.vmap(lambda own: jnp.searchsorted(jnp.cumsum(uneven_parts(own, DOC_COUNT, LENGTH, LENGTH // 2, 2)), jnp.arange(LENGTH), side="right"))(jax.random.split(splits[1], SEQS)).reshape((SEQS, LENGTH)).astype(jnp.int32),
        "norm_gain": jnp.clip(1.0 + 0.1 * jax.random.normal(splits[2], (D,), jnp.float32), 0.5, 1.5),
        "query_weight": scatter_about(splits[3], (D, D), D ** -0.5, 0.15625, ((0, 32),), jnp.float32),
        "key_weight": scatter_about(splits[4], (D, D), D ** -0.5, 0.15625, ((0, 32),), jnp.float32),
        "value_weight": scatter_about(splits[5], (D, D), D ** -0.5, 0.15625, ((0, 32),), jnp.float32),
        "house_weight": scatter_about(splits[6], (D, D), D ** -0.5, 0.15625, ((0, 32),), jnp.float32),
        "beta_weight": scatter_about(splits[7], (D, HEADS), (D // 4) ** -0.5, 0.3125, ((0, 32),), jnp.float32),
        "out_weight": scatter_about(splits[8], (D, D), (D // 128) ** -0.5, 1.75, ((0, 32),), jnp.float32),
        "ffn_gain": jnp.clip(1.0 + 0.1 * jax.random.normal(splits[9], (D,), jnp.float32), 0.5, 1.5),
        "gate_weight": scatter_about(splits[10], (D, FF), D ** -0.5, 0.15625, ((0, 32),), jnp.float32),
        "up_weight": scatter_about(splits[11], (D, FF), D ** -0.5, 0.15625, ((0, 32),), jnp.float32),
        "down_weight": scatter_about(splits[12], (FF, D), FF ** -0.5, 0.09375, ((0, 32),), jnp.float32),
        "cotangent": scatter_about(splits[13], (SEQS, LENGTH, D), 1.0, 6.0, ((0, 2), (1, 16))),
    }


PRECISE = lax.Precision.HIGHEST
EPSILON = 1e-06
NEGATIVE = -1e+30

@jax.custom_vjp
def low(v):
    return lax.optimization_barrier(v.astype(jnp.bfloat16)).astype(jnp.float32)

@jax.custom_vjp
def low_back(v):
    return v

def low_keep(v):
    return (low(v), None)

def low_pass(kept, grad):
    return (grad,)

def back_keep(v):
    return (v, None)

def back_low(kept, grad):
    return (low(grad),)
low.defvjp(low_keep, low_pass)
low_back.defvjp(back_keep, back_low)

def matmul(left, right):
    return jnp.matmul(left, right, precision=PRECISE)

def rms_scale(values, gain):
    return values * lax.rsqrt(lax.optimization_barrier(jnp.mean(values * values, axis=-1, keepdims=True)) + EPSILON) * gain

def split_heads(values):
    return jnp.transpose(values.reshape(values.shape[0], HEADS, HEAD_DIM), (1, 0, 2))

def merge_heads(values):
    return jnp.transpose(values, (1, 0, 2)).reshape(values.shape[1], HEADS * HEAD_DIM)

def prepare(query_rows, key_rows, house_rows, rate_rows):
    block_rows = query_rows.shape[0]
    query_heads = split_heads(query_rows)
    key_heads = split_heads(key_rows)
    house_heads = split_heads(house_rows)
    unit_dirs = house_heads * lax.rsqrt(lax.optimization_barrier(jnp.sum(house_heads * house_heads, axis=-1, keepdims=True)) + EPSILON)
    strength = 2.0 * jax.nn.sigmoid(jnp.transpose(rate_rows))
    row_index = lax.broadcasted_iota(jnp.int32, (block_rows, block_rows), 0)
    col_index = lax.broadcasted_iota(jnp.int32, (block_rows, block_rows), 1)
    lower_mask = row_index > col_index
    causal_mask = row_index >= col_index
    zero_block = jnp.zeros((HEADS, block_rows, block_rows), query_rows.dtype)
    inner_dots = jnp.einsum('hsd,htd->hst', unit_dirs, unit_dirs, precision=PRECISE)
    system = jnp.eye(block_rows, dtype=query_rows.dtype)[None] + jnp.where(lower_mask[None], strength[:, :, None] * inner_dots, zero_block)
    project = jnp.where(causal_mask[None], jnp.einsum('hid,htd->hit', query_heads, unit_dirs, precision=PRECISE), zero_block)
    coeffs = lax.linalg.triangular_solve(system, project, left_side=False, lower=True, transpose_a=False, unit_diagonal=True)
    carry_basis = lax.linalg.triangular_solve(system, unit_dirs, left_side=True, lower=True, transpose_a=True, unit_diagonal=True)
    reach_terms = jnp.where(lower_mask[None], strength[:, :, None] * jnp.einsum('htd,hjd->htj', unit_dirs, key_heads, precision=PRECISE), zero_block)
    within = jnp.einsum('hid,hjd->hij', query_heads, key_heads, precision=PRECISE) - jnp.einsum('hit,htj->hij', coeffs, reach_terms, precision=PRECISE)
    query_hat = query_heads - jnp.einsum('hit,htd->hid', coeffs, strength[:, :, None] * unit_dirs, precision=PRECISE)
    key_hat = key_heads - jnp.einsum('htj,htd->hjd', reach_terms, carry_basis, precision=PRECISE)
    return (query_hat, key_hat, within, carry_basis, unit_dirs, strength)

def carry_keys(travel, carry_basis, unit_dirs, strength):
    weights_on = jnp.einsum('hnd,htd->hnt', travel, unit_dirs, precision=PRECISE) * strength[:, None, :]
    return travel - jnp.einsum('hnt,htd->hnd', weights_on, carry_basis, precision=PRECISE)

def attend_sequence(query_rows, key_rows, value_rows, house_rows, rate_rows, doc_row):
    blocks = LENGTH // TOK_DEV
    inner_count = math.gcd(blocks, 8)
    outer_count = blocks // inner_count
    score_scale = HEAD_DIM ** (-0.5)
    prepared = jax.vmap(prepare)(query_rows.reshape(blocks, TOK_DEV, D), key_rows.reshape(blocks, TOK_DEV, D), house_rows.reshape(blocks, TOK_DEV, D), rate_rows.reshape(blocks, TOK_DEV, HEADS))
    query_hat, key_hat, within, carry_basis, unit_dirs, strength = prepared
    query_hat = low(query_hat)
    key_hat = low(key_hat)
    value_heads = split_heads(low(value_rows))
    value_blocks = jnp.transpose(value_heads.reshape(HEADS, blocks, TOK_DEV, HEAD_DIM), (1, 0, 2, 3))
    block_docs = doc_row.reshape(blocks, TOK_DEV)
    key_block = lax.broadcasted_iota(jnp.int32, (LENGTH,), 0) // TOK_DEV
    row_index = lax.broadcasted_iota(jnp.int32, (TOK_DEV, TOK_DEV), 0)
    col_index = lax.broadcasted_iota(jnp.int32, (TOK_DEV, TOK_DEV), 1)
    indices = jnp.arange(blocks, dtype=jnp.int32)

    def block_step(travel, block_items):
        index_now, query_now, key_now, within_now, basis_now, unit_now, strength_now, value_now, docs_now = block_items
        cross_scores = low_back(jnp.einsum('hid,hnd->hin', query_now, travel, precision=PRECISE)) * score_scale
        cross_mask = (key_block[None, :] < index_now) & (docs_now[:, None] == doc_row[None, :])
        cross_scores = jnp.where(cross_mask[None], cross_scores, NEGATIVE)
        local_mask = (row_index >= col_index) & (docs_now[:, None] == docs_now[None, :])
        local_scores = jnp.where(local_mask[None], within_now * score_scale, NEGATIVE)
        row_top = jnp.maximum(lax.optimization_barrier(jnp.max(cross_scores, axis=-1)), lax.optimization_barrier(jnp.max(local_scores, axis=-1)))
        cross_weights = jnp.exp(cross_scores - row_top[..., None])
        local_weights = jnp.exp(local_scores - row_top[..., None])
        row_total = lax.optimization_barrier(jnp.sum(cross_weights, axis=-1)) + lax.optimization_barrier(jnp.sum(local_weights, axis=-1))
        unnorm = jnp.einsum('hin,hnd->hid', low(cross_weights), value_heads, precision=PRECISE) + jnp.einsum('hij,hjd->hid', low(local_weights), value_now, precision=PRECISE)
        unnorm = low_back(unnorm)
        attended = unnorm / row_total[..., None]
        travel_next = low(carry_keys(travel, basis_now, unit_now, strength_now))
        travel_next = lax.dynamic_update_slice(travel_next, key_now, (jnp.int32(0), (index_now * TOK_DEV).astype(jnp.int32), jnp.int32(0)))
        return (travel_next, attended)

    def regroup(values):
        return values.reshape((outer_count, inner_count) + values.shape[1:])

    def block_group(travel, group_items):
        return lax.scan(jax.checkpoint(block_step), travel, group_items)
    grouped = tuple((regroup(values) for values in (indices, query_hat, key_hat, within, carry_basis, unit_dirs, strength, value_blocks, block_docs)))
    travel_start = jnp.zeros((HEADS, LENGTH, HEAD_DIM), query_rows.dtype)
    unused, attended = lax.scan(jax.checkpoint(block_group), travel_start, grouped)
    attended = attended.reshape(blocks, HEADS, TOK_DEV, HEAD_DIM)
    return jnp.transpose(attended, (0, 2, 1, 3)).reshape(LENGTH, D)

def attend_all(bundle):
    return attend_sequence(*bundle)

def block_layer(tokens, norm_gain, query_weight, key_weight, value_weight, house_weight, beta_weight, out_weight, ffn_gain, gate_weight, up_weight, down_weight, doc_ids):
    normed = low(rms_scale(tokens, low(norm_gain)))
    query_rows = low_back(matmul(normed, low(query_weight)))
    key_rows = low_back(matmul(normed, low(key_weight)))
    value_rows = low_back(matmul(normed, low(value_weight)))
    house_rows = low_back(matmul(normed, low(house_weight)))
    rate_rows = low_back(matmul(normed, low(beta_weight)))
    attended = lax.map(attend_all, (query_rows, key_rows, value_rows, house_rows, rate_rows, doc_ids))
    attended = low(low_back(attended))
    branch = low_back(matmul(attended, low(out_weight)))
    hidden = tokens + branch
    normed_two = low(rms_scale(hidden, low(ffn_gain)))
    gate_rows = low_back(matmul(normed_two, low(gate_weight)))
    upward = low_back(matmul(normed_two, low(up_weight)))
    active = low(jax.nn.silu(gate_rows) * upward)
    return hidden + low_back(matmul(active, low(down_weight)))

def reference(tokens, doc_ids, norm_gain, query_weight, key_weight, value_weight, house_weight, beta_weight, out_weight, ffn_gain, gate_weight, up_weight, down_weight, cotangent):

    def forward(tokens_f, gain_one, query_w, key_w, value_w, house_w, beta_w, out_w, gain_two, gate_w, up_w, down_w):
        return block_layer(tokens_f, gain_one, query_w, key_w, value_w, house_w, beta_w, out_w, gain_two, gate_w, up_w, down_w, doc_ids)
    result, pull_back = jax.vjp(forward, tokens.astype(jnp.float32), norm_gain.astype(jnp.float32), query_weight.astype(jnp.float32), key_weight.astype(jnp.float32), value_weight.astype(jnp.float32), house_weight.astype(jnp.float32), beta_weight.astype(jnp.float32), out_weight.astype(jnp.float32), ffn_gain.astype(jnp.float32), gate_weight.astype(jnp.float32), up_weight.astype(jnp.float32), down_weight.astype(jnp.float32))
    grads = pull_back(cotangent.astype(jnp.float32))
    return (result.astype(jnp.bfloat16), grads[0].astype(jnp.bfloat16), grads[1], grads[2], grads[3], grads[4], grads[5], grads[6], grads[7], grads[8], grads[9], grads[10], grads[11])
```

```python
import functools

import jax
import jax.numpy as jnp
from jax import lax
from jax.experimental import pallas as pl
from jax.experimental.pallas import tpu as pltpu
from jax.sharding import Mesh
from jax.sharding import PartitionSpec as P

HEADS = 12
HEAD_DIM = 128
GROUP = 4
OWN = HEADS // GROUP
WIDE = OWN * HEAD_DIM
BLOCK = 128
EXTRA = 128
EPSILON = 1e-06
NEGATIVE = -1e30
SCALE = HEAD_DIM ** (-0.5)
MESH = pl.DeviceIdType.MESH
F32 = jnp.float32
BF16 = jnp.bfloat16
NN = (((1,), (0,)), ((), ()))
NT = (((1,), (1,)), ((), ()))
TN = (((0,), (0,)), ((), ()))


def dot(left, right, dims=NN):
    return lax.dot_general(left, right, dims, preferred_element_type=F32)


def split(value):
    high = value.astype(BF16)
    return high, (value - high.astype(F32)).astype(BF16)


def dot3(left, right, dims=NN):
    left_high, left_low = split(left)
    right_high, right_low = split(right)
    return dot(left_high, right_high, dims) + (
        dot(left_high, right_low, dims) + dot(left_low, right_high, dims)
    )


def dot2(left, right, dims=NN):
    high, low = split(right)
    return dot(left, high, dims) + dot(left, low, dims)


def tile(index, count=1):
    return pl.ds(index * BLOCK, count * BLOCK)


def iota(axis, shape=(BLOCK, BLOCK)):
    return lax.broadcasted_iota(jnp.int32, shape, axis)


def invert(strict):
    row, col = iota(0), iota(1)
    eye = jnp.where(row == col, 1.0, 0.0)

    def part(size):
        return (row // (2 * size) == col // (2 * size)) & (row // size > col // size)

    totals = [eye - jnp.where(part(1), value, 0.0) for value in strict]
    size = 2
    while size < BLOCK:
        mask = part(size)
        pieces = [jnp.where(mask, value, 0.0) for value in strict]
        inner = [dot3(piece, total) for piece, total in zip(pieces, totals)]
        outer = [dot3(total, value) for total, value in zip(totals, inner)]
        totals = [total - value for total, value in zip(totals, outer)]
        size *= 2
    return totals


def unit_of(house):
    scale = lax.rsqrt(jnp.sum(house * house, axis=-1, keepdims=True) + EPSILON)
    return house * scale, scale


def products(query, key, unit):
    both = dot3(jnp.concatenate([unit, query], 0), jnp.concatenate([unit, key], 0), NT)
    return both[:BLOCK, :BLOCK], both[:BLOCK, BLOCK:], both[BLOCK:, :BLOCK], both[BLOCK:, BLOCK:]


def prepare_kernel(rows_ref, query_ref, key_ref, value_ref, within_ref, map_ref, inverse_ref):
    row, col = iota(0), iota(1)

    def one_block(block, carry):
        at = tile(block)
        kept, strict = [], []
        for head in range(OWN):
            query, key, value, house = [
                rows_ref[at, pl.ds(part * WIDE + head * BLOCK, BLOCK)] for part in range(4)
            ]
            rate = rows_ref[at, pl.ds(4 * WIDE, EXTRA)][:, head : head + 1]
            value_ref[at, tile(head)] = value.astype(BF16)
            unit, _ = unit_of(house)
            strength = 2.0 * jax.nn.sigmoid(rate)
            unit_unit, unit_key, query_unit, query_key = products(query, key, unit)
            strict.append(jnp.where(row > col, strength * unit_unit, 0.0))
            reach = jnp.where(row > col, strength * unit_key, 0.0)
            project = jnp.where(row >= col, query_unit, 0.0)
            kept.append((query, key, unit, strength, reach, project, query_key))
        inverses = invert(strict)
        for head in range(OWN):
            query, key, unit, strength, reach, project, query_key = kept[head]
            inverse = inverses[head]
            solved = dot3(inverse, jnp.concatenate([strength * unit, reach], 1))
            from_query = dot3(project, solved)
            from_unit = dot3(solved, unit, TN)
            query_ref[at, tile(head)] = (query - from_query[:, :BLOCK]).astype(BF16)
            within_ref[at, tile(head)] = query_key - from_query[:, BLOCK:]
            map_ref[at, tile(head)] = jnp.where(row == col, 1.0, 0.0) - from_unit[:BLOCK]
            key_ref[at, tile(head)] = (key - from_unit[BLOCK:]).astype(BF16)
            inverse_ref[at, tile(head)] = inverse
        return carry

    lax.fori_loop(0, GROUP, one_block, 0)


def prepare(rows):
    length = rows.shape[0]
    return pl.pallas_call(
        prepare_kernel,
        out_shape=[jax.ShapeDtypeStruct((length, WIDE), kind) for kind in (BF16, BF16, BF16, F32, F32, F32)],
        compiler_params=pltpu.CompilerParams(vmem_limit_bytes=48 << 20),
        name="prepare",
    )(rows)


def prepare_back_kernel(rows_ref, inverse_ref, query_grad_ref, key_grad_ref, within_grad_ref, map_grad_ref, value_grad_ref, out_ref):
    row, col = iota(0), iota(1)

    def one_block(block, carry):
        at = tile(block)
        rates = jnp.zeros((BLOCK, EXTRA), F32)
        for head in range(OWN):
            query, key, value, house = [
                rows_ref[at, pl.ds(part * WIDE + head * BLOCK, BLOCK)] for part in range(4)
            ]
            rate = rows_ref[at, pl.ds(4 * WIDE, EXTRA)][:, head : head + 1]
            query_grad = query_grad_ref[at, tile(head)]
            key_grad = key_grad_ref[at, tile(head)]
            within_grad = within_grad_ref[at, tile(head)]
            map_grad = map_grad_ref[at, tile(head)]
            inverse = inverse_ref[at, tile(head)]
            unit, scale = unit_of(house)
            strength = 2.0 * jax.nn.sigmoid(rate)
            unit_unit, unit_key, query_unit, query_key = products(query, key, unit)
            reach = jnp.where(row > col, strength * unit_key, 0.0)
            project = jnp.where(row >= col, query_unit, 0.0)
            solved = dot3(inverse, jnp.concatenate([strength * unit, reach], 1))
            both_grad = jnp.concatenate([query_grad, within_grad], 1)
            project_grad = jnp.where(row >= col, -dot3(both_grad, solved, NT), 0.0)
            solved_grad = -(
                dot3(project, both_grad, TN)
                + dot3(unit, jnp.concatenate([map_grad, key_grad], 0), NT)
            )
            given_grad = dot3(inverse, solved_grad, TN)
            strict_grad = jnp.where(row > col, -dot3(given_grad, solved, NT), 0.0)
            scaled_grad = given_grad[:, :BLOCK]
            reach_grad = jnp.where(row > col, given_grad[:, BLOCK:], 0.0)
            strength_grad = jnp.sum(
                scaled_grad * unit + reach_grad * unit_key + strict_grad * unit_unit, axis=1, keepdims=True
            )
            reach_part = strength * reach_grad
            inner_part = strength * strict_grad
            unit_grad = (
                strength * scaled_grad
                + dot3(reach_part, key)
                + dot3(inner_part + inner_part.T, unit)
                + dot3(project_grad, query, TN)
                - dot3(solved[:, :BLOCK], map_grad)
                - dot3(solved[:, BLOCK:], key_grad)
            )
            query_out = query_grad + dot3(within_grad, key) + dot3(project_grad, unit)
            key_out = key_grad + dot3(within_grad, query, TN) + dot3(reach_part, unit, TN)
            house_out = scale * (unit_grad - unit * jnp.sum(unit * unit_grad, axis=1, keepdims=True))
            rate_out = strength_grad * strength * (1.0 - 0.5 * strength)
            rates = jnp.where(iota(1, (BLOCK, EXTRA)) == head, rate_out, rates)
            out_ref[at, pl.ds(head * BLOCK, BLOCK)] = query_out.astype(BF16)
            out_ref[at, pl.ds(WIDE + head * BLOCK, BLOCK)] = key_out.astype(BF16)
            out_ref[at, pl.ds(2 * WIDE + head * BLOCK, BLOCK)] = value_grad_ref[at, tile(head)].astype(BF16)
            out_ref[at, pl.ds(3 * WIDE + head * BLOCK, BLOCK)] = house_out.astype(BF16)
        out_ref[at, pl.ds(4 * WIDE, EXTRA)] = rates.astype(BF16)
        return carry

    lax.fori_loop(0, GROUP, one_block, 0)


def prepare_back(*args):
    return pl.pallas_call(
        prepare_back_kernel,
        out_shape=jax.ShapeDtypeStruct(args[0].shape, BF16),
        compiler_params=pltpu.CompilerParams(vmem_limit_bytes=48 << 20),
        name="prepare_back",
    )(*args)


def meet_neighbours(groups):
    place = lax.axis_index("g")
    others = {"m": lax.axis_index("m"), "b": lax.axis_index("b")}
    barrier = pltpu.get_barrier_semaphore()

    @pl.when(place > 0)
    def _():
        pl.semaphore_signal(barrier, 1, device_id={"g": place - 1, **others}, device_id_type=MESH)

    @pl.when(place < groups - 1)
    def _():
        pl.semaphore_signal(barrier, 1, device_id={"g": place + 1, **others}, device_id_type=MESH)

    pl.semaphore_wait(barrier, (place > 0).astype(jnp.int32) + (place < groups - 1).astype(jnp.int32))
    return place, others


def masked(scores, counts):
    return jnp.where(counts, scores * SCALE, NEGATIVE)


def attend_kernel(
    groups,
    hops,
    query_ref,
    key_ref,
    value_ref,
    within_ref,
    map_ref,
    doc_query_ref,
    doc_key_ref,
    attended_ref,
    low_ref,
    stats_ref,
    moved_ref,
    values_ref,
    leave_ref,
    top_ref,
    total_ref,
    accum_ref,
    key_send,
    key_recv,
    value_send,
    value_recv,
):
    place, others = meet_neighbours(groups)
    following = {"g": place + 1, **others}
    has_next = place < groups - 1

    def value_copy(source, slot):
        return pltpu.make_async_remote_copy(
            src_ref=source,
            dst_ref=values_ref.at[slot],
            send_sem=value_send.at[slot],
            recv_sem=value_recv.at[slot],
            device_id=following,
            device_id_type=MESH,
        )

    def key_copy(slot):
        return pltpu.make_async_remote_copy(
            src_ref=leave_ref.at[slot],
            dst_ref=moved_ref.at[slot + 1, 0],
            send_sem=key_send.at[slot],
            recv_sem=key_recv.at[slot],
            device_id=following,
            device_id_type=MESH,
        )

    def move(keys, block, head):
        return dot2(keys, map_ref[tile(block), tile(head)]).astype(BF16)

    for head in range(OWN):
        keys = key_ref[tile(0), tile(head)]
        for block in range(1, GROUP):
            moved_ref[0, block, tile(0, block), tile(head)] = keys
            keys = jnp.concatenate([move(keys, block, head), key_ref[tile(block), tile(head)]], 0)
        leave_ref[0, :, tile(head)] = keys

    @pl.when(has_next)
    def _():
        key_copy(0).start()
        value_copy(value_ref, 0).start()

    def row_counts(block, hop, first, count):
        return doc_query_ref[tile(block), :] == doc_key_ref[hop, :, tile(first, count)]

    for block in range(GROUP):
        counts = row_counts(block, 0, 0, block + 1)
        wide = (BLOCK, (block + 1) * BLOCK)
        counts = counts & (iota(0, wide) + block * BLOCK >= iota(1, wide))
        for head in range(OWN):
            scores = within_ref[tile(block), tile(head)]
            if block:
                before = dot(query_ref[tile(block), tile(head)], moved_ref[0, block, tile(0, block), tile(head)], NT)
                scores = jnp.concatenate([before, scores], 1)
            scores = masked(scores, counts)
            top = jnp.max(scores, axis=1, keepdims=True)
            weights = jnp.exp(scores - top)
            top_ref[head, tile(block), :] = jnp.broadcast_to(top, (BLOCK, BLOCK))
            total_ref[head, tile(block), :] = jnp.broadcast_to(jnp.sum(weights, axis=1, keepdims=True), (BLOCK, BLOCK))
            accum_ref[tile(block), tile(head)] = dot(weights.astype(BF16), value_ref[tile(0, block + 1), tile(head)])

    def hop_step(hop, last):
        @pl.when(place >= hop)
        def _():
            key_copy(hop - 1).wait_recv()
            for head in range(OWN):
                keys = moved_ref[hop, 0, :, tile(head)]
                for block in range(GROUP):
                    if last:
                        if block == GROUP - 1:
                            break
                        keys = move(keys[BLOCK:], block, head)
                        moved_ref[hop, block + 1, tile(block + 1, GROUP - 1 - block), tile(head)] = keys
                    else:
                        keys = move(keys, block, head)
                        if block < GROUP - 1:
                            moved_ref[hop, block + 1, :, tile(head)] = keys
                        else:
                            leave_ref[hop, :, tile(head)] = keys
            value_copy(value_ref, hop - 1).wait_recv()
            if not last:

                @pl.when(has_next)
                def _():
                    key_copy(hop).start()
                    value_copy(values_ref.at[hop - 1], hop).start()

            for block in range(GROUP):
                first = block if last else 0
                count = GROUP - first
                counts = row_counts(block, hop, first, count)
                for head in range(OWN):
                    scores = masked(
                        dot(query_ref[tile(block), tile(head)], moved_ref[hop, block, tile(first, count), tile(head)], NT),
                        counts,
                    )
                    old = top_ref[head, tile(block), :]
                    top = jnp.maximum(old, jnp.broadcast_to(jnp.max(scores, axis=1, keepdims=True), (BLOCK, BLOCK)))
                    factor = jnp.exp(old - top)
                    weights = jnp.exp(scores - jnp.concatenate([top] * count, 1))
                    top_ref[head, tile(block), :] = top
                    total_ref[head, tile(block), :] = total_ref[head, tile(block), :] * factor + jnp.sum(
                        weights, axis=1, keepdims=True
                    )
                    accum_ref[tile(block), tile(head)] = accum_ref[tile(block), tile(head)] * factor + dot(
                        weights.astype(BF16), values_ref[hop - 1, tile(first, count), tile(head)]
                    )

    if hops > 2:

        def between(hop, carry):
            hop_step(hop, False)
            return carry

        lax.fori_loop(1, hops, between, 0)
    else:
        for hop in range(1, hops):
            hop_step(hop, False)
    hop_step(hops, True)

    for block in range(GROUP):
        stats = jnp.zeros((BLOCK, BLOCK), F32)
        for head in range(OWN):
            total = total_ref[head, tile(block), :]
            result = accum_ref[tile(block), tile(head)] / total
            attended_ref[tile(block), tile(head)] = result
            low_ref[tile(block), tile(head)] = result.astype(BF16)
            stats = jnp.where(iota(1) == head, top_ref[head, tile(block), :], stats)
            stats = jnp.where(iota(1) == OWN + head, total, stats)
        stats_ref[tile(block), :] = stats

    def settle(slot, carry):
        @pl.when(has_next & (place >= slot))
        def _():
            key_copy(slot).wait_send()
            value_copy(value_ref, slot).wait_send()

        return carry

    lax.fori_loop(0, hops, settle, 0)


def attend(groups, hops, *args):
    length = args[0].shape[0]
    out = [
        jax.ShapeDtypeStruct((length, WIDE), F32),
        jax.ShapeDtypeStruct((length, WIDE), BF16),
        jax.ShapeDtypeStruct((length, BLOCK), F32),
        jax.ShapeDtypeStruct((hops + 1, GROUP, length, WIDE), BF16),
        jax.ShapeDtypeStruct((hops, length, WIDE), BF16),
    ]
    return pl.pallas_call(
        functools.partial(attend_kernel, groups, hops),
        out_shape=out,
        in_specs=[pl.BlockSpec(memory_space=pltpu.VMEM)] * len(args),
        out_specs=[pl.BlockSpec(memory_space=pltpu.VMEM)] * len(out),
        scratch_shapes=[
            pltpu.VMEM((hops, length, WIDE), BF16),
            pltpu.VMEM((OWN, length, BLOCK), F32),
            pltpu.VMEM((OWN, length, BLOCK), F32),
            pltpu.VMEM((length, WIDE), F32),
            pltpu.SemaphoreType.DMA((hops,)),
            pltpu.SemaphoreType.DMA((hops,)),
            pltpu.SemaphoreType.DMA((hops,)),
            pltpu.SemaphoreType.DMA((hops,)),
        ],
        compiler_params=pltpu.CompilerParams(collective_id=1, has_side_effects=True, vmem_limit_bytes=58 << 20),
        name="attend",
    )(*args)


def attend_back_kernel(
    groups,
    hops,
    query_ref,
    value_ref,
    within_ref,
    map_ref,
    doc_query_ref,
    doc_key_ref,
    attended_ref,
    stats_ref,
    moved_ref,
    values_ref,
    att_grad_ref,
    query_grad_ref,
    key_grad_ref,
    within_grad_ref,
    map_grad_ref,
    value_grad_ref,
    scaled_ref,
    dots_ref,
    direct_ref,
    direct_value_ref,
    running_ref,
    key_leave_ref,
    value_leave_ref,
    key_land_ref,
    value_land_ref,
    key_send,
    key_recv,
    value_send,
    value_recv,
):
    place, others = meet_neighbours(groups)
    previous = {"g": place - 1, **others}
    has_next = place < groups - 1

    def key_copy(hop):
        slot = hop - 1
        return pltpu.make_async_remote_copy(
            src_ref=key_leave_ref.at[slot],
            dst_ref=key_land_ref.at[slot],
            send_sem=key_send.at[slot],
            recv_sem=key_recv.at[slot],
            device_id=previous,
            device_id_type=MESH,
        )

    def value_copy(hop):
        slot = hop - 1
        return pltpu.make_async_remote_copy(
            src_ref=value_leave_ref.at[slot],
            dst_ref=value_land_ref.at[slot],
            send_sem=value_send.at[slot],
            recv_sem=value_recv.at[slot],
            device_id=previous,
            device_id_type=MESH,
        )

    map_grad_ref[...] = jnp.zeros_like(map_grad_ref)
    query_grad_ref[...] = jnp.zeros_like(query_grad_ref)
    for block in range(GROUP):
        for head in range(OWN):
            at = (tile(block), tile(head))
            grad = att_grad_ref[at].astype(F32)
            total = stats_ref[tile(block), OWN + head : OWN + head + 1]
            scaled_ref[at] = (grad / total).astype(BF16)
            dots = -jnp.sum(grad * attended_ref[at], axis=1, keepdims=True) / total
            dots_ref[head, tile(block), :] = jnp.broadcast_to(dots, (BLOCK, BLOCK))

    def pair(block, head, scores, counts, values):
        count = scores.shape[1] // BLOCK
        top = stats_ref[tile(block), head : head + 1]
        weights = jnp.exp(masked(scores, counts) - top)
        weight_grad = dot(scaled_ref[tile(block), tile(head)], values, NT)
        dots = jnp.concatenate([dots_ref[head, tile(block), :]] * count, 1)
        return weights, weights * (weight_grad + dots) * SCALE

    def row_counts(block, hop, first, count):
        return doc_query_ref[tile(block), :] == doc_key_ref[hop, :, tile(first, count)]

    def hop_direct(hop, slot, last):
        for head in range(OWN):
            direct_value_ref[slot, :, tile(head)] = jnp.zeros((GROUP * BLOCK, BLOCK), F32)
        for block in range(GROUP):
            first = block if last else 0
            count = GROUP - first
            counts = row_counts(block, hop, first, count)
            for head in range(OWN):
                query = query_ref[tile(block), tile(head)]
                keys = moved_ref[hop, block, tile(first, count), tile(head)]
                weights, grad = pair(
                    block, head, dot(query, keys, NT), counts, values_ref[hop - 1, tile(first, count), tile(head)]
                )
                raw = grad.astype(BF16)
                query_grad_ref[tile(block), tile(head)] += dot(raw, keys)
                direct_ref[slot, block, tile(first, count), tile(head)] = dot(raw, query, TN)
                direct_value_ref[slot, tile(first, count), tile(head)] += dot(
                    weights.astype(BF16), scaled_ref[tile(block), tile(head)], TN
                )

    def collect_map(block, head, keys, grads):
        map_grad_ref[tile(block), tile(head)] += dot2(keys, grads, TN)

    def hop_chain(hop, slot, last):
        for head in range(OWN):
            if last:
                grads = direct_ref[slot, GROUP - 1, tile(GROUP - 1), tile(head)]
                for block in range(GROUP - 2, -1, -1):
                    rows = tile(block + 1, GROUP - 1 - block)
                    collect_map(block, head, moved_ref[hop, block, rows, tile(head)], grads)
                    back = dot3(grads, map_ref[tile(block), tile(head)], NT)
                    direct = direct_ref[slot, block, tile(block, GROUP - block), tile(head)]
                    grads = jnp.concatenate([direct[:BLOCK], direct[BLOCK:] + back], 0)
                key_leave_ref[hop - 1, :, tile(head)] = grads.astype(BF16)
                value_leave_ref[hop - 1, :, tile(head)] = direct_value_ref[slot, :, tile(head)].astype(BF16)
            else:
                grads = running_ref[:, tile(head)]
                for block in range(GROUP - 1, -1, -1):
                    collect_map(block, head, moved_ref[hop, block, :, tile(head)], grads)
                    grads = direct_ref[slot, block, :, tile(head)] + dot3(grads, map_ref[tile(block), tile(head)], NT)
                key_leave_ref[hop - 1, :, tile(head)] = grads.astype(BF16)

    def take(hop):
        @pl.when(has_next)
        def _():
            key_copy(hop).wait_recv()
            running_ref[...] = key_land_ref[hop - 1].astype(F32)

        @pl.when(jnp.logical_not(has_next))
        def _():
            running_ref[...] = jnp.zeros_like(running_ref)

    @pl.when(place >= hops)
    def _():
        hop_direct(hops, hops % 2, True)
        hop_chain(hops, hops % 2, True)
        key_copy(hops).start()
        value_copy(hops).start()

    def between(hop):
        @pl.when(place >= hop)
        def _():
            slot = lax.rem(hop, 2) if hops > 2 else hop % 2
            hop_direct(hop, slot, False)
            take(hop + 1)
            hop_chain(hop, slot, False)
            key_copy(hop).start()

            @pl.when(has_next)
            def _():
                value_copy(hop + 1).wait_recv()
                for head in range(OWN):
                    value_leave_ref[hop - 1, :, tile(head)] = (
                        direct_value_ref[slot, :, tile(head)] + value_land_ref[hop, :, tile(head)].astype(F32)
                    ).astype(BF16)

            @pl.when(jnp.logical_not(has_next))
            def _():
                for head in range(OWN):
                    value_leave_ref[hop - 1, :, tile(head)] = direct_value_ref[slot, :, tile(head)].astype(BF16)

            value_copy(hop).start()

    if hops > 2:

        def step(counter, carry):
            between(hops - 1 - counter)
            return carry

        lax.fori_loop(0, hops - 1, step, 0)
    else:
        for hop in range(hops - 1, 0, -1):
            between(hop)

    for head in range(OWN):
        direct_value_ref[0, :, tile(head)] = jnp.zeros((GROUP * BLOCK, BLOCK), F32)
    for block in range(GROUP):
        wide = (BLOCK, (block + 1) * BLOCK)
        counts = row_counts(block, 0, 0, block + 1) & (iota(0, wide) + block * BLOCK >= iota(1, wide))
        for head in range(OWN):
            query = query_ref[tile(block), tile(head)]
            scores = within_ref[tile(block), tile(head)]
            if block:
                keys = moved_ref[0, block, tile(0, block), tile(head)]
                scores = jnp.concatenate([dot(query, keys, NT), scores], 1)
            weights, grad = pair(block, head, scores, counts, value_ref[tile(0, block + 1), tile(head)])
            within_grad_ref[tile(block), tile(head)] = grad[:, block * BLOCK :]
            direct_value_ref[0, tile(0, block + 1), tile(head)] += dot(
                weights.astype(BF16), scaled_ref[tile(block), tile(head)], TN
            )
            if block:
                raw = grad[:, : block * BLOCK].astype(BF16)
                query_grad_ref[tile(block), tile(head)] += dot(raw, keys)
                direct_ref[0, block, tile(0, block), tile(head)] = dot(raw, query, TN)
    take(1)
    for head in range(OWN):
        grads = running_ref[:, tile(head)]
        for block in range(GROUP - 1, 0, -1):
            key_grad_ref[tile(block), tile(head)] = grads[block * BLOCK :]
            grads = grads[: block * BLOCK]
            collect_map(block, head, moved_ref[0, block, tile(0, block), tile(head)], grads)
            grads = direct_ref[0, block, tile(0, block), tile(head)] + dot3(grads, map_ref[tile(block), tile(head)], NT)
        key_grad_ref[tile(0), tile(head)] = grads

    @pl.when(has_next)
    def _():
        value_copy(1).wait_recv()
        value_grad_ref[...] = direct_value_ref[0] + value_land_ref[0].astype(F32)

    @pl.when(jnp.logical_not(has_next))
    def _():
        value_grad_ref[...] = direct_value_ref[0]

    def settle(hop, carry):
        @pl.when(place >= hop)
        def _():
            key_copy(hop).wait_send()
            value_copy(hop).wait_send()

        return carry

    lax.fori_loop(1, hops + 1, settle, 0)


def attend_back(groups, hops, *args):
    length = args[0].shape[0]
    out = [jax.ShapeDtypeStruct((length, WIDE), F32)] * 5
    return pl.pallas_call(
        functools.partial(attend_back_kernel, groups, hops),
        out_shape=out,
        in_specs=[pl.BlockSpec(memory_space=pltpu.VMEM)] * len(args),
        out_specs=[pl.BlockSpec(memory_space=pltpu.VMEM)] * len(out),
        scratch_shapes=[
            pltpu.VMEM((length, WIDE), BF16),
            pltpu.VMEM((OWN, length, BLOCK), F32),
            pltpu.VMEM((2, GROUP, length, WIDE), F32),
            pltpu.VMEM((2, length, WIDE), F32),
            pltpu.VMEM((length, WIDE), F32),
            pltpu.VMEM((hops, length, WIDE), BF16),
            pltpu.VMEM((hops, length, WIDE), BF16),
            pltpu.VMEM((hops, length, WIDE), BF16),
            pltpu.VMEM((hops, length, WIDE), BF16),
            pltpu.SemaphoreType.DMA((hops,)),
            pltpu.SemaphoreType.DMA((hops,)),
            pltpu.SemaphoreType.DMA((hops,)),
            pltpu.SemaphoreType.DMA((hops,)),
        ],
        compiler_params=pltpu.CompilerParams(collective_id=2, has_side_effects=True, vmem_limit_bytes=58 << 20),
        name="attend_back",
    )(*args)


def rms_scale(values, gain):
    return values * lax.rsqrt(jnp.mean(values * values, axis=-1, keepdims=True) + EPSILON) * gain


def rms_back(values, gain, grad):
    scale = lax.rsqrt(jnp.mean(values * values, axis=-1, keepdims=True) + EPSILON)
    straight = values * scale
    lifted = grad * gain
    back = scale * (lifted - straight * jnp.mean(lifted * straight, axis=-1, keepdims=True))
    return back, jnp.sum(grad * straight, axis=0)


def on_device(
    tokens,
    doc_ids,
    norm_gain,
    query_weight,
    key_weight,
    value_weight,
    house_weight,
    beta_weight,
    out_weight,
    ffn_gain,
    gate_weight,
    up_weight,
    down_weight,
    cotangent,
):
    groups, batch = lax.axis_size("g"), lax.axis_size("b")
    devices = groups * GROUP * batch
    rows, width = query_weight.shape
    hidden_rows = down_weight.shape[0]
    hidden_own = gate_weight.shape[1] // GROUP
    block_rows = tokens.shape[1]
    hops = groups // 2
    doc_columns = -(-block_rows // rows)
    place, member, line = lax.axis_index("g"), lax.axis_index("m"), lax.axis_index("b")

    def columns(weight):
        return jnp.transpose(weight.astype(BF16).reshape(rows, GROUP, -1), (1, 0, 2))

    docs = jnp.pad(doc_ids[0].astype(BF16), (0, rows * doc_columns - block_rows)).reshape(rows, doc_columns)
    same = jnp.concatenate([norm_gain.astype(BF16)[:, None], ffn_gain.astype(BF16)[:, None], docs], 1)
    same = jnp.broadcast_to(same[None], (GROUP,) + same.shape)
    same = jnp.pad(same, ((0, 0), (0, 0), (0, EXTRA - OWN - same.shape[2])))
    first_parts = jnp.concatenate(
        [columns(w) for w in (query_weight, key_weight, value_weight, house_weight, beta_weight)] + [same], 2
    )

    def gather(parts):
        parts = lax.all_to_all(parts, "m", 0, 0, tiled=True)
        whole = lax.all_gather(parts, ("g", "b"), axis=0, tiled=False)
        whole = whole.reshape((groups, batch) + parts.shape)
        return jnp.transpose(whole, (0, 2, 1, 3, 4)).reshape(devices * parts.shape[1], parts.shape[2])

    def unit_columns(weight):
        parts = weight.astype(BF16).reshape(rows, groups, GROUP, batch, hidden_rows)
        return jnp.transpose(parts, (2, 0, 1, 3, 4)).reshape(GROUP, rows, hidden_own)

    first = gather(first_parts)
    feed = gather(jnp.concatenate([unit_columns(gate_weight), unit_columns(up_weight)], 2))
    gate_full, up_full = feed[:, :hidden_own], feed[:, hidden_own:]
    down_full = lax.all_gather(down_weight.astype(BF16), ("g", "b"), axis=0, tiled=True)
    out_all = lax.all_gather(out_weight.astype(BF16), ("g", "m", "b"), axis=0, tiled=True)
    out_full = lax.dynamic_slice_in_dim(out_all, member * WIDE, WIDE)

    def group_gather(value):
        return lax.all_gather(value, "m", axis=0, tiled=True)

    def group_sum(value):
        return lax.psum_scatter(value.astype(BF16), "m", scatter_dimension=0, tiled=True).astype(F32)

    extra = first[:, 4 * WIDE :]
    gain_one = extra[:, OWN].astype(F32)
    gain_two = extra[:, OWN + 1].astype(F32)
    docs = extra[:, OWN + 2 : OWN + 2 + doc_columns].astype(jnp.int32)
    docs = docs.reshape(devices, -1)[:, :block_rows].reshape(groups, GROUP, batch, block_rows)
    docs = lax.dynamic_index_in_dim(docs, line, 2, keepdims=False).reshape(groups, GROUP * block_rows)
    doc_key = jnp.stack(
        [
            jnp.where(place >= hop, lax.dynamic_index_in_dim(docs, jnp.maximum(place - hop, 0), 0, keepdims=False), -1)
            for hop in range(hops + 1)
        ]
    )[:, None, :]
    doc_query = lax.dynamic_index_in_dim(docs, place, 0, keepdims=False)[:, None]

    tokens_all = group_gather(tokens[0])
    cotangent_all = group_gather(cotangent[0])
    inputs = tokens[0].astype(F32)
    normed = rms_scale(tokens_all.astype(F32), gain_one).astype(BF16)
    projected = dot(normed, first)
    query, key, value, within, maps, inverse = prepare(projected)
    attended, attended_low, stats, moved, values = attend(
        groups, hops, query, key, value, within, maps, doc_query, doc_key
    )
    hidden = inputs + group_sum(dot(attended_low, out_full))
    normed_two = group_gather(rms_scale(hidden, gain_two).astype(BF16))
    gate = dot(normed_two, gate_full)
    up = dot(normed_two, up_full)
    sigmoid = jax.nn.sigmoid(gate)
    silu = gate * sigmoid
    active = (silu * up).astype(BF16)
    output = (hidden + group_sum(dot(active, down_full))).astype(BF16)[None]

    active_grad = dot(cotangent_all, down_full, NT)
    gate_grad = (active_grad * up * (sigmoid * (1.0 + gate * (1.0 - sigmoid)))).astype(BF16)
    up_grad = (active_grad * silu).astype(BF16)
    normed_two_grad = group_sum(dot(gate_grad, gate_full, NT) + dot(up_grad, up_full, NT))
    hidden_back, gain_two_grad = rms_back(hidden, gain_two, normed_two_grad)
    hidden_grad = cotangent[0].astype(F32) + hidden_back
    branch_grad = group_gather(hidden_grad.astype(BF16))
    att_grad = dot(branch_grad, out_full, NT).astype(BF16)
    query_grad, key_grad, within_grad, map_grad, value_grad = attend_back(
        groups, hops, query, value, within, maps, doc_query, doc_key, attended, stats, moved, values, att_grad
    )
    rows_grad = prepare_back(projected, inverse, query_grad, key_grad, within_grad, map_grad, value_grad)
    normed_grad = group_sum(dot(rows_grad, first, NT))
    inputs_back, gain_one_grad = rms_back(inputs, gain_one, normed_grad)
    tokens_grad = (hidden_grad + inputs_back).astype(BF16)[None]

    def scatter(full):
        parts = full.astype(BF16).reshape(groups, GROUP, batch, rows, full.shape[1])
        parts = jnp.transpose(parts, (0, 2, 1, 3, 4)).reshape(groups * batch, GROUP, rows, full.shape[1])
        parts = lax.psum_scatter(parts, ("g", "b"), scatter_dimension=0, tiled=False)
        return lax.all_to_all(parts, "m", 0, 0, tiled=True).astype(F32)

    first_grad = dot(normed, rows_grad, TN)
    lane = iota(1, (1, first_grad.shape[1]))
    first_grad = jnp.where(lane == 4 * WIDE + OWN, gain_one_grad[:, None], first_grad)
    first_grad = jnp.where(lane == 4 * WIDE + OWN + 1, gain_two_grad[:, None], first_grad)
    first_grad = scatter(first_grad)

    def whole_columns(parts):
        return jnp.transpose(parts, (1, 0, 2)).reshape(rows, -1)

    query_weight_grad, key_weight_grad, value_weight_grad, house_weight_grad = [
        whole_columns(first_grad[:, :, part * WIDE : (part + 1) * WIDE]) for part in range(4)
    ]
    beta_weight_grad = whole_columns(first_grad[:, :, 4 * WIDE : 4 * WIDE + OWN])
    gains_grad = jnp.sum(first_grad[:, :, 4 * WIDE + OWN : 4 * WIDE + OWN + 2], axis=0)
    feed_grad = scatter(
        jnp.concatenate([dot(normed_two, gate_grad, TN), dot(normed_two, up_grad, TN)], 1)
    )

    def unit_whole(parts):
        parts = parts.reshape(GROUP, rows, groups, batch, hidden_rows)
        return jnp.transpose(parts, (1, 2, 0, 3, 4)).reshape(rows, -1)

    gate_weight_grad = unit_whole(feed_grad[:, :, :hidden_own])
    up_weight_grad = unit_whole(feed_grad[:, :, hidden_own:])
    down_weight_grad = lax.psum_scatter(
        dot(active, cotangent_all, TN).astype(BF16), ("g", "b"), scatter_dimension=0, tiled=True
    ).astype(F32)
    out_grad = lax.psum(dot(attended_low, branch_grad, TN).astype(BF16), ("g", "b"))
    out_grad = group_gather(out_grad)
    own = (place * GROUP + member) * batch + line
    out_weight_grad = lax.dynamic_slice_in_dim(out_grad, own * rows, rows).astype(F32)
    return (
        output,
        tokens_grad,
        gains_grad[:, 0],
        query_weight_grad,
        key_weight_grad,
        value_weight_grad,
        house_weight_grad,
        beta_weight_grad,
        out_weight_grad,
        gains_grad[:, 1],
        gate_weight_grad,
        up_weight_grad,
        down_weight_grad,
    )


def solution(mesh):
    groups = mesh.shape["seq"] // GROUP
    inner = Mesh(mesh.devices.reshape(groups, GROUP, mesh.shape["batch"]), ("g", "m", "b"))
    line = P("b", ("g", "m"), None)
    vector = P(("g", "m", "b"))
    matrix = P(("g", "m", "b"), None)
    in_specs = (line, P("b", ("g", "m")), vector) + (matrix,) * 6 + (vector,) + (matrix,) * 3 + (line,)
    out_specs = (line, line, vector) + (matrix,) * 6 + (vector,) + (matrix,) * 3
    return jax.shard_map(on_device, mesh=inner, in_specs=in_specs, out_specs=out_specs, check_vma=False)
```

```python
import functools

import jax
import jax.numpy as jnp
from jax import lax
from jax.experimental import pallas as pl
from jax.experimental.pallas import tpu as pltpu
from jax.sharding import Mesh
from jax.sharding import PartitionSpec as P

HEADS = 12
HEAD_DIM = 128
GROUP = 4
OWN = HEADS // GROUP
WIDE = OWN * HEAD_DIM
BLOCK = 128
EXTRA = 128
EPSILON = 1e-06
NEGATIVE = -1e30
SCALE = HEAD_DIM ** (-0.5)
MESH = pl.DeviceIdType.MESH
F32 = jnp.float32
BF16 = jnp.bfloat16
NN = (((1,), (0,)), ((), ()))
NT = (((1,), (1,)), ((), ()))
TN = (((0,), (0,)), ((), ()))


def dot(left, right, dims=NN):
    return lax.dot_general(left, right, dims, preferred_element_type=F32)


def split(value):
    high = value.astype(BF16)
    return high, (value - high.astype(F32)).astype(BF16)


def dot3(left, right, dims=NN):
    left_high, left_low = split(left)
    right_high, right_low = split(right)
    return dot(left_high, right_high, dims) + (
        dot(left_high, right_low, dims) + dot(left_low, right_high, dims)
    )


def dot2(left, right, dims=NN):
    high, low = split(right)
    return dot(left, high, dims) + dot(left, low, dims)


def tile(index, count=1):
    return pl.ds(index * BLOCK, count * BLOCK)


def iota(axis, shape=(BLOCK, BLOCK)):
    return lax.broadcasted_iota(jnp.int32, shape, axis)


def invert(strict):
    row, col = iota(0), iota(1)
    eye = jnp.where(row == col, 1.0, 0.0)

    def part(size):
        return (row // (2 * size) == col // (2 * size)) & (row // size > col // size)

    totals = [eye - jnp.where(part(1), value, 0.0) for value in strict]
    size = 2
    while size < BLOCK:
        mask = part(size)
        pieces = [jnp.where(mask, value, 0.0) for value in strict]
        inner = [dot3(piece, total) for piece, total in zip(pieces, totals)]
        outer = [dot3(total, value) for total, value in zip(totals, inner)]
        totals = [total - value for total, value in zip(totals, outer)]
        size *= 2
    return totals


def unit_of(house):
    scale = lax.rsqrt(jnp.sum(house * house, axis=-1, keepdims=True) + EPSILON)
    return house * scale, scale


def products(query, key, unit):
    both = dot3(jnp.concatenate([unit, query], 0), jnp.concatenate([unit, key], 0), NT)
    return both[:BLOCK, :BLOCK], both[:BLOCK, BLOCK:], both[BLOCK:, :BLOCK], both[BLOCK:, BLOCK:]


def prepare_blocks(first, last, rows_ref, query_ref, key_ref, value_ref, within_ref, map_ref, inverse_ref):
    row, col = iota(0), iota(1)

    def one_block(block, carry):
        at = tile(block)
        kept, strict = [], []
        for head in range(OWN):
            query, key, value, house = [
                rows_ref[at, pl.ds(part * WIDE + head * BLOCK, BLOCK)] for part in range(4)
            ]
            rate = rows_ref[at, pl.ds(4 * WIDE, EXTRA)][:, head : head + 1]
            value_ref[at, tile(head)] = value.astype(BF16)
            unit, _ = unit_of(house)
            strength = 2.0 * jax.nn.sigmoid(rate)
            unit_unit, unit_key, query_unit, query_key = products(query, key, unit)
            strict.append(jnp.where(row > col, strength * unit_unit, 0.0))
            reach = jnp.where(row > col, strength * unit_key, 0.0)
            project = jnp.where(row >= col, query_unit, 0.0)
            kept.append((query, key, unit, strength, reach, project, query_key))
        inverses = invert(strict)
        for head in range(OWN):
            query, key, unit, strength, reach, project, query_key = kept[head]
            inverse = inverses[head]
            solved = dot3(inverse, jnp.concatenate([strength * unit, reach], 1))
            from_query = dot3(project, solved)
            from_unit = dot3(solved, unit, TN)
            query_ref[at, tile(head)] = (query - from_query[:, :BLOCK]).astype(BF16)
            within_ref[at, tile(head)] = query_key - from_query[:, BLOCK:]
            map_ref[at, tile(head)] = jnp.where(row == col, 1.0, 0.0) - from_unit[:BLOCK]
            key_ref[at, tile(head)] = (key - from_unit[BLOCK:]).astype(BF16)
            inverse_ref[at, tile(head)] = inverse
        return carry

    lax.fori_loop(first, last, one_block, 0)


def prepare_back_blocks(rows_ref, inverse_ref, query_grad_ref, key_grad_ref, within_grad_ref, map_grad_ref, value_grad_ref, out_ref):
    row, col = iota(0), iota(1)

    def one_block(block, carry):
        at = tile(block)
        rates = jnp.zeros((BLOCK, EXTRA), F32)
        for head in range(OWN):
            query, key, value, house = [
                rows_ref[at, pl.ds(part * WIDE + head * BLOCK, BLOCK)] for part in range(4)
            ]
            rate = rows_ref[at, pl.ds(4 * WIDE, EXTRA)][:, head : head + 1]
            query_grad = query_grad_ref[at, tile(head)]
            key_grad = key_grad_ref[at, tile(head)]
            within_grad = within_grad_ref[at, tile(head)]
            map_grad = map_grad_ref[at, tile(head)]
            inverse = inverse_ref[at, tile(head)]
            unit, scale = unit_of(house)
            strength = 2.0 * jax.nn.sigmoid(rate)
            unit_unit, unit_key, query_unit, query_key = products(query, key, unit)
            reach = jnp.where(row > col, strength * unit_key, 0.0)
            project = jnp.where(row >= col, query_unit, 0.0)
            solved = dot3(inverse, jnp.concatenate([strength * unit, reach], 1))
            both_grad = jnp.concatenate([query_grad, within_grad], 1)
            project_grad = jnp.where(row >= col, -dot3(both_grad, solved, NT), 0.0)
            solved_grad = -(
                dot3(project, both_grad, TN)
                + dot3(unit, jnp.concatenate([map_grad, key_grad], 0), NT)
            )
            given_grad = dot3(inverse, solved_grad, TN)
            strict_grad = jnp.where(row > col, -dot3(given_grad, solved, NT), 0.0)
            scaled_grad = given_grad[:, :BLOCK]
            reach_grad = jnp.where(row > col, given_grad[:, BLOCK:], 0.0)
            strength_grad = jnp.sum(
                scaled_grad * unit + reach_grad * unit_key + strict_grad * unit_unit, axis=1, keepdims=True
            )
            reach_part = strength * reach_grad
            inner_part = strength * strict_grad
            unit_grad = (
                strength * scaled_grad
                + dot3(reach_part, key)
                + dot3(inner_part + inner_part.T, unit)
                + dot3(project_grad, query, TN)
                - dot3(solved[:, :BLOCK], map_grad)
                - dot3(solved[:, BLOCK:], key_grad)
            )
            query_out = query_grad + dot3(within_grad, key) + dot3(project_grad, unit)
            key_out = key_grad + dot3(within_grad, query, TN) + dot3(reach_part, unit, TN)
            house_out = scale * (unit_grad - unit * jnp.sum(unit * unit_grad, axis=1, keepdims=True))
            rate_out = strength_grad * strength * (1.0 - 0.5 * strength)
            rates = jnp.where(iota(1, (BLOCK, EXTRA)) == head, rate_out, rates)
            out_ref[at, pl.ds(head * BLOCK, BLOCK)] = query_out.astype(BF16)
            out_ref[at, pl.ds(WIDE + head * BLOCK, BLOCK)] = key_out.astype(BF16)
            out_ref[at, pl.ds(2 * WIDE + head * BLOCK, BLOCK)] = value_grad_ref[at, tile(head)].astype(BF16)
            out_ref[at, pl.ds(3 * WIDE + head * BLOCK, BLOCK)] = house_out.astype(BF16)
        out_ref[at, pl.ds(4 * WIDE, EXTRA)] = rates.astype(BF16)
        return carry

    lax.fori_loop(0, GROUP, one_block, 0)


def remote(source, target, send, recv, device):
    return pltpu.make_async_remote_copy(
        src_ref=source, dst_ref=target, send_sem=send, recv_sem=recv, device_id=device, device_id_type=MESH
    )


class Place:
    def __init__(self, groups, lines):
        self.groups, self.lines = groups, lines
        self.g, self.m, self.b = lax.axis_index("g"), lax.axis_index("m"), lax.axis_index("b")
        self.below, self.above = self.g > 0, self.g < groups - 1

    def other(self, offset):
        return {1: self.m + 1 - 2 * (self.m % 2), 2: (self.m + 2) % GROUP, 3: GROUP - 1 - self.m}[offset]

    def member(self, offset):
        return {"g": self.g, "m": self.other(offset), "b": self.b}

    def up(self):
        return {"g": self.g + 1, "m": self.m, "b": self.b}

    def down(self):
        return {"g": self.g - 1, "m": self.m, "b": self.b}

    def across(self):
        return {"g": self.g, "m": self.m, "b": 1 - self.b}

    def meet(self, members=True, chain=True, lines=True):
        barrier = pltpu.get_barrier_semaphore()

        def greet(device):
            pl.semaphore_signal(barrier, 1, device_id=device, device_id_type=MESH)

        count = 0
        if members:
            for offset in range(1, GROUP):
                greet(self.member(offset))
            count = count + GROUP - 1
        if lines:
            greet(self.across())
            count = count + 1
        if chain:
            pl.when(self.above)(lambda: greet(self.up()))
            pl.when(self.below)(lambda: greet(self.down()))
            count = count + self.above.astype(jnp.int32) + self.below.astype(jnp.int32)
        pl.semaphore_wait(barrier, count)


class Gather:
    SEMS = 8

    def __init__(self, place, parts, full, sems, mixed=True):
        self.place, self.parts, self.full, self.mixed = place, parts, full, mixed
        (self.part_send, self.part_recv, self.up_send, self.down_send, self.chain_recv, self.line_send, self.line_recv,
         self.own_sem) = sems

    @staticmethod
    def scratch(groups):
        dma = pltpu.SemaphoreType.DMA
        return [dma((GROUP,)), dma((GROUP,)), dma((groups,)), dma((groups,)), dma((groups,)), dma((groups,)), dma((groups,)), dma((1,))]

    def unit(self, group, line):
        return self.full.at[group, :, line] if self.mixed else self.full.at[group, line]

    def own(self):
        p = self.place
        if self.mixed:
            return pltpu.make_async_copy(self.parts.at[p.m], self.full.at[p.g, p.m, p.b], self.own_sem.at[0])
        return pltpu.make_async_copy(self.parts, self.full.at[p.g, p.b], self.own_sem.at[0])

    def part(self, offset):
        p = self.place
        other = p.other(offset)
        return remote(
            self.parts.at[other], self.full.at[p.g, p.m, p.b], self.part_send.at[offset], self.part_recv.at[offset], p.member(offset)
        )

    def start(self):
        if self.mixed:
            for offset in (2, 3, 1):
                self.part(offset).start()
        self.own().start()

    def chain(self, source, up):
        p = self.place
        unit = self.unit(source, p.b)
        sems = self.up_send if up else self.down_send
        return remote(unit, unit, sems.at[source], self.chain_recv.at[source], p.up() if up else p.down())

    def across(self, source):
        p = self.place
        unit = self.unit(source, p.b)
        return remote(unit, unit, self.line_send.at[source], self.line_recv.at[source], p.across())

    def begin(self):
        p = self.place
        self.own().wait()
        if self.mixed:
            for offset in (2, 3, 1):
                self.part(offset).wait()
        pl.when(p.above)(lambda: self.chain(p.g, True).start())
        pl.when(p.below)(lambda: self.chain(p.g, False).start())
        self.across(p.g).start()

    def step(self, distance):
        p = self.place

        @pl.when(p.g >= distance)
        def _():
            source = p.g - distance
            self.chain(source, True).wait_recv()
            pl.when(p.above)(lambda: self.chain(source, True).start())
            self.across(source).start()

        @pl.when(p.g + distance < p.groups)
        def _():
            source = p.g + distance
            self.chain(source, False).wait_recv()
            pl.when(p.below)(lambda: self.chain(source, False).start())
            self.across(source).start()

    def finish(self):
        p = self.place

        def settle(source, carry):
            self.across(source).wait()
            pl.when(p.above & (source <= p.g))(lambda: self.chain(source, True).wait_send())
            pl.when(p.below & (source >= p.g))(lambda: self.chain(source, False).wait_send())
            return carry

        lax.fori_loop(0, p.groups, settle, 0)


class HomeGather:
    def __init__(self, place, part, full, sems):
        self.place, self.part_ref, self.full = place, part, full
        self.home = place.groups // GROUP
        self.part_send, self.part_recv, self.up_send, self.down_send, self.chain_recv, self.line_send, self.line_recv = sems

    @staticmethod
    def scratch(groups):
        home = groups // GROUP
        dma = pltpu.SemaphoreType.DMA
        return [dma((1,)), dma((GROUP,)), dma((home,)), dma((home,)), dma((home,)), dma((home,)), dma((home,))]

    def at_home(self):
        return self.place.m == self.place.g // self.home

    def slot(self):
        p = self.place
        return self.full.at[p.g % self.home, p.m, p.b]

    def hand(self):
        p = self.place
        keeper = p.g // self.home
        device = {"g": p.g, "m": keeper, "b": p.b}
        return remote(self.part_ref, self.slot(), self.part_send.at[0], self.part_recv.at[p.m], device)

    def taken(self, source):
        p = self.place
        target = self.full.at[p.g % self.home, source, p.b]
        return remote(self.part_ref, target, self.part_send.at[0], self.part_recv.at[source], p.member(1))

    def own(self):
        return pltpu.make_async_copy(self.part_ref, self.slot(), self.part_send.at[0])

    def start(self):
        pl.when(self.at_home())(lambda: self.own().start())
        pl.when(jnp.logical_not(self.at_home()))(lambda: self.hand().start())

    def chain(self, slot, up):
        p = self.place
        unit = self.full.at[slot, :, p.b]
        sems = self.up_send if up else self.down_send
        return remote(unit, unit, sems.at[slot], self.chain_recv.at[slot], p.up() if up else p.down())

    def across(self, slot):
        p = self.place
        unit = self.full.at[slot, :, p.b]
        return remote(unit, unit, self.line_send.at[slot], self.line_recv.at[slot], p.across())

    def begin(self):
        p = self.place

        @pl.when(self.at_home())
        def _():
            self.own().wait()
            for offset in range(1, GROUP):
                self.taken(p.other(offset)).wait_recv()
            slot = p.g % self.home
            pl.when(p.above)(lambda: self.chain(slot, True).start())
            pl.when(p.below)(lambda: self.chain(slot, False).start())
            self.across(slot).start()

        pl.when(jnp.logical_not(self.at_home()))(lambda: self.hand().wait_send())

    def step(self, distance):
        p = self.place
        for slot in range(self.home):
            source = p.m * self.home + slot

            @pl.when(p.g - source == distance)
            def _():
                self.chain(slot, True).wait_recv()
                pl.when(p.above)(lambda: self.chain(slot, True).start())
                self.across(slot).start()

            @pl.when(source - p.g == distance)
            def _():
                self.chain(slot, False).wait_recv()
                pl.when(p.below)(lambda: self.chain(slot, False).start())
                self.across(slot).start()

    def finish(self):
        p = self.place
        for slot in range(self.home):
            source = p.m * self.home + slot
            self.across(slot).wait()
            pl.when(p.above & (p.g >= source))(lambda: self.chain(slot, True).wait_send())
            pl.when(p.below & (p.g <= source))(lambda: self.chain(slot, False).wait_send())


class Scatter:
    def __init__(self, place, partial, result, refs):
        self.place, self.partial, self.result = place, partial, result
        (self.land, self.chain_land, self.leave, self.mine_sem, self.line_send, self.line_recv, self.chain_send,
         self.chain_recv, self.part_send, self.part_recv) = refs
        self.parts = partial.shape[1]

    @staticmethod
    def scratch(groups, shape):
        dma = pltpu.SemaphoreType.DMA
        unit = (shape[1],) + tuple(shape[3:])
        return [
            pltpu.VMEM((groups,) + unit, BF16),
            pltpu.VMEM((groups + 1,) + unit, BF16),
            pltpu.VMEM((groups,) + unit, BF16),
            dma((groups,)),
            dma((groups,)),
            dma((groups,)),
            dma((groups,)),
            dma((groups + 1,)),
            dma((GROUP,)),
            dma((GROUP,)),
        ]

    def load(self, target):
        return pltpu.make_async_copy(self.partial.at[target, :, self.place.b], self.leave.at[target], self.mine_sem.at[target])

    def line(self, target):
        p = self.place
        return remote(
            self.partial.at[target, :, 1 - p.b], self.land.at[target], self.line_send.at[target], self.line_recv.at[target], p.across()
        )

    def up(self, target):
        p = self.place
        return remote(
            self.leave.at[target], self.chain_land.at[target], self.chain_send.at[target], self.chain_recv.at[target], p.up()
        )

    def down(self, target, slot):
        p = self.place
        return remote(
            self.leave.at[target], self.chain_land.at[slot], self.chain_send.at[target], self.chain_recv.at[slot], p.down()
        )

    def send_up(self, target):
        self.up(target).start()

    def send_down(self, target):
        p = self.place
        pl.when(p.g - 1 == target)(lambda: self.down(target, p.groups).start())
        pl.when(p.g - 1 != target)(lambda: self.down(target, target).start())

    def arrived(self, slot):
        p = self.place
        return remote(self.leave.at[0], self.chain_land.at[slot], self.chain_send.at[0], self.chain_recv.at[slot], p.across())

    def order(self, act):
        p = self.place
        for step in range(p.groups - 1):
            pl.when(p.groups - 1 - step > p.g)(lambda: act(p.groups - 1 - step))
            pl.when(step < p.g)(lambda: act(step))
        act(p.g)

    def start(self):
        p = self.place

        def act(target):
            self.line(target).start()
            self.load(target).start()

        self.order(act)

        @pl.when(jnp.logical_not(p.below))
        def _():
            self.chain_land[p.g] = jnp.zeros(self.chain_land.shape[1:], BF16)

        @pl.when(jnp.logical_not(p.above))
        def _():
            self.chain_land[p.groups] = jnp.zeros(self.chain_land.shape[1:], BF16)

    def both(self, target, part):
        return self.leave[target, part].astype(F32) + self.land[target, part].astype(F32)

    def step(self, step):
        p = self.place
        above, below = p.groups - 1 - step, step

        def ready(target):
            self.load(target).wait()
            self.line(target).wait_recv()

        def send(target, inner, copy):
            @pl.when(inner)
            def _():
                self.arrived(target).wait_recv()
                for part in range(self.parts):
                    self.leave[target, part] = (self.both(target, part) + self.chain_land[target, part].astype(F32)).astype(BF16)

            @pl.when(jnp.logical_not(inner))
            def _():
                for part in range(self.parts):
                    self.leave[target, part] = self.both(target, part).astype(BF16)

            copy(target)

        @pl.when(above > p.g)
        def _():
            ready(above)
            send(above, p.below, self.send_up)

        @pl.when(below < p.g)
        def _():
            ready(below)
            send(below, p.above, self.send_down)

    def hand(self, offset):
        p = self.place
        return remote(
            self.leave.at[p.g, p.other(offset)], self.result.at[p.m], self.part_send.at[offset], self.part_recv.at[offset], p.member(offset)
        )

    def last(self):
        p = self.place
        self.load(p.g).wait()
        self.line(p.g).wait_recv()
        pl.when(p.below)(lambda: self.arrived(p.g).wait_recv())
        pl.when(p.above)(lambda: self.arrived(p.groups).wait_recv())
        for part in range(self.parts):
            total = self.both(p.g, part) + self.chain_land[p.g, part].astype(F32) + self.chain_land[p.groups, part].astype(F32)
            if self.parts == 1:
                self.result[part] = total.astype(self.result.dtype)
            else:
                self.leave[p.g, part] = total.astype(BF16)
        if self.parts > 1:
            for offset in (2, 3, 1):
                self.hand(offset).start()
            self.result[p.m] = self.leave[p.g, p.m]

    def finish(self):
        p = self.place
        for target in range(p.groups):
            self.line(target).wait_send()
            pl.when(p.g != target)(lambda: self.up(target).wait_send())
        if self.parts > 1:
            for offset in (2, 3, 1):
                self.hand(offset).wait()


class HomeScatter:
    def __init__(self, place, partial, result, refs):
        self.place, self.partial, self.result = place, partial, result
        (self.land, self.chain_land, self.leave, self.mine_sem, self.line_send, self.line_recv, self.chain_send,
         self.chain_recv, self.part_send, self.part_recv) = refs
        self.home = place.groups // GROUP

    @staticmethod
    def scratch(groups, shape):
        dma = pltpu.SemaphoreType.DMA
        home = groups // GROUP
        unit = (GROUP,) + tuple(shape[3:])
        return [
            pltpu.VMEM((home,) + unit, BF16),
            pltpu.VMEM((home, 2) + unit, BF16),
            pltpu.VMEM((home,) + unit, BF16),
            dma((home,)),
            dma((home,)),
            dma((home,)),
            dma((home,)),
            dma((home, 2)),
            dma((GROUP,)),
            dma((1,)),
        ]

    def load(self, slot):
        return pltpu.make_async_copy(self.partial.at[slot, :, self.place.b], self.leave.at[slot], self.mine_sem.at[slot])

    def line(self, slot):
        p = self.place
        return remote(self.partial.at[slot, :, 1 - p.b], self.land.at[slot], self.line_send.at[slot], self.line_recv.at[slot], p.across())

    def chain(self, slot, up):
        p = self.place
        side = 0 if up else 1
        return remote(
            self.leave.at[slot], self.chain_land.at[slot, side], self.chain_send.at[slot], self.chain_recv.at[slot, side],
            p.up() if up else p.down(),
        )

    def start(self):
        p = self.place
        for slot in range(self.home):
            self.line(slot).start()
            self.load(slot).start()
        for side, present in ((0, p.below), (1, p.above)):

            @pl.when(jnp.logical_not(present))
            def _():
                for slot in range(self.home):
                    self.chain_land[slot, side] = jnp.zeros(self.chain_land.shape[2:], BF16)

    def add(self, slot, sides):
        for part in range(GROUP):
            total = self.leave[slot, part].astype(F32) + self.land[slot, part].astype(F32)
            for side in sides:
                total = total + self.chain_land[slot, side, part].astype(F32)
            self.leave[slot, part] = total.astype(BF16)

    def step(self, step):
        p = self.place
        for slot in range(self.home):
            target = p.m * self.home + slot

            @pl.when((p.g < target) & (p.g == step))
            def _():
                self.load(slot).wait()
                self.line(slot).wait_recv()
                pl.when(p.below)(lambda: self.chain(slot, True).wait_recv())
                self.add(slot, [0])
                self.chain(slot, True).start()

            @pl.when((p.g > target) & (p.groups - 1 - p.g == step))
            def _():
                self.load(slot).wait()
                self.line(slot).wait_recv()
                pl.when(p.above)(lambda: self.chain(slot, False).wait_recv())
                self.add(slot, [1])
                self.chain(slot, False).start()

    def hand(self, slot, other):
        p = self.place
        return remote(
            self.leave.at[slot, other], self.result, self.part_send.at[other], self.part_recv.at[0], {"g": p.g, "m": other, "b": p.b}
        )

    def last(self):
        p = self.place

        @pl.when(p.m == p.g // self.home)
        def _():
            slot = p.g % self.home
            self.load(slot).wait()
            self.line(slot).wait_recv()
            pl.when(p.below)(lambda: self.chain(slot, True).wait_recv())
            pl.when(p.above)(lambda: self.chain(slot, False).wait_recv())
            self.add(slot, [0, 1])
            for offset in range(1, GROUP):
                self.hand(slot, p.other(offset)).start()
            self.result[...] = self.leave[slot, p.m]

    def finish(self):
        p = self.place
        keeper = p.m == p.g // self.home

        @pl.when(keeper)
        def _():
            for offset in range(1, GROUP):
                self.hand(p.g % self.home, p.other(offset)).wait_send()

        pl.when(jnp.logical_not(keeper))(lambda: self.hand(0, p.other(1)).wait_recv())
        for slot in range(self.home):
            self.line(slot).wait_send()
            pl.when(p.g != p.m * self.home + slot)(lambda: self.chain(slot, True).wait_send())


CHUNKS = 4


class GroupSum:
    def __init__(self, place, partial, refs):
        self.place, self.partial = place, partial
        self.pair_land, self.leave, self.land, self.pair_send, self.pair_recv, self.send, self.recv = refs
        self.size = partial.shape[0] // GROUP
        self.rows = self.size // CHUNKS

    @staticmethod
    def scratch(size, width):
        dma = pltpu.SemaphoreType.DMA
        return [
            pltpu.VMEM((2, size, width), BF16),
            pltpu.VMEM((size, width), BF16),
            pltpu.VMEM((size, width), BF16),
            dma((2, CHUNKS)),
            dma((2, CHUNKS)),
            dma((CHUNKS,)),
            dma((CHUNKS,)),
        ]

    def at(self, chunk, member=0):
        return pl.ds(pl.multiple_of(member * self.size + chunk * self.rows, self.rows), self.rows)

    def pair(self, chunk, far):
        p = self.place
        member = p.other(3 if far else 1)
        slot = 1 if far else 0
        return remote(
            self.partial.at[self.at(chunk, member)], self.pair_land.at[slot, self.at(chunk)], self.pair_send.at[slot, chunk],
            self.pair_recv.at[slot, chunk], p.member(1),
        )

    def cross(self, chunk):
        return remote(
            self.leave.at[self.at(chunk)], self.land.at[self.at(chunk)], self.send.at[chunk], self.recv.at[chunk], self.place.member(2)
        )

    def start(self):
        for chunk in range(CHUNKS):
            self.pair(chunk, True).start()
        for chunk in range(CHUNKS):
            self.pair(chunk, False).start()

    def pass_on(self, chunk):
        self.pair(chunk, True).wait_recv()
        own = self.partial[self.at(chunk, self.place.other(2)), :].astype(F32)
        self.leave[self.at(chunk), :] = (own + self.pair_land[1, self.at(chunk), :].astype(F32)).astype(BF16)
        self.cross(chunk).start()

    def take(self, chunk):
        self.pair(chunk, False).wait_recv()
        self.cross(chunk).wait_recv()
        own = self.partial[self.at(chunk, self.place.m), :].astype(F32)
        return own + self.pair_land[0, self.at(chunk), :].astype(F32) + self.land[self.at(chunk), :].astype(F32)

    def finish(self):
        for chunk in range(CHUNKS):
            self.pair(chunk, True).wait_send()
            self.pair(chunk, False).wait_send()
            self.cross(chunk).wait_send()


class GroupGather:
    def __init__(self, place, whole, refs):
        self.place, self.whole = place, whole
        self.send, self.recv = refs
        self.size = whole.shape[0] // GROUP
        self.rows = self.size // CHUNKS

    @staticmethod
    def scratch():
        dma = pltpu.SemaphoreType.DMA
        return [dma((3, CHUNKS)), dma((3, CHUNKS))]

    def at(self, chunk, member):
        return pl.ds(pl.multiple_of(member * self.size + chunk * self.rows, self.rows), self.rows)

    def copy(self, chunk, way):
        p = self.place
        rows = self.whole.at[self.at(chunk, p.other(2) if way == 2 else p.m)]
        return remote(rows, rows, self.send.at[way, chunk], self.recv.at[way, chunk], p.member(2 if way == 0 else 1))

    def give(self, chunk):
        self.copy(chunk, 0).start()
        self.copy(chunk, 1).start()

    def pass_on(self, chunk):
        self.copy(chunk, 0).wait_recv()
        self.copy(chunk, 2).start()

    def finish(self):
        for chunk in range(CHUNKS):
            self.copy(chunk, 1).wait_recv()
            self.copy(chunk, 2).wait_recv()
            for way in range(3):
                self.copy(chunk, way).wait_send()


def masked(scores, counts):
    return jnp.where(counts, scores * SCALE, NEGATIVE)


class Pauses:
    def __init__(self, *steps):
        self.steps = list(steps)

    def __call__(self):
        if self.steps:
            for act in self.steps.pop(0):
                act()

    def rest(self):
        while self.steps:
            self()


def several(refs, *counts):
    refs = list(refs)
    taken = []
    for count in counts:
        taken.append(refs[:count])
        refs = refs[count:]
    return taken


def attend_kernel(
    groups,
    hops,
    rows_ref,
    doc_query_ref,
    doc_key_ref,
    out_part_ref,
    feed_parts_ref,
    query_ref,
    value_ref,
    within_ref,
    map_ref,
    inverse_ref,
    attended_ref,
    low_ref,
    stats_ref,
    moved_ref,
    values_ref,
    out_full_ref,
    feed_full_ref,
    key_ref,
    leave_ref,
    top_ref,
    total_ref,
    accum_ref,
    key_send,
    key_recv,
    value_send,
    value_recv,
    *sems,
):
    here = Place(groups, feed_full_ref.shape[2])
    here.meet()
    place, has_next, following = here.g, here.above, here.up()
    home_sems, feed_sems = several(sems, len(HomeGather.scratch(groups)), len(Gather.scratch(groups)))
    out_gather = HomeGather(here, out_part_ref, out_full_ref, home_sems)
    feed_gather = Gather(here, feed_parts_ref, feed_full_ref, feed_sems)
    out_gather.start()
    feed_gather.start()
    pauses = Pauses(
        *[
            (functools.partial(out_gather.step, distance), functools.partial(feed_gather.step, distance))
            for distance in range(1, groups)
        ]
    )
    prepared = (rows_ref, query_ref, key_ref, value_ref, within_ref, map_ref, inverse_ref)
    prepare_blocks(0, GROUP // 2, *prepared)
    out_gather.begin()
    feed_gather.begin()
    prepare_blocks(GROUP // 2, GROUP, *prepared)

    def value_copy(source, slot):
        return pltpu.make_async_remote_copy(
            src_ref=source,
            dst_ref=values_ref.at[slot],
            send_sem=value_send.at[slot],
            recv_sem=value_recv.at[slot],
            device_id=following,
            device_id_type=MESH,
        )

    def key_copy(slot):
        return pltpu.make_async_remote_copy(
            src_ref=leave_ref.at[slot],
            dst_ref=moved_ref.at[slot + 1, 0],
            send_sem=key_send.at[slot],
            recv_sem=key_recv.at[slot],
            device_id=following,
            device_id_type=MESH,
        )

    def move(keys, block, head):
        return dot2(keys, map_ref[tile(block), tile(head)]).astype(BF16)

    for head in range(OWN):
        keys = key_ref[tile(0), tile(head)]
        for block in range(1, GROUP):
            moved_ref[0, block, tile(0, block), tile(head)] = keys
            keys = jnp.concatenate([move(keys, block, head), key_ref[tile(block), tile(head)]], 0)
        leave_ref[0, :, tile(head)] = keys

    @pl.when(has_next)
    def _():
        key_copy(0).start()
        value_copy(value_ref, 0).start()

    pauses()

    def row_counts(block, hop, first, count):
        return doc_query_ref[tile(block), :] == doc_key_ref[hop, :, tile(first, count)]

    for block in range(GROUP):
        counts = row_counts(block, 0, 0, block + 1)
        wide = (BLOCK, (block + 1) * BLOCK)
        counts = counts & (iota(0, wide) + block * BLOCK >= iota(1, wide))
        for head in range(OWN):
            scores = within_ref[tile(block), tile(head)]
            if block:
                before = dot(query_ref[tile(block), tile(head)], moved_ref[0, block, tile(0, block), tile(head)], NT)
                scores = jnp.concatenate([before, scores], 1)
            scores = masked(scores, counts)
            top = jnp.max(scores, axis=1, keepdims=True)
            weights = jnp.exp(scores - top)
            top_ref[head, tile(block), :] = jnp.broadcast_to(top, (BLOCK, BLOCK))
            total_ref[head, tile(block), :] = jnp.broadcast_to(jnp.sum(weights, axis=1, keepdims=True), (BLOCK, BLOCK))
            accum_ref[tile(block), tile(head)] = dot(weights.astype(BF16), value_ref[tile(0, block + 1), tile(head)])

    def hop_step(hop, last):
        @pl.when(place >= hop)
        def _():
            key_copy(hop - 1).wait_recv()
            for head in range(OWN):
                keys = moved_ref[hop, 0, :, tile(head)]
                for block in range(GROUP):
                    if last:
                        if block == GROUP - 1:
                            break
                        keys = move(keys[BLOCK:], block, head)
                        moved_ref[hop, block + 1, tile(block + 1, GROUP - 1 - block), tile(head)] = keys
                    else:
                        keys = move(keys, block, head)
                        if block < GROUP - 1:
                            moved_ref[hop, block + 1, :, tile(head)] = keys
                        else:
                            leave_ref[hop, :, tile(head)] = keys
            value_copy(value_ref, hop - 1).wait_recv()
            if not last:

                @pl.when(has_next)
                def _():
                    key_copy(hop).start()
                    value_copy(values_ref.at[hop - 1], hop).start()

            for block in range(GROUP):
                first = block if last else 0
                count = GROUP - first
                counts = row_counts(block, hop, first, count)
                for head in range(OWN):
                    scores = masked(
                        dot(query_ref[tile(block), tile(head)], moved_ref[hop, block, tile(first, count), tile(head)], NT),
                        counts,
                    )
                    old = top_ref[head, tile(block), :]
                    top = jnp.maximum(old, jnp.broadcast_to(jnp.max(scores, axis=1, keepdims=True), (BLOCK, BLOCK)))
                    factor = jnp.exp(old - top)
                    weights = jnp.exp(scores - jnp.concatenate([top] * count, 1))
                    top_ref[head, tile(block), :] = top
                    total_ref[head, tile(block), :] = total_ref[head, tile(block), :] * factor + jnp.sum(
                        weights, axis=1, keepdims=True
                    )
                    accum_ref[tile(block), tile(head)] = accum_ref[tile(block), tile(head)] * factor + dot(
                        weights.astype(BF16), values_ref[hop - 1, tile(first, count), tile(head)]
                    )

    if hops > 2:

        def between(hop, carry):
            hop_step(hop, False)
            return carry

        lax.fori_loop(1, hops, between, 0)
    else:
        for hop in range(1, hops):
            pauses()
            hop_step(hop, False)
    pauses()
    hop_step(hops, True)

    for block in range(GROUP):
        stats = jnp.zeros((BLOCK, BLOCK), F32)
        for head in range(OWN):
            total = total_ref[head, tile(block), :]
            result = accum_ref[tile(block), tile(head)] / total
            attended_ref[tile(block), tile(head)] = result
            low_ref[tile(block), tile(head)] = result.astype(BF16)
            stats = jnp.where(iota(1) == head, top_ref[head, tile(block), :], stats)
            stats = jnp.where(iota(1) == OWN + head, total, stats)
        stats_ref[tile(block), :] = stats

    def settle(slot, carry):
        @pl.when(has_next & (place >= slot))
        def _():
            key_copy(slot).wait_send()
            value_copy(value_ref, slot).wait_send()

        return carry

    lax.fori_loop(0, hops, settle, 0)
    pauses.rest()
    out_gather.finish()
    feed_gather.finish()


def in_vmem(count):
    return [pl.BlockSpec(memory_space=pltpu.VMEM)] * count


def anywhere(count):
    return [pl.BlockSpec(memory_space=pl.ANY)] * count


def shape(kind, *dims):
    return jax.ShapeDtypeStruct(dims, kind)


def communicating(number, name, vmem=58):
    return {
        "compiler_params": pltpu.CompilerParams(collective_id=number, has_side_effects=True, vmem_limit_bytes=vmem << 20),
        "name": name,
    }


def attend(groups, lines, hops, projected, doc_query, doc_key, out_part, feed_parts):
    length = projected.shape[0]
    rows, width = out_part.shape
    dma = pltpu.SemaphoreType.DMA
    return pl.pallas_call(
        functools.partial(attend_kernel, groups, hops),
        out_shape=[
            shape(BF16, length, WIDE),
            shape(BF16, length, WIDE),
            shape(F32, length, WIDE),
            shape(F32, length, WIDE),
            shape(F32, length, WIDE),
            shape(F32, length, WIDE),
            shape(BF16, length, WIDE),
            shape(F32, length, BLOCK),
            shape(BF16, hops + 1, GROUP, length, WIDE),
            shape(BF16, hops, length, WIDE),
            shape(BF16, groups // GROUP, GROUP, lines, rows, width),
            shape(BF16, groups, GROUP, lines, rows, feed_parts.shape[2]),
        ],
        in_specs=in_vmem(3) + anywhere(2),
        out_specs=in_vmem(10) + anywhere(2),
        scratch_shapes=[
            pltpu.VMEM((length, WIDE), BF16),
            pltpu.VMEM((hops, length, WIDE), BF16),
            pltpu.VMEM((OWN, length, BLOCK), F32),
            pltpu.VMEM((OWN, length, BLOCK), F32),
            pltpu.VMEM((length, WIDE), F32),
            dma((hops,)),
            dma((hops,)),
            dma((hops,)),
            dma((hops,)),
        ]
        + HomeGather.scratch(groups)
        + Gather.scratch(groups),
        **communicating(1, "attend"),
    )(projected, doc_query, doc_key, out_part, feed_parts)


def attend_back_kernel(
    groups,
    hops,
    query_ref,
    value_ref,
    within_ref,
    map_ref,
    doc_query_ref,
    doc_key_ref,
    attended_ref,
    stats_ref,
    moved_ref,
    values_ref,
    att_grad_ref,
    rows_ref,
    inverse_ref,
    feed_partial_ref,
    rows_grad_ref,
    feed_result_ref,
    query_grad_ref,
    key_grad_ref,
    within_grad_ref,
    map_grad_ref,
    value_grad_ref,
    scaled_ref,
    dots_ref,
    direct_ref,
    direct_value_ref,
    running_ref,
    key_slots_ref,
    value_slots_ref,
    key_send,
    key_recv,
    value_send,
    value_recv,
    *refs,
):
    here = Place(groups, feed_partial_ref.shape[2])
    here.meet()
    place, has_next, previous = here.g, here.above, here.down()
    feed_scatter = Scatter(here, feed_partial_ref, feed_result_ref, refs)
    feed_scatter.start()
    pauses = Pauses(*[(functools.partial(feed_scatter.step, step),) for step in range(groups - 1)])

    def key_copy(hop):
        slot = hop - 1
        return pltpu.make_async_remote_copy(
            src_ref=key_slots_ref.at[hop],
            dst_ref=key_slots_ref.at[slot],
            send_sem=key_send.at[slot],
            recv_sem=key_recv.at[slot],
            device_id=previous,
            device_id_type=MESH,
        )

    def value_copy(hop):
        slot = hop - 1
        return pltpu.make_async_remote_copy(
            src_ref=value_slots_ref.at[hop],
            dst_ref=value_slots_ref.at[slot],
            send_sem=value_send.at[slot],
            recv_sem=value_recv.at[slot],
            device_id=previous,
            device_id_type=MESH,
        )

    map_grad_ref[...] = jnp.zeros_like(map_grad_ref)
    query_grad_ref[...] = jnp.zeros_like(query_grad_ref)
    for block in range(GROUP):
        for head in range(OWN):
            at = (tile(block), tile(head))
            grad = att_grad_ref[at].astype(F32)
            total = stats_ref[tile(block), OWN + head : OWN + head + 1]
            scaled_ref[at] = (grad / total).astype(BF16)
            dots = -jnp.sum(grad * attended_ref[at], axis=1, keepdims=True) / total
            dots_ref[head, tile(block), :] = jnp.broadcast_to(dots, (BLOCK, BLOCK))

    def pair(block, head, scores, counts, values):
        count = scores.shape[1] // BLOCK
        top = stats_ref[tile(block), head : head + 1]
        weights = jnp.exp(masked(scores, counts) - top)
        weight_grad = dot(scaled_ref[tile(block), tile(head)], values, NT)
        dots = jnp.concatenate([dots_ref[head, tile(block), :]] * count, 1)
        return weights, weights * (weight_grad + dots) * SCALE

    def row_counts(block, hop, first, count):
        return doc_query_ref[tile(block), :] == doc_key_ref[hop, :, tile(first, count)]

    def hop_direct(hop, last):
        for head in range(OWN):
            direct_value_ref[:, tile(head)] = jnp.zeros((GROUP * BLOCK, BLOCK), F32)
        for block in range(GROUP):
            first = block if last else 0
            count = GROUP - first
            counts = row_counts(block, hop, first, count)
            for head in range(OWN):
                query = query_ref[tile(block), tile(head)]
                keys = moved_ref[hop, block, tile(first, count), tile(head)]
                weights, grad = pair(
                    block, head, dot(query, keys, NT), counts, values_ref[hop - 1, tile(first, count), tile(head)]
                )
                raw = grad.astype(BF16)
                query_grad_ref[tile(block), tile(head)] += dot(raw, keys)
                direct_ref[block, tile(first, count), tile(head)] = dot(raw, query, TN)
                direct_value_ref[tile(first, count), tile(head)] += dot(
                    weights.astype(BF16), scaled_ref[tile(block), tile(head)], TN
                )

    def collect_map(block, head, keys, grads):
        map_grad_ref[tile(block), tile(head)] += dot2(keys, grads, TN)

    def hop_chain(hop, last):
        for head in range(OWN):
            if last:
                grads = direct_ref[GROUP - 1, tile(GROUP - 1), tile(head)]
                for block in range(GROUP - 2, -1, -1):
                    rows = tile(block + 1, GROUP - 1 - block)
                    collect_map(block, head, moved_ref[hop, block, rows, tile(head)], grads)
                    back = dot3(grads, map_ref[tile(block), tile(head)], NT)
                    direct = direct_ref[block, tile(block, GROUP - block), tile(head)]
                    grads = jnp.concatenate([direct[:BLOCK], direct[BLOCK:] + back], 0)
                key_slots_ref[hop, :, tile(head)] = grads.astype(BF16)
                value_slots_ref[hop, :, tile(head)] = direct_value_ref[:, tile(head)].astype(BF16)
            else:
                grads = running_ref[:, tile(head)]
                for block in range(GROUP - 1, -1, -1):
                    collect_map(block, head, moved_ref[hop, block, :, tile(head)], grads)
                    grads = direct_ref[block, :, tile(head)] + dot3(grads, map_ref[tile(block), tile(head)], NT)
                key_slots_ref[hop, :, tile(head)] = grads.astype(BF16)

    def take(hop):
        @pl.when(has_next)
        def _():
            key_copy(hop).wait_recv()
            running_ref[...] = key_slots_ref[hop - 1].astype(F32)

        @pl.when(jnp.logical_not(has_next))
        def _():
            running_ref[...] = jnp.zeros_like(running_ref)

    @pl.when(place >= hops)
    def _():
        hop_direct(hops, True)
        hop_chain(hops, True)
        key_copy(hops).start()
        value_copy(hops).start()

    pauses()

    def between(hop):
        @pl.when(place >= hop)
        def _():
            hop_direct(hop, False)
            take(hop + 1)
            hop_chain(hop, False)
            key_copy(hop).start()

            @pl.when(has_next)
            def _():
                value_copy(hop + 1).wait_recv()
                for head in range(OWN):
                    value_slots_ref[hop, :, tile(head)] = (
                        direct_value_ref[:, tile(head)] + value_slots_ref[hop, :, tile(head)].astype(F32)
                    ).astype(BF16)

            @pl.when(jnp.logical_not(has_next))
            def _():
                for head in range(OWN):
                    value_slots_ref[hop, :, tile(head)] = direct_value_ref[:, tile(head)].astype(BF16)

            value_copy(hop).start()

    if hops > 2:

        def step(counter, carry):
            between(hops - 1 - counter)
            return carry

        lax.fori_loop(0, hops - 1, step, 0)
    else:
        for hop in range(hops - 1, 0, -1):
            between(hop)
            pauses()

    for head in range(OWN):
        direct_value_ref[:, tile(head)] = jnp.zeros((GROUP * BLOCK, BLOCK), F32)
    for block in range(GROUP):
        wide = (BLOCK, (block + 1) * BLOCK)
        counts = row_counts(block, 0, 0, block + 1) & (iota(0, wide) + block * BLOCK >= iota(1, wide))
        for head in range(OWN):
            query = query_ref[tile(block), tile(head)]
            scores = within_ref[tile(block), tile(head)]
            if block:
                keys = moved_ref[0, block, tile(0, block), tile(head)]
                scores = jnp.concatenate([dot(query, keys, NT), scores], 1)
            weights, grad = pair(block, head, scores, counts, value_ref[tile(0, block + 1), tile(head)])
            within_grad_ref[tile(block), tile(head)] = grad[:, block * BLOCK :]
            direct_value_ref[tile(0, block + 1), tile(head)] += dot(
                weights.astype(BF16), scaled_ref[tile(block), tile(head)], TN
            )
            if block:
                raw = grad[:, : block * BLOCK].astype(BF16)
                query_grad_ref[tile(block), tile(head)] += dot(raw, keys)
                direct_ref[block, tile(0, block), tile(head)] = dot(raw, query, TN)
    take(1)
    for head in range(OWN):
        grads = running_ref[:, tile(head)]
        for block in range(GROUP - 1, 0, -1):
            key_grad_ref[tile(block), tile(head)] = grads[block * BLOCK :]
            grads = grads[: block * BLOCK]
            collect_map(block, head, moved_ref[0, block, tile(0, block), tile(head)], grads)
            grads = direct_ref[block, tile(0, block), tile(head)] + dot3(grads, map_ref[tile(block), tile(head)], NT)
        key_grad_ref[tile(0), tile(head)] = grads

    @pl.when(has_next)
    def _():
        value_copy(1).wait_recv()
        value_grad_ref[...] = direct_value_ref[...] + value_slots_ref[0].astype(F32)

    @pl.when(jnp.logical_not(has_next))
    def _():
        value_grad_ref[...] = direct_value_ref[...]

    def settle(hop, carry):
        @pl.when(place >= hop)
        def _():
            key_copy(hop).wait_send()
            value_copy(hop).wait_send()

        return carry

    lax.fori_loop(1, hops + 1, settle, 0)
    pauses.rest()
    prepare_back_blocks(
        rows_ref, inverse_ref, query_grad_ref, key_grad_ref, within_grad_ref, map_grad_ref, value_grad_ref, rows_grad_ref
    )
    feed_scatter.last()
    feed_scatter.finish()


def attend_back(groups, hops, *args):
    length = args[0].shape[0]
    feed = args[-1]
    dma = pltpu.SemaphoreType.DMA
    return pl.pallas_call(
        functools.partial(attend_back_kernel, groups, hops),
        out_shape=[shape(BF16, *args[-3].shape), shape(BF16, GROUP, *feed.shape[3:])],
        in_specs=in_vmem(len(args) - 1) + anywhere(1),
        out_specs=in_vmem(2),
        scratch_shapes=[pltpu.VMEM((length, WIDE), F32)] * 5
        + [
            pltpu.VMEM((length, WIDE), BF16),
            pltpu.VMEM((OWN, length, BLOCK), F32),
            pltpu.VMEM((GROUP, length, WIDE), F32),
            pltpu.VMEM((length, WIDE), F32),
            pltpu.VMEM((length, WIDE), F32),
            pltpu.VMEM((hops + 1, length, WIDE), BF16),
            pltpu.VMEM((hops + 1, length, WIDE), BF16),
            dma((hops,)),
            dma((hops,)),
            dma((hops,)),
            dma((hops,)),
        ]
        + Scatter.scratch(groups, feed.shape),
        **communicating(2, "attend_back", 60),
    )(*args)


def gather_kernel(groups, parts_ref, tokens_ref, cotangent_ref, full_ref, tokens_all_ref, cotangent_all_ref, send, recv, local, *sems):
    here = Place(groups, full_ref.shape[2])
    here.meet()
    gather = Gather(here, parts_ref, full_ref, sems)
    gather.start()
    size = tokens_ref.shape[0]
    own = pl.ds(pl.multiple_of(here.m * size, size), size)
    copies = []
    for index, (source, target) in enumerate(((tokens_ref, tokens_all_ref), (cotangent_ref, cotangent_all_ref))):
        copies.append(pltpu.make_async_copy(source, target.at[own], local.at[index]))
        for offset in (2, 3, 1):
            copies.append(
                remote(source, target.at[own], send.at[index, offset], recv.at[index, offset], here.member(offset))
            )
    for copy in copies:
        copy.start()
    gather.begin()
    for distance in range(1, groups):
        gather.step(distance)
    for copy in copies:
        copy.wait()
    gather.finish()


def gather_first(groups, lines, parts, tokens, cotangent):
    dma = pltpu.SemaphoreType.DMA
    size, width = tokens.shape
    return pl.pallas_call(
        functools.partial(gather_kernel, groups),
        out_shape=[
            shape(BF16, groups, GROUP, lines, *parts.shape[1:]),
            shape(BF16, GROUP * size, width),
            shape(BF16, GROUP * size, width),
        ],
        in_specs=anywhere(3),
        out_specs=anywhere(3),
        scratch_shapes=[dma((2, GROUP)), dma((2, GROUP)), dma((2,))] + Gather.scratch(groups),
        **communicating(0, "gather_first", 16),
    )(parts, tokens, cotangent)


def rms_norm(values, gain):
    return values * lax.rsqrt(jnp.mean(values * values, axis=-1, keepdims=True) + EPSILON) * gain


def rms_back(values, gain, grad):
    scale = lax.rsqrt(jnp.mean(values * values, axis=-1, keepdims=True) + EPSILON)
    straight = values * scale
    lifted = grad * gain
    back = scale * (lifted - straight * jnp.mean(lifted * straight, axis=-1, keepdims=True))
    return back, grad * straight


def branch_kernel(groups, partial_ref, tokens_ref, gain_ref, down_ref, hidden_ref, normed_ref, down_full_ref, *refs):
    here = Place(groups, down_full_ref.shape[1])
    here.meet()
    sum_refs, gather_refs, down_refs = several(refs, 7, 2, len(Gather.scratch(groups)))
    total = GroupSum(here, partial_ref, sum_refs)
    whole = GroupGather(here, normed_ref, gather_refs)
    down = Gather(here, down_ref, down_full_ref, down_refs, mixed=False)
    pauses = Pauses(*[(functools.partial(down.step, distance),) for distance in range(1, groups)])
    total.start()
    down.start()
    down.begin()
    for chunk in range(CHUNKS):
        total.pass_on(chunk)
    pauses()
    for chunk in range(CHUNKS):
        hidden = tokens_ref[total.at(chunk), :].astype(F32) + total.take(chunk)
        hidden_ref[total.at(chunk), :] = hidden
        normed_ref[whole.at(chunk, here.m), :] = rms_norm(hidden, gain_ref[...]).astype(BF16)
        whole.give(chunk)
    pauses()
    for chunk in range(CHUNKS):
        whole.pass_on(chunk)
    pauses.rest()
    whole.finish()
    total.finish()
    down.finish()


def branch(groups, lines, partial, tokens, gain, down):
    size, width = tokens.shape
    return pl.pallas_call(
        functools.partial(branch_kernel, groups),
        out_shape=[shape(F32, size, width), shape(BF16, GROUP * size, width), shape(BF16, groups, lines, *down.shape)],
        in_specs=in_vmem(3) + anywhere(1),
        out_specs=in_vmem(2) + anywhere(1),
        scratch_shapes=GroupSum.scratch(size, width) + GroupGather.scratch() + Gather.scratch(groups),
        **communicating(3, "branch", 32),
    )(partial, tokens, gain, down)


def branch_back_kernel(
    groups, partial_ref, hidden_ref, cotangent_ref, gain_ref, down_ref, grad_ref, grad_low_ref, gain_grad_ref, down_result_ref, *refs
):
    here = Place(groups, down_ref.shape[2])
    here.meet()
    sum_refs, gather_refs, down_refs = several(refs, 7, 2, len(Scatter.scratch(groups, down_ref.shape)))
    total = GroupSum(here, partial_ref, sum_refs)
    whole = GroupGather(here, grad_low_ref, gather_refs)
    down = Scatter(here, down_ref, down_result_ref, down_refs)
    pauses = Pauses(*[(functools.partial(down.step, step),) for step in range(groups - 1)])
    total.start()
    down.start()
    for chunk in range(CHUNKS):
        total.pass_on(chunk)
    pauses()
    gain_grad = jnp.zeros((1, gain_ref.shape[1]), F32)
    for chunk in range(CHUNKS):
        back, gain_rows = rms_back(hidden_ref[total.at(chunk), :], gain_ref[...], total.take(chunk))
        grad = cotangent_ref[total.at(chunk), :].astype(F32) + back
        gain_grad = gain_grad + jnp.sum(gain_rows, axis=0, keepdims=True)
        grad_ref[total.at(chunk), :] = grad
        grad_low_ref[whole.at(chunk, here.m), :] = grad.astype(BF16)
        whole.give(chunk)
    gain_grad_ref[...] = gain_grad
    pauses()
    for chunk in range(CHUNKS):
        whole.pass_on(chunk)
    pauses.rest()
    whole.finish()
    total.finish()
    down.last()
    down.finish()


def branch_back(groups, partial, hidden, cotangent, gain, down):
    size, width = hidden.shape
    return pl.pallas_call(
        functools.partial(branch_back_kernel, groups),
        out_shape=[shape(F32, size, width), shape(BF16, GROUP * size, width), shape(F32, 1, width), shape(F32, 1, *down.shape[3:])],
        in_specs=in_vmem(4) + anywhere(1),
        out_specs=in_vmem(4),
        scratch_shapes=GroupSum.scratch(size, width) + GroupGather.scratch() + Scatter.scratch(groups, down.shape),
        **communicating(4, "branch_back", 48),
    )(partial, hidden, cotangent, gain, down)


def finish_kernel(
    groups,
    first_ref,
    out_ref,
    normed_partial_ref,
    output_partial_ref,
    tokens_ref,
    hidden_ref,
    grad_ref,
    gain_ref,
    first_result_ref,
    out_result_ref,
    tokens_grad_ref,
    output_ref,
    *refs,
):
    here = Place(groups, first_ref.shape[2])
    here.meet()
    first_refs, out_refs, normed_refs, output_refs = several(
        refs, len(Scatter.scratch(groups, first_ref.shape)), len(HomeScatter.scratch(groups, out_ref.shape)), 7, 7
    )
    first = Scatter(here, first_ref, first_result_ref, first_refs)
    out = HomeScatter(here, out_ref, out_result_ref, out_refs)
    normed = GroupSum(here, normed_partial_ref, normed_refs)
    output = GroupSum(here, output_partial_ref, output_refs)
    out.start()
    first.start()
    normed.start()
    output.start()
    for chunk in range(CHUNKS):
        normed.pass_on(chunk)
    for chunk in range(CHUNKS):
        output.pass_on(chunk)
    for step in range(groups - 1):
        out.step(step)
        first.step(step)
    for chunk in range(CHUNKS):
        back, _ = rms_back(tokens_ref[normed.at(chunk), :].astype(F32), gain_ref[...], normed.take(chunk))
        tokens_grad_ref[normed.at(chunk), :] = (grad_ref[normed.at(chunk), :] + back).astype(BF16)
    for chunk in range(CHUNKS):
        output_ref[output.at(chunk), :] = (hidden_ref[output.at(chunk), :] + output.take(chunk)).astype(BF16)
    out.last()
    first.last()
    normed.finish()
    output.finish()
    out.finish()
    first.finish()


def finish(groups, first, out, normed_partial, output_partial, tokens, hidden, grad, gain):
    size, width = tokens.shape
    return pl.pallas_call(
        functools.partial(finish_kernel, groups),
        out_shape=[shape(BF16, GROUP, *first.shape[3:]), shape(BF16, *out.shape[3:]), shape(BF16, size, width), shape(BF16, size, width)],
        in_specs=anywhere(2) + in_vmem(6),
        out_specs=in_vmem(4),
        scratch_shapes=Scatter.scratch(groups, first.shape)
        + HomeScatter.scratch(groups, out.shape)
        + GroupSum.scratch(size, width)
        + GroupSum.scratch(size, width),
        **communicating(5, "finish"),
    )(first, out, normed_partial, output_partial, tokens, hidden, grad, gain)


def on_device(
    tokens,
    doc_ids,
    norm_gain,
    query_weight,
    key_weight,
    value_weight,
    house_weight,
    beta_weight,
    out_weight,
    ffn_gain,
    gate_weight,
    up_weight,
    down_weight,
    cotangent,
):
    groups, batch = lax.axis_size("g"), lax.axis_size("b")
    devices = groups * GROUP * batch
    rows, width = query_weight.shape
    hidden_rows = down_weight.shape[0]
    hidden_own = gate_weight.shape[1] // GROUP
    block_rows = tokens.shape[1]
    hops = groups // 2
    doc_columns = -(-block_rows // rows)
    place, line = lax.axis_index("g"), lax.axis_index("b")

    def columns(weight):
        return jnp.transpose(weight.astype(BF16).reshape(rows, GROUP, -1), (1, 0, 2))

    docs = jnp.pad(doc_ids[0].astype(BF16), (0, rows * doc_columns - block_rows)).reshape(rows, doc_columns)
    same = jnp.concatenate([norm_gain.astype(BF16)[:, None], ffn_gain.astype(BF16)[:, None], docs], 1)
    same = jnp.broadcast_to(same[None], (GROUP,) + same.shape)
    same = jnp.pad(same, ((0, 0), (0, 0), (0, EXTRA - OWN - same.shape[2])))
    first_parts = jnp.concatenate(
        [columns(w) for w in (query_weight, key_weight, value_weight, house_weight, beta_weight)] + [same], 2
    )

    def unit_columns(weight):
        parts = weight.astype(BF16).reshape(rows, groups, GROUP, batch, hidden_rows)
        return jnp.transpose(parts, (2, 0, 1, 3, 4)).reshape(GROUP, rows, hidden_own)

    feed_parts = jnp.concatenate([unit_columns(gate_weight), unit_columns(up_weight)], 2)
    first, tokens_all, cotangent_all = gather_first(groups, batch, first_parts, tokens[0], cotangent[0])
    first = first.reshape(width, -1)

    extra = first[:, 4 * WIDE :]
    gain_one = extra[:, OWN].astype(F32)[None]
    gain_two = extra[:, OWN + 1].astype(F32)[None]
    docs = extra[:, OWN + 2 : OWN + 2 + doc_columns].astype(jnp.int32)
    docs = docs.reshape(devices, -1)[:, :block_rows].reshape(groups, GROUP, batch, block_rows)
    docs = lax.dynamic_index_in_dim(docs, line, 2, keepdims=False).reshape(groups, GROUP * block_rows)
    doc_key = jnp.stack(
        [
            jnp.where(place >= hop, lax.dynamic_index_in_dim(docs, jnp.maximum(place - hop, 0), 0, keepdims=False), -1)
            for hop in range(hops + 1)
        ]
    )[:, None, :]
    doc_query = lax.dynamic_index_in_dim(docs, place, 0, keepdims=False)[:, None]

    tokens_wide = tokens_all.astype(F32)
    straight = tokens_wide * lax.rsqrt(jnp.mean(tokens_wide * tokens_wide, axis=-1, keepdims=True) + EPSILON)
    normed = (straight * gain_one).astype(BF16)
    projected = dot(normed, first)
    (query, value, within, maps, inverse, attended, attended_low, stats, moved, values, out_full, feed) = attend(
        groups, batch, hops, projected, doc_query, doc_key, out_weight.astype(BF16), feed_parts
    )
    out_full = out_full.reshape(WIDE, width)
    feed = feed.reshape(width, -1)
    hidden, normed_two, down_full = branch(
        groups, batch, dot(attended_low, out_full).astype(BF16), tokens[0], gain_two, down_weight.astype(BF16)
    )
    down_full = down_full.reshape(hidden_own, width)
    both = dot(normed_two, feed)
    gate, up = both[:, :hidden_own], both[:, hidden_own:]
    sigmoid = jax.nn.sigmoid(gate)
    silu = gate * sigmoid
    active = (silu * up).astype(BF16)
    output_partial = dot(active, down_full).astype(BF16)

    active_grad = dot(cotangent_all, down_full, NT)
    gate_grad = (active_grad * up * (sigmoid * (1.0 + gate * (1.0 - sigmoid)))).astype(BF16)
    up_grad = (active_grad * silu).astype(BF16)
    feed_grads = jnp.concatenate([gate_grad, up_grad], 1)
    down_partial = dot(active, cotangent_all, TN).astype(BF16).reshape(groups, 1, batch, hidden_rows, width)
    hidden_grad, branch_grad, gain_two_grad, down_weight_grad = branch_back(
        groups, dot(feed_grads, feed, NT).astype(BF16), hidden, cotangent[0], gain_two, down_partial
    )
    att_grad = dot(branch_grad, out_full, NT).astype(BF16)
    feed_partial = dot(normed_two, feed_grads, TN).astype(BF16).reshape(groups, GROUP, batch, rows, -1)
    rows_grad, feed_grad = attend_back(
        groups, hops, query, value, within, maps, doc_query, doc_key, attended, stats, moved, values, att_grad, projected, inverse,
        feed_partial,
    )
    normed_grad = dot(rows_grad, first, NT)
    gain_one_grad = jnp.sum(normed_grad * straight, axis=0)
    first_partial = dot(normed, rows_grad, TN)
    lane = iota(1, (1, first_partial.shape[1]))
    first_partial = jnp.where(lane == 4 * WIDE + OWN, gain_one_grad[:, None], first_partial)
    first_partial = jnp.where(lane == 4 * WIDE + OWN + 1, gain_two_grad[0][:, None], first_partial)
    first_partial = first_partial.astype(BF16).reshape(groups, GROUP, batch, rows, -1)
    out_partial = dot(attended_low, branch_grad, TN).astype(BF16).reshape(groups // GROUP, GROUP, batch, rows, width)
    first_grad, out_weight_grad, tokens_grad, output = finish(
        groups, first_partial, out_partial, normed_grad.astype(BF16), output_partial, tokens[0], hidden, hidden_grad, gain_one
    )
    first_grad = first_grad.astype(F32)
    output, tokens_grad = output[None], tokens_grad[None]
    out_weight_grad = out_weight_grad.astype(F32)
    down_weight_grad = down_weight_grad[0]

    def whole_columns(parts):
        return jnp.transpose(parts, (1, 0, 2)).reshape(rows, -1)

    query_weight_grad, key_weight_grad, value_weight_grad, house_weight_grad = [
        whole_columns(first_grad[:, :, part * WIDE : (part + 1) * WIDE]) for part in range(4)
    ]
    beta_weight_grad = whole_columns(first_grad[:, :, 4 * WIDE : 4 * WIDE + OWN])
    gains_grad = jnp.sum(first_grad[:, :, 4 * WIDE + OWN : 4 * WIDE + OWN + 2], axis=0)

    def unit_whole(parts):
        parts = parts.astype(F32).reshape(GROUP, rows, groups, batch, hidden_rows)
        return jnp.transpose(parts, (1, 2, 0, 3, 4)).reshape(rows, -1)

    gate_weight_grad = unit_whole(feed_grad[:, :, :hidden_own])
    up_weight_grad = unit_whole(feed_grad[:, :, hidden_own:])
    return (
        output,
        tokens_grad,
        gains_grad[:, 0],
        query_weight_grad,
        key_weight_grad,
        value_weight_grad,
        house_weight_grad,
        beta_weight_grad,
        out_weight_grad,
        gains_grad[:, 1],
        gate_weight_grad,
        up_weight_grad,
        down_weight_grad,
    )


def solution(mesh):
    groups = mesh.shape["seq"] // GROUP
    inner = Mesh(mesh.devices.reshape(groups, GROUP, mesh.shape["batch"]), ("g", "m", "b"))
    line = P("b", ("g", "m"), None)
    vector = P(("g", "m", "b"))
    matrix = P(("g", "m", "b"), None)
    in_specs = (line, P("b", ("g", "m")), vector) + (matrix,) * 6 + (vector,) + (matrix,) * 3 + (line,)
    out_specs = (line, line, vector) + (matrix,) * 6 + (vector,) + (matrix,) * 3
    return jax.shard_map(on_device, mesh=inner, in_specs=in_specs, out_specs=out_specs, check_vma=False)
```

```python
import functools

import jax
import jax.numpy as jnp
from jax import lax
from jax.experimental import pallas as pl
from jax.experimental.pallas import tpu as pltpu
from jax.sharding import Mesh
from jax.sharding import PartitionSpec as P

HEADS = 12
HEAD_DIM = 128
GROUP = 4
OWN = HEADS // GROUP
WIDE = OWN * HEAD_DIM
BLOCK = 128
EXTRA = 128
EPSILON = 1e-06
NEGATIVE = -1e30
SCALE = HEAD_DIM ** (-0.5)
MESH = pl.DeviceIdType.MESH
F32 = jnp.float32
BF16 = jnp.bfloat16
NN = (((1,), (0,)), ((), ()))
NT = (((1,), (1,)), ((), ()))
TN = (((0,), (0,)), ((), ()))


def dot(left, right, dims=NN):
    return lax.dot_general(left, right, dims, preferred_element_type=F32)


def split(value):
    high = value.astype(BF16)
    return high, (value - high.astype(F32)).astype(BF16)


def dot3(left, right, dims=NN):
    left_high, left_low = split(left)
    right_high, right_low = split(right)
    return dot(left_high, right_high, dims) + (
        dot(left_high, right_low, dims) + dot(left_low, right_high, dims)
    )


def dot2(left, right, dims=NN):
    high, low = split(right)
    return dot(left, high, dims) + dot(left, low, dims)


def tile(index, count=1):
    return pl.ds(index * BLOCK, count * BLOCK)


def iota(axis, shape=(BLOCK, BLOCK)):
    return lax.broadcasted_iota(jnp.int32, shape, axis)


def invert(strict):
    row, col = iota(0), iota(1)
    eye = jnp.where(row == col, 1.0, 0.0)

    def part(size):
        return (row // (2 * size) == col // (2 * size)) & (row // size > col // size)

    totals = [eye - jnp.where(part(1), value, 0.0) for value in strict]
    size = 2
    while size < BLOCK:
        mask = part(size)
        pieces = [jnp.where(mask, value, 0.0) for value in strict]
        inner = [dot3(piece, total) for piece, total in zip(pieces, totals)]
        outer = [dot3(total, value) for total, value in zip(totals, inner)]
        totals = [total - value for total, value in zip(totals, outer)]
        size *= 2
    return totals


def unit_of(house):
    scale = lax.rsqrt(jnp.sum(house * house, axis=-1, keepdims=True) + EPSILON)
    return house * scale, scale


def products(query, key, unit):
    both = dot3(jnp.concatenate([unit, query], 0), jnp.concatenate([unit, key], 0), NT)
    return both[:BLOCK, :BLOCK], both[:BLOCK, BLOCK:], both[BLOCK:, :BLOCK], both[BLOCK:, BLOCK:]


def prepare_blocks(first, last, rows_ref, query_ref, key_ref, value_ref, within_ref, map_ref, inverse_ref):
    row, col = iota(0), iota(1)

    def one_block(block, carry):
        at = tile(block)
        kept, strict = [], []
        for head in range(OWN):
            query, key, value, house = [
                rows_ref[at, pl.ds(part * WIDE + head * BLOCK, BLOCK)] for part in range(4)
            ]
            rate = rows_ref[at, pl.ds(4 * WIDE, EXTRA)][:, head : head + 1]
            value_ref[at, tile(head)] = value.astype(BF16)
            unit, _ = unit_of(house)
            strength = 2.0 * jax.nn.sigmoid(rate)
            unit_unit, unit_key, query_unit, query_key = products(query, key, unit)
            strict.append(jnp.where(row > col, strength * unit_unit, 0.0))
            reach = jnp.where(row > col, strength * unit_key, 0.0)
            project = jnp.where(row >= col, query_unit, 0.0)
            kept.append((query, key, unit, strength, reach, project, query_key))
        inverses = invert(strict)
        for head in range(OWN):
            query, key, unit, strength, reach, project, query_key = kept[head]
            inverse = inverses[head]
            solved = dot3(inverse, jnp.concatenate([strength * unit, reach], 1))
            from_query = dot3(project, solved)
            from_unit = dot3(solved, unit, TN)
            query_ref[at, tile(head)] = (query - from_query[:, :BLOCK]).astype(BF16)
            within_ref[at, tile(head)] = query_key - from_query[:, BLOCK:]
            map_ref[at, tile(head)] = jnp.where(row == col, 1.0, 0.0) - from_unit[:BLOCK]
            key_ref[at, tile(head)] = (key - from_unit[BLOCK:]).astype(BF16)
            inverse_ref[at, tile(head)] = inverse
        return carry

    lax.fori_loop(first, last, one_block, 0)


def prepare_back_blocks(first, last, rows_ref, inverse_ref, query_grad_ref, key_grad_ref, within_grad_ref, map_grad_ref, value_grad_ref, out_ref):
    row, col = iota(0), iota(1)

    def one_block(block, carry):
        at = tile(block)
        rates = jnp.zeros((BLOCK, EXTRA), F32)
        for head in range(OWN):
            query, key, value, house = [
                rows_ref[at, pl.ds(part * WIDE + head * BLOCK, BLOCK)] for part in range(4)
            ]
            rate = rows_ref[at, pl.ds(4 * WIDE, EXTRA)][:, head : head + 1]
            query_grad = query_grad_ref[at, tile(head)]
            key_grad = key_grad_ref[at, tile(head)]
            within_grad = within_grad_ref[at, tile(head)]
            map_grad = map_grad_ref[at, tile(head)]
            inverse = inverse_ref[at, tile(head)]
            unit, scale = unit_of(house)
            strength = 2.0 * jax.nn.sigmoid(rate)
            unit_unit, unit_key, query_unit, query_key = products(query, key, unit)
            reach = jnp.where(row > col, strength * unit_key, 0.0)
            project = jnp.where(row >= col, query_unit, 0.0)
            solved = dot3(inverse, jnp.concatenate([strength * unit, reach], 1))
            both_grad = jnp.concatenate([query_grad, within_grad], 1)
            project_grad = jnp.where(row >= col, -dot3(both_grad, solved, NT), 0.0)
            solved_grad = -(
                dot3(project, both_grad, TN)
                + dot3(unit, jnp.concatenate([map_grad, key_grad], 0), NT)
            )
            given_grad = dot3(inverse, solved_grad, TN)
            strict_grad = jnp.where(row > col, -dot3(given_grad, solved, NT), 0.0)
            scaled_grad = given_grad[:, :BLOCK]
            reach_grad = jnp.where(row > col, given_grad[:, BLOCK:], 0.0)
            strength_grad = jnp.sum(
                scaled_grad * unit + reach_grad * unit_key + strict_grad * unit_unit, axis=1, keepdims=True
            )
            reach_part = strength * reach_grad
            inner_part = strength * strict_grad
            unit_grad = (
                strength * scaled_grad
                + dot3(reach_part, key)
                + dot3(inner_part + inner_part.T, unit)
                + dot3(project_grad, query, TN)
                - dot3(solved[:, :BLOCK], map_grad)
                - dot3(solved[:, BLOCK:], key_grad)
            )
            query_out = query_grad + dot3(within_grad, key) + dot3(project_grad, unit)
            key_out = key_grad + dot3(within_grad, query, TN) + dot3(reach_part, unit, TN)
            house_out = scale * (unit_grad - unit * jnp.sum(unit * unit_grad, axis=1, keepdims=True))
            rate_out = strength_grad * strength * (1.0 - 0.5 * strength)
            rates = jnp.where(iota(1, (BLOCK, EXTRA)) == head, rate_out, rates)
            out_ref[at, pl.ds(head * BLOCK, BLOCK)] = query_out.astype(BF16)
            out_ref[at, pl.ds(WIDE + head * BLOCK, BLOCK)] = key_out.astype(BF16)
            out_ref[at, pl.ds(2 * WIDE + head * BLOCK, BLOCK)] = value_grad_ref[at, tile(head)].astype(BF16)
            out_ref[at, pl.ds(3 * WIDE + head * BLOCK, BLOCK)] = house_out.astype(BF16)
        out_ref[at, pl.ds(4 * WIDE, EXTRA)] = rates.astype(BF16)
        return carry

    lax.fori_loop(first, last, one_block, 0)


def remote(source, target, send, recv, device):
    return pltpu.make_async_remote_copy(
        src_ref=source, dst_ref=target, send_sem=send, recv_sem=recv, device_id=device, device_id_type=MESH
    )


class Place:
    def __init__(self, groups, lines):
        self.groups, self.lines = groups, lines
        self.g, self.m, self.b = lax.axis_index("g"), lax.axis_index("m"), lax.axis_index("b")
        self.below, self.above = self.g > 0, self.g < groups - 1

    def other(self, offset):
        return {1: self.m + 1 - 2 * (self.m % 2), 2: (self.m + 2) % GROUP, 3: GROUP - 1 - self.m}[offset]

    def member(self, offset):
        return {"g": self.g, "m": self.other(offset), "b": self.b}

    def up(self):
        return {"g": self.g + 1, "m": self.m, "b": self.b}

    def down(self):
        return {"g": self.g - 1, "m": self.m, "b": self.b}

    def across(self):
        return {"g": self.g, "m": self.m, "b": 1 - self.b}

    def column(self, group):
        return {"g": group, "m": self.m, "b": self.b}

    def meet(self, column=False):
        barrier = pltpu.get_barrier_semaphore()

        def greet(device):
            pl.semaphore_signal(barrier, 1, device_id=device, device_id_type=MESH)

        for offset in range(1, GROUP):
            greet(self.member(offset))
        greet(self.across())
        if column:
            for step in range(1, self.groups):
                greet(self.column((self.g + step) % self.groups))
            count = GROUP + self.groups - 1
        else:
            pl.when(self.above)(lambda: greet(self.up()))
            pl.when(self.below)(lambda: greet(self.down()))
            count = GROUP + self.above.astype(jnp.int32) + self.below.astype(jnp.int32)
        pl.semaphore_wait(barrier, count)


class Gather:
    SEMS = 8

    def __init__(self, place, parts, full, sems, mixed=True):
        self.place, self.parts, self.full, self.mixed = place, parts, full, mixed
        (self.part_send, self.part_recv, self.up_send, self.down_send, self.chain_recv, self.line_send, self.line_recv,
         self.own_sem) = sems

    @staticmethod
    def scratch(groups):
        dma = pltpu.SemaphoreType.DMA
        return [dma((GROUP,)), dma((GROUP,)), dma((groups,)), dma((groups,)), dma((groups,)), dma((groups,)), dma((groups,)), dma((1,))]

    def unit(self, group, line):
        return self.full.at[group, :, line] if self.mixed else self.full.at[group, line]

    def own(self):
        p = self.place
        if self.mixed:
            return pltpu.make_async_copy(self.parts.at[p.m], self.full.at[p.g, p.m, p.b], self.own_sem.at[0])
        return pltpu.make_async_copy(self.parts, self.full.at[p.g, p.b], self.own_sem.at[0])

    def part(self, offset):
        p = self.place
        other = p.other(offset)
        return remote(
            self.parts.at[other], self.full.at[p.g, p.m, p.b], self.part_send.at[offset], self.part_recv.at[offset], p.member(offset)
        )

    def start(self):
        if self.mixed:
            for offset in (2, 3, 1):
                self.part(offset).start()
        self.own().start()

    def chain(self, source, up):
        p = self.place
        unit = self.unit(source, p.b)
        sems = self.up_send if up else self.down_send
        return remote(unit, unit, sems.at[source], self.chain_recv.at[source], p.up() if up else p.down())

    def across(self, source):
        p = self.place
        unit = self.unit(source, p.b)
        return remote(unit, unit, self.line_send.at[source], self.line_recv.at[source], p.across())

    def begin(self):
        p = self.place
        self.own().wait()
        if self.mixed:
            for offset in (2, 3, 1):
                self.part(offset).wait()
        pl.when(p.above)(lambda: self.chain(p.g, True).start())
        pl.when(p.below)(lambda: self.chain(p.g, False).start())
        self.across(p.g).start()

    def step(self, distance):
        p = self.place

        @pl.when(p.g >= distance)
        def _():
            source = p.g - distance
            self.chain(source, True).wait_recv()
            pl.when(p.above)(lambda: self.chain(source, True).start())
            self.across(source).start()

        @pl.when(p.g + distance < p.groups)
        def _():
            source = p.g + distance
            self.chain(source, False).wait_recv()
            pl.when(p.below)(lambda: self.chain(source, False).start())
            self.across(source).start()

    def finish(self):
        p = self.place

        def settle(source, carry):
            self.across(source).wait()
            pl.when(p.above & (source <= p.g))(lambda: self.chain(source, True).wait_send())
            pl.when(p.below & (source >= p.g))(lambda: self.chain(source, False).wait_send())
            return carry

        lax.fori_loop(0, p.groups, settle, 0)


class HomeGather:
    def __init__(self, place, part, full, sems):
        self.place, self.part_ref, self.full = place, part, full
        self.home = place.groups // GROUP
        self.part_send, self.part_recv, self.up_send, self.down_send, self.chain_recv, self.line_send, self.line_recv = sems

    @staticmethod
    def scratch(groups):
        home = groups // GROUP
        dma = pltpu.SemaphoreType.DMA
        return [dma((1,)), dma((GROUP,)), dma((home,)), dma((home,)), dma((home,)), dma((home,)), dma((home,))]

    def at_home(self):
        return self.place.m == self.place.g // self.home

    def slot(self):
        p = self.place
        return self.full.at[p.g % self.home, p.m, p.b]

    def hand(self):
        p = self.place
        keeper = p.g // self.home
        device = {"g": p.g, "m": keeper, "b": p.b}
        return remote(self.part_ref, self.slot(), self.part_send.at[0], self.part_recv.at[p.m], device)

    def taken(self, source):
        p = self.place
        target = self.full.at[p.g % self.home, source, p.b]
        return remote(self.part_ref, target, self.part_send.at[0], self.part_recv.at[source], p.member(1))

    def own(self):
        return pltpu.make_async_copy(self.part_ref, self.slot(), self.part_send.at[0])

    def start(self):
        pl.when(self.at_home())(lambda: self.own().start())
        pl.when(jnp.logical_not(self.at_home()))(lambda: self.hand().start())

    def chain(self, slot, up):
        p = self.place
        unit = self.full.at[slot, :, p.b]
        sems = self.up_send if up else self.down_send
        return remote(unit, unit, sems.at[slot], self.chain_recv.at[slot], p.up() if up else p.down())

    def across(self, slot):
        p = self.place
        unit = self.full.at[slot, :, p.b]
        return remote(unit, unit, self.line_send.at[slot], self.line_recv.at[slot], p.across())

    def begin(self):
        p = self.place

        @pl.when(self.at_home())
        def _():
            self.own().wait()
            for offset in range(1, GROUP):
                self.taken(p.other(offset)).wait_recv()
            slot = p.g % self.home
            pl.when(p.above)(lambda: self.chain(slot, True).start())
            pl.when(p.below)(lambda: self.chain(slot, False).start())
            self.across(slot).start()

        pl.when(jnp.logical_not(self.at_home()))(lambda: self.hand().wait_send())

    def step(self, distance):
        p = self.place
        for slot in range(self.home):
            source = p.m * self.home + slot

            @pl.when(p.g - source == distance)
            def _():
                self.chain(slot, True).wait_recv()
                pl.when(p.above)(lambda: self.chain(slot, True).start())
                self.across(slot).start()

            @pl.when(source - p.g == distance)
            def _():
                self.chain(slot, False).wait_recv()
                pl.when(p.below)(lambda: self.chain(slot, False).start())
                self.across(slot).start()

    def finish(self):
        p = self.place
        for slot in range(self.home):
            source = p.m * self.home + slot
            self.across(slot).wait()
            pl.when(p.above & (p.g >= source))(lambda: self.chain(slot, True).wait_send())
            pl.when(p.below & (p.g <= source))(lambda: self.chain(slot, False).wait_send())


class Scatter:
    def __init__(self, place, partial, result, refs):
        self.place, self.partial, self.result = place, partial, result
        (self.land, self.chain_land, self.leave, self.mine_sem, self.line_send, self.line_recv, self.chain_send,
         self.chain_recv, self.part_send, self.part_recv) = refs
        self.parts = partial.shape[1]

    @staticmethod
    def scratch(groups, shape):
        dma = pltpu.SemaphoreType.DMA
        unit = (shape[1],) + tuple(shape[3:])
        return [
            pltpu.VMEM((groups,) + unit, BF16),
            pltpu.VMEM((groups + 1,) + unit, BF16),
            pltpu.VMEM((groups,) + unit, BF16),
            dma((groups,)),
            dma((groups,)),
            dma((groups,)),
            dma((groups,)),
            dma((groups + 1,)),
            dma((GROUP,)),
            dma((GROUP,)),
        ]

    def load(self, target):
        return pltpu.make_async_copy(self.partial.at[target, :, self.place.b], self.leave.at[target], self.mine_sem.at[target])

    def line(self, target):
        p = self.place
        return remote(
            self.partial.at[target, :, 1 - p.b], self.land.at[target], self.line_send.at[target], self.line_recv.at[target], p.across()
        )

    def up(self, target):
        p = self.place
        return remote(
            self.leave.at[target], self.chain_land.at[target], self.chain_send.at[target], self.chain_recv.at[target], p.up()
        )

    def down(self, target, slot):
        p = self.place
        return remote(
            self.leave.at[target], self.chain_land.at[slot], self.chain_send.at[target], self.chain_recv.at[slot], p.down()
        )

    def send_up(self, target):
        self.up(target).start()

    def send_down(self, target):
        p = self.place
        pl.when(p.g - 1 == target)(lambda: self.down(target, p.groups).start())
        pl.when(p.g - 1 != target)(lambda: self.down(target, target).start())

    def arrived(self, slot):
        p = self.place
        return remote(self.leave.at[0], self.chain_land.at[slot], self.chain_send.at[0], self.chain_recv.at[slot], p.across())

    def wave(self, wave, act_up, act_down):
        p = self.place
        pl.when(wave > p.g)(lambda: act_up(p.groups - wave + p.g))
        pl.when(wave >= p.groups - p.g)(lambda: act_down(wave - p.groups + p.g))

    def start(self, before_own=None):
        p = self.place

        def act(target):
            self.line(target).start()
            self.load(target).start()

        for wave in range(1, p.groups):
            self.wave(wave, act, act)
        if before_own is not None:
            before_own()
        act(p.g)

        @pl.when(jnp.logical_not(p.below))
        def _():
            self.chain_land[p.g] = jnp.zeros(self.chain_land.shape[1:], BF16)

        @pl.when(jnp.logical_not(p.above))
        def _():
            self.chain_land[p.groups] = jnp.zeros(self.chain_land.shape[1:], BF16)

    def both(self, target, part):
        return self.leave[target, part].astype(F32) + self.land[target, part].astype(F32)

    def step(self, wave):
        p = self.place

        def send(target, inner, copy):
            self.load(target).wait()
            self.line(target).wait_recv()

            @pl.when(inner)
            def _():
                self.arrived(target).wait_recv()
                for part in range(self.parts):
                    self.leave[target, part] = (self.both(target, part) + self.chain_land[target, part].astype(F32)).astype(BF16)

            @pl.when(jnp.logical_not(inner))
            def _():
                for part in range(self.parts):
                    self.leave[target, part] = self.both(target, part).astype(BF16)

            copy(target)

        self.wave(
            wave,
            lambda target: send(target, p.below, self.send_up),
            lambda target: send(target, p.above, self.send_down),
        )

    def hand(self, offset):
        p = self.place
        return remote(
            self.leave.at[p.g, p.other(offset)], self.result.at[p.m], self.part_send.at[offset], self.part_recv.at[offset], p.member(offset)
        )

    def last(self):
        p = self.place
        self.load(p.g).wait()
        self.line(p.g).wait_recv()
        pl.when(p.below)(lambda: self.arrived(p.g).wait_recv())
        pl.when(p.above)(lambda: self.arrived(p.groups).wait_recv())
        for part in range(self.parts):
            total = self.both(p.g, part) + self.chain_land[p.g, part].astype(F32) + self.chain_land[p.groups, part].astype(F32)
            if self.parts == 1:
                self.result[part] = total.astype(self.result.dtype)
            else:
                self.leave[p.g, part] = total.astype(BF16)
        if self.parts > 1:
            for offset in (2, 3, 1):
                self.hand(offset).start()
            self.result[p.m] = self.leave[p.g, p.m]

    def finish(self):
        p = self.place
        for target in range(p.groups):
            self.line(target).wait_send()
            pl.when(p.g != target)(lambda: self.up(target).wait_send())
        if self.parts > 1:
            for offset in (2, 3, 1):
                self.hand(offset).wait()


class HomeScatter:
    def __init__(self, place, partial, result, refs):
        self.place, self.partial, self.result = place, partial, result
        (self.land, self.home_land, self.leave, self.mine_sem, self.line_send, self.line_recv, self.home_send, self.home_recv,
         self.part_send, self.part_recv) = refs
        self.home = place.groups // GROUP

    @staticmethod
    def scratch(groups, shape):
        dma = pltpu.SemaphoreType.DMA
        home = groups // GROUP
        unit = (GROUP,) + tuple(shape[3:])
        return [
            pltpu.VMEM((home,) + unit, BF16),
            pltpu.VMEM((groups - 1,) + unit, BF16),
            pltpu.VMEM((home,) + unit, BF16),
            dma((home,)),
            dma((home,)),
            dma((home,)),
            dma((home,)),
            dma((groups - 1,)),
            dma((GROUP,)),
            dma((1,)),
        ]

    def load(self, slot):
        return pltpu.make_async_copy(self.partial.at[slot, :, self.place.b], self.leave.at[slot], self.mine_sem.at[slot])

    def line(self, slot):
        p = self.place
        return remote(self.partial.at[slot, :, 1 - p.b], self.land.at[slot], self.line_send.at[slot], self.line_recv.at[slot], p.across())

    def start(self):
        for slot in range(self.home):
            self.line(slot).start()
            self.load(slot).start()

    def home_copy(self, slot):
        p = self.place
        target = p.m * self.home + slot
        index = (p.g - target + p.groups - 1) % p.groups
        return remote(
            self.leave.at[slot], self.home_land.at[index], self.home_send.at[slot], self.home_recv.at[index], p.column(target)
        )

    def landed(self, index):
        p = self.place
        return remote(self.leave.at[0], self.home_land.at[index], self.home_send.at[0], self.home_recv.at[index], p.across())

    def push(self):
        p = self.place
        for slot in range(self.home):

            @pl.when(p.g != p.m * self.home + slot)
            def _():
                self.load(slot).wait()
                self.line(slot).wait_recv()
                for part in range(GROUP):
                    total = self.leave[slot, part].astype(F32) + self.land[slot, part].astype(F32)
                    self.leave[slot, part] = total.astype(BF16)
                self.home_copy(slot).start()

    def hand(self, slot, other):
        p = self.place
        return remote(
            self.leave.at[slot, other], self.result, self.part_send.at[other], self.part_recv.at[0], {"g": p.g, "m": other, "b": p.b}
        )

    def last(self):
        p = self.place

        @pl.when(p.m == p.g // self.home)
        def _():
            slot = p.g % self.home
            self.load(slot).wait()
            self.line(slot).wait_recv()
            for index in range(p.groups - 1):
                self.landed(index).wait_recv()
            for part in range(GROUP):
                total = self.leave[slot, part].astype(F32) + self.land[slot, part].astype(F32)
                for index in range(p.groups - 1):
                    total = total + self.home_land[index, part].astype(F32)
                self.leave[slot, part] = total.astype(BF16)
            for offset in range(1, GROUP):
                self.hand(slot, p.other(offset)).start()
            self.result[...] = self.leave[slot, p.m]

    def finish(self):
        p = self.place
        keeper = p.m == p.g // self.home

        @pl.when(keeper)
        def _():
            for offset in range(1, GROUP):
                self.hand(p.g % self.home, p.other(offset)).wait_send()

        pl.when(jnp.logical_not(keeper))(lambda: self.hand(0, p.other(1)).wait_recv())
        for slot in range(self.home):
            self.line(slot).wait_send()
            pl.when(p.g != p.m * self.home + slot)(lambda: self.home_copy(slot).wait_send())


CHUNKS = 4


class GroupSum:
    def __init__(self, place, partial, refs):
        self.place, self.partial = place, partial
        self.pair_land, self.leave, self.land, self.pair_send, self.pair_recv, self.send, self.recv = refs
        self.size = partial.shape[0] // GROUP
        self.rows = self.size // CHUNKS

    @staticmethod
    def scratch(size, width):
        dma = pltpu.SemaphoreType.DMA
        return [
            pltpu.VMEM((2, size, width), BF16),
            pltpu.VMEM((size, width), BF16),
            pltpu.VMEM((size, width), BF16),
            dma((2, CHUNKS)),
            dma((2, CHUNKS)),
            dma((CHUNKS,)),
            dma((CHUNKS,)),
        ]

    def at(self, chunk, member=0):
        return pl.ds(pl.multiple_of(member * self.size + chunk * self.rows, self.rows), self.rows)

    def pair(self, chunk, far):
        p = self.place
        member = p.other(3 if far else 1)
        slot = 1 if far else 0
        return remote(
            self.partial.at[self.at(chunk, member)], self.pair_land.at[slot, self.at(chunk)], self.pair_send.at[slot, chunk],
            self.pair_recv.at[slot, chunk], p.member(1),
        )

    def cross(self, chunk):
        return remote(
            self.leave.at[self.at(chunk)], self.land.at[self.at(chunk)], self.send.at[chunk], self.recv.at[chunk], self.place.member(2)
        )

    def start(self):
        for chunk in range(CHUNKS):
            self.pair(chunk, True).start()
        for chunk in range(CHUNKS):
            self.pair(chunk, False).start()

    def pass_on(self, chunk):
        self.pair(chunk, True).wait_recv()
        own = self.partial[self.at(chunk, self.place.other(2)), :].astype(F32)
        self.leave[self.at(chunk), :] = (own + self.pair_land[1, self.at(chunk), :].astype(F32)).astype(BF16)
        self.cross(chunk).start()

    def take(self, chunk):
        self.pair(chunk, False).wait_recv()
        self.cross(chunk).wait_recv()
        own = self.partial[self.at(chunk, self.place.m), :].astype(F32)
        return own + self.pair_land[0, self.at(chunk), :].astype(F32) + self.land[self.at(chunk), :].astype(F32)

    def finish(self):
        for chunk in range(CHUNKS):
            self.pair(chunk, True).wait_send()
            self.pair(chunk, False).wait_send()
            self.cross(chunk).wait_send()


class GroupGather:
    def __init__(self, place, whole, refs):
        self.place, self.whole = place, whole
        self.send, self.recv = refs
        self.size = whole.shape[0] // GROUP
        self.rows = self.size // CHUNKS

    @staticmethod
    def scratch():
        dma = pltpu.SemaphoreType.DMA
        return [dma((3, CHUNKS)), dma((3, CHUNKS))]

    def at(self, chunk, member):
        return pl.ds(pl.multiple_of(member * self.size + chunk * self.rows, self.rows), self.rows)

    def copy(self, chunk, way):
        p = self.place
        rows = self.whole.at[self.at(chunk, p.other(2) if way == 2 else p.m)]
        return remote(rows, rows, self.send.at[way, chunk], self.recv.at[way, chunk], p.member(2 if way == 0 else 1))

    def give(self, chunk):
        self.copy(chunk, 0).start()
        self.copy(chunk, 1).start()

    def pass_on(self, chunk):
        self.copy(chunk, 0).wait_recv()
        self.copy(chunk, 2).start()

    def finish(self):
        for chunk in range(CHUNKS):
            self.copy(chunk, 1).wait_recv()
            self.copy(chunk, 2).wait_recv()
            for way in range(3):
                self.copy(chunk, way).wait_send()


def masked(scores, counts):
    return jnp.where(counts, scores * SCALE, NEGATIVE)


class Pauses:
    def __init__(self, *steps):
        self.steps = list(steps)

    def __call__(self):
        if self.steps:
            for act in self.steps.pop(0):
                act()

    def rest(self):
        while self.steps:
            self()


def several(refs, *counts):
    refs = list(refs)
    taken = []
    for count in counts:
        taken.append(refs[:count])
        refs = refs[count:]
    return taken


def attend_kernel(
    groups,
    hops,
    rows_ref,
    doc_query_ref,
    doc_key_ref,
    out_part_ref,
    feed_parts_ref,
    query_ref,
    value_ref,
    within_ref,
    map_ref,
    inverse_ref,
    attended_ref,
    low_ref,
    stats_ref,
    moved_ref,
    values_ref,
    out_full_ref,
    feed_full_ref,
    key_ref,
    leave_ref,
    top_ref,
    total_ref,
    accum_ref,
    key_send,
    key_recv,
    value_send,
    value_recv,
    *sems,
):
    here = Place(groups, feed_full_ref.shape[2])
    here.meet()
    place, has_next, following = here.g, here.above, here.up()
    home_sems, feed_sems = several(sems, len(HomeGather.scratch(groups)), len(Gather.scratch(groups)))
    out_gather = HomeGather(here, out_part_ref, out_full_ref, home_sems)
    feed_gather = Gather(here, feed_parts_ref, feed_full_ref, feed_sems)
    out_gather.start()
    feed_gather.start()
    pauses = Pauses(
        *[
            (functools.partial(out_gather.step, distance), functools.partial(feed_gather.step, distance))
            for distance in range(1, groups)
        ]
    )
    prepared = (rows_ref, query_ref, key_ref, value_ref, within_ref, map_ref, inverse_ref)
    prepare_blocks(0, GROUP // 2, *prepared)
    out_gather.begin()
    feed_gather.begin()
    prepare_blocks(GROUP // 2, GROUP, *prepared)

    def value_copy(source, slot):
        return pltpu.make_async_remote_copy(
            src_ref=source,
            dst_ref=values_ref.at[slot],
            send_sem=value_send.at[slot],
            recv_sem=value_recv.at[slot],
            device_id=following,
            device_id_type=MESH,
        )

    def key_copy(slot):
        return pltpu.make_async_remote_copy(
            src_ref=leave_ref.at[slot],
            dst_ref=moved_ref.at[slot + 1, 0],
            send_sem=key_send.at[slot],
            recv_sem=key_recv.at[slot],
            device_id=following,
            device_id_type=MESH,
        )

    def move(keys, block, head):
        return dot2(keys, map_ref[tile(block), tile(head)]).astype(BF16)

    for head in range(OWN):
        keys = key_ref[tile(0), tile(head)]
        for block in range(1, GROUP):
            moved_ref[0, block, tile(0, block), tile(head)] = keys
            keys = jnp.concatenate([move(keys, block, head), key_ref[tile(block), tile(head)]], 0)
        leave_ref[0, :, tile(head)] = keys

    @pl.when(has_next)
    def _():
        key_copy(0).start()
        value_copy(value_ref, 0).start()

    pauses()

    def row_counts(block, hop, first, count):
        return doc_query_ref[tile(block), :] == doc_key_ref[hop, :, tile(first, count)]

    for block in range(GROUP):
        counts = row_counts(block, 0, 0, block + 1)
        wide = (BLOCK, (block + 1) * BLOCK)
        counts = counts & (iota(0, wide) + block * BLOCK >= iota(1, wide))
        for head in range(OWN):
            scores = within_ref[tile(block), tile(head)]
            if block:
                before = dot(query_ref[tile(block), tile(head)], moved_ref[0, block, tile(0, block), tile(head)], NT)
                scores = jnp.concatenate([before, scores], 1)
            scores = masked(scores, counts)
            top = jnp.max(scores, axis=1, keepdims=True)
            weights = jnp.exp(scores - top)
            top_ref[head, tile(block), :] = jnp.broadcast_to(top, (BLOCK, BLOCK))
            total_ref[head, tile(block), :] = jnp.broadcast_to(jnp.sum(weights, axis=1, keepdims=True), (BLOCK, BLOCK))
            accum_ref[tile(block), tile(head)] = dot(weights.astype(BF16), value_ref[tile(0, block + 1), tile(head)])

    def hop_step(hop, last):
        @pl.when(place >= hop)
        def _():
            key_copy(hop - 1).wait_recv()
            for head in range(OWN):
                keys = moved_ref[hop, 0, :, tile(head)]
                for block in range(GROUP):
                    if last:
                        if block == GROUP - 1:
                            break
                        keys = move(keys[BLOCK:], block, head)
                        moved_ref[hop, block + 1, tile(block + 1, GROUP - 1 - block), tile(head)] = keys
                    else:
                        keys = move(keys, block, head)
                        if block < GROUP - 1:
                            moved_ref[hop, block + 1, :, tile(head)] = keys
                        else:
                            leave_ref[hop, :, tile(head)] = keys
            value_copy(value_ref, hop - 1).wait_recv()
            if not last:

                @pl.when(has_next)
                def _():
                    key_copy(hop).start()
                    value_copy(values_ref.at[hop - 1], hop).start()

            for block in range(GROUP):
                first = block if last else 0
                count = GROUP - first
                counts = row_counts(block, hop, first, count)
                for head in range(OWN):
                    scores = masked(
                        dot(query_ref[tile(block), tile(head)], moved_ref[hop, block, tile(first, count), tile(head)], NT),
                        counts,
                    )
                    old = top_ref[head, tile(block), :]
                    top = jnp.maximum(old, jnp.broadcast_to(jnp.max(scores, axis=1, keepdims=True), (BLOCK, BLOCK)))
                    factor = jnp.exp(old - top)
                    weights = jnp.exp(scores - jnp.concatenate([top] * count, 1))
                    top_ref[head, tile(block), :] = top
                    total_ref[head, tile(block), :] = total_ref[head, tile(block), :] * factor + jnp.sum(
                        weights, axis=1, keepdims=True
                    )
                    accum_ref[tile(block), tile(head)] = accum_ref[tile(block), tile(head)] * factor + dot(
                        weights.astype(BF16), values_ref[hop - 1, tile(first, count), tile(head)]
                    )

    if hops > 2:

        def between(hop, carry):
            hop_step(hop, False)
            return carry

        lax.fori_loop(1, hops, between, 0)
    else:
        for hop in range(1, hops):
            pauses()
            hop_step(hop, False)
    pauses()
    hop_step(hops, True)

    for block in range(GROUP):
        stats = jnp.zeros((BLOCK, BLOCK), F32)
        for head in range(OWN):
            total = total_ref[head, tile(block), :]
            result = accum_ref[tile(block), tile(head)] / total
            attended_ref[tile(block), tile(head)] = result
            low_ref[tile(block), tile(head)] = result.astype(BF16)
            stats = jnp.where(iota(1) == head, top_ref[head, tile(block), :], stats)
            stats = jnp.where(iota(1) == OWN + head, total, stats)
        stats_ref[tile(block), :] = stats

    def settle(slot, carry):
        @pl.when(has_next & (place >= slot))
        def _():
            key_copy(slot).wait_send()
            value_copy(value_ref, slot).wait_send()

        return carry

    lax.fori_loop(0, hops, settle, 0)
    pauses.rest()
    out_gather.finish()
    feed_gather.finish()


def in_vmem(count):
    return [pl.BlockSpec(memory_space=pltpu.VMEM)] * count


def anywhere(count):
    return [pl.BlockSpec(memory_space=pl.ANY)] * count


def shape(kind, *dims):
    return jax.ShapeDtypeStruct(dims, kind)


def communicating(number, name, vmem=58):
    return {
        "compiler_params": pltpu.CompilerParams(collective_id=number, has_side_effects=True, vmem_limit_bytes=vmem << 20),
        "name": name,
    }


def attend(groups, lines, hops, projected, doc_query, doc_key, out_part, feed_parts):
    length = projected.shape[0]
    rows, width = out_part.shape
    dma = pltpu.SemaphoreType.DMA
    return pl.pallas_call(
        functools.partial(attend_kernel, groups, hops),
        out_shape=[
            shape(BF16, length, WIDE),
            shape(BF16, length, WIDE),
            shape(F32, length, WIDE),
            shape(F32, length, WIDE),
            shape(F32, length, WIDE),
            shape(F32, length, WIDE),
            shape(BF16, length, WIDE),
            shape(F32, length, BLOCK),
            shape(BF16, hops + 1, GROUP, length, WIDE),
            shape(BF16, hops, length, WIDE),
            shape(BF16, groups // GROUP, GROUP, lines, rows, width),
            shape(BF16, groups, GROUP, lines, rows, feed_parts.shape[2]),
        ],
        in_specs=in_vmem(3) + anywhere(2),
        out_specs=in_vmem(10) + anywhere(2),
        scratch_shapes=[
            pltpu.VMEM((length, WIDE), BF16),
            pltpu.VMEM((hops, length, WIDE), BF16),
            pltpu.VMEM((OWN, length, BLOCK), F32),
            pltpu.VMEM((OWN, length, BLOCK), F32),
            pltpu.VMEM((length, WIDE), F32),
            dma((hops,)),
            dma((hops,)),
            dma((hops,)),
            dma((hops,)),
        ]
        + HomeGather.scratch(groups)
        + Gather.scratch(groups),
        **communicating(1, "attend"),
    )(projected, doc_query, doc_key, out_part, feed_parts)


def attend_back_kernel(
    groups,
    hops,
    query_ref,
    value_ref,
    within_ref,
    map_ref,
    doc_query_ref,
    doc_key_ref,
    attended_ref,
    stats_ref,
    moved_ref,
    values_ref,
    att_grad_ref,
    rows_ref,
    inverse_ref,
    out_partial_ref,
    feed_partial_ref,
    rows_grad_ref,
    feed_result_ref,
    out_result_ref,
    query_grad_ref,
    key_grad_ref,
    within_grad_ref,
    map_grad_ref,
    value_grad_ref,
    scaled_ref,
    dots_ref,
    direct_ref,
    key_slots_ref,
    value_slots_ref,
    key_send,
    key_recv,
    value_send,
    value_recv,
    *refs,
):
    here = Place(groups, feed_partial_ref.shape[2])
    here.meet(column=True)
    place, has_next, previous = here.g, here.above, here.down()
    feed_refs, out_refs = several(
        refs, len(Scatter.scratch(groups, feed_partial_ref.shape)), len(HomeScatter.scratch(groups, out_partial_ref.shape))
    )
    feed_scatter = Scatter(here, feed_partial_ref, feed_result_ref, feed_refs)
    out_scatter = HomeScatter(here, out_partial_ref, out_result_ref, out_refs)
    feed_scatter.start(out_scatter.start)
    pauses = Pauses(*[(functools.partial(feed_scatter.step, wave),) for wave in range(1, groups)])

    def key_copy(hop):
        slot = hop - 1
        return pltpu.make_async_remote_copy(
            src_ref=key_slots_ref.at[hop],
            dst_ref=key_slots_ref.at[slot],
            send_sem=key_send.at[slot],
            recv_sem=key_recv.at[slot],
            device_id=previous,
            device_id_type=MESH,
        )

    def value_copy(hop):
        slot = hop - 1
        return pltpu.make_async_remote_copy(
            src_ref=value_slots_ref.at[hop],
            dst_ref=value_slots_ref.at[slot],
            send_sem=value_send.at[slot],
            recv_sem=value_recv.at[slot],
            device_id=previous,
            device_id_type=MESH,
        )

    map_grad_ref[...] = jnp.zeros_like(map_grad_ref)
    query_grad_ref[...] = jnp.zeros_like(query_grad_ref)
    for block in range(GROUP):
        for head in range(OWN):
            at = (tile(block), tile(head))
            grad = att_grad_ref[at].astype(F32)
            total = stats_ref[tile(block), OWN + head : OWN + head + 1]
            scaled_ref[at] = (grad / total).astype(BF16)
            dots = -jnp.sum(grad * attended_ref[at], axis=1, keepdims=True) / total
            dots_ref[head, tile(block), :] = jnp.broadcast_to(dots, (BLOCK, BLOCK))

    def pair(block, head, scores, counts, values):
        count = scores.shape[1] // BLOCK
        top = stats_ref[tile(block), head : head + 1]
        weights = jnp.exp(masked(scores, counts) - top)
        weight_grad = dot(scaled_ref[tile(block), tile(head)], values, NT)
        dots = jnp.concatenate([dots_ref[head, tile(block), :]] * count, 1)
        return weights, weights * (weight_grad + dots) * SCALE

    def row_counts(block, hop, first, count):
        return doc_query_ref[tile(block), :] == doc_key_ref[hop, :, tile(first, count)]

    def hop_direct(hop, last):
        for head in range(OWN):
            value_grad_ref[:, tile(head)] = jnp.zeros((GROUP * BLOCK, BLOCK), F32)
        for block in range(GROUP):
            first = block if last else 0
            count = GROUP - first
            counts = row_counts(block, hop, first, count)
            for head in range(OWN):
                query = query_ref[tile(block), tile(head)]
                keys = moved_ref[hop, block, tile(first, count), tile(head)]
                weights, grad = pair(
                    block, head, dot(query, keys, NT), counts, values_ref[hop - 1, tile(first, count), tile(head)]
                )
                raw = grad.astype(BF16)
                query_grad_ref[tile(block), tile(head)] += dot(raw, keys)
                direct_ref[block, tile(first, count), tile(head)] = dot(raw, query, TN)
                value_grad_ref[tile(first, count), tile(head)] += dot(
                    weights.astype(BF16), scaled_ref[tile(block), tile(head)], TN
                )

    def collect_map(block, head, keys, grads):
        map_grad_ref[tile(block), tile(head)] += dot2(keys, grads, TN)

    def hop_chain(hop, last):
        for head in range(OWN):
            if last:
                grads = direct_ref[GROUP - 1, tile(GROUP - 1), tile(head)]
                for block in range(GROUP - 2, -1, -1):
                    rows = tile(block + 1, GROUP - 1 - block)
                    collect_map(block, head, moved_ref[hop, block, rows, tile(head)], grads)
                    back = dot3(grads, map_ref[tile(block), tile(head)], NT)
                    direct = direct_ref[block, tile(block, GROUP - block), tile(head)]
                    grads = jnp.concatenate([direct[:BLOCK], direct[BLOCK:] + back], 0)
                key_slots_ref[hop, :, tile(head)] = grads.astype(BF16)
                value_slots_ref[hop, :, tile(head)] = value_grad_ref[:, tile(head)].astype(BF16)
            else:
                grads = key_grad_ref[:, tile(head)]
                for block in range(GROUP - 1, -1, -1):
                    collect_map(block, head, moved_ref[hop, block, :, tile(head)], grads)
                    grads = direct_ref[block, :, tile(head)] + dot3(grads, map_ref[tile(block), tile(head)], NT)
                key_slots_ref[hop, :, tile(head)] = grads.astype(BF16)

    def take(hop):
        @pl.when(has_next)
        def _():
            key_copy(hop).wait_recv()
            key_grad_ref[...] = key_slots_ref[hop - 1].astype(F32)

        @pl.when(jnp.logical_not(has_next))
        def _():
            key_grad_ref[...] = jnp.zeros_like(key_grad_ref)

    @pl.when(place >= hops)
    def _():
        hop_direct(hops, True)
        hop_chain(hops, True)
        key_copy(hops).start()
        value_copy(hops).start()

    def between(hop, pause=None):
        pl.when(place >= hop)(lambda: hop_direct(hop, False))
        if pause is not None:
            pause()

        @pl.when(place >= hop)
        def _():
            take(hop + 1)
            hop_chain(hop, False)
            key_copy(hop).start()

            @pl.when(has_next)
            def _():
                value_copy(hop + 1).wait_recv()
                for head in range(OWN):
                    value_slots_ref[hop, :, tile(head)] = (
                        value_grad_ref[:, tile(head)] + value_slots_ref[hop, :, tile(head)].astype(F32)
                    ).astype(BF16)

            @pl.when(jnp.logical_not(has_next))
            def _():
                for head in range(OWN):
                    value_slots_ref[hop, :, tile(head)] = value_grad_ref[:, tile(head)].astype(BF16)

            value_copy(hop).start()

    if hops > 2:

        def step(counter, carry):
            between(hops - 1 - counter)
            return carry

        lax.fori_loop(0, hops - 1, step, 0)
    else:
        for hop in range(hops - 1, 0, -1):
            between(hop, pauses)

    for head in range(OWN):
        value_grad_ref[:, tile(head)] = jnp.zeros((GROUP * BLOCK, BLOCK), F32)
    for block in range(GROUP):
        wide = (BLOCK, (block + 1) * BLOCK)
        counts = row_counts(block, 0, 0, block + 1) & (iota(0, wide) + block * BLOCK >= iota(1, wide))
        for head in range(OWN):
            query = query_ref[tile(block), tile(head)]
            scores = within_ref[tile(block), tile(head)]
            if block:
                keys = moved_ref[0, block, tile(0, block), tile(head)]
                scores = jnp.concatenate([dot(query, keys, NT), scores], 1)
            weights, grad = pair(block, head, scores, counts, value_ref[tile(0, block + 1), tile(head)])
            within_grad_ref[tile(block), tile(head)] = grad[:, block * BLOCK :]
            value_grad_ref[tile(0, block + 1), tile(head)] += dot(
                weights.astype(BF16), scaled_ref[tile(block), tile(head)], TN
            )
            if block:
                raw = grad[:, : block * BLOCK].astype(BF16)
                query_grad_ref[tile(block), tile(head)] += dot(raw, keys)
                direct_ref[block, tile(0, block), tile(head)] = dot(raw, query, TN)
    pauses()
    take(1)
    for head in range(OWN):
        grads = key_grad_ref[:, tile(head)]
        for block in range(GROUP - 1, 0, -1):
            key_grad_ref[tile(block), tile(head)] = grads[block * BLOCK :]
            grads = grads[: block * BLOCK]
            collect_map(block, head, moved_ref[0, block, tile(0, block), tile(head)], grads)
            grads = direct_ref[block, tile(0, block), tile(head)] + dot3(grads, map_ref[tile(block), tile(head)], NT)
        key_grad_ref[tile(0), tile(head)] = grads

    @pl.when(has_next)
    def _():
        value_copy(1).wait_recv()
        value_grad_ref[...] += value_slots_ref[0].astype(F32)

    def settle(hop, carry):
        @pl.when(place >= hop)
        def _():
            key_copy(hop).wait_send()
            value_copy(hop).wait_send()

        return carry

    lax.fori_loop(1, hops + 1, settle, 0)
    pieces = (rows_ref, inverse_ref, query_grad_ref, key_grad_ref, within_grad_ref, map_grad_ref, value_grad_ref, rows_grad_ref)
    prepare_back_blocks(0, GROUP // 2, *pieces)
    pauses.rest()
    out_scatter.push()
    prepare_back_blocks(GROUP // 2, GROUP, *pieces)
    feed_scatter.last()
    out_scatter.last()
    feed_scatter.finish()
    out_scatter.finish()


def attend_back(groups, hops, *args):
    length = args[0].shape[0]
    out, feed = args[-2:]
    dma = pltpu.SemaphoreType.DMA
    return pl.pallas_call(
        functools.partial(attend_back_kernel, groups, hops),
        out_shape=[shape(BF16, *args[-4].shape), shape(BF16, GROUP, *feed.shape[3:]), shape(BF16, *out.shape[3:])],
        in_specs=in_vmem(len(args) - 2) + anywhere(2),
        out_specs=in_vmem(3),
        scratch_shapes=[pltpu.VMEM((length, WIDE), F32)] * 5
        + [
            pltpu.VMEM((length, WIDE), BF16),
            pltpu.VMEM((OWN, length, BLOCK), F32),
            pltpu.VMEM((GROUP, length, WIDE), F32),
            pltpu.VMEM((hops + 1, length, WIDE), BF16),
            pltpu.VMEM((hops + 1, length, WIDE), BF16),
            dma((hops,)),
            dma((hops,)),
            dma((hops,)),
            dma((hops,)),
        ]
        + Scatter.scratch(groups, feed.shape)
        + HomeScatter.scratch(groups, out.shape),
        **communicating(2, "attend_back", 60),
    )(*args)


def gather_kernel(groups, parts_ref, tokens_ref, cotangent_ref, full_ref, tokens_all_ref, cotangent_all_ref, send, recv, local, *sems):
    here = Place(groups, full_ref.shape[2])
    here.meet()
    gather = Gather(here, parts_ref, full_ref, sems)
    gather.start()
    size = tokens_ref.shape[0]
    own = pl.ds(pl.multiple_of(here.m * size, size), size)
    copies = []
    for index, (source, target) in enumerate(((tokens_ref, tokens_all_ref), (cotangent_ref, cotangent_all_ref))):
        copies.append(pltpu.make_async_copy(source, target.at[own], local.at[index]))
        for offset in (2, 3, 1):
            copies.append(
                remote(source, target.at[own], send.at[index, offset], recv.at[index, offset], here.member(offset))
            )
    for copy in copies:
        copy.start()
    gather.begin()
    for distance in range(1, groups):
        gather.step(distance)
    for copy in copies:
        copy.wait()
    gather.finish()


def gather_first(groups, lines, parts, tokens, cotangent):
    dma = pltpu.SemaphoreType.DMA
    size, width = tokens.shape
    return pl.pallas_call(
        functools.partial(gather_kernel, groups),
        out_shape=[
            shape(BF16, groups, GROUP, lines, *parts.shape[1:]),
            shape(BF16, GROUP * size, width),
            shape(BF16, GROUP * size, width),
        ],
        in_specs=anywhere(3),
        out_specs=anywhere(3),
        scratch_shapes=[dma((2, GROUP)), dma((2, GROUP)), dma((2,))] + Gather.scratch(groups),
        **communicating(0, "gather_first", 16),
    )(parts, tokens, cotangent)


def rms_norm(values, gain):
    return values * lax.rsqrt(jnp.mean(values * values, axis=-1, keepdims=True) + EPSILON) * gain


def rms_back(values, gain, grad):
    scale = lax.rsqrt(jnp.mean(values * values, axis=-1, keepdims=True) + EPSILON)
    straight = values * scale
    lifted = grad * gain
    back = scale * (lifted - straight * jnp.mean(lifted * straight, axis=-1, keepdims=True))
    return back, grad * straight


def branch_kernel(groups, partial_ref, tokens_ref, gain_ref, down_ref, hidden_ref, normed_ref, down_full_ref, *refs):
    here = Place(groups, down_full_ref.shape[1])
    here.meet()
    sum_refs, gather_refs, down_refs = several(refs, 7, 2, len(Gather.scratch(groups)))
    total = GroupSum(here, partial_ref, sum_refs)
    whole = GroupGather(here, normed_ref, gather_refs)
    down = Gather(here, down_ref, down_full_ref, down_refs, mixed=False)
    pauses = Pauses(*[(functools.partial(down.step, distance),) for distance in range(1, groups)])
    total.start()
    down.start()
    down.begin()
    for chunk in range(CHUNKS):
        total.pass_on(chunk)
    pauses()
    for chunk in range(CHUNKS):
        hidden = tokens_ref[total.at(chunk), :].astype(F32) + total.take(chunk)
        hidden_ref[total.at(chunk), :] = hidden
        normed_ref[whole.at(chunk, here.m), :] = rms_norm(hidden, gain_ref[...]).astype(BF16)
        whole.give(chunk)
    pauses()
    for chunk in range(CHUNKS):
        whole.pass_on(chunk)
    pauses.rest()
    whole.finish()
    total.finish()
    down.finish()


def branch(groups, lines, partial, tokens, gain, down):
    size, width = tokens.shape
    return pl.pallas_call(
        functools.partial(branch_kernel, groups),
        out_shape=[shape(F32, size, width), shape(BF16, GROUP * size, width), shape(BF16, groups, lines, *down.shape)],
        in_specs=in_vmem(3) + anywhere(1),
        out_specs=in_vmem(2) + anywhere(1),
        scratch_shapes=GroupSum.scratch(size, width) + GroupGather.scratch() + Gather.scratch(groups),
        **communicating(3, "branch", 32),
    )(partial, tokens, gain, down)


def branch_back_kernel(
    groups, partial_ref, hidden_ref, cotangent_ref, gain_ref, down_ref, grad_ref, grad_low_ref, gain_grad_ref, down_result_ref, *refs
):
    here = Place(groups, down_ref.shape[2])
    here.meet()
    sum_refs, gather_refs, down_refs = several(refs, 7, 2, len(Scatter.scratch(groups, down_ref.shape)))
    total = GroupSum(here, partial_ref, sum_refs)
    whole = GroupGather(here, grad_low_ref, gather_refs)
    down = Scatter(here, down_ref, down_result_ref, down_refs)
    pauses = Pauses(*[(functools.partial(down.step, wave),) for wave in range(1, groups)])
    total.start()
    down.start()
    for chunk in range(CHUNKS):
        total.pass_on(chunk)
    pauses()
    gain_grad = jnp.zeros((1, gain_ref.shape[1]), F32)
    for chunk in range(CHUNKS):
        back, gain_rows = rms_back(hidden_ref[total.at(chunk), :], gain_ref[...], total.take(chunk))
        grad = cotangent_ref[total.at(chunk), :].astype(F32) + back
        gain_grad = gain_grad + jnp.sum(gain_rows, axis=0, keepdims=True)
        grad_ref[total.at(chunk), :] = grad
        grad_low_ref[whole.at(chunk, here.m), :] = grad.astype(BF16)
        whole.give(chunk)
    gain_grad_ref[...] = gain_grad
    pauses()
    for chunk in range(CHUNKS):
        whole.pass_on(chunk)
    pauses.rest()
    whole.finish()
    total.finish()
    down.last()
    down.finish()


def branch_back(groups, partial, hidden, cotangent, gain, down):
    size, width = hidden.shape
    return pl.pallas_call(
        functools.partial(branch_back_kernel, groups),
        out_shape=[shape(F32, size, width), shape(BF16, GROUP * size, width), shape(F32, 1, width), shape(F32, 1, *down.shape[3:])],
        in_specs=in_vmem(4) + anywhere(1),
        out_specs=in_vmem(4),
        scratch_shapes=GroupSum.scratch(size, width) + GroupGather.scratch() + Scatter.scratch(groups, down.shape),
        **communicating(4, "branch_back", 48),
    )(partial, hidden, cotangent, gain, down)


def finish_kernel(
    groups,
    first_ref,
    normed_partial_ref,
    output_partial_ref,
    tokens_ref,
    hidden_ref,
    grad_ref,
    gain_ref,
    first_result_ref,
    tokens_grad_ref,
    output_ref,
    *refs,
):
    here = Place(groups, first_ref.shape[2])
    here.meet()
    first_refs, normed_refs, output_refs = several(refs, len(Scatter.scratch(groups, first_ref.shape)), 7, 7)
    first = Scatter(here, first_ref, first_result_ref, first_refs)
    normed = GroupSum(here, normed_partial_ref, normed_refs)
    output = GroupSum(here, output_partial_ref, output_refs)
    first.start()
    normed.start()
    output.start()
    for chunk in range(CHUNKS):
        normed.pass_on(chunk)
    for chunk in range(CHUNKS):
        output.pass_on(chunk)
    for wave in range(1, groups):
        first.step(wave)
    for chunk in range(CHUNKS):
        back, _ = rms_back(tokens_ref[normed.at(chunk), :].astype(F32), gain_ref[...], normed.take(chunk))
        tokens_grad_ref[normed.at(chunk), :] = (grad_ref[normed.at(chunk), :] + back).astype(BF16)
    for chunk in range(CHUNKS):
        output_ref[output.at(chunk), :] = (hidden_ref[output.at(chunk), :] + output.take(chunk)).astype(BF16)
    first.last()
    normed.finish()
    output.finish()
    first.finish()


def finish(groups, first, normed_partial, output_partial, tokens, hidden, grad, gain):
    size, width = tokens.shape
    return pl.pallas_call(
        functools.partial(finish_kernel, groups),
        out_shape=[shape(BF16, GROUP, *first.shape[3:]), shape(BF16, size, width), shape(BF16, size, width)],
        in_specs=anywhere(1) + in_vmem(6),
        out_specs=in_vmem(3),
        scratch_shapes=Scatter.scratch(groups, first.shape)
        + GroupSum.scratch(size, width)
        + GroupSum.scratch(size, width),
        **communicating(5, "finish"),
    )(first, normed_partial, output_partial, tokens, hidden, grad, gain)


def on_device(
    tokens,
    doc_ids,
    norm_gain,
    query_weight,
    key_weight,
    value_weight,
    house_weight,
    beta_weight,
    out_weight,
    ffn_gain,
    gate_weight,
    up_weight,
    down_weight,
    cotangent,
):
    groups, batch = lax.axis_size("g"), lax.axis_size("b")
    devices = groups * GROUP * batch
    rows, width = query_weight.shape
    hidden_rows = down_weight.shape[0]
    hidden_own = gate_weight.shape[1] // GROUP
    block_rows = tokens.shape[1]
    hops = groups // 2
    doc_columns = -(-block_rows // rows)
    place, line = lax.axis_index("g"), lax.axis_index("b")

    def columns(weight):
        return jnp.transpose(weight.astype(BF16).reshape(rows, GROUP, -1), (1, 0, 2))

    docs = jnp.pad(doc_ids[0].astype(BF16), (0, rows * doc_columns - block_rows)).reshape(rows, doc_columns)
    same = jnp.concatenate([norm_gain.astype(BF16)[:, None], ffn_gain.astype(BF16)[:, None], docs], 1)
    same = jnp.broadcast_to(same[None], (GROUP,) + same.shape)
    same = jnp.pad(same, ((0, 0), (0, 0), (0, EXTRA - OWN - same.shape[2])))
    first_parts = jnp.concatenate(
        [columns(w) for w in (query_weight, key_weight, value_weight, house_weight, beta_weight)] + [same], 2
    )

    def unit_columns(weight):
        parts = weight.astype(BF16).reshape(rows, groups, GROUP, batch, hidden_rows)
        return jnp.transpose(parts, (2, 0, 1, 3, 4)).reshape(GROUP, rows, hidden_own)

    feed_parts = jnp.concatenate([unit_columns(gate_weight), unit_columns(up_weight)], 2)
    first, tokens_all, cotangent_all = gather_first(groups, batch, first_parts, tokens[0], cotangent[0])
    first = first.reshape(width, -1)

    extra = first[:, 4 * WIDE :]
    gain_one = extra[:, OWN].astype(F32)[None]
    gain_two = extra[:, OWN + 1].astype(F32)[None]
    docs = extra[:, OWN + 2 : OWN + 2 + doc_columns].astype(jnp.int32)
    docs = docs.reshape(devices, -1)[:, :block_rows].reshape(groups, GROUP, batch, block_rows)
    docs = lax.dynamic_index_in_dim(docs, line, 2, keepdims=False).reshape(groups, GROUP * block_rows)
    doc_key = jnp.stack(
        [
            jnp.where(place >= hop, lax.dynamic_index_in_dim(docs, jnp.maximum(place - hop, 0), 0, keepdims=False), -1)
            for hop in range(hops + 1)
        ]
    )[:, None, :]
    doc_query = lax.dynamic_index_in_dim(docs, place, 0, keepdims=False)[:, None]

    tokens_wide = tokens_all.astype(F32)
    straight = tokens_wide * lax.rsqrt(jnp.mean(tokens_wide * tokens_wide, axis=-1, keepdims=True) + EPSILON)
    normed = (straight * gain_one).astype(BF16)
    projected = dot(normed, first)
    (query, value, within, maps, inverse, attended, attended_low, stats, moved, values, out_full, feed) = attend(
        groups, batch, hops, projected, doc_query, doc_key, out_weight.astype(BF16), feed_parts
    )
    out_full = out_full.reshape(WIDE, width)
    feed = feed.reshape(width, -1)
    hidden, normed_two, down_full = branch(
        groups, batch, dot(attended_low, out_full).astype(BF16), tokens[0], gain_two, down_weight.astype(BF16)
    )
    down_full = down_full.reshape(hidden_own, width)
    both = dot(normed_two, feed)
    gate, up = both[:, :hidden_own], both[:, hidden_own:]
    sigmoid = jax.nn.sigmoid(gate)
    silu = gate * sigmoid
    active = (silu * up).astype(BF16)
    output_partial = dot(active, down_full).astype(BF16)

    active_grad = dot(cotangent_all, down_full, NT)
    gate_grad = (active_grad * up * (sigmoid * (1.0 + gate * (1.0 - sigmoid)))).astype(BF16)
    up_grad = (active_grad * silu).astype(BF16)
    feed_grads = jnp.concatenate([gate_grad, up_grad], 1)
    down_partial = dot(active, cotangent_all, TN).astype(BF16).reshape(groups, 1, batch, hidden_rows, width)
    hidden_grad, branch_grad, gain_two_grad, down_weight_grad = branch_back(
        groups, dot(feed_grads, feed, NT).astype(BF16), hidden, cotangent[0], gain_two, down_partial
    )
    att_grad = dot(branch_grad, out_full, NT).astype(BF16)
    feed_partial = dot(normed_two, feed_grads, TN).astype(BF16).reshape(groups, GROUP, batch, rows, -1)
    out_partial = dot(attended_low, branch_grad, TN).astype(BF16).reshape(groups // GROUP, GROUP, batch, rows, width)
    rows_grad, feed_grad, out_weight_grad = attend_back(
        groups, hops, query, value, within, maps, doc_query, doc_key, attended, stats, moved, values, att_grad, projected, inverse,
        out_partial, feed_partial,
    )
    normed_grad = dot(rows_grad, first, NT)
    gain_one_grad = jnp.sum(normed_grad * straight, axis=0)
    first_partial = dot(normed, rows_grad, TN)
    lane = iota(1, (1, first_partial.shape[1]))
    first_partial = jnp.where(lane == 4 * WIDE + OWN, gain_one_grad[:, None], first_partial)
    first_partial = jnp.where(lane == 4 * WIDE + OWN + 1, gain_two_grad[0][:, None], first_partial)
    first_partial = first_partial.astype(BF16).reshape(groups, GROUP, batch, rows, -1)
    first_grad, tokens_grad, output = finish(
        groups, first_partial, normed_grad.astype(BF16), output_partial, tokens[0], hidden, hidden_grad, gain_one
    )
    first_grad = first_grad.astype(F32)
    output, tokens_grad = output[None], tokens_grad[None]
    out_weight_grad = out_weight_grad.astype(F32)
    down_weight_grad = down_weight_grad[0]

    def whole_columns(parts):
        return jnp.transpose(parts, (1, 0, 2)).reshape(rows, -1)

    query_weight_grad, key_weight_grad, value_weight_grad, house_weight_grad = [
        whole_columns(first_grad[:, :, part * WIDE : (part + 1) * WIDE]) for part in range(4)
    ]
    beta_weight_grad = whole_columns(first_grad[:, :, 4 * WIDE : 4 * WIDE + OWN])
    gains_grad = jnp.sum(first_grad[:, :, 4 * WIDE + OWN : 4 * WIDE + OWN + 2], axis=0)

    def unit_whole(parts):
        parts = parts.astype(F32).reshape(GROUP, rows, groups, batch, hidden_rows)
        return jnp.transpose(parts, (1, 2, 0, 3, 4)).reshape(rows, -1)

    gate_weight_grad = unit_whole(feed_grad[:, :, :hidden_own])
    up_weight_grad = unit_whole(feed_grad[:, :, hidden_own:])
    return (
        output,
        tokens_grad,
        gains_grad[:, 0],
        query_weight_grad,
        key_weight_grad,
        value_weight_grad,
        house_weight_grad,
        beta_weight_grad,
        out_weight_grad,
        gains_grad[:, 1],
        gate_weight_grad,
        up_weight_grad,
        down_weight_grad,
    )


def solution(mesh):
    groups = mesh.shape["seq"] // GROUP
    inner = Mesh(mesh.devices.reshape(groups, GROUP, mesh.shape["batch"]), ("g", "m", "b"))
    line = P("b", ("g", "m"), None)
    vector = P(("g", "m", "b"))
    matrix = P(("g", "m", "b"), None)
    in_specs = (line, P("b", ("g", "m")), vector) + (matrix,) * 6 + (vector,) + (matrix,) * 3 + (line,)
    out_specs = (line, line, vector) + (matrix,) * 6 + (vector,) + (matrix,) * 3
    return jax.shard_map(on_device, mesh=inner, in_specs=in_specs, out_specs=out_specs, check_vma=False)
```

```python
import functools

import jax
import jax.numpy as jnp
from jax import lax
from jax.experimental import pallas as pl
from jax.experimental.pallas import tpu as pltpu
from jax.sharding import Mesh
from jax.sharding import PartitionSpec as P

HEADS = 12
HEAD_DIM = 128
GROUP = 4
OWN = HEADS // GROUP
WIDE = OWN * HEAD_DIM
BLOCK = 128
EXTRA = 128
EPSILON = 1e-06
NEGATIVE = -1e30
SCALE = HEAD_DIM ** (-0.5)
MESH = pl.DeviceIdType.MESH
F32 = jnp.float32
BF16 = jnp.bfloat16
NN = (((1,), (0,)), ((), ()))
NT = (((1,), (1,)), ((), ()))
TN = (((0,), (0,)), ((), ()))


def dot(left, right, dims=NN):
    return lax.dot_general(left, right, dims, preferred_element_type=F32)


def split(value):
    high = value.astype(BF16)
    return high, (value - high.astype(F32)).astype(BF16)


def dot3(left, right, dims=NN):
    left_high, left_low = split(left)
    right_high, right_low = split(right)
    return dot(left_high, right_high, dims) + (
        dot(left_high, right_low, dims) + dot(left_low, right_high, dims)
    )


def dot2(left, right, dims=NN):
    high, low = split(right)
    return dot(left, high, dims) + dot(left, low, dims)


def tile(index, count=1):
    return pl.ds(index * BLOCK, count * BLOCK)


def iota(axis, shape=(BLOCK, BLOCK)):
    return lax.broadcasted_iota(jnp.int32, shape, axis)


def invert(strict):
    row, col = iota(0), iota(1)
    eye = jnp.where(row == col, 1.0, 0.0)

    def part(size):
        return (row // (2 * size) == col // (2 * size)) & (row // size > col // size)

    totals = [eye - jnp.where(part(1), value, 0.0) for value in strict]
    size = 2
    while size < BLOCK:
        mask = part(size)
        pieces = [jnp.where(mask, value, 0.0) for value in strict]
        inner = [dot3(piece, total) for piece, total in zip(pieces, totals)]
        outer = [dot3(total, value) for total, value in zip(totals, inner)]
        totals = [total - value for total, value in zip(totals, outer)]
        size *= 2
    return totals


def unit_of(house):
    scale = lax.rsqrt(jnp.sum(house * house, axis=-1, keepdims=True) + EPSILON)
    return house * scale, scale


def products(query, key, unit):
    both = dot3(jnp.concatenate([unit, query], 0), jnp.concatenate([unit, key], 0), NT)
    return both[:BLOCK, :BLOCK], both[:BLOCK, BLOCK:], both[BLOCK:, :BLOCK], both[BLOCK:, BLOCK:]


def prepare_blocks(first, last, rows_ref, query_ref, key_ref, value_ref, within_ref, map_ref, inverse_ref):
    row, col = iota(0), iota(1)

    def one_block(block, carry):
        at = tile(block)
        kept, strict = [], []
        for head in range(OWN):
            query, key, value, house = [
                rows_ref[at, pl.ds(part * WIDE + head * BLOCK, BLOCK)] for part in range(4)
            ]
            rate = rows_ref[at, pl.ds(4 * WIDE, EXTRA)][:, head : head + 1]
            value_ref[at, tile(head)] = value.astype(BF16)
            unit, _ = unit_of(house)
            strength = 2.0 * jax.nn.sigmoid(rate)
            unit_unit, unit_key, query_unit, query_key = products(query, key, unit)
            strict.append(jnp.where(row > col, strength * unit_unit, 0.0))
            reach = jnp.where(row > col, strength * unit_key, 0.0)
            project = jnp.where(row >= col, query_unit, 0.0)
            kept.append((query, key, unit, strength, reach, project, query_key))
        inverses = invert(strict)
        for head in range(OWN):
            query, key, unit, strength, reach, project, query_key = kept[head]
            inverse = inverses[head]
            solved = dot3(inverse, jnp.concatenate([strength * unit, reach], 1))
            from_query = dot3(project, solved)
            from_unit = dot3(solved, unit, TN)
            query_ref[at, tile(head)] = (query - from_query[:, :BLOCK]).astype(BF16)
            within_ref[at, tile(head)] = query_key - from_query[:, BLOCK:]
            map_ref[at, tile(head)] = jnp.where(row == col, 1.0, 0.0) - from_unit[:BLOCK]
            key_ref[at, tile(head)] = (key - from_unit[BLOCK:]).astype(BF16)
            inverse_ref[at, tile(head)] = inverse
        return carry

    lax.fori_loop(first, last, one_block, 0)


def prepare_back_blocks(first, last, panels_ref, extra_ref, query_grad_ref, key_grad_ref, within_grad_ref, map_grad_ref, value_grad_ref, out_ref):
    row, col = iota(0), iota(1)

    def one_block(block, carry):
        at = tile(block)
        rates = jnp.zeros((BLOCK, EXTRA), F32)
        for head in range(OWN):
            query, key, house, inverse = [panels_ref[part, at, tile(head)] for part in range(4)]
            rate = extra_ref[at, :][:, head : head + 1]
            query_grad = query_grad_ref[at, tile(head)]
            key_grad = key_grad_ref[at, tile(head)]
            within_grad = within_grad_ref[at, tile(head)]
            map_grad = map_grad_ref[at, tile(head)]
            unit, scale = unit_of(house)
            strength = 2.0 * jax.nn.sigmoid(rate)
            unit_unit, unit_key, query_unit, query_key = products(query, key, unit)
            reach = jnp.where(row > col, strength * unit_key, 0.0)
            project = jnp.where(row >= col, query_unit, 0.0)
            solved = dot3(inverse, jnp.concatenate([strength * unit, reach], 1))
            both_grad = jnp.concatenate([query_grad, within_grad], 1)
            project_grad = jnp.where(row >= col, -dot3(both_grad, solved, NT), 0.0)
            solved_grad = -(
                dot3(project, both_grad, TN)
                + dot3(unit, jnp.concatenate([map_grad, key_grad], 0), NT)
            )
            given_grad = dot3(inverse, solved_grad, TN)
            strict_grad = jnp.where(row > col, -dot3(given_grad, solved, NT), 0.0)
            scaled_grad = given_grad[:, :BLOCK]
            reach_grad = jnp.where(row > col, given_grad[:, BLOCK:], 0.0)
            strength_grad = jnp.sum(
                scaled_grad * unit + reach_grad * unit_key + strict_grad * unit_unit, axis=1, keepdims=True
            )
            reach_part = strength * reach_grad
            inner_part = strength * strict_grad
            unit_grad = (
                strength * scaled_grad
                + dot3(reach_part, key)
                + dot3(inner_part + inner_part.T, unit)
                + dot3(project_grad, query, TN)
                - dot3(solved[:, :BLOCK], map_grad)
                - dot3(solved[:, BLOCK:], key_grad)
            )
            query_out = query_grad + dot3(within_grad, key) + dot3(project_grad, unit)
            key_out = key_grad + dot3(within_grad, query, TN) + dot3(reach_part, unit, TN)
            house_out = scale * (unit_grad - unit * jnp.sum(unit * unit_grad, axis=1, keepdims=True))
            rate_out = strength_grad * strength * (1.0 - 0.5 * strength)
            rates = jnp.where(iota(1, (BLOCK, EXTRA)) == head, rate_out, rates)
            out_ref[at, pl.ds(head * BLOCK, BLOCK)] = query_out.astype(BF16)
            out_ref[at, pl.ds(WIDE + head * BLOCK, BLOCK)] = key_out.astype(BF16)
            out_ref[at, pl.ds(2 * WIDE + head * BLOCK, BLOCK)] = value_grad_ref[at, tile(head)].astype(BF16)
            out_ref[at, pl.ds(3 * WIDE + head * BLOCK, BLOCK)] = house_out.astype(BF16)
        out_ref[at, pl.ds(4 * WIDE, EXTRA)] = rates.astype(BF16)
        return carry

    lax.fori_loop(first, last, one_block, 0)


def remote(source, target, send, recv, device):
    return pltpu.make_async_remote_copy(
        src_ref=source, dst_ref=target, send_sem=send, recv_sem=recv, device_id=device, device_id_type=MESH
    )


class Place:
    def __init__(self, groups, lines):
        self.groups, self.lines = groups, lines
        self.g, self.m, self.b = lax.axis_index("g"), lax.axis_index("m"), lax.axis_index("b")
        self.below, self.above = self.g > 0, self.g < groups - 1

    def other(self, offset):
        return {1: self.m + 1 - 2 * (self.m % 2), 2: (self.m + 2) % GROUP, 3: GROUP - 1 - self.m}[offset]

    def member(self, offset):
        return {"g": self.g, "m": self.other(offset), "b": self.b}

    def up(self):
        return {"g": self.g + 1, "m": self.m, "b": self.b}

    def down(self):
        return {"g": self.g - 1, "m": self.m, "b": self.b}

    def across(self):
        return {"g": self.g, "m": self.m, "b": 1 - self.b}

    def column(self, group):
        return {"g": group, "m": self.m, "b": self.b}

    def meet(self, column=False):
        barrier = pltpu.get_barrier_semaphore()

        def greet(device):
            pl.semaphore_signal(barrier, 1, device_id=device, device_id_type=MESH)

        for offset in range(1, GROUP):
            greet(self.member(offset))
        greet(self.across())
        if column:
            for step in range(1, self.groups):
                greet(self.column((self.g + step) % self.groups))
            count = GROUP + self.groups - 1
        else:
            pl.when(self.above)(lambda: greet(self.up()))
            pl.when(self.below)(lambda: greet(self.down()))
            count = GROUP + self.above.astype(jnp.int32) + self.below.astype(jnp.int32)
        pl.semaphore_wait(barrier, count)


class Gather:
    def __init__(self, place, parts, full, sems, mixed=True):
        self.place, self.parts, self.full, self.mixed = place, parts, full, mixed
        sems = list(sems)
        if parts is not None:
            self.part_send, self.part_recv, self.own_sem = sems[:3]
            sems = sems[3:]
        if sems:
            self.up_send, self.down_send, self.chain_recv, self.line_send, self.line_recv = sems

    @staticmethod
    def inside():
        dma = pltpu.SemaphoreType.DMA
        return [dma((GROUP,)), dma((GROUP,)), dma((1,))]

    @staticmethod
    def outside(groups):
        return [pltpu.SemaphoreType.DMA((groups,))] * 5

    def unit(self, group, line):
        return self.full.at[group, :, line] if self.mixed else self.full.at[group, line]

    def own(self):
        p = self.place
        if self.mixed:
            return pltpu.make_async_copy(self.parts.at[p.m], self.full.at[p.g, p.m, p.b], self.own_sem.at[0])
        return pltpu.make_async_copy(self.parts, self.full.at[p.g, p.b], self.own_sem.at[0])

    def part(self, offset):
        p = self.place
        other = p.other(offset)
        return remote(
            self.parts.at[other], self.full.at[p.g, p.m, p.b], self.part_send.at[offset], self.part_recv.at[offset], p.member(offset)
        )

    def start(self):
        if self.mixed:
            for offset in (2, 3, 1):
                self.part(offset).start()
        self.own().start()

    def chain(self, source, up):
        p = self.place
        unit = self.unit(source, p.b)
        sems = self.up_send if up else self.down_send
        return remote(unit, unit, sems.at[source], self.chain_recv.at[source], p.up() if up else p.down())

    def across(self, source):
        p = self.place
        unit = self.unit(source, p.b)
        return remote(unit, unit, self.line_send.at[source], self.line_recv.at[source], p.across())

    def settle(self):
        self.own().wait()
        if self.mixed:
            for offset in (2, 3, 1):
                self.part(offset).wait()

    def spread(self):
        p = self.place
        pl.when(p.above)(lambda: self.chain(p.g, True).start())
        pl.when(p.below)(lambda: self.chain(p.g, False).start())
        self.across(p.g).start()

    def step(self, distance):
        p = self.place

        @pl.when(p.g >= distance)
        def _():
            source = p.g - distance
            self.chain(source, True).wait_recv()
            pl.when(p.above)(lambda: self.chain(source, True).start())
            self.across(source).start()

        @pl.when(p.g + distance < p.groups)
        def _():
            source = p.g + distance
            self.chain(source, False).wait_recv()
            pl.when(p.below)(lambda: self.chain(source, False).start())
            self.across(source).start()

    def finish(self):
        p = self.place

        def settle(source, carry):
            self.across(source).wait()
            pl.when(p.above & (source <= p.g))(lambda: self.chain(source, True).wait_send())
            pl.when(p.below & (source >= p.g))(lambda: self.chain(source, False).wait_send())
            return carry

        lax.fori_loop(0, p.groups, settle, 0)


class HomeGather:
    def __init__(self, place, part, full, sems):
        self.place, self.part_ref, self.full = place, part, full
        self.home = place.groups // GROUP
        if part is not None:
            self.part_send, self.part_recv = sems
        else:
            self.up_send, self.down_send, self.chain_recv, self.line_send, self.line_recv = sems

    @staticmethod
    def inside():
        dma = pltpu.SemaphoreType.DMA
        return [dma((1,)), dma((GROUP,))]

    @staticmethod
    def outside(groups):
        return [pltpu.SemaphoreType.DMA((groups // GROUP,))] * 5

    def at_home(self):
        return self.place.m == self.place.g // self.home

    def slot(self):
        p = self.place
        return self.full.at[p.g % self.home, p.m, p.b]

    def hand(self):
        p = self.place
        keeper = p.g // self.home
        device = {"g": p.g, "m": keeper, "b": p.b}
        return remote(self.part_ref, self.slot(), self.part_send.at[0], self.part_recv.at[p.m], device)

    def taken(self, source):
        p = self.place
        target = self.full.at[p.g % self.home, source, p.b]
        return remote(self.part_ref, target, self.part_send.at[0], self.part_recv.at[source], p.member(1))

    def own(self):
        return pltpu.make_async_copy(self.part_ref, self.slot(), self.part_send.at[0])

    def start(self):
        pl.when(self.at_home())(lambda: self.own().start())
        pl.when(jnp.logical_not(self.at_home()))(lambda: self.hand().start())

    def chain(self, slot, up):
        p = self.place
        unit = self.full.at[slot, :, p.b]
        sems = self.up_send if up else self.down_send
        return remote(unit, unit, sems.at[slot], self.chain_recv.at[slot], p.up() if up else p.down())

    def across(self, slot):
        p = self.place
        unit = self.full.at[slot, :, p.b]
        return remote(unit, unit, self.line_send.at[slot], self.line_recv.at[slot], p.across())

    def settle(self):
        p = self.place

        @pl.when(self.at_home())
        def _():
            self.own().wait()
            for offset in range(1, GROUP):
                self.taken(p.other(offset)).wait_recv()

        pl.when(jnp.logical_not(self.at_home()))(lambda: self.hand().wait_send())

    def spread(self):
        p = self.place

        @pl.when(self.at_home())
        def _():
            slot = p.g % self.home
            pl.when(p.above)(lambda: self.chain(slot, True).start())
            pl.when(p.below)(lambda: self.chain(slot, False).start())
            self.across(slot).start()

    def step(self, distance):
        p = self.place
        for slot in range(self.home):
            source = p.m * self.home + slot

            @pl.when(p.g - source == distance)
            def _():
                self.chain(slot, True).wait_recv()
                pl.when(p.above)(lambda: self.chain(slot, True).start())
                self.across(slot).start()

            @pl.when(source - p.g == distance)
            def _():
                self.chain(slot, False).wait_recv()
                pl.when(p.below)(lambda: self.chain(slot, False).start())
                self.across(slot).start()

    def finish(self):
        p = self.place
        for slot in range(self.home):
            source = p.m * self.home + slot
            self.across(slot).wait()
            pl.when(p.above & (p.g >= source))(lambda: self.chain(slot, True).wait_send())
            pl.when(p.below & (p.g <= source))(lambda: self.chain(slot, False).wait_send())


class Scatter:
    def __init__(self, place, partial, result, refs):
        self.place, self.partial, self.result = place, partial, result
        (self.land, self.chain_land, self.leave, self.mine_sem, self.line_send, self.line_recv, self.chain_send,
         self.chain_recv, self.part_send, self.part_recv) = refs
        self.parts = partial.shape[1]

    @staticmethod
    def scratch(groups, shape):
        dma = pltpu.SemaphoreType.DMA
        unit = (shape[1],) + tuple(shape[3:])
        return [
            pltpu.VMEM((groups,) + unit, BF16),
            pltpu.VMEM((groups + 1,) + unit, BF16),
            pltpu.VMEM((groups,) + unit, BF16),
            dma((groups,)),
            dma((groups,)),
            dma((groups,)),
            dma((groups,)),
            dma((groups + 1,)),
            dma((GROUP,)),
            dma((GROUP,)),
        ]

    def load(self, target):
        return pltpu.make_async_copy(self.partial.at[target, :, self.place.b], self.leave.at[target], self.mine_sem.at[target])

    def line(self, target):
        p = self.place
        return remote(
            self.partial.at[target, :, 1 - p.b], self.land.at[target], self.line_send.at[target], self.line_recv.at[target], p.across()
        )

    def up(self, target):
        p = self.place
        return remote(
            self.leave.at[target], self.chain_land.at[target], self.chain_send.at[target], self.chain_recv.at[target], p.up()
        )

    def down(self, target, slot):
        p = self.place
        return remote(
            self.leave.at[target], self.chain_land.at[slot], self.chain_send.at[target], self.chain_recv.at[slot], p.down()
        )

    def send_up(self, target):
        self.up(target).start()

    def send_down(self, target):
        p = self.place
        pl.when(p.g - 1 == target)(lambda: self.down(target, p.groups).start())
        pl.when(p.g - 1 != target)(lambda: self.down(target, target).start())

    def arrived(self, slot):
        p = self.place
        return remote(self.leave.at[0], self.chain_land.at[slot], self.chain_send.at[0], self.chain_recv.at[slot], p.across())

    def wave(self, wave, act_up, act_down):
        p = self.place
        pl.when(wave > p.g)(lambda: act_up(p.groups - wave + p.g))
        pl.when(wave >= p.groups - p.g)(lambda: act_down(wave - p.groups + p.g))

    def act(self, target):
        self.line(target).start()
        self.load(target).start()

    def start(self):
        self.start_far()
        self.act(self.place.g)

    def start_far(self, first=1, last=None):
        p = self.place
        for wave in range(first, p.groups if last is None else last + 1):
            self.wave(wave, self.act, self.act)
        if first > 1:
            return

        @pl.when(jnp.logical_not(p.below))
        def _():
            self.chain_land[p.g] = jnp.zeros(self.chain_land.shape[1:], BF16)

        @pl.when(jnp.logical_not(p.above))
        def _():
            self.chain_land[p.groups] = jnp.zeros(self.chain_land.shape[1:], BF16)

    def both(self, target, part):
        return self.leave[target, part].astype(F32) + self.land[target, part].astype(F32)

    def step(self, wave):
        p = self.place

        def send(target, inner, copy):
            self.load(target).wait()
            self.line(target).wait_recv()

            @pl.when(inner)
            def _():
                self.arrived(target).wait_recv()
                for part in range(self.parts):
                    self.leave[target, part] = (self.both(target, part) + self.chain_land[target, part].astype(F32)).astype(BF16)

            @pl.when(jnp.logical_not(inner))
            def _():
                for part in range(self.parts):
                    self.leave[target, part] = self.both(target, part).astype(BF16)

            copy(target)

        self.wave(
            wave,
            lambda target: send(target, p.below, self.send_up),
            lambda target: send(target, p.above, self.send_down),
        )

    def hand(self, offset):
        p = self.place
        return remote(
            self.leave.at[p.g, p.other(offset)], self.result.at[p.m], self.part_send.at[offset], self.part_recv.at[offset], p.member(offset)
        )

    def last(self):
        p = self.place
        self.load(p.g).wait()
        self.line(p.g).wait_recv()
        pl.when(p.below)(lambda: self.arrived(p.g).wait_recv())
        pl.when(p.above)(lambda: self.arrived(p.groups).wait_recv())
        for part in range(self.parts):
            total = self.both(p.g, part) + self.chain_land[p.g, part].astype(F32) + self.chain_land[p.groups, part].astype(F32)
            if self.parts == 1:
                self.result[part] = total.astype(self.result.dtype)
            else:
                self.leave[p.g, part] = total.astype(BF16)
        if self.parts > 1:
            for offset in (2, 3, 1):
                self.hand(offset).start()
            self.result[p.m] = self.leave[p.g, p.m]

    def finish(self):
        p = self.place
        for target in range(p.groups):
            self.line(target).wait_send()
            pl.when(p.g != target)(lambda: self.up(target).wait_send())
        if self.parts > 1:
            for offset in (2, 3, 1):
                self.hand(offset).wait()


class HomeScatter:
    def __init__(self, place, partial, result, refs):
        self.place, self.partial, self.result = place, partial, result
        (self.land, self.home_land, self.leave, self.mine_sem, self.line_send, self.line_recv, self.home_send, self.home_recv,
         self.part_send, self.part_recv) = refs
        self.home = place.groups // GROUP

    @staticmethod
    def scratch(groups, shape):
        dma = pltpu.SemaphoreType.DMA
        home = groups // GROUP
        unit = (GROUP,) + tuple(shape[3:])
        return [
            pltpu.VMEM((home,) + unit, BF16),
            pltpu.VMEM((groups - 1,) + unit, BF16),
            pltpu.VMEM((home,) + unit, BF16),
            dma((home,)),
            dma((home,)),
            dma((home,)),
            dma((home,)),
            dma((groups - 1,)),
            dma((GROUP,)),
            dma((1,)),
        ]

    def load(self, slot):
        return pltpu.make_async_copy(self.partial.at[slot, :, self.place.b], self.leave.at[slot], self.mine_sem.at[slot])

    def line(self, slot):
        p = self.place
        return remote(self.partial.at[slot, :, 1 - p.b], self.land.at[slot], self.line_send.at[slot], self.line_recv.at[slot], p.across())

    def start(self):
        for slot in range(self.home):
            self.line(slot).start()
            self.load(slot).start()

    def home_copy(self, slot):
        p = self.place
        target = p.m * self.home + slot
        index = (p.g - target + p.groups - 1) % p.groups
        return remote(
            self.leave.at[slot], self.home_land.at[index], self.home_send.at[slot], self.home_recv.at[index], p.column(target)
        )

    def landed(self, index):
        p = self.place
        return remote(self.leave.at[0], self.home_land.at[index], self.home_send.at[0], self.home_recv.at[index], p.across())

    def push(self):
        p = self.place
        for slot in range(self.home):

            @pl.when(p.g != p.m * self.home + slot)
            def _():
                self.load(slot).wait()
                self.line(slot).wait_recv()
                for part in range(GROUP):
                    total = self.leave[slot, part].astype(F32) + self.land[slot, part].astype(F32)
                    self.leave[slot, part] = total.astype(BF16)
                self.home_copy(slot).start()

    def hand(self, slot, other):
        p = self.place
        return remote(
            self.leave.at[slot, other], self.result, self.part_send.at[other], self.part_recv.at[0], {"g": p.g, "m": other, "b": p.b}
        )

    def last(self):
        p = self.place

        @pl.when(p.m == p.g // self.home)
        def _():
            slot = p.g % self.home
            self.load(slot).wait()
            self.line(slot).wait_recv()
            for index in range(p.groups - 1):
                self.landed(index).wait_recv()
            for part in range(GROUP):
                total = self.leave[slot, part].astype(F32) + self.land[slot, part].astype(F32)
                for index in range(p.groups - 1):
                    total = total + self.home_land[index, part].astype(F32)
                self.leave[slot, part] = total.astype(BF16)
            for offset in range(1, GROUP):
                self.hand(slot, p.other(offset)).start()
            self.result[...] = self.leave[slot, p.m]

    def finish(self):
        p = self.place
        keeper = p.m == p.g // self.home

        @pl.when(keeper)
        def _():
            for offset in range(1, GROUP):
                self.hand(p.g % self.home, p.other(offset)).wait_send()

        pl.when(jnp.logical_not(keeper))(lambda: self.hand(0, p.other(1)).wait_recv())
        for slot in range(self.home):
            self.line(slot).wait_send()
            pl.when(p.g != p.m * self.home + slot)(lambda: self.home_copy(slot).wait_send())


CHUNKS = 4


class GroupSum:
    def __init__(self, place, partial, refs):
        self.place, self.partial = place, partial
        self.pair_land, self.leave, self.land, self.pair_send, self.pair_recv, self.send, self.recv = refs
        self.size = partial.shape[0] // GROUP
        self.rows = self.size // CHUNKS

    @staticmethod
    def scratch(size, width):
        dma = pltpu.SemaphoreType.DMA
        return [
            pltpu.VMEM((2, size, width), BF16),
            pltpu.VMEM((size, width), BF16),
            pltpu.VMEM((size, width), BF16),
            dma((2, CHUNKS)),
            dma((2, CHUNKS)),
            dma((CHUNKS,)),
            dma((CHUNKS,)),
        ]

    def at(self, chunk, member=0):
        return pl.ds(pl.multiple_of(member * self.size + chunk * self.rows, self.rows), self.rows)

    def pair(self, chunk, far):
        p = self.place
        member = p.other(3 if far else 1)
        slot = 1 if far else 0
        return remote(
            self.partial.at[self.at(chunk, member)], self.pair_land.at[slot, self.at(chunk)], self.pair_send.at[slot, chunk],
            self.pair_recv.at[slot, chunk], p.member(1),
        )

    def cross(self, chunk):
        return remote(
            self.leave.at[self.at(chunk)], self.land.at[self.at(chunk)], self.send.at[chunk], self.recv.at[chunk], self.place.member(2)
        )

    def start(self):
        for chunk in range(CHUNKS):
            self.pair(chunk, True).start()
        for chunk in range(CHUNKS):
            self.pair(chunk, False).start()

    def pass_on(self, chunk):
        self.pair(chunk, True).wait_recv()
        own = self.partial[self.at(chunk, self.place.other(2)), :].astype(F32)
        self.leave[self.at(chunk), :] = (own + self.pair_land[1, self.at(chunk), :].astype(F32)).astype(BF16)
        self.cross(chunk).start()

    def take(self, chunk):
        self.pair(chunk, False).wait_recv()
        self.cross(chunk).wait_recv()
        own = self.partial[self.at(chunk, self.place.m), :].astype(F32)
        return own + self.pair_land[0, self.at(chunk), :].astype(F32) + self.land[self.at(chunk), :].astype(F32)

    def finish(self):
        for chunk in range(CHUNKS):
            self.pair(chunk, True).wait_send()
            self.pair(chunk, False).wait_send()
            self.cross(chunk).wait_send()


class GroupGather:
    def __init__(self, place, whole, refs):
        self.place, self.whole = place, whole
        self.send, self.recv = refs
        self.size = whole.shape[0] // GROUP
        self.rows = self.size // CHUNKS

    @staticmethod
    def scratch():
        dma = pltpu.SemaphoreType.DMA
        return [dma((3, CHUNKS)), dma((3, CHUNKS))]

    def at(self, chunk, member):
        return pl.ds(pl.multiple_of(member * self.size + chunk * self.rows, self.rows), self.rows)

    def copy(self, chunk, way):
        p = self.place
        rows = self.whole.at[self.at(chunk, p.other(2) if way == 2 else p.m)]
        return remote(rows, rows, self.send.at[way, chunk], self.recv.at[way, chunk], p.member(2 if way == 0 else 1))

    def give(self, chunk):
        self.copy(chunk, 0).start()
        self.copy(chunk, 1).start()

    def pass_on(self, chunk):
        self.copy(chunk, 0).wait_recv()
        self.copy(chunk, 2).start()

    def finish(self):
        for chunk in range(CHUNKS):
            self.copy(chunk, 1).wait_recv()
            self.copy(chunk, 2).wait_recv()
            for way in range(3):
                self.copy(chunk, way).wait_send()


def masked(scores, counts):
    return jnp.where(counts, scores * SCALE, NEGATIVE)


class Pauses:
    def __init__(self, *steps):
        self.steps = list(steps)

    def __call__(self):
        if self.steps:
            for act in self.steps.pop(0):
                act()

    def rest(self):
        while self.steps:
            self()


def several(refs, *counts):
    refs = list(refs)
    taken = []
    for count in counts:
        taken.append(refs[:count])
        refs = refs[count:]
    return taken


def attend_kernel(
    groups,
    hops,
    rows_ref,
    doc_query_ref,
    doc_key_ref,
    out_home_ref,
    feed_unit_ref,
    query_ref,
    value_ref,
    within_ref,
    map_ref,
    inverse_ref,
    attended_ref,
    low_ref,
    stats_ref,
    moved_ref,
    values_ref,
    out_full_ref,
    feed_full_ref,
    key_ref,
    leave_ref,
    top_ref,
    total_ref,
    accum_ref,
    key_send,
    key_recv,
    value_send,
    value_recv,
    *sems,
):
    here = Place(groups, feed_full_ref.shape[2])
    here.meet()
    place, has_next, following = here.g, here.above, here.up()
    home_sems, feed_sems = several(sems, 5, 5)
    out_gather = HomeGather(here, None, out_full_ref, home_sems)
    feed_gather = Gather(here, None, feed_full_ref, feed_sems)
    out_gather.spread()
    feed_gather.spread()
    pauses = Pauses(
        *[
            (functools.partial(out_gather.step, distance), functools.partial(feed_gather.step, distance))
            for distance in range(1, groups)
        ]
    )
    prepared = (rows_ref, query_ref, key_ref, value_ref, within_ref, map_ref, inverse_ref)
    prepare_blocks(0, GROUP, *prepared)

    def value_copy(source, slot):
        return remote(source, values_ref.at[slot], value_send.at[slot], value_recv.at[slot], following)

    def key_copy(slot):
        return remote(leave_ref.at[slot], moved_ref.at[slot + 1, 0], key_send.at[slot], key_recv.at[slot], following)

    def move(keys, block, head):
        return dot2(keys, map_ref[tile(block), tile(head)]).astype(BF16)

    for head in range(OWN):
        keys = key_ref[tile(0), tile(head)]
        for block in range(1, GROUP):
            moved_ref[0, block, tile(0, block), tile(head)] = keys
            keys = jnp.concatenate([move(keys, block, head), key_ref[tile(block), tile(head)]], 0)
        leave_ref[0, :, tile(head)] = keys

    @pl.when(has_next)
    def _():
        key_copy(0).start()
        value_copy(value_ref, 0).start()

    pauses()

    def row_counts(block, hop, first, count):
        return doc_query_ref[tile(block), :] == doc_key_ref[hop, :, tile(first, count)]

    for block in range(GROUP):
        counts = row_counts(block, 0, 0, block + 1)
        wide = (BLOCK, (block + 1) * BLOCK)
        counts = counts & (iota(0, wide) + block * BLOCK >= iota(1, wide))
        for head in range(OWN):
            scores = within_ref[tile(block), tile(head)]
            if block:
                before = dot(query_ref[tile(block), tile(head)], moved_ref[0, block, tile(0, block), tile(head)], NT)
                scores = jnp.concatenate([before, scores], 1)
            scores = masked(scores, counts)
            top = jnp.max(scores, axis=1, keepdims=True)
            weights = jnp.exp(scores - top)
            top_ref[head, tile(block), :] = jnp.broadcast_to(top, (BLOCK, BLOCK))
            total_ref[head, tile(block), :] = jnp.broadcast_to(jnp.sum(weights, axis=1, keepdims=True), (BLOCK, BLOCK))
            accum_ref[tile(block), tile(head)] = dot(weights.astype(BF16), value_ref[tile(0, block + 1), tile(head)])

    def hop_step(hop, last):
        @pl.when(place >= hop)
        def _():
            key_copy(hop - 1).wait_recv()
            for head in range(OWN):
                keys = moved_ref[hop, 0, :, tile(head)]
                for block in range(GROUP):
                    if last:
                        if block == GROUP - 1:
                            break
                        keys = move(keys[BLOCK:], block, head)
                        moved_ref[hop, block + 1, tile(block + 1, GROUP - 1 - block), tile(head)] = keys
                    else:
                        keys = move(keys, block, head)
                        if block < GROUP - 1:
                            moved_ref[hop, block + 1, :, tile(head)] = keys
                        else:
                            leave_ref[hop, :, tile(head)] = keys
            value_copy(value_ref, hop - 1).wait_recv()
            if not last:

                @pl.when(has_next)
                def _():
                    key_copy(hop).start()
                    value_copy(values_ref.at[hop - 1], hop).start()

            for block in range(GROUP):
                first = block if last else 0
                count = GROUP - first
                counts = row_counts(block, hop, first, count)
                for head in range(OWN):
                    scores = masked(
                        dot(query_ref[tile(block), tile(head)], moved_ref[hop, block, tile(first, count), tile(head)], NT),
                        counts,
                    )
                    old = top_ref[head, tile(block), :]
                    top = jnp.maximum(old, jnp.broadcast_to(jnp.max(scores, axis=1, keepdims=True), (BLOCK, BLOCK)))
                    factor = jnp.exp(old - top)
                    weights = jnp.exp(scores - jnp.concatenate([top] * count, 1))
                    top_ref[head, tile(block), :] = top
                    total_ref[head, tile(block), :] = total_ref[head, tile(block), :] * factor + jnp.sum(
                        weights, axis=1, keepdims=True
                    )
                    accum_ref[tile(block), tile(head)] = accum_ref[tile(block), tile(head)] * factor + dot(
                        weights.astype(BF16), values_ref[hop - 1, tile(first, count), tile(head)]
                    )

    if hops > 2:

        def between(hop, carry):
            hop_step(hop, False)
            return carry

        lax.fori_loop(1, hops, between, 0)
    else:
        for hop in range(1, hops):
            pauses()
            hop_step(hop, False)
    pauses()
    hop_step(hops, True)

    for block in range(GROUP):
        stats = jnp.zeros((BLOCK, BLOCK), F32)
        for head in range(OWN):
            total = total_ref[head, tile(block), :]
            result = accum_ref[tile(block), tile(head)] / total
            attended_ref[tile(block), tile(head)] = result
            low_ref[tile(block), tile(head)] = result.astype(BF16)
            stats = jnp.where(iota(1) == head, top_ref[head, tile(block), :], stats)
            stats = jnp.where(iota(1) == OWN + head, total, stats)
        stats_ref[tile(block), :] = stats

    def settle(slot, carry):
        @pl.when(has_next & (place >= slot))
        def _():
            key_copy(slot).wait_send()
            value_copy(value_ref, slot).wait_send()

        return carry

    lax.fori_loop(0, hops, settle, 0)
    pauses.rest()
    out_gather.finish()
    feed_gather.finish()


def in_vmem(count):
    return [pl.BlockSpec(memory_space=pltpu.VMEM)] * count


def anywhere(count):
    return [pl.BlockSpec(memory_space=pl.ANY)] * count


def shape(kind, *dims):
    return jax.ShapeDtypeStruct(dims, kind)


def communicating(number, name, vmem=58):
    return {
        "compiler_params": pltpu.CompilerParams(collective_id=number, has_side_effects=True, vmem_limit_bytes=vmem << 20),
        "name": name,
    }


def attend(groups, hops, projected, doc_query, doc_key, out_full, feed_full):
    length = projected.shape[0]
    dma = pltpu.SemaphoreType.DMA
    return pl.pallas_call(
        functools.partial(attend_kernel, groups, hops),
        out_shape=[
            shape(BF16, length, WIDE),
            shape(BF16, length, WIDE),
            shape(F32, length, WIDE),
            shape(F32, length, WIDE),
            shape(F32, length, WIDE),
            shape(F32, length, WIDE),
            shape(BF16, length, WIDE),
            shape(F32, length, BLOCK),
            shape(BF16, hops + 1, GROUP, length, WIDE),
            shape(BF16, hops, length, WIDE),
            shape(BF16, *out_full.shape),
            shape(BF16, *feed_full.shape),
        ],
        in_specs=in_vmem(3) + anywhere(2),
        out_specs=in_vmem(10) + anywhere(2),
        scratch_shapes=[
            pltpu.VMEM((length, WIDE), BF16),
            pltpu.VMEM((hops, length, WIDE), BF16),
            pltpu.VMEM((OWN, length, BLOCK), F32),
            pltpu.VMEM((OWN, length, BLOCK), F32),
            pltpu.VMEM((length, WIDE), F32),
            dma((hops,)),
            dma((hops,)),
            dma((hops,)),
            dma((hops,)),
        ]
        + HomeGather.outside(groups)
        + Gather.outside(groups),
        input_output_aliases={3: 10, 4: 11},
        **communicating(1, "attend"),
    )(projected, doc_query, doc_key, out_full, feed_full)


def back_kernel(
    groups,
    hops,
    partial_ref,
    hidden_ref,
    cotangent_ref,
    gain_ref,
    low_ref,
    out_ref,
    query_ref,
    value_ref,
    within_ref,
    map_ref,
    doc_query_ref,
    doc_key_ref,
    attended_ref,
    stats_ref,
    values_hbm,
    moved_hbm,
    rows_hbm,
    inverse_hbm,
    down_partial_ref,
    feed_partial_ref,
    grad_ref,
    down_result_ref,
    rows_grad_ref,
    feed_result_ref,
    out_result_ref,
    grad_low_ref,
    att_grad_ref,
    out_partial_ref,
    moved_ref,
    values_ref,
    extra_ref,
    load_sem,
    query_grad_ref,
    key_grad_ref,
    within_grad_ref,
    map_grad_ref,
    value_grad_ref,
    scaled_ref,
    dots_ref,
    direct_ref,
    panels_ref,
    key_slots_ref,
    value_slots_ref,
    key_send,
    key_recv,
    value_send,
    value_recv,
    *refs,
):
    lines = feed_partial_ref.shape[2]
    here = Place(groups, lines)
    here.meet(column=True)
    place, has_next, previous = here.g, here.above, here.down()
    sum_refs, gather_refs, down_refs, feed_refs, out_refs = several(
        refs,
        7,
        2,
        len(Scatter.scratch(groups, down_partial_ref.shape)),
        len(Scatter.scratch(groups, feed_partial_ref.shape)),
        len(HomeScatter.scratch(groups, out_partial_ref.shape)),
    )
    sums = GroupSum(here, partial_ref, sum_refs)
    whole = GroupGather(here, grad_low_ref, gather_refs)
    down = Scatter(here, down_partial_ref, down_result_ref, down_refs)
    feed_scatter = Scatter(here, feed_partial_ref, feed_result_ref, feed_refs)
    out_scatter = HomeScatter(here, out_partial_ref, out_result_ref, out_refs)
    pauses = Pauses(*[(functools.partial(feed_scatter.step, wave),) for wave in range(1, groups)])

    def load(hop):
        return pltpu.make_async_copy(moved_hbm.at[hop], moved_ref.at[hop % 2], load_sem.at[hop % 2])

    def load_values(hop):
        return pltpu.make_async_copy(values_hbm.at[hop - 1], values_ref.at[hop % 2], load_sem.at[2 + hop % 2])

    short = hops > 2
    loads = [pltpu.make_async_copy(rows_hbm.at[:, pl.ds(4 * WIDE, EXTRA)], extra_ref, load_sem.at[4])]
    panels = direct_ref if short else panels_ref
    for index, panel in enumerate((0, 1, 3)):
        loads.append(pltpu.make_async_copy(rows_hbm.at[:, pl.ds(panel * WIDE, WIDE)], panels.at[index], load_sem.at[5 + index]))
    loads.append(pltpu.make_async_copy(inverse_hbm, panels.at[3], load_sem.at[8]))
    sums.start()
    down.start()
    load(hops).start()
    load_values(hops).start()
    if not short:
        for copy in loads:
            copy.start()
    feed_scatter.start_far(1, 1)
    for chunk in range(CHUNKS):
        sums.pass_on(chunk)
    for chunk in range(CHUNKS):
        back = rms_back(hidden_ref[sums.at(chunk), :], gain_ref[...], sums.take(chunk))
        grad = cotangent_ref[sums.at(chunk), :].astype(F32) + back
        grad_ref[sums.at(chunk), :] = grad
        grad_low_ref[whole.at(chunk, here.m), :] = grad.astype(BF16)
        whole.give(chunk)
    down.step(1)
    for chunk in range(CHUNKS):
        whole.pass_on(chunk)
    if groups > 2:
        down.step(2)
    whole.finish()
    att_grad_ref[...] = dot(grad_low_ref[...], out_ref[...], NT).astype(BF16)
    turned = low_ref[...].T
    units = out_partial_ref.shape[3]

    def out_tile(at):
        value = dot(turned, grad_low_ref[:, at])
        for index in range(WIDE // units):
            slot, member, line = index // (GROUP * lines), index // lines % GROUP, index % lines
            out_partial_ref[slot, member, line, :, at] = value[index * units : (index + 1) * units].astype(BF16)

    in_tiles(out_partial_ref.shape[4], out_tile)
    out_scatter.start()
    feed_scatter.start_far(2)
    feed_scatter.act(here.g)
    for wave in range(3, groups):
        down.step(wave)

    def key_copy(hop):
        slot = hop - 1
        return remote(key_slots_ref.at[hop], key_slots_ref.at[slot], key_send.at[slot], key_recv.at[slot], previous)

    def value_copy(hop):
        slot = hop - 1
        return remote(value_slots_ref.at[hop], value_slots_ref.at[slot], value_send.at[slot], value_recv.at[slot], previous)

    map_grad_ref[...] = jnp.zeros_like(map_grad_ref)
    query_grad_ref[...] = jnp.zeros_like(query_grad_ref)
    for block in range(GROUP):
        for head in range(OWN):
            at = (tile(block), tile(head))
            grad = att_grad_ref[at].astype(F32)
            total = stats_ref[tile(block), OWN + head : OWN + head + 1]
            scaled_ref[at] = (grad / total).astype(BF16)
            dots = -jnp.sum(grad * attended_ref[at], axis=1, keepdims=True) / total
            dots_ref[head, tile(block), :] = jnp.broadcast_to(dots, (BLOCK, BLOCK))

    def pair(block, head, scores, counts, values):
        count = scores.shape[1] // BLOCK
        top = stats_ref[tile(block), head : head + 1]
        weights = jnp.exp(masked(scores, counts) - top)
        weight_grad = dot(scaled_ref[tile(block), tile(head)], values, NT)
        dots = jnp.concatenate([dots_ref[head, tile(block), :]] * count, 1)
        return weights, weights * (weight_grad + dots) * SCALE

    def row_counts(block, hop, first, count):
        return doc_query_ref[tile(block), :] == doc_key_ref[hop, :, tile(first, count)]

    def hop_direct(hop, last):
        for head in range(OWN):
            value_grad_ref[:, tile(head)] = jnp.zeros((GROUP * BLOCK, BLOCK), F32)
        for block in range(GROUP):
            first = block if last else 0
            count = GROUP - first
            counts = row_counts(block, hop, first, count)
            for head in range(OWN):
                query = query_ref[tile(block), tile(head)]
                keys = moved_ref[hop % 2, block, tile(first, count), tile(head)]
                weights, grad = pair(
                    block, head, dot(query, keys, NT), counts, values_ref[hop % 2, tile(first, count), tile(head)]
                )
                raw = grad.astype(BF16)
                query_grad_ref[tile(block), tile(head)] += dot(raw, keys)
                direct_ref[block, tile(first, count), tile(head)] = dot(raw, query, TN)
                value_grad_ref[tile(first, count), tile(head)] += dot(
                    weights.astype(BF16), scaled_ref[tile(block), tile(head)], TN
                )

    def collect_map(block, head, keys, grads):
        map_grad_ref[tile(block), tile(head)] += dot2(keys, grads, TN)

    def hop_chain(hop, last):
        for head in range(OWN):
            if last:
                grads = direct_ref[GROUP - 1, tile(GROUP - 1), tile(head)]
                for block in range(GROUP - 2, -1, -1):
                    rows = tile(block + 1, GROUP - 1 - block)
                    collect_map(block, head, moved_ref[hop % 2, block, rows, tile(head)], grads)
                    back = dot3(grads, map_ref[tile(block), tile(head)], NT)
                    direct = direct_ref[block, tile(block, GROUP - block), tile(head)]
                    grads = jnp.concatenate([direct[:BLOCK], direct[BLOCK:] + back], 0)
                key_slots_ref[hop, :, tile(head)] = grads.astype(BF16)
                value_slots_ref[hop, :, tile(head)] = value_grad_ref[:, tile(head)].astype(BF16)
            else:
                grads = key_grad_ref[:, tile(head)]
                for block in range(GROUP - 1, -1, -1):
                    collect_map(block, head, moved_ref[hop % 2, block, :, tile(head)], grads)
                    grads = direct_ref[block, :, tile(head)] + dot3(grads, map_ref[tile(block), tile(head)], NT)
                key_slots_ref[hop, :, tile(head)] = grads.astype(BF16)

    def take(hop):
        @pl.when(has_next)
        def _():
            key_copy(hop).wait_recv()
            key_grad_ref[...] = key_slots_ref[hop - 1].astype(F32)

        @pl.when(jnp.logical_not(has_next))
        def _():
            key_grad_ref[...] = jnp.zeros_like(key_grad_ref)

    load(hops - 1).start()
    load_values(hops - 1).start()
    load(hops).wait()
    load_values(hops).wait()

    @pl.when(place >= hops)
    def _():
        hop_direct(hops, True)
        hop_chain(hops, True)
        key_copy(hops).start()
        value_copy(hops).start()

    down.last()

    def between(hop, pause=None):
        load(hop - 1).start()
        pl.when(jnp.asarray(hop) > 1)(lambda: load_values(hop - 1).start())
        load(hop).wait()
        load_values(hop).wait()
        pl.when(place >= hop)(lambda: hop_direct(hop, False))
        if pause is not None:
            pause()

        @pl.when(place >= hop)
        def _():
            take(hop + 1)
            hop_chain(hop, False)
            key_copy(hop).start()

            @pl.when(has_next)
            def _():
                value_copy(hop + 1).wait_recv()
                for head in range(OWN):
                    value_slots_ref[hop, :, tile(head)] = (
                        value_grad_ref[:, tile(head)] + value_slots_ref[hop, :, tile(head)].astype(F32)
                    ).astype(BF16)

            @pl.when(jnp.logical_not(has_next))
            def _():
                for head in range(OWN):
                    value_slots_ref[hop, :, tile(head)] = value_grad_ref[:, tile(head)].astype(BF16)

            value_copy(hop).start()

    if hops > 2:

        def step(counter, carry):
            between(hops - 1 - counter)
            return carry

        lax.fori_loop(0, hops - 1, step, 0)
    else:
        for hop in range(hops - 1, 0, -1):
            between(hop, pauses)

    load(0).wait()
    for head in range(OWN):
        value_grad_ref[:, tile(head)] = jnp.zeros((GROUP * BLOCK, BLOCK), F32)
    for block in range(GROUP):
        wide = (BLOCK, (block + 1) * BLOCK)
        counts = row_counts(block, 0, 0, block + 1) & (iota(0, wide) + block * BLOCK >= iota(1, wide))
        for head in range(OWN):
            query = query_ref[tile(block), tile(head)]
            scores = within_ref[tile(block), tile(head)]
            if block:
                keys = moved_ref[0, block, tile(0, block), tile(head)]
                scores = jnp.concatenate([dot(query, keys, NT), scores], 1)
            weights, grad = pair(block, head, scores, counts, value_ref[tile(0, block + 1), tile(head)])
            within_grad_ref[tile(block), tile(head)] = grad[:, block * BLOCK :]
            value_grad_ref[tile(0, block + 1), tile(head)] += dot(
                weights.astype(BF16), scaled_ref[tile(block), tile(head)], TN
            )
            if block:
                raw = grad[:, : block * BLOCK].astype(BF16)
                query_grad_ref[tile(block), tile(head)] += dot(raw, keys)
                direct_ref[block, tile(0, block), tile(head)] = dot(raw, query, TN)
    out_scatter.push()
    take(1)
    for head in range(OWN):
        grads = key_grad_ref[:, tile(head)]
        for block in range(GROUP - 1, 0, -1):
            key_grad_ref[tile(block), tile(head)] = grads[block * BLOCK :]
            grads = grads[: block * BLOCK]
            collect_map(block, head, moved_ref[0, block, tile(0, block), tile(head)], grads)
            grads = direct_ref[block, tile(0, block), tile(head)] + dot3(grads, map_ref[tile(block), tile(head)], NT)
        key_grad_ref[tile(0), tile(head)] = grads

    @pl.when(has_next)
    def _():
        value_copy(1).wait_recv()
        value_grad_ref[...] += value_slots_ref[0].astype(F32)

    def settle(hop, carry):
        @pl.when(place >= hop)
        def _():
            key_copy(hop).wait_send()
            value_copy(hop).wait_send()

        return carry

    lax.fori_loop(1, hops + 1, settle, 0)
    if short:
        for copy in loads:
            copy.start()
    for copy in loads:
        copy.wait()
    pauses()
    pieces = (panels, extra_ref, query_grad_ref, key_grad_ref, within_grad_ref, map_grad_ref, value_grad_ref, rows_grad_ref)
    prepare_back_blocks(0, GROUP // 2, *pieces)
    pauses.rest()
    prepare_back_blocks(GROUP // 2, GROUP, *pieces)
    feed_scatter.last()
    out_scatter.last()
    sums.finish()
    down.finish()
    feed_scatter.finish()
    out_scatter.finish()


def back(groups, hops, partial, hidden, cotangent, gain, low, out, *args):
    values, moved, rows, inverse, down, feed = args[-6:]
    size, width = hidden.shape
    length = partial.shape[0]
    lines, units = feed.shape[2:4]
    out_shape = (groups // GROUP, GROUP, lines, units, width)
    dma = pltpu.SemaphoreType.DMA
    inputs = (partial, hidden, cotangent, gain, low, out) + args
    return pl.pallas_call(
        functools.partial(back_kernel, groups, hops),
        out_shape=[
            shape(F32, size, width),
            shape(F32, 1, *down.shape[3:]),
            shape(BF16, *rows.shape),
            shape(BF16, GROUP, *feed.shape[3:]),
            shape(BF16, units, width),
        ],
        in_specs=in_vmem(len(inputs) - 6) + anywhere(6),
        out_specs=in_vmem(5),
        scratch_shapes=[
            pltpu.VMEM((length, width), BF16),
            pltpu.VMEM((length, WIDE), BF16),
            pltpu.VMEM(out_shape, BF16),
            pltpu.VMEM((2,) + moved.shape[1:], BF16),
            pltpu.VMEM((2,) + values.shape[1:], BF16),
            pltpu.VMEM((length, EXTRA), F32),
            dma((9,)),
        ]
        + [pltpu.VMEM((length, WIDE), F32)] * 5
        + [
            pltpu.VMEM((length, WIDE), BF16),
            pltpu.VMEM((OWN, length, BLOCK), F32),
            pltpu.VMEM((GROUP, length, WIDE), F32),
            pltpu.VMEM((1 if hops > 2 else GROUP, BLOCK if hops > 2 else length, WIDE), F32),
            pltpu.VMEM((hops + 1, length, WIDE), BF16),
            pltpu.VMEM((hops + 1, length, WIDE), BF16),
            dma((hops,)),
            dma((hops,)),
            dma((hops,)),
            dma((hops,)),
        ]
        + GroupSum.scratch(size, width)
        + GroupGather.scratch()
        + Scatter.scratch(groups, down.shape)
        + Scatter.scratch(groups, feed.shape)
        + HomeScatter.scratch(groups, out_shape),
        **communicating(2, "back", 60),
    )(*inputs)


def gather_kernel(
    groups, first_ref, gate_ref, up_ref, out_ref, down_ref, tokens_ref, cotangent_ref, full_ref, feed_full_ref, out_full_ref,
    down_low_ref, tokens_all_ref, cotangent_all_ref, feed_parts_ref, out_low_ref, send, recv, local, *sems
):
    lines = full_ref.shape[2]
    here = Place(groups, lines)
    here.meet()
    first_sems, feed_sems, out_sems = several(sems, 8, 3, 2)
    first = Gather(here, first_ref, full_ref, first_sems)
    feed = Gather(here, feed_parts_ref, feed_full_ref, feed_sems)
    out = HomeGather(here, out_low_ref, out_full_ref, out_sems)
    first.start()
    size = tokens_ref.shape[0]
    own = pl.ds(pl.multiple_of(here.m * size, size), size)
    copies = []
    for index, (source, target) in enumerate(((tokens_ref, tokens_all_ref), (cotangent_ref, cotangent_all_ref))):
        copies.append(pltpu.make_async_copy(source, target.at[own], local.at[index]))
        for offset in (2, 3, 1):
            copies.append(
                remote(source, target.at[own], send.at[index, offset], recv.at[index, offset], here.member(offset))
            )
    for copy in copies:
        copy.start()
    out_low_ref[...] = out_ref[...].astype(BF16)
    down_low_ref[...] = down_ref[...].astype(BF16)
    own_units = feed_parts_ref.shape[2] // 2
    for at, weight_ref in ((0, gate_ref), (own_units, up_ref)):
        if len(weight_ref.shape) == 3:
            feed_parts_ref[:, :, at : at + own_units] = weight_ref[...]
        else:
            for member in range(GROUP):
                for index in range(groups * lines):
                    block = (index // lines * GROUP + member) * lines + index % lines
                    feed_parts_ref[member, :, pl.ds(at + index * BLOCK, BLOCK)] = weight_ref[:, tile(block)].astype(BF16)
    feed.start()
    out.start()
    first.settle()
    first.spread()
    for distance in range(1, groups):
        first.step(distance)
    feed.settle()
    out.settle()
    for copy in copies:
        copy.wait()
    first.finish()


def gather_first(groups, lines, first, gate, up, out, down, tokens, cotangent):
    dma = pltpu.SemaphoreType.DMA
    size, width = tokens.shape
    rows = out.shape[0]
    units = 2 * down.shape[0] * groups * lines
    return pl.pallas_call(
        functools.partial(gather_kernel, groups),
        out_shape=[
            shape(BF16, groups, GROUP, lines, *first.shape[1:]),
            shape(BF16, groups, GROUP, lines, rows, units),
            shape(BF16, groups // GROUP, GROUP, lines, rows, width),
            shape(BF16, *down.shape),
            shape(BF16, GROUP * size, width),
            shape(BF16, GROUP * size, width),
        ],
        in_specs=anywhere(1) + in_vmem(4) + anywhere(2),
        out_specs=anywhere(3) + in_vmem(1) + anywhere(2),
        scratch_shapes=[
            pltpu.VMEM((GROUP, rows, units), BF16),
            pltpu.VMEM((rows, width), BF16),
            dma((2, GROUP)),
            dma((2, GROUP)),
            dma((2,)),
        ]
        + Gather.inside()
        + Gather.outside(groups)
        + Gather.inside()
        + HomeGather.inside(),
        **communicating(0, "gather_first", 24),
    )(first, gate, up, out, down, tokens, cotangent)


def rms_norm(values, gain):
    return values * lax.rsqrt(jnp.mean(values * values, axis=-1, keepdims=True) + EPSILON) * gain


def rms_back(values, gain, grad):
    scale = lax.rsqrt(jnp.mean(values * values, axis=-1, keepdims=True) + EPSILON)
    straight = values * scale
    lifted = grad * gain
    return scale * (lifted - straight * jnp.mean(lifted * straight, axis=-1, keepdims=True))


def in_tiles(size, act, step=2 * BLOCK):
    def one(index, carry):
        act(pl.ds(pl.multiple_of(index * step, step), step))
        return carry

    lax.fori_loop(0, size // step, one, 0)


def branch_kernel(
    groups, partial_ref, tokens_ref, gain_ref, down_ref, feed_hbm, hidden_ref, normed_ref, active_ref, gate_slope_ref, up_slope_ref,
    down_full_ref, feed_ref, feed_sem, *refs
):
    here = Place(groups, down_full_ref.shape[1])
    here.meet()
    sum_refs, gather_refs, down_refs = several(refs, 7, 2, 8)
    total = GroupSum(here, partial_ref, sum_refs)
    whole = GroupGather(here, normed_ref, gather_refs)
    down = Gather(here, down_ref, down_full_ref, down_refs, mixed=False)
    pauses = Pauses(*[(functools.partial(down.step, distance),) for distance in range(1, groups)])
    total.start()
    down.start()
    down.settle()
    down.spread()
    feed_copy = pltpu.make_async_copy(feed_hbm, feed_ref, feed_sem.at[0])
    feed_copy.start()
    for chunk in range(CHUNKS):
        total.pass_on(chunk)
    pauses()
    for chunk in range(CHUNKS):
        hidden = tokens_ref[total.at(chunk), :].astype(F32) + total.take(chunk)
        hidden_ref[total.at(chunk), :] = hidden
        normed_ref[whole.at(chunk, here.m), :] = rms_norm(hidden, gain_ref[...]).astype(BF16)
        whole.give(chunk)
    pauses()
    for chunk in range(CHUNKS):
        whole.pass_on(chunk)
    pauses.rest()
    feed_copy.wait()
    whole.finish()
    units = active_ref.shape[1]

    def act(at):
        normed = normed_ref[...]
        gate = dot(normed, feed_ref[:, at])
        up = dot(normed, feed_ref[:, pl.ds(pl.multiple_of(at.start + units, BLOCK), at.size)])
        sigmoid = jax.nn.sigmoid(gate)
        silu = gate * sigmoid
        active_ref[:, at] = (silu * up).astype(BF16)
        gate_slope_ref[:, at] = up * (sigmoid * (1.0 + gate * (1.0 - sigmoid)))
        up_slope_ref[:, at] = silu

    in_tiles(units, act)
    total.finish()
    down.finish()


def branch(groups, lines, partial, tokens, gain, down, feed):
    size, width = tokens.shape
    length, units = partial.shape[0], feed.shape[1] // 2
    dma = pltpu.SemaphoreType.DMA
    return pl.pallas_call(
        functools.partial(branch_kernel, groups),
        out_shape=[
            shape(F32, size, width),
            shape(BF16, length, width),
            shape(BF16, length, units),
            shape(F32, length, units),
            shape(F32, length, units),
            shape(BF16, groups, lines, *down.shape),
        ],
        in_specs=in_vmem(3) + anywhere(2),
        out_specs=in_vmem(5) + anywhere(1),
        scratch_shapes=[pltpu.VMEM(feed.shape, BF16), dma((1,))]
        + GroupSum.scratch(size, width)
        + GroupGather.scratch()
        + Gather.inside()
        + Gather.outside(groups),
        **communicating(3, "branch", 48),
    )(partial, tokens, gain, down, feed)


def finish_kernel(groups, whole_tiles, first_partial_ref, first_hbm, rows_grad_ref, output_partial_ref, tokens_ref, hidden_ref, grad_ref,
                  gain_ref, beta_ref, feed_result_ref, *refs):
    lines = first_partial_ref.shape[2]
    here = Place(groups, lines)
    here.meet()
    weights, (query_out, key_out, value_out, house_out, extra_ref, sums_ref, tokens_grad_ref, output_ref), refs = (
        refs[:6], refs[6:14], refs[14:]
    )
    if whole_tiles:
        gate_out, up_out = refs[:2]
        refs = refs[2:]
    first_result_ref, first_full_ref, normed_partial_ref, first_sem = refs[:4]
    first_refs, normed_refs, output_refs = several(refs[4:], len(Scatter.scratch(groups, first_partial_ref.shape)), 7, 7)
    first = Scatter(here, first_partial_ref, first_result_ref, first_refs)
    normed = GroupSum(here, normed_partial_ref, normed_refs)
    output = GroupSum(here, output_partial_ref, output_refs)
    first.start()
    first_copy = pltpu.make_async_copy(first_hbm, first_full_ref, first_sem.at[0])
    first_copy.start()
    output.start()
    for chunk in range(CHUNKS):
        output.pass_on(chunk)
    first_copy.wait()

    def normed_tile(at):
        normed_partial_ref[:, at] = dot(rows_grad_ref[...], first_full_ref[at, :], NT).astype(BF16)

    in_tiles(normed_partial_ref.shape[1], normed_tile)
    normed.start()
    for chunk in range(CHUNKS):
        normed.pass_on(chunk)
    first.step(1)
    rows = sums_ref.shape[0]
    sums_ref[...] = jnp.zeros_like(sums_ref)
    lane = iota(1, (rows, BLOCK))
    if whole_tiles:
        units = feed_result_ref.shape[2] // 2
        feed_sum = jnp.zeros((rows, BLOCK), F32)
        for at, weight_ref, target_ref in ((0, weights[4], gate_out), (units, weights[5], up_out)):
            for member in range(GROUP):
                for index in range(groups * lines):
                    block = (index // lines * GROUP + member) * lines + index % lines
                    value = feed_result_ref[member, :, pl.ds(at + index * BLOCK, BLOCK)].astype(F32)
                    target_ref[:, tile(block)] = value
                    feed_sum = feed_sum + value * weight_ref[:, tile(block)].astype(BF16).astype(F32)
        sums_ref[...] = jnp.where(lane == 1, jnp.sum(feed_sum, axis=1, keepdims=True), sums_ref[...])
    if groups > 2:
        first.step(2)
    for chunk in range(CHUNKS):
        output_ref[output.at(chunk), :] = (hidden_ref[output.at(chunk), :] + output.take(chunk)).astype(BF16)
    for chunk in range(CHUNKS):
        back = rms_back(tokens_ref[normed.at(chunk), :].astype(F32), gain_ref[...], normed.take(chunk))
        tokens_grad_ref[normed.at(chunk), :] = (grad_ref[normed.at(chunk), :] + back).astype(BF16)
    for wave in range(3, groups):
        first.step(wave)
    normed.finish()
    output.finish()
    first.last()
    first.finish()
    first_sum = jnp.zeros((rows, WIDE), F32)
    extra_sum = jnp.zeros((rows, EXTRA), F32)
    for member in range(GROUP):
        for part, target_ref in enumerate((query_out, key_out, value_out, house_out)):
            value = first_result_ref[member, :, pl.ds(part * WIDE, WIDE)].astype(F32)
            at = pl.ds(member * WIDE, WIDE)
            target_ref[:, at] = value
            first_sum = first_sum + value * weights[part][:, at].astype(BF16).astype(F32)
        extra = first_result_ref[member, :, pl.ds(4 * WIDE, EXTRA)].astype(F32)
        extra_ref[member] = extra
        extra_sum = extra_sum + extra * beta_ref[member].astype(F32)
    total = jnp.sum(first_sum, axis=1, keepdims=True) + jnp.sum(extra_sum, axis=1, keepdims=True)
    sums_ref[...] = jnp.where(lane == 0, total, sums_ref[...])


def finish(groups, whole_tiles, first_partial, first, rows_grad, output_partial, tokens, hidden, grad, gain, beta, feed_result, weights):
    size, width = tokens.shape
    length = rows_grad.shape[0]
    rows = weights[0].shape[0]
    dma = pltpu.SemaphoreType.DMA
    out = [shape(F32, rows, width)] * 4 + [
        shape(F32, GROUP, rows, EXTRA),
        shape(F32, rows, BLOCK),
        shape(BF16, size, width),
        shape(BF16, size, width),
    ]
    if whole_tiles:
        out = out + [shape(F32, *weights[4].shape)] * 2
    return pl.pallas_call(
        functools.partial(finish_kernel, groups, whole_tiles),
        out_shape=out,
        in_specs=anywhere(2) + in_vmem(8 + len(weights)),
        out_specs=in_vmem(len(out)),
        scratch_shapes=[
            pltpu.VMEM((GROUP,) + first_partial.shape[3:], BF16),
            pltpu.VMEM(first.shape, BF16),
            pltpu.VMEM((length, width), BF16),
            dma((1,)),
        ]
        + Scatter.scratch(groups, first_partial.shape)
        + GroupSum.scratch(size, width)
        + GroupSum.scratch(size, width),
        **communicating(5, "finish"),
    )(first_partial, first, rows_grad, output_partial, tokens, hidden, grad, gain, beta, feed_result, *weights)


def on_device(
    tokens,
    doc_ids,
    norm_gain,
    query_weight,
    key_weight,
    value_weight,
    house_weight,
    beta_weight,
    out_weight,
    ffn_gain,
    gate_weight,
    up_weight,
    down_weight,
    cotangent,
):
    groups, batch = lax.axis_size("g"), lax.axis_size("b")
    devices = groups * GROUP * batch
    rows, width = query_weight.shape
    hidden_rows = down_weight.shape[0]
    hidden_own = gate_weight.shape[1] // GROUP
    block_rows = tokens.shape[1]
    hops = groups // 2
    doc_columns = -(-block_rows // rows)
    place, line = lax.axis_index("g"), lax.axis_index("b")

    def columns(weight):
        return jnp.transpose(weight.astype(BF16).reshape(rows, GROUP, -1), (1, 0, 2))

    docs = jnp.pad(doc_ids[0].astype(BF16), (0, rows * doc_columns - block_rows)).reshape(rows, doc_columns)
    same = jnp.concatenate([norm_gain.astype(BF16)[:, None], ffn_gain.astype(BF16)[:, None], docs], 1)
    same = jnp.broadcast_to(same[None], (GROUP,) + same.shape)
    same = jnp.pad(same, ((0, 0), (0, 0), (0, EXTRA - OWN - same.shape[2])))
    first_parts = jnp.concatenate(
        [columns(w) for w in (query_weight, key_weight, value_weight, house_weight, beta_weight)] + [same], 2
    )

    def unit_columns(weight):
        parts = weight.astype(BF16).reshape(rows, groups, GROUP, batch, hidden_rows)
        return jnp.transpose(parts, (2, 0, 1, 3, 4)).reshape(GROUP, rows, hidden_own)

    whole_tiles = hidden_rows == BLOCK
    feed_weights = (gate_weight, up_weight) if whole_tiles else (unit_columns(gate_weight), unit_columns(up_weight))
    first, feed, out_full, down_low, tokens_all, cotangent_all = gather_first(
        groups, batch, first_parts, *feed_weights, out_weight, down_weight, tokens[0], cotangent[0]
    )
    first = first.reshape(width, -1)

    extra = first[:, 4 * WIDE :]
    gain_one = extra[:, OWN].astype(F32)[None]
    gain_two = extra[:, OWN + 1].astype(F32)[None]
    docs = extra[:, OWN + 2 : OWN + 2 + doc_columns].astype(jnp.int32)
    docs = docs.reshape(devices, -1)[:, :block_rows].reshape(groups, GROUP, batch, block_rows)
    docs = lax.dynamic_index_in_dim(docs, line, 2, keepdims=False).reshape(groups, GROUP * block_rows)
    doc_key = jnp.stack(
        [
            jnp.where(place >= hop, lax.dynamic_index_in_dim(docs, jnp.maximum(place - hop, 0), 0, keepdims=False), -1)
            for hop in range(hops + 1)
        ]
    )[:, None, :]
    doc_query = lax.dynamic_index_in_dim(docs, place, 0, keepdims=False)[:, None]

    normed = rms_norm(tokens_all.astype(F32), gain_one).astype(BF16)
    projected = dot(normed, first)
    (query, value, within, maps, inverse, attended, attended_low, stats, moved, values, out_full, feed) = attend(
        groups, hops, projected, doc_query, doc_key, out_full, feed
    )
    out_full = out_full.reshape(WIDE, width)
    feed = feed.reshape(width, -1)
    hidden, normed_two, active, gate_slope, up_slope, down_full = branch(
        groups, batch, dot(attended_low, out_full).astype(BF16), tokens[0], gain_two, down_low, feed
    )
    down_full = down_full.reshape(hidden_own, width)
    active_grad = dot(cotangent_all, down_full, NT)
    feed_grads = jnp.concatenate([(active_grad * gate_slope).astype(BF16), (active_grad * up_slope).astype(BF16)], 1)
    down_partial = dot(active, cotangent_all, TN).astype(BF16).reshape(groups, 1, batch, hidden_rows, width)
    feed_partial = dot(normed_two, feed_grads, TN).astype(BF16).reshape(groups, GROUP, batch, rows, -1)
    hidden_grad, down_weight_grad, rows_grad, feed_grad, out_weight_grad = back(
        groups, hops, dot(feed_grads, feed, NT).astype(BF16), hidden, cotangent[0], gain_two, attended_low, out_full, query, value,
        within, maps, doc_query, doc_key, attended, stats, values, moved, projected, inverse, down_partial, feed_partial,
    )
    output_partial = dot(active, down_full).astype(BF16)
    first_partial = dot(normed, rows_grad, TN).astype(BF16).reshape(groups, GROUP, batch, rows, -1)
    beta_parts = jnp.pad(columns(beta_weight), ((0, 0), (0, 0), (0, EXTRA - OWN)))
    weights = (query_weight, key_weight, value_weight, house_weight) + feed_weights
    results = finish(
        groups, whole_tiles, first_partial, first, rows_grad, output_partial, tokens[0], hidden, hidden_grad, gain_one, beta_parts, feed_grad,
        weights,
    )
    query_weight_grad, key_weight_grad, value_weight_grad, house_weight_grad, extra_grad, sums, tokens_grad, output = results[:8]
    output, tokens_grad = output[None], tokens_grad[None]
    out_weight_grad = out_weight_grad.astype(F32)
    down_weight_grad = down_weight_grad[0]
    beta_weight_grad = jnp.transpose(extra_grad[:, :, :OWN], (1, 0, 2)).reshape(rows, -1)

    def unit_whole(parts):
        parts = parts.astype(F32).reshape(GROUP, rows, groups, batch, hidden_rows)
        return jnp.transpose(parts, (1, 2, 0, 3, 4)).reshape(rows, -1)

    norm_gain_grad = sums[:, 0] / norm_gain.astype(BF16).astype(F32)
    if whole_tiles:
        gate_weight_grad, up_weight_grad = results[8:]
        feed_sum = sums[:, 1]
    else:
        gate_weight_grad, up_weight_grad = unit_whole(feed_grad[:, :, :hidden_own]), unit_whole(feed_grad[:, :, hidden_own:])
        feed_sum = jnp.sum(gate_weight_grad * gate_weight.astype(BF16).astype(F32), axis=1) + jnp.sum(
            up_weight_grad * up_weight.astype(BF16).astype(F32), axis=1
        )
    ffn_gain_grad = feed_sum / ffn_gain.astype(BF16).astype(F32)
    return (
        output,
        tokens_grad,
        norm_gain_grad,
        query_weight_grad,
        key_weight_grad,
        value_weight_grad,
        house_weight_grad,
        beta_weight_grad,
        out_weight_grad,
        ffn_gain_grad,
        gate_weight_grad,
        up_weight_grad,
        down_weight_grad,
    )


def solution(mesh):
    groups = mesh.shape["seq"] // GROUP
    inner = Mesh(mesh.devices.reshape(groups, GROUP, mesh.shape["batch"]), ("g", "m", "b"))
    line = P("b", ("g", "m"), None)
    vector = P(("g", "m", "b"))
    matrix = P(("g", "m", "b"), None)
    in_specs = (line, P("b", ("g", "m")), vector) + (matrix,) * 6 + (vector,) + (matrix,) * 3 + (line,)
    out_specs = (line, line, vector) + (matrix,) * 6 + (vector,) + (matrix,) * 3
    return jax.shard_map(on_device, mesh=inner, in_specs=in_specs, out_specs=out_specs, check_vma=False)
```

```python
import functools

import jax
import jax.numpy as jnp
from jax import lax
from jax.experimental import pallas as pl
from jax.experimental.pallas import tpu as pltpu
from jax.sharding import Mesh
from jax.sharding import PartitionSpec as P

HEADS = 12
HEAD_DIM = 128
GROUP = 4
OWN = HEADS // GROUP
WIDE = OWN * HEAD_DIM
BLOCK = 128
EXTRA = 128
EPSILON = 1e-06
NEGATIVE = -1e30
SCALE = HEAD_DIM ** (-0.5)
MESH = pl.DeviceIdType.MESH
F32 = jnp.float32
BF16 = jnp.bfloat16
NN = (((1,), (0,)), ((), ()))
NT = (((1,), (1,)), ((), ()))
TN = (((0,), (0,)), ((), ()))


def dot(left, right, dims=NN):
    return lax.dot_general(left, right, dims, preferred_element_type=F32)


def split(value):
    high = value.astype(BF16)
    return high, (value - high.astype(F32)).astype(BF16)


def dot3(left, right, dims=NN):
    left_high, left_low = split(left)
    right_high, right_low = split(right)
    return dot(left_high, right_high, dims) + (
        dot(left_high, right_low, dims) + dot(left_low, right_high, dims)
    )


def dot2(left, right, dims=NN):
    high, low = split(right)
    return dot(left, high, dims) + dot(left, low, dims)


def tile(index, count=1):
    return pl.ds(index * BLOCK, count * BLOCK)


def iota(axis, shape=(BLOCK, BLOCK)):
    return lax.broadcasted_iota(jnp.int32, shape, axis)


def invert(strict):
    row, col = iota(0), iota(1)
    eye = jnp.where(row == col, 1.0, 0.0)

    def part(size):
        return (row // (2 * size) == col // (2 * size)) & (row // size > col // size)

    totals = [eye - jnp.where(part(1), value, 0.0) for value in strict]
    size = 2
    while size < BLOCK:
        mask = part(size)
        pieces = [jnp.where(mask, value, 0.0) for value in strict]
        inner = [dot3(piece, total) for piece, total in zip(pieces, totals)]
        outer = [dot3(total, value) for total, value in zip(totals, inner)]
        totals = [total - value for total, value in zip(totals, outer)]
        size *= 2
    return totals


def unit_of(house):
    scale = lax.rsqrt(jnp.sum(house * house, axis=-1, keepdims=True) + EPSILON)
    return house * scale, scale


def products(query, key, unit):
    both = dot3(jnp.concatenate([unit, query], 0), jnp.concatenate([unit, key], 0), NT)
    return both[:BLOCK, :BLOCK], both[:BLOCK, BLOCK:], both[BLOCK:, :BLOCK], both[BLOCK:, BLOCK:]


def prepare_blocks(first, last, rows_ref, query_ref, key_ref, value_ref, within_ref, map_ref, inverse_ref):
    row, col = iota(0), iota(1)

    def one_block(block, carry):
        at = tile(block)
        kept, strict = [], []
        for head in range(OWN):
            query, key, value, house = [
                rows_ref[at, pl.ds(part * WIDE + head * BLOCK, BLOCK)] for part in range(4)
            ]
            rate = rows_ref[at, pl.ds(4 * WIDE, EXTRA)][:, head : head + 1]
            value_ref[at, tile(head)] = value.astype(BF16)
            unit, _ = unit_of(house)
            strength = 2.0 * jax.nn.sigmoid(rate)
            unit_unit, unit_key, query_unit, query_key = products(query, key, unit)
            strict.append(jnp.where(row > col, strength * unit_unit, 0.0))
            reach = jnp.where(row > col, strength * unit_key, 0.0)
            project = jnp.where(row >= col, query_unit, 0.0)
            kept.append((query, key, unit, strength, reach, project, query_key))
        inverses = invert(strict)
        for head in range(OWN):
            query, key, unit, strength, reach, project, query_key = kept[head]
            inverse = inverses[head]
            solved = dot3(inverse, jnp.concatenate([strength * unit, reach], 1))
            from_query = dot3(project, solved)
            from_unit = dot3(solved, unit, TN)
            query_ref[at, tile(head)] = (query - from_query[:, :BLOCK]).astype(BF16)
            within_ref[at, tile(head)] = query_key - from_query[:, BLOCK:]
            map_ref[at, tile(head)] = jnp.where(row == col, 1.0, 0.0) - from_unit[:BLOCK]
            key_ref[at, tile(head)] = (key - from_unit[BLOCK:]).astype(BF16)
            inverse_ref[at, tile(head)] = inverse
        return carry

    lax.fori_loop(first, last, one_block, 0)


def prepare_back_blocks(first, last, panels_ref, extra_ref, query_grad_ref, key_grad_ref, within_grad_ref, map_grad_ref, value_grad_ref, out_ref):
    row, col = iota(0), iota(1)

    def one_block(block, carry):
        at = tile(block)
        rates = jnp.zeros((BLOCK, EXTRA), F32)
        for head in range(OWN):
            query, key, house, inverse = [panels_ref[part, at, tile(head)] for part in range(4)]
            rate = extra_ref[at, :][:, head : head + 1]
            query_grad = query_grad_ref[at, tile(head)]
            key_grad = key_grad_ref[at, tile(head)]
            within_grad = within_grad_ref[at, tile(head)]
            map_grad = map_grad_ref[at, tile(head)]
            unit, scale = unit_of(house)
            strength = 2.0 * jax.nn.sigmoid(rate)
            unit_unit, unit_key, query_unit, query_key = products(query, key, unit)
            reach = jnp.where(row > col, strength * unit_key, 0.0)
            project = jnp.where(row >= col, query_unit, 0.0)
            solved = dot3(inverse, jnp.concatenate([strength * unit, reach], 1))
            both_grad = jnp.concatenate([query_grad, within_grad], 1)
            project_grad = jnp.where(row >= col, -dot3(both_grad, solved, NT), 0.0)
            solved_grad = -(
                dot3(project, both_grad, TN)
                + dot3(unit, jnp.concatenate([map_grad, key_grad], 0), NT)
            )
            given_grad = dot3(inverse, solved_grad, TN)
            strict_grad = jnp.where(row > col, -dot3(given_grad, solved, NT), 0.0)
            scaled_grad = given_grad[:, :BLOCK]
            reach_grad = jnp.where(row > col, given_grad[:, BLOCK:], 0.0)
            strength_grad = jnp.sum(
                scaled_grad * unit + reach_grad * unit_key + strict_grad * unit_unit, axis=1, keepdims=True
            )
            reach_part = strength * reach_grad
            inner_part = strength * strict_grad
            unit_grad = (
                strength * scaled_grad
                + dot3(reach_part, key)
                + dot3(inner_part + inner_part.T, unit)
                + dot3(project_grad, query, TN)
                - dot3(solved[:, :BLOCK], map_grad)
                - dot3(solved[:, BLOCK:], key_grad)
            )
            query_out = query_grad + dot3(within_grad, key) + dot3(project_grad, unit)
            key_out = key_grad + dot3(within_grad, query, TN) + dot3(reach_part, unit, TN)
            house_out = scale * (unit_grad - unit * jnp.sum(unit * unit_grad, axis=1, keepdims=True))
            rate_out = strength_grad * strength * (1.0 - 0.5 * strength)
            rates = jnp.where(iota(1, (BLOCK, EXTRA)) == head, rate_out, rates)
            out_ref[at, pl.ds(head * BLOCK, BLOCK)] = query_out.astype(BF16)
            out_ref[at, pl.ds(WIDE + head * BLOCK, BLOCK)] = key_out.astype(BF16)
            out_ref[at, pl.ds(2 * WIDE + head * BLOCK, BLOCK)] = value_grad_ref[at, tile(head)].astype(BF16)
            out_ref[at, pl.ds(3 * WIDE + head * BLOCK, BLOCK)] = house_out.astype(BF16)
        out_ref[at, pl.ds(4 * WIDE, EXTRA)] = rates.astype(BF16)
        return carry

    lax.fori_loop(first, last, one_block, 0)


def remote(source, target, send, recv, device):
    return pltpu.make_async_remote_copy(
        src_ref=source, dst_ref=target, send_sem=send, recv_sem=recv, device_id=device, device_id_type=MESH
    )


class Place:
    def __init__(self, groups, lines):
        self.groups, self.lines = groups, lines
        self.g, self.m, self.b = lax.axis_index("g"), lax.axis_index("m"), lax.axis_index("b")
        self.below, self.above = self.g > 0, self.g < groups - 1

    def other(self, offset):
        return {1: self.m + 1 - 2 * (self.m % 2), 2: (self.m + 2) % GROUP, 3: GROUP - 1 - self.m}[offset]

    def member(self, offset):
        return {"g": self.g, "m": self.other(offset), "b": self.b}

    def up(self):
        return {"g": self.g + 1, "m": self.m, "b": self.b}

    def down(self):
        return {"g": self.g - 1, "m": self.m, "b": self.b}

    def across(self):
        return {"g": self.g, "m": self.m, "b": 1 - self.b}

    def column(self, group):
        return {"g": group, "m": self.m, "b": self.b}

    def meet(self, column=False):
        barrier = pltpu.get_barrier_semaphore()

        def greet(device):
            pl.semaphore_signal(barrier, 1, device_id=device, device_id_type=MESH)

        for offset in range(1, GROUP):
            greet(self.member(offset))
        greet(self.across())
        if column:
            for step in range(1, self.groups):
                greet(self.column((self.g + step) % self.groups))
            count = GROUP + self.groups - 1
        else:
            pl.when(self.above)(lambda: greet(self.up()))
            pl.when(self.below)(lambda: greet(self.down()))
            count = GROUP + self.above.astype(jnp.int32) + self.below.astype(jnp.int32)
        pl.semaphore_wait(barrier, count)


class Gather:
    def __init__(self, place, parts, full, sems, mixed=True):
        self.place, self.parts, self.full, self.mixed = place, parts, full, mixed
        sems = list(sems)
        if parts is not None:
            self.part_send, self.part_recv, self.own_sem = sems[:3]
            sems = sems[3:]
        if sems:
            self.up_send, self.down_send, self.chain_recv, self.line_send, self.line_recv = sems

    @staticmethod
    def inside():
        dma = pltpu.SemaphoreType.DMA
        return [dma((GROUP,)), dma((GROUP,)), dma((1,))]

    @staticmethod
    def outside(groups):
        return [pltpu.SemaphoreType.DMA((groups,))] * 5

    def unit(self, group, line):
        return self.full.at[group, :, line] if self.mixed else self.full.at[group, line]

    def own(self):
        p = self.place
        if self.mixed:
            return pltpu.make_async_copy(self.parts.at[p.m], self.full.at[p.g, p.m, p.b], self.own_sem.at[0])
        return pltpu.make_async_copy(self.parts, self.full.at[p.g, p.b], self.own_sem.at[0])

    def part(self, offset):
        p = self.place
        other = p.other(offset)
        return remote(
            self.parts.at[other], self.full.at[p.g, p.m, p.b], self.part_send.at[offset], self.part_recv.at[offset], p.member(offset)
        )

    def start(self):
        if self.mixed:
            for offset in (2, 3, 1):
                self.part(offset).start()
        self.own().start()

    def chain(self, source, up):
        p = self.place
        unit = self.unit(source, p.b)
        sems = self.up_send if up else self.down_send
        return remote(unit, unit, sems.at[source], self.chain_recv.at[source], p.up() if up else p.down())

    def across(self, source):
        p = self.place
        unit = self.unit(source, p.b)
        return remote(unit, unit, self.line_send.at[source], self.line_recv.at[source], p.across())

    def settle(self):
        self.own().wait()
        if self.mixed:
            for offset in (2, 3, 1):
                self.part(offset).wait()

    def spread(self):
        p = self.place
        pl.when(p.above)(lambda: self.chain(p.g, True).start())
        pl.when(p.below)(lambda: self.chain(p.g, False).start())
        self.across(p.g).start()

    def step(self, distance):
        p = self.place

        @pl.when(p.g >= distance)
        def _():
            source = p.g - distance
            self.chain(source, True).wait_recv()
            pl.when(p.above)(lambda: self.chain(source, True).start())
            self.across(source).start()

        @pl.when(p.g + distance < p.groups)
        def _():
            source = p.g + distance
            self.chain(source, False).wait_recv()
            pl.when(p.below)(lambda: self.chain(source, False).start())
            self.across(source).start()

    def finish(self):
        p = self.place

        def settle(source, carry):
            self.across(source).wait()
            pl.when(p.above & (source <= p.g))(lambda: self.chain(source, True).wait_send())
            pl.when(p.below & (source >= p.g))(lambda: self.chain(source, False).wait_send())
            return carry

        lax.fori_loop(0, p.groups, settle, 0)


class HomeGather:
    def __init__(self, place, part, full, sems):
        self.place, self.part_ref, self.full = place, part, full
        self.home = place.groups // GROUP
        self.part_send, self.part_recv, self.up_send, self.down_send, self.chain_recv = sems

    @staticmethod
    def scratch(groups):
        dma = pltpu.SemaphoreType.DMA
        return [dma((1,)), dma((GROUP,))] + [dma((groups // GROUP,))] * 3

    def at_home(self):
        return self.place.m == self.place.g // self.home

    def slot(self):
        p = self.place
        return self.full.at[p.g % self.home, p.m, p.b]

    def hand(self):
        p = self.place
        keeper = p.g // self.home
        device = {"g": p.g, "m": keeper, "b": p.b}
        return remote(self.part_ref, self.slot(), self.part_send.at[0], self.part_recv.at[p.m], device)

    def taken(self, source):
        p = self.place
        target = self.full.at[p.g % self.home, source, p.b]
        return remote(self.part_ref, target, self.part_send.at[0], self.part_recv.at[source], p.member(1))

    def own(self):
        return pltpu.make_async_copy(self.part_ref, self.slot(), self.part_send.at[0])

    def start(self):
        pl.when(self.at_home())(lambda: self.own().start())
        pl.when(jnp.logical_not(self.at_home()))(lambda: self.hand().start())

    def chain(self, slot, up):
        p = self.place
        unit = self.full.at[slot, :, p.b]
        sems = self.up_send if up else self.down_send
        return remote(unit, unit, sems.at[slot], self.chain_recv.at[slot], p.up() if up else p.down())

    def spread(self):
        p = self.place

        @pl.when(self.at_home())
        def _():
            self.own().wait()
            for offset in range(1, GROUP):
                self.taken(p.other(offset)).wait_recv()
            slot = p.g % self.home
            pl.when(p.above)(lambda: self.chain(slot, True).start())
            pl.when(p.below)(lambda: self.chain(slot, False).start())

    def step(self, distance):
        p = self.place
        for slot in range(self.home):
            source = p.m * self.home + slot

            @pl.when(p.g - source == distance)
            def _():
                self.chain(slot, True).wait_recv()
                pl.when(p.above)(lambda: self.chain(slot, True).start())

            @pl.when(source - p.g == distance)
            def _():
                self.chain(slot, False).wait_recv()
                pl.when(p.below)(lambda: self.chain(slot, False).start())

    def finish(self):
        p = self.place
        pl.when(jnp.logical_not(self.at_home()))(lambda: self.hand().wait_send())
        for slot in range(self.home):
            source = p.m * self.home + slot
            pl.when(p.above & (p.g >= source))(lambda: self.chain(slot, True).wait_send())
            pl.when(p.below & (p.g <= source))(lambda: self.chain(slot, False).wait_send())


def home_lines(place, full, send, recv):
    copies = []
    for slot in range(place.groups // GROUP):
        unit = full.at[slot, :, place.b]
        copies.append(remote(unit, unit, send.at[slot], recv.at[slot], place.across()))
    return copies


class Scatter:
    def __init__(self, place, partial, result, refs):
        self.place, self.partial, self.result = place, partial, result
        (self.land, self.chain_land, self.leave, self.mine_sem, self.line_send, self.line_recv, self.chain_send,
         self.chain_recv, self.part_send, self.part_recv) = refs
        self.parts = partial.shape[1]

    @staticmethod
    def scratch(groups, shape):
        dma = pltpu.SemaphoreType.DMA
        unit = (shape[1],) + tuple(shape[3:])
        return [
            pltpu.VMEM((groups,) + unit, BF16),
            pltpu.VMEM((groups + 1,) + unit, BF16),
            pltpu.VMEM((groups,) + unit, BF16),
            dma((groups,)),
            dma((groups,)),
            dma((groups,)),
            dma((groups,)),
            dma((groups + 1,)),
            dma((GROUP,)),
            dma((GROUP,)),
        ]

    def load(self, target):
        return pltpu.make_async_copy(self.partial.at[target, :, self.place.b], self.leave.at[target], self.mine_sem.at[target])

    def line(self, target):
        p = self.place
        return remote(
            self.partial.at[target, :, 1 - p.b], self.land.at[target], self.line_send.at[target], self.line_recv.at[target], p.across()
        )

    def up(self, target):
        p = self.place
        return remote(
            self.leave.at[target], self.chain_land.at[target], self.chain_send.at[target], self.chain_recv.at[target], p.up()
        )

    def down(self, target, slot):
        p = self.place
        return remote(
            self.leave.at[target], self.chain_land.at[slot], self.chain_send.at[target], self.chain_recv.at[slot], p.down()
        )

    def send_up(self, target):
        self.up(target).start()

    def send_down(self, target):
        p = self.place
        pl.when(p.g - 1 == target)(lambda: self.down(target, p.groups).start())
        pl.when(p.g - 1 != target)(lambda: self.down(target, target).start())

    def arrived(self, slot):
        p = self.place
        return remote(self.leave.at[0], self.chain_land.at[slot], self.chain_send.at[0], self.chain_recv.at[slot], p.across())

    def wave(self, wave, act_up, act_down):
        p = self.place
        pl.when(wave > p.g)(lambda: act_up(p.groups - wave + p.g))
        pl.when(wave >= p.groups - p.g)(lambda: act_down(wave - p.groups + p.g))

    def act(self, target):
        self.line(target).start()
        self.load(target).start()

    def start(self):
        self.start_far()
        self.act(self.place.g)

    def start_far(self, first=1, last=None):
        p = self.place
        for wave in range(first, p.groups if last is None else last + 1):
            self.wave(wave, self.act, self.act)
        if first > 1:
            return

        @pl.when(jnp.logical_not(p.below))
        def _():
            self.chain_land[p.g] = jnp.zeros(self.chain_land.shape[1:], BF16)

        @pl.when(jnp.logical_not(p.above))
        def _():
            self.chain_land[p.groups] = jnp.zeros(self.chain_land.shape[1:], BF16)

    def both(self, target, part):
        return self.leave[target, part].astype(F32) + self.land[target, part].astype(F32)

    def step(self, wave):
        p = self.place

        def send(target, inner, copy):
            self.load(target).wait()
            self.line(target).wait_recv()

            @pl.when(inner)
            def _():
                self.arrived(target).wait_recv()
                for part in range(self.parts):
                    self.leave[target, part] = (self.both(target, part) + self.chain_land[target, part].astype(F32)).astype(BF16)

            @pl.when(jnp.logical_not(inner))
            def _():
                for part in range(self.parts):
                    self.leave[target, part] = self.both(target, part).astype(BF16)

            copy(target)

        self.wave(
            wave,
            lambda target: send(target, p.below, self.send_up),
            lambda target: send(target, p.above, self.send_down),
        )

    def hand(self, offset):
        p = self.place
        return remote(
            self.leave.at[p.g, p.other(offset)], self.result.at[p.m], self.part_send.at[offset], self.part_recv.at[offset], p.member(offset)
        )

    def last(self):
        p = self.place
        self.load(p.g).wait()
        self.line(p.g).wait_recv()
        pl.when(p.below)(lambda: self.arrived(p.g).wait_recv())
        pl.when(p.above)(lambda: self.arrived(p.groups).wait_recv())
        for part in range(self.parts):
            total = self.both(p.g, part) + self.chain_land[p.g, part].astype(F32) + self.chain_land[p.groups, part].astype(F32)
            if self.parts == 1:
                self.result[part] = total.astype(self.result.dtype)
            else:
                self.leave[p.g, part] = total.astype(BF16)
        if self.parts > 1:
            for offset in (2, 3, 1):
                self.hand(offset).start()
            self.result[p.m] = self.leave[p.g, p.m]

    def finish(self):
        p = self.place
        for target in range(p.groups):
            self.line(target).wait_send()
            pl.when(p.g != target)(lambda: self.up(target).wait_send())
        if self.parts > 1:
            for offset in (2, 3, 1):
                self.hand(offset).wait()


class LineSum:
    def __init__(self, place, partial, result, refs):
        self.place, self.partial, self.result = place, partial, result
        self.land, self.mine_sem, self.send, self.recv = refs

    @staticmethod
    def scratch(groups, shape):
        home = groups // GROUP
        return [pltpu.VMEM((home, GROUP) + tuple(shape[3:]), BF16)] + [pltpu.SemaphoreType.DMA((home,))] * 3

    def load(self, slot):
        return pltpu.make_async_copy(self.partial.at[slot, :, self.place.b], self.result.at[slot], self.mine_sem.at[slot])

    def line(self, slot):
        p = self.place
        return remote(self.partial.at[slot, :, 1 - p.b], self.land.at[slot], self.send.at[slot], self.recv.at[slot], p.across())

    def start(self):
        for slot in range(self.partial.shape[0]):
            self.line(slot).start()
            self.load(slot).start()

    def finish(self):
        for slot in range(self.partial.shape[0]):
            self.load(slot).wait()
            self.line(slot).wait()
            for part in range(GROUP):
                total = self.result[slot, part].astype(F32) + self.land[slot, part].astype(F32)
                self.result[slot, part] = total.astype(BF16)


class HomeScatter:
    def __init__(self, place, partial, result, refs):
        self.place, self.partial, self.result = place, partial, result
        self.home_land, self.leave, self.home_send, self.home_recv, self.part_send, self.part_recv = refs
        self.home = place.groups // GROUP

    @staticmethod
    def scratch(groups, shape):
        dma = pltpu.SemaphoreType.DMA
        unit = tuple(shape[1:])
        return [
            pltpu.VMEM((groups - 1,) + unit, BF16),
            pltpu.VMEM(unit, BF16),
            dma((shape[0],)),
            dma((groups - 1,)),
            dma((GROUP,)),
            dma((1,)),
        ]

    def home_copy(self, slot):
        p = self.place
        target = p.m * self.home + slot
        index = (p.g - target + p.groups - 1) % p.groups
        return remote(
            self.partial.at[slot], self.home_land.at[index], self.home_send.at[slot], self.home_recv.at[index], p.column(target)
        )

    def landed(self, index):
        p = self.place
        return remote(self.leave, self.home_land.at[index], self.home_send.at[0], self.home_recv.at[index], p.across())

    def start(self):
        p = self.place
        for slot in range(self.home):
            pl.when(p.g != p.m * self.home + slot)(lambda: self.home_copy(slot).start())

    def hand(self, other):
        p = self.place
        return remote(
            self.leave.at[other], self.result, self.part_send.at[other], self.part_recv.at[0], {"g": p.g, "m": other, "b": p.b}
        )

    def last(self):
        p = self.place

        @pl.when(p.m == p.g // self.home)
        def _():
            for index in range(p.groups - 1):
                self.landed(index).wait_recv()
            for part in range(GROUP):
                total = self.partial[p.g % self.home, part].astype(F32)
                for index in range(p.groups - 1):
                    total = total + self.home_land[index, part].astype(F32)
                self.leave[part] = total.astype(BF16)
            for offset in range(1, GROUP):
                self.hand(p.other(offset)).start()
            self.result[...] = self.leave[p.m]

    def finish(self):
        p = self.place
        keeper = p.m == p.g // self.home

        @pl.when(keeper)
        def _():
            for offset in range(1, GROUP):
                self.hand(p.other(offset)).wait_send()

        pl.when(jnp.logical_not(keeper))(lambda: self.hand(p.other(1)).wait_recv())
        for slot in range(self.home):
            pl.when(p.g != p.m * self.home + slot)(lambda: self.home_copy(slot).wait_send())


CHUNKS = 4


class GroupSum:
    def __init__(self, place, partial, refs):
        self.place, self.partial = place, partial
        self.pair_land, self.leave, self.land, self.pair_send, self.pair_recv, self.send, self.recv = refs
        self.size = partial.shape[0] // GROUP
        self.rows = self.size // CHUNKS

    @staticmethod
    def scratch(size, width):
        dma = pltpu.SemaphoreType.DMA
        return [
            pltpu.VMEM((2, size, width), BF16),
            pltpu.VMEM((size, width), BF16),
            pltpu.VMEM((size, width), BF16),
            dma((2, CHUNKS)),
            dma((2, CHUNKS)),
            dma((CHUNKS,)),
            dma((CHUNKS,)),
        ]

    def at(self, chunk, member=0):
        return pl.ds(pl.multiple_of(member * self.size + chunk * self.rows, self.rows), self.rows)

    def pair(self, chunk, far):
        p = self.place
        member = p.other(3 if far else 1)
        slot = 1 if far else 0
        return remote(
            self.partial.at[self.at(chunk, member)], self.pair_land.at[slot, self.at(chunk)], self.pair_send.at[slot, chunk],
            self.pair_recv.at[slot, chunk], p.member(1),
        )

    def cross(self, chunk):
        return remote(
            self.leave.at[self.at(chunk)], self.land.at[self.at(chunk)], self.send.at[chunk], self.recv.at[chunk], self.place.member(2)
        )

    def start(self):
        for chunk in range(CHUNKS):
            self.pair(chunk, True).start()
        for chunk in range(CHUNKS):
            self.pair(chunk, False).start()

    def pass_on(self, chunk):
        self.pair(chunk, True).wait_recv()
        own = self.partial[self.at(chunk, self.place.other(2)), :].astype(F32)
        self.leave[self.at(chunk), :] = (own + self.pair_land[1, self.at(chunk), :].astype(F32)).astype(BF16)
        self.cross(chunk).start()

    def take(self, chunk):
        self.pair(chunk, False).wait_recv()
        self.cross(chunk).wait_recv()
        own = self.partial[self.at(chunk, self.place.m), :].astype(F32)
        return own + self.pair_land[0, self.at(chunk), :].astype(F32) + self.land[self.at(chunk), :].astype(F32)

    def finish(self):
        for chunk in range(CHUNKS):
            self.pair(chunk, True).wait_send()
            self.pair(chunk, False).wait_send()
            self.cross(chunk).wait_send()


class GroupGather:
    def __init__(self, place, whole, refs):
        self.place, self.whole = place, whole
        self.send, self.recv = refs
        self.size = whole.shape[0] // GROUP
        self.rows = self.size // CHUNKS

    @staticmethod
    def scratch():
        dma = pltpu.SemaphoreType.DMA
        return [dma((3, CHUNKS)), dma((3, CHUNKS))]

    def at(self, chunk, member):
        return pl.ds(pl.multiple_of(member * self.size + chunk * self.rows, self.rows), self.rows)

    def copy(self, chunk, way):
        p = self.place
        rows = self.whole.at[self.at(chunk, p.other(2) if way == 2 else p.m)]
        return remote(rows, rows, self.send.at[way, chunk], self.recv.at[way, chunk], p.member(2 if way == 0 else 1))

    def give(self, chunk):
        self.copy(chunk, 0).start()
        self.copy(chunk, 1).start()

    def pass_on(self, chunk):
        self.copy(chunk, 0).wait_recv()
        self.copy(chunk, 2).start()

    def finish(self):
        for chunk in range(CHUNKS):
            self.copy(chunk, 1).wait_recv()
            self.copy(chunk, 2).wait_recv()
            for way in range(3):
                self.copy(chunk, way).wait_send()


def masked(scores, counts):
    return jnp.where(counts, scores * SCALE, NEGATIVE)


class Pauses:
    def __init__(self, *steps):
        self.steps = list(steps)

    def __call__(self):
        if self.steps:
            for act in self.steps.pop(0):
                act()

    def rest(self):
        while self.steps:
            self()


def several(refs, *counts):
    refs = list(refs)
    taken = []
    for count in counts:
        taken.append(refs[:count])
        refs = refs[count:]
    return taken


def attend_kernel(
    groups,
    hops,
    rows_ref,
    doc_query_ref,
    doc_key_ref,
    out_home_ref,
    feed_unit_ref,
    query_ref,
    value_ref,
    within_ref,
    map_ref,
    inverse_ref,
    attended_ref,
    low_ref,
    stats_ref,
    moved_ref,
    values_ref,
    out_full_ref,
    feed_full_ref,
    key_ref,
    leave_ref,
    top_ref,
    total_ref,
    accum_ref,
    key_send,
    key_recv,
    value_send,
    value_recv,
    *sems,
):
    here = Place(groups, feed_full_ref.shape[2])
    here.meet()
    place, has_next, following = here.g, here.above, here.up()
    home_sems, feed_sems = several(sems, 2, 5)
    out_copies = home_lines(here, out_full_ref, *home_sems)
    feed_gather = Gather(here, None, feed_full_ref, feed_sems)
    feed_gather.spread()
    for copy in out_copies:
        copy.start()
    pauses = Pauses(
        *[
            (functools.partial(feed_gather.step, distance),)
            for distance in range(1, groups)
        ]
    )
    prepared = (rows_ref, query_ref, key_ref, value_ref, within_ref, map_ref, inverse_ref)
    prepare_blocks(0, GROUP, *prepared)

    def value_copy(source, slot):
        return remote(source, values_ref.at[slot], value_send.at[slot], value_recv.at[slot], following)

    def key_copy(slot):
        return remote(leave_ref.at[slot], moved_ref.at[slot + 1, 0], key_send.at[slot], key_recv.at[slot], following)

    def move(keys, block, head):
        return dot2(keys, map_ref[tile(block), tile(head)]).astype(BF16)

    for head in range(OWN):
        keys = key_ref[tile(0), tile(head)]
        for block in range(1, GROUP):
            moved_ref[0, block, tile(0, block), tile(head)] = keys
            keys = jnp.concatenate([move(keys, block, head), key_ref[tile(block), tile(head)]], 0)
        leave_ref[0, :, tile(head)] = keys

    @pl.when(has_next)
    def _():
        key_copy(0).start()
        value_copy(value_ref, 0).start()

    pauses()

    def row_counts(block, hop, first, count):
        return doc_query_ref[tile(block), :] == doc_key_ref[hop, :, tile(first, count)]

    for block in range(GROUP):
        counts = row_counts(block, 0, 0, block + 1)
        wide = (BLOCK, (block + 1) * BLOCK)
        counts = counts & (iota(0, wide) + block * BLOCK >= iota(1, wide))
        for head in range(OWN):
            scores = within_ref[tile(block), tile(head)]
            if block:
                before = dot(query_ref[tile(block), tile(head)], moved_ref[0, block, tile(0, block), tile(head)], NT)
                scores = jnp.concatenate([before, scores], 1)
            scores = masked(scores, counts)
            top = jnp.max(scores, axis=1, keepdims=True)
            weights = jnp.exp(scores - top)
            top_ref[head, tile(block), :] = jnp.broadcast_to(top, (BLOCK, BLOCK))
            total_ref[head, tile(block), :] = jnp.broadcast_to(jnp.sum(weights, axis=1, keepdims=True), (BLOCK, BLOCK))
            accum_ref[tile(block), tile(head)] = dot(weights.astype(BF16), value_ref[tile(0, block + 1), tile(head)])

    def hop_step(hop, last):
        @pl.when(place >= hop)
        def _():
            key_copy(hop - 1).wait_recv()
            for head in range(OWN):
                keys = moved_ref[hop, 0, :, tile(head)]
                for block in range(GROUP):
                    if last:
                        if block == GROUP - 1:
                            break
                        keys = move(keys[BLOCK:], block, head)
                        moved_ref[hop, block + 1, tile(block + 1, GROUP - 1 - block), tile(head)] = keys
                    else:
                        keys = move(keys, block, head)
                        if block < GROUP - 1:
                            moved_ref[hop, block + 1, :, tile(head)] = keys
                        else:
                            leave_ref[hop, :, tile(head)] = keys
            value_copy(value_ref, hop - 1).wait_recv()
            if not last:

                @pl.when(has_next)
                def _():
                    key_copy(hop).start()
                    value_copy(values_ref.at[hop - 1], hop).start()

            for block in range(GROUP):
                first = block if last else 0
                count = GROUP - first
                counts = row_counts(block, hop, first, count)
                for head in range(OWN):
                    scores = masked(
                        dot(query_ref[tile(block), tile(head)], moved_ref[hop, block, tile(first, count), tile(head)], NT),
                        counts,
                    )
                    old = top_ref[head, tile(block), :]
                    top = jnp.maximum(old, jnp.broadcast_to(jnp.max(scores, axis=1, keepdims=True), (BLOCK, BLOCK)))
                    factor = jnp.exp(old - top)
                    weights = jnp.exp(scores - jnp.concatenate([top] * count, 1))
                    top_ref[head, tile(block), :] = top
                    total_ref[head, tile(block), :] = total_ref[head, tile(block), :] * factor + jnp.sum(
                        weights, axis=1, keepdims=True
                    )
                    accum_ref[tile(block), tile(head)] = accum_ref[tile(block), tile(head)] * factor + dot(
                        weights.astype(BF16), values_ref[hop - 1, tile(first, count), tile(head)]
                    )

    if hops > 2:

        def between(hop, carry):
            hop_step(hop, False)
            return carry

        lax.fori_loop(1, hops, between, 0)
    else:
        for hop in range(1, hops):
            pauses()
            hop_step(hop, False)
    pauses()
    hop_step(hops, True)

    for block in range(GROUP):
        stats = jnp.zeros((BLOCK, BLOCK), F32)
        for head in range(OWN):
            total = total_ref[head, tile(block), :]
            result = accum_ref[tile(block), tile(head)] / total
            attended_ref[tile(block), tile(head)] = result
            low_ref[tile(block), tile(head)] = result.astype(BF16)
            stats = jnp.where(iota(1) == head, top_ref[head, tile(block), :], stats)
            stats = jnp.where(iota(1) == OWN + head, total, stats)
        stats_ref[tile(block), :] = stats

    def settle(slot, carry):
        @pl.when(has_next & (place >= slot))
        def _():
            key_copy(slot).wait_send()
            value_copy(value_ref, slot).wait_send()

        return carry

    lax.fori_loop(0, hops, settle, 0)
    pauses.rest()
    for copy in out_copies:
        copy.wait()
    feed_gather.finish()


def in_vmem(count):
    return [pl.BlockSpec(memory_space=pltpu.VMEM)] * count


def anywhere(count):
    return [pl.BlockSpec(memory_space=pl.ANY)] * count


def shape(kind, *dims):
    return jax.ShapeDtypeStruct(dims, kind)


def communicating(number, name, vmem=58):
    return {
        "compiler_params": pltpu.CompilerParams(collective_id=number, has_side_effects=True, vmem_limit_bytes=vmem << 20),
        "name": name,
    }


def attend(groups, hops, projected, doc_query, doc_key, out_full, feed_full):
    length = projected.shape[0]
    dma = pltpu.SemaphoreType.DMA
    return pl.pallas_call(
        functools.partial(attend_kernel, groups, hops),
        out_shape=[
            shape(BF16, length, WIDE),
            shape(BF16, length, WIDE),
            shape(F32, length, WIDE),
            shape(F32, length, WIDE),
            shape(F32, length, WIDE),
            shape(F32, length, WIDE),
            shape(BF16, length, WIDE),
            shape(F32, length, BLOCK),
            shape(BF16, hops + 1, GROUP, length, WIDE),
            shape(BF16, hops, length, WIDE),
            shape(BF16, *out_full.shape),
            shape(BF16, *feed_full.shape),
        ],
        in_specs=in_vmem(3) + anywhere(2),
        out_specs=in_vmem(10) + anywhere(2),
        scratch_shapes=[
            pltpu.VMEM((length, WIDE), BF16),
            pltpu.VMEM((hops, length, WIDE), BF16),
            pltpu.VMEM((OWN, length, BLOCK), F32),
            pltpu.VMEM((OWN, length, BLOCK), F32),
            pltpu.VMEM((length, WIDE), F32),
            dma((hops,)),
            dma((hops,)),
            dma((hops,)),
            dma((hops,)),
        ]
        + [dma((groups // GROUP,))] * 2
        + Gather.outside(groups),
        input_output_aliases={3: 10, 4: 11},
        **communicating(1, "attend"),
    )(projected, doc_query, doc_key, out_full, feed_full)


def back_kernel(
    groups,
    hops,
    partial_ref,
    hidden_ref,
    cotangent_ref,
    gain_ref,
    low_ref,
    out_ref,
    query_ref,
    value_ref,
    within_ref,
    map_ref,
    doc_query_ref,
    doc_key_ref,
    attended_ref,
    stats_ref,
    values_hbm,
    moved_hbm,
    rows_hbm,
    inverse_hbm,
    down_partial_ref,
    feed_partial_ref,
    grad_ref,
    down_result_ref,
    rows_grad_ref,
    feed_result_ref,
    out_result_ref,
    grad_low_ref,
    att_grad_ref,
    out_partial_ref,
    moved_ref,
    values_ref,
    extra_ref,
    load_sem,
    query_grad_ref,
    key_grad_ref,
    within_grad_ref,
    map_grad_ref,
    value_grad_ref,
    scaled_ref,
    dots_ref,
    direct_ref,
    panels_ref,
    key_slots_ref,
    value_slots_ref,
    key_send,
    key_recv,
    value_send,
    value_recv,
    *refs,
):
    lines = feed_partial_ref.shape[2]
    here = Place(groups, lines)
    here.meet()
    place, has_next, previous = here.g, here.above, here.down()
    sum_refs, gather_refs, down_refs, feed_refs, out_refs = several(
        refs,
        7,
        2,
        len(Scatter.scratch(groups, down_partial_ref.shape)),
        len(Scatter.scratch(groups, feed_partial_ref.shape)),
        len(LineSum.scratch(groups, out_partial_ref.shape)),
    )
    sums = GroupSum(here, partial_ref, sum_refs)
    whole = GroupGather(here, grad_low_ref, gather_refs)
    down = Scatter(here, down_partial_ref, down_result_ref, down_refs)
    feed_scatter = Scatter(here, feed_partial_ref, feed_result_ref, feed_refs)
    out_lines = LineSum(here, out_partial_ref, out_result_ref, out_refs)
    pauses = Pauses(*[(functools.partial(feed_scatter.step, wave),) for wave in range(1, groups)])

    def load(hop):
        return pltpu.make_async_copy(moved_hbm.at[hop], moved_ref.at[hop % 2], load_sem.at[hop % 2])

    def load_values(hop):
        return pltpu.make_async_copy(values_hbm.at[hop - 1], values_ref.at[hop % 2], load_sem.at[2 + hop % 2])

    short = hops > 2
    loads = [pltpu.make_async_copy(rows_hbm.at[:, pl.ds(4 * WIDE, EXTRA)], extra_ref, load_sem.at[4])]
    panels = direct_ref if short else panels_ref
    for index, panel in enumerate((0, 1, 3)):
        loads.append(pltpu.make_async_copy(rows_hbm.at[:, pl.ds(panel * WIDE, WIDE)], panels.at[index], load_sem.at[5 + index]))
    loads.append(pltpu.make_async_copy(inverse_hbm, panels.at[3], load_sem.at[8]))
    sums.start()
    down.start()
    load(hops).start()
    load_values(hops).start()
    if not short:
        for copy in loads:
            copy.start()
    feed_scatter.start_far(1, 1)
    for chunk in range(CHUNKS):
        sums.pass_on(chunk)
    for chunk in range(CHUNKS):
        back = rms_back(hidden_ref[sums.at(chunk), :], gain_ref[...], sums.take(chunk))
        grad = cotangent_ref[sums.at(chunk), :].astype(F32) + back
        grad_ref[sums.at(chunk), :] = grad
        grad_low_ref[whole.at(chunk, here.m), :] = grad.astype(BF16)
        whole.give(chunk)
    down.step(1)
    for chunk in range(CHUNKS):
        whole.pass_on(chunk)
    if groups > 2:
        down.step(2)
    whole.finish()
    att_grad_ref[...] = dot(grad_low_ref[...], out_ref[...], NT).astype(BF16)
    turned = low_ref[...].T
    units = out_partial_ref.shape[3]

    def out_tile(at):
        value = dot(turned, grad_low_ref[:, at])
        for index in range(WIDE // units):
            slot, member, line = index // (GROUP * lines), index // lines % GROUP, index % lines
            out_partial_ref[slot, member, line, :, at] = value[index * units : (index + 1) * units].astype(BF16)

    in_tiles(out_partial_ref.shape[4], out_tile)
    out_lines.start()
    feed_scatter.start_far(2)
    feed_scatter.act(here.g)
    for wave in range(3, groups):
        down.step(wave)

    def key_copy(hop):
        slot = hop - 1
        return remote(key_slots_ref.at[hop], key_slots_ref.at[slot], key_send.at[slot], key_recv.at[slot], previous)

    def value_copy(hop):
        slot = hop - 1
        return remote(value_slots_ref.at[hop], value_slots_ref.at[slot], value_send.at[slot], value_recv.at[slot], previous)

    map_grad_ref[...] = jnp.zeros_like(map_grad_ref)
    query_grad_ref[...] = jnp.zeros_like(query_grad_ref)
    for block in range(GROUP):
        for head in range(OWN):
            at = (tile(block), tile(head))
            grad = att_grad_ref[at].astype(F32)
            total = stats_ref[tile(block), OWN + head : OWN + head + 1]
            scaled_ref[at] = (grad / total).astype(BF16)
            dots = -jnp.sum(grad * attended_ref[at], axis=1, keepdims=True) / total
            dots_ref[head, tile(block), :] = jnp.broadcast_to(dots, (BLOCK, BLOCK))

    def pair(block, head, scores, counts, values):
        count = scores.shape[1] // BLOCK
        top = stats_ref[tile(block), head : head + 1]
        weights = jnp.exp(masked(scores, counts) - top)
        weight_grad = dot(scaled_ref[tile(block), tile(head)], values, NT)
        dots = jnp.concatenate([dots_ref[head, tile(block), :]] * count, 1)
        return weights, weights * (weight_grad + dots) * SCALE

    def row_counts(block, hop, first, count):
        return doc_query_ref[tile(block), :] == doc_key_ref[hop, :, tile(first, count)]

    def hop_direct(hop, last):
        for head in range(OWN):
            value_grad_ref[:, tile(head)] = jnp.zeros((GROUP * BLOCK, BLOCK), F32)
        for block in range(GROUP):
            first = block if last else 0
            count = GROUP - first
            counts = row_counts(block, hop, first, count)
            for head in range(OWN):
                query = query_ref[tile(block), tile(head)]
                keys = moved_ref[hop % 2, block, tile(first, count), tile(head)]
                weights, grad = pair(
                    block, head, dot(query, keys, NT), counts, values_ref[hop % 2, tile(first, count), tile(head)]
                )
                raw = grad.astype(BF16)
                query_grad_ref[tile(block), tile(head)] += dot(raw, keys)
                direct_ref[block, tile(first, count), tile(head)] = dot(raw, query, TN)
                value_grad_ref[tile(first, count), tile(head)] += dot(
                    weights.astype(BF16), scaled_ref[tile(block), tile(head)], TN
                )

    def collect_map(block, head, keys, grads):
        map_grad_ref[tile(block), tile(head)] += dot2(keys, grads, TN)

    def hop_chain(hop, last):
        for head in range(OWN):
            if last:
                grads = direct_ref[GROUP - 1, tile(GROUP - 1), tile(head)]
                for block in range(GROUP - 2, -1, -1):
                    rows = tile(block + 1, GROUP - 1 - block)
                    collect_map(block, head, moved_ref[hop % 2, block, rows, tile(head)], grads)
                    back = dot3(grads, map_ref[tile(block), tile(head)], NT)
                    direct = direct_ref[block, tile(block, GROUP - block), tile(head)]
                    grads = jnp.concatenate([direct[:BLOCK], direct[BLOCK:] + back], 0)
                key_slots_ref[hop, :, tile(head)] = grads.astype(BF16)
                value_slots_ref[hop, :, tile(head)] = value_grad_ref[:, tile(head)].astype(BF16)
            else:
                grads = key_grad_ref[:, tile(head)]
                for block in range(GROUP - 1, -1, -1):
                    collect_map(block, head, moved_ref[hop % 2, block, :, tile(head)], grads)
                    grads = direct_ref[block, :, tile(head)] + dot3(grads, map_ref[tile(block), tile(head)], NT)
                key_slots_ref[hop, :, tile(head)] = grads.astype(BF16)

    def take(hop):
        @pl.when(has_next)
        def _():
            key_copy(hop).wait_recv()
            key_grad_ref[...] = key_slots_ref[hop - 1].astype(F32)

        @pl.when(jnp.logical_not(has_next))
        def _():
            key_grad_ref[...] = jnp.zeros_like(key_grad_ref)

    load(hops - 1).start()
    load_values(hops - 1).start()
    load(hops).wait()
    load_values(hops).wait()

    @pl.when(place >= hops)
    def _():
        hop_direct(hops, True)
        hop_chain(hops, True)
        key_copy(hops).start()
        value_copy(hops).start()

    down.last()

    def between(hop, pause=None):
        load(hop - 1).start()
        pl.when(jnp.asarray(hop) > 1)(lambda: load_values(hop - 1).start())
        load(hop).wait()
        load_values(hop).wait()
        pl.when(place >= hop)(lambda: hop_direct(hop, False))
        if pause is not None:
            pause()

        @pl.when(place >= hop)
        def _():
            take(hop + 1)
            hop_chain(hop, False)
            key_copy(hop).start()

            @pl.when(has_next)
            def _():
                value_copy(hop + 1).wait_recv()
                for head in range(OWN):
                    value_slots_ref[hop, :, tile(head)] = (
                        value_grad_ref[:, tile(head)] + value_slots_ref[hop, :, tile(head)].astype(F32)
                    ).astype(BF16)

            @pl.when(jnp.logical_not(has_next))
            def _():
                for head in range(OWN):
                    value_slots_ref[hop, :, tile(head)] = value_grad_ref[:, tile(head)].astype(BF16)

            value_copy(hop).start()

    if hops > 2:

        def step(counter, carry):
            between(hops - 1 - counter)
            return carry

        lax.fori_loop(0, hops - 1, step, 0)
    else:
        for hop in range(hops - 1, 0, -1):
            between(hop, pauses)

    load(0).wait()
    for head in range(OWN):
        value_grad_ref[:, tile(head)] = jnp.zeros((GROUP * BLOCK, BLOCK), F32)
    for block in range(GROUP):
        wide = (BLOCK, (block + 1) * BLOCK)
        counts = row_counts(block, 0, 0, block + 1) & (iota(0, wide) + block * BLOCK >= iota(1, wide))
        for head in range(OWN):
            query = query_ref[tile(block), tile(head)]
            scores = within_ref[tile(block), tile(head)]
            if block:
                keys = moved_ref[0, block, tile(0, block), tile(head)]
                scores = jnp.concatenate([dot(query, keys, NT), scores], 1)
            weights, grad = pair(block, head, scores, counts, value_ref[tile(0, block + 1), tile(head)])
            within_grad_ref[tile(block), tile(head)] = grad[:, block * BLOCK :]
            value_grad_ref[tile(0, block + 1), tile(head)] += dot(
                weights.astype(BF16), scaled_ref[tile(block), tile(head)], TN
            )
            if block:
                raw = grad[:, : block * BLOCK].astype(BF16)
                query_grad_ref[tile(block), tile(head)] += dot(raw, keys)
                direct_ref[block, tile(0, block), tile(head)] = dot(raw, query, TN)
    take(1)
    for head in range(OWN):
        grads = key_grad_ref[:, tile(head)]
        for block in range(GROUP - 1, 0, -1):
            key_grad_ref[tile(block), tile(head)] = grads[block * BLOCK :]
            grads = grads[: block * BLOCK]
            collect_map(block, head, moved_ref[0, block, tile(0, block), tile(head)], grads)
            grads = direct_ref[block, tile(0, block), tile(head)] + dot3(grads, map_ref[tile(block), tile(head)], NT)
        key_grad_ref[tile(0), tile(head)] = grads

    @pl.when(has_next)
    def _():
        value_copy(1).wait_recv()
        value_grad_ref[...] += value_slots_ref[0].astype(F32)

    def settle(hop, carry):
        @pl.when(place >= hop)
        def _():
            key_copy(hop).wait_send()
            value_copy(hop).wait_send()

        return carry

    lax.fori_loop(1, hops + 1, settle, 0)
    if short:
        for copy in loads:
            copy.start()
    for copy in loads:
        copy.wait()
    pauses()
    pieces = (panels, extra_ref, query_grad_ref, key_grad_ref, within_grad_ref, map_grad_ref, value_grad_ref, rows_grad_ref)
    prepare_back_blocks(0, GROUP // 2, *pieces)
    pauses.rest()
    prepare_back_blocks(GROUP // 2, GROUP, *pieces)
    out_lines.finish()
    feed_scatter.last()
    sums.finish()
    down.finish()
    feed_scatter.finish()


def back(groups, hops, partial, hidden, cotangent, gain, low, out, *args):
    values, moved, rows, inverse, down, feed = args[-6:]
    size, width = hidden.shape
    length = partial.shape[0]
    lines, units = feed.shape[2:4]
    out_shape = (groups // GROUP, GROUP, lines, units, width)
    dma = pltpu.SemaphoreType.DMA
    inputs = (partial, hidden, cotangent, gain, low, out) + args
    return pl.pallas_call(
        functools.partial(back_kernel, groups, hops),
        out_shape=[
            shape(F32, size, width),
            shape(F32, 1, *down.shape[3:]),
            shape(BF16, *rows.shape),
            shape(BF16, GROUP, *feed.shape[3:]),
            shape(BF16, groups // GROUP, GROUP, units, width),
        ],
        in_specs=in_vmem(len(inputs) - 6) + anywhere(6),
        out_specs=in_vmem(5),
        scratch_shapes=[
            pltpu.VMEM((length, width), BF16),
            pltpu.VMEM((length, WIDE), BF16),
            pltpu.VMEM(out_shape, BF16),
            pltpu.VMEM((2,) + moved.shape[1:], BF16),
            pltpu.VMEM((2,) + values.shape[1:], BF16),
            pltpu.VMEM((length, EXTRA), F32),
            dma((9,)),
        ]
        + [pltpu.VMEM((length, WIDE), F32)] * 5
        + [
            pltpu.VMEM((length, WIDE), BF16),
            pltpu.VMEM((OWN, length, BLOCK), F32),
            pltpu.VMEM((GROUP, length, WIDE), F32),
            pltpu.VMEM((1 if hops > 2 else GROUP, BLOCK if hops > 2 else length, WIDE), F32),
            pltpu.VMEM((hops + 1, length, WIDE), BF16),
            pltpu.VMEM((hops + 1, length, WIDE), BF16),
            dma((hops,)),
            dma((hops,)),
            dma((hops,)),
            dma((hops,)),
        ]
        + GroupSum.scratch(size, width)
        + GroupGather.scratch()
        + Scatter.scratch(groups, down.shape)
        + Scatter.scratch(groups, feed.shape)
        + LineSum.scratch(groups, out_shape),
        **communicating(2, "back", 60),
    )(*inputs)


def gather_kernel(
    groups, first_ref, gate_ref, up_ref, out_ref, down_ref, tokens_ref, cotangent_ref, full_ref, feed_full_ref, out_full_ref,
    down_low_ref, tokens_all_ref, cotangent_all_ref, feed_parts_ref, out_low_ref, send, recv, local, *sems
):
    lines = full_ref.shape[2]
    here = Place(groups, lines)
    here.meet()
    first_sems, feed_sems, out_sems = several(sems, 8, 3, 5)
    first = Gather(here, first_ref, full_ref, first_sems)
    feed = Gather(here, feed_parts_ref, feed_full_ref, feed_sems)
    out = HomeGather(here, out_low_ref, out_full_ref, out_sems)
    first.start()
    out_low_ref[...] = out_ref[...].astype(BF16)
    out.start()
    size = tokens_ref.shape[0]
    own = pl.ds(pl.multiple_of(here.m * size, size), size)
    copies = []
    for index, (source, target) in enumerate(((tokens_ref, tokens_all_ref), (cotangent_ref, cotangent_all_ref))):
        copies.append(pltpu.make_async_copy(source, target.at[own], local.at[index]))
        for offset in (2, 3, 1):
            copies.append(
                remote(source, target.at[own], send.at[index, offset], recv.at[index, offset], here.member(offset))
            )
    for copy in copies:
        copy.start()
    down_low_ref[...] = down_ref[...].astype(BF16)
    own_units = feed_parts_ref.shape[2] // 2
    for at, weight_ref in ((0, gate_ref), (own_units, up_ref)):
        if len(weight_ref.shape) == 3:
            feed_parts_ref[:, :, at : at + own_units] = weight_ref[...]
        else:
            for member in range(GROUP):
                for index in range(groups * lines):
                    block = (index // lines * GROUP + member) * lines + index % lines
                    feed_parts_ref[member, :, pl.ds(at + index * BLOCK, BLOCK)] = weight_ref[:, tile(block)].astype(BF16)
    feed.start()
    first.settle()
    first.spread()
    out.spread()
    for distance in range(1, groups):
        first.step(distance)
        out.step(distance)
    feed.settle()
    out.finish()
    for copy in copies:
        copy.wait()
    first.finish()


def gather_first(groups, lines, first, gate, up, out, down, tokens, cotangent):
    dma = pltpu.SemaphoreType.DMA
    size, width = tokens.shape
    rows = out.shape[0]
    units = 2 * down.shape[0] * groups * lines
    return pl.pallas_call(
        functools.partial(gather_kernel, groups),
        out_shape=[
            shape(BF16, groups, GROUP, lines, *first.shape[1:]),
            shape(BF16, groups, GROUP, lines, rows, units),
            shape(BF16, groups // GROUP, GROUP, lines, rows, width),
            shape(BF16, *down.shape),
            shape(BF16, GROUP * size, width),
            shape(BF16, GROUP * size, width),
        ],
        in_specs=anywhere(1) + in_vmem(4) + anywhere(2),
        out_specs=anywhere(3) + in_vmem(1) + anywhere(2),
        scratch_shapes=[
            pltpu.VMEM((GROUP, rows, units), BF16),
            pltpu.VMEM((rows, width), BF16),
            dma((2, GROUP)),
            dma((2, GROUP)),
            dma((2,)),
        ]
        + Gather.inside()
        + Gather.outside(groups)
        + Gather.inside()
        + HomeGather.scratch(groups),
        **communicating(0, "gather_first", 24),
    )(first, gate, up, out, down, tokens, cotangent)


def rms_norm(values, gain):
    return values * lax.rsqrt(jnp.mean(values * values, axis=-1, keepdims=True) + EPSILON) * gain


def rms_back(values, gain, grad):
    scale = lax.rsqrt(jnp.mean(values * values, axis=-1, keepdims=True) + EPSILON)
    straight = values * scale
    lifted = grad * gain
    return scale * (lifted - straight * jnp.mean(lifted * straight, axis=-1, keepdims=True))


def in_tiles(size, act, step=2 * BLOCK):
    def one(index, carry):
        act(pl.ds(pl.multiple_of(index * step, step), step))
        return carry

    lax.fori_loop(0, size // step, one, 0)


def branch_kernel(
    groups, partial_ref, tokens_ref, gain_ref, down_ref, feed_hbm, hidden_ref, normed_ref, active_ref, gate_slope_ref, up_slope_ref,
    down_full_ref, feed_ref, feed_sem, *refs
):
    here = Place(groups, down_full_ref.shape[1])
    here.meet()
    sum_refs, gather_refs, down_refs = several(refs, 7, 2, 8)
    total = GroupSum(here, partial_ref, sum_refs)
    whole = GroupGather(here, normed_ref, gather_refs)
    down = Gather(here, down_ref, down_full_ref, down_refs, mixed=False)
    pauses = Pauses(*[(functools.partial(down.step, distance),) for distance in range(1, groups)])
    total.start()
    down.start()
    down.settle()
    down.spread()
    feed_copy = pltpu.make_async_copy(feed_hbm, feed_ref, feed_sem.at[0])
    feed_copy.start()
    for chunk in range(CHUNKS):
        total.pass_on(chunk)
    pauses()
    for chunk in range(CHUNKS):
        hidden = tokens_ref[total.at(chunk), :].astype(F32) + total.take(chunk)
        hidden_ref[total.at(chunk), :] = hidden
        normed_ref[whole.at(chunk, here.m), :] = rms_norm(hidden, gain_ref[...]).astype(BF16)
        whole.give(chunk)
    pauses()
    for chunk in range(CHUNKS):
        whole.pass_on(chunk)
    pauses.rest()
    feed_copy.wait()
    whole.finish()
    units = active_ref.shape[1]

    def act(at):
        normed = normed_ref[...]
        gate = dot(normed, feed_ref[:, at])
        up = dot(normed, feed_ref[:, pl.ds(pl.multiple_of(at.start + units, BLOCK), at.size)])
        sigmoid = jax.nn.sigmoid(gate)
        silu = gate * sigmoid
        active_ref[:, at] = (silu * up).astype(BF16)
        gate_slope_ref[:, at] = up * (sigmoid * (1.0 + gate * (1.0 - sigmoid)))
        up_slope_ref[:, at] = silu

    in_tiles(units, act)
    total.finish()
    down.finish()


def branch(groups, lines, partial, tokens, gain, down, feed):
    size, width = tokens.shape
    length, units = partial.shape[0], feed.shape[1] // 2
    dma = pltpu.SemaphoreType.DMA
    return pl.pallas_call(
        functools.partial(branch_kernel, groups),
        out_shape=[
            shape(F32, size, width),
            shape(BF16, length, width),
            shape(BF16, length, units),
            shape(F32, length, units),
            shape(F32, length, units),
            shape(BF16, groups, lines, *down.shape),
        ],
        in_specs=in_vmem(3) + anywhere(2),
        out_specs=in_vmem(5) + anywhere(1),
        scratch_shapes=[pltpu.VMEM(feed.shape, BF16), dma((1,))]
        + GroupSum.scratch(size, width)
        + GroupGather.scratch()
        + Gather.inside()
        + Gather.outside(groups),
        **communicating(3, "branch", 48),
    )(partial, tokens, gain, down, feed)


def finish_kernel(
    groups, first_partial_ref, first_hbm, down_hbm, rows_grad_ref, active_ref, out_lines_ref, tokens_ref, hidden_ref, grad_ref, gain_ref,
    first_result_ref, out_result_ref, tokens_grad_ref, output_ref, first_full_ref, down_full_ref, normed_partial_ref,
    output_partial_ref, load_sem, *refs
):
    here = Place(groups, first_partial_ref.shape[2])
    here.meet(column=True)
    first_refs, out_refs, normed_refs, output_refs = several(
        refs, len(Scatter.scratch(groups, first_partial_ref.shape)), len(HomeScatter.scratch(groups, out_lines_ref.shape)), 7, 7
    )
    first = Scatter(here, first_partial_ref, first_result_ref, first_refs)
    out = HomeScatter(here, out_lines_ref, out_result_ref, out_refs)
    normed = GroupSum(here, normed_partial_ref, normed_refs)
    output = GroupSum(here, output_partial_ref, output_refs)
    first.start()
    first_copy = pltpu.make_async_copy(first_hbm, first_full_ref, load_sem.at[0])
    down_copy = pltpu.make_async_copy(down_hbm, down_full_ref, load_sem.at[1])
    first_copy.start()
    down_copy.start()
    out.start()
    first_copy.wait()

    def normed_tile(at):
        normed_partial_ref[:, at] = dot(rows_grad_ref[...], first_full_ref[at, :], NT).astype(BF16)

    in_tiles(normed_partial_ref.shape[1], normed_tile)
    normed.start()
    down_copy.wait()
    for chunk in range(CHUNKS):
        normed.pass_on(chunk)

    def output_tile(at):
        output_partial_ref[:, at] = dot(active_ref[...], down_full_ref[:, at]).astype(BF16)

    in_tiles(output_partial_ref.shape[1], output_tile)
    output.start()
    first.step(1)
    for chunk in range(CHUNKS):
        output.pass_on(chunk)
    for chunk in range(CHUNKS):
        back = rms_back(tokens_ref[normed.at(chunk), :].astype(F32), gain_ref[...], normed.take(chunk))
        tokens_grad_ref[normed.at(chunk), :] = (grad_ref[normed.at(chunk), :] + back).astype(BF16)
    if groups > 2:
        first.step(2)
    for chunk in range(CHUNKS):
        output_ref[output.at(chunk), :] = (hidden_ref[output.at(chunk), :] + output.take(chunk)).astype(BF16)
    for wave in range(3, groups):
        first.step(wave)
    out.last()
    normed.finish()
    output.finish()
    first.last()
    out.finish()
    first.finish()


def finish(groups, first_partial, first, down, rows_grad, active, out_lines, tokens, hidden, grad, gain):
    size, width = tokens.shape
    length = rows_grad.shape[0]
    return pl.pallas_call(
        functools.partial(finish_kernel, groups),
        out_shape=[
            shape(BF16, GROUP, *first_partial.shape[3:]),
            shape(BF16, *out_lines.shape[2:]),
            shape(BF16, size, width),
            shape(BF16, size, width),
        ],
        in_specs=anywhere(3) + in_vmem(7),
        out_specs=in_vmem(4),
        scratch_shapes=[
            pltpu.VMEM(first.shape, BF16),
            pltpu.VMEM(down.shape, BF16),
            pltpu.VMEM((length, width), BF16),
            pltpu.VMEM((length, width), BF16),
            pltpu.SemaphoreType.DMA((2,)),
        ]
        + Scatter.scratch(groups, first_partial.shape)
        + HomeScatter.scratch(groups, out_lines.shape)
        + GroupSum.scratch(size, width)
        + GroupSum.scratch(size, width),
        **communicating(5, "finish"),
    )(first_partial, first, down, rows_grad, active, out_lines, tokens, hidden, grad, gain)


def layout_kernel(groups, lines, first_ref, feed_ref, out_ref, beta_ref, gains_ref, *refs):
    weights, targets = refs[:6], refs[6:]
    query_out, key_out, value_out, house_out, out_out, norm_gain_out = targets[:6]
    rows = gains_ref.shape[0]
    first_sum = jnp.zeros((rows, WIDE), F32)
    extra_sum = jnp.zeros((rows, EXTRA), F32)
    for member in range(GROUP):
        for part, target_ref in enumerate((query_out, key_out, value_out, house_out)):
            value = first_ref[member, :, pl.ds(part * WIDE, WIDE)].astype(F32)
            at = pl.ds(member * WIDE, WIDE)
            target_ref[:, at] = value
            first_sum = first_sum + value * weights[part][:, at].astype(BF16).astype(F32)
        extra_sum = extra_sum + first_ref[member, :, pl.ds(4 * WIDE, EXTRA)].astype(F32) * beta_ref[member].astype(F32)
    total = jnp.sum(first_sum, axis=1, keepdims=True) + jnp.sum(extra_sum, axis=1, keepdims=True)
    norm_gain_out[...] = total / gains_ref[:, 0:1]
    out_out[...] = out_ref[...].astype(F32)
    if len(targets) > 6:
        gate_out, up_out, ffn_gain_out = targets[6:]
        units = feed_ref.shape[2] // 2
        feed_sum = jnp.zeros((rows, BLOCK), F32)
        for at, weight_ref, target_ref in ((0, weights[4], gate_out), (units, weights[5], up_out)):
            for member in range(GROUP):
                for index in range(groups * lines):
                    block = (index // lines * GROUP + member) * lines + index % lines
                    value = feed_ref[member, :, pl.ds(at + index * BLOCK, BLOCK)].astype(F32)
                    target_ref[:, tile(block)] = value
                    feed_sum = feed_sum + value * weight_ref[:, tile(block)].astype(BF16).astype(F32)
        ffn_gain_out[...] = jnp.sum(feed_sum, axis=1, keepdims=True) / gains_ref[:, 1:2]


def layout(groups, lines, whole_tiles, first, feed, out, beta, gains, weights):
    rows, width = out.shape
    outs = [shape(F32, rows, width)] * 5 + [shape(F32, rows, 1)]
    if whole_tiles:
        outs = outs + [shape(F32, *weights[4].shape)] * 2 + [shape(F32, rows, 1)]
    return pl.pallas_call(
        functools.partial(layout_kernel, groups, lines),
        out_shape=outs,
        in_specs=in_vmem(5 + len(weights)),
        out_specs=in_vmem(len(outs)),
        compiler_params=pltpu.CompilerParams(vmem_limit_bytes=32 << 20),
        name="layout",
    )(first, feed, out, beta, gains, *weights)


def on_device(
    tokens,
    doc_ids,
    norm_gain,
    query_weight,
    key_weight,
    value_weight,
    house_weight,
    beta_weight,
    out_weight,
    ffn_gain,
    gate_weight,
    up_weight,
    down_weight,
    cotangent,
):
    groups, batch = lax.axis_size("g"), lax.axis_size("b")
    devices = groups * GROUP * batch
    rows, width = query_weight.shape
    hidden_rows = down_weight.shape[0]
    hidden_own = gate_weight.shape[1] // GROUP
    block_rows = tokens.shape[1]
    hops = groups // 2
    doc_columns = -(-block_rows // rows)
    place, line = lax.axis_index("g"), lax.axis_index("b")

    def columns(weight):
        return jnp.transpose(weight.astype(BF16).reshape(rows, GROUP, -1), (1, 0, 2))

    docs = jnp.pad(doc_ids[0].astype(BF16), (0, rows * doc_columns - block_rows)).reshape(rows, doc_columns)
    same = jnp.concatenate([norm_gain.astype(BF16)[:, None], ffn_gain.astype(BF16)[:, None], docs], 1)
    same = jnp.broadcast_to(same[None], (GROUP,) + same.shape)
    same = jnp.pad(same, ((0, 0), (0, 0), (0, EXTRA - OWN - same.shape[2])))
    first_parts = jnp.concatenate(
        [columns(w) for w in (query_weight, key_weight, value_weight, house_weight, beta_weight)] + [same], 2
    )

    def unit_columns(weight):
        parts = weight.astype(BF16).reshape(rows, groups, GROUP, batch, hidden_rows)
        return jnp.transpose(parts, (2, 0, 1, 3, 4)).reshape(GROUP, rows, hidden_own)

    whole_tiles = hidden_rows == BLOCK
    feed_weights = (gate_weight, up_weight) if whole_tiles else (unit_columns(gate_weight), unit_columns(up_weight))
    first, feed, out_full, down_low, tokens_all, cotangent_all = gather_first(
        groups, batch, first_parts, *feed_weights, out_weight, down_weight, tokens[0], cotangent[0]
    )
    first = first.reshape(width, -1)

    extra = first[:, 4 * WIDE :]
    gain_one = extra[:, OWN].astype(F32)[None]
    gain_two = extra[:, OWN + 1].astype(F32)[None]
    docs = extra[:, OWN + 2 : OWN + 2 + doc_columns].astype(jnp.int32)
    docs = docs.reshape(devices, -1)[:, :block_rows].reshape(groups, GROUP, batch, block_rows)
    docs = lax.dynamic_index_in_dim(docs, line, 2, keepdims=False).reshape(groups, GROUP * block_rows)
    doc_key = jnp.stack(
        [
            jnp.where(place >= hop, lax.dynamic_index_in_dim(docs, jnp.maximum(place - hop, 0), 0, keepdims=False), -1)
            for hop in range(hops + 1)
        ]
    )[:, None, :]
    doc_query = lax.dynamic_index_in_dim(docs, place, 0, keepdims=False)[:, None]

    normed = rms_norm(tokens_all.astype(F32), gain_one).astype(BF16)
    projected = dot(normed, first)
    (query, value, within, maps, inverse, attended, attended_low, stats, moved, values, out_full, feed) = attend(
        groups, hops, projected, doc_query, doc_key, out_full, feed
    )
    out_full = out_full.reshape(WIDE, width)
    feed = feed.reshape(width, -1)
    hidden, normed_two, active, gate_slope, up_slope, down_full = branch(
        groups, batch, dot(attended_low, out_full).astype(BF16), tokens[0], gain_two, down_low, feed
    )
    down_full = down_full.reshape(hidden_own, width)
    active_grad = dot(cotangent_all, down_full, NT)
    feed_grads = jnp.concatenate([(active_grad * gate_slope).astype(BF16), (active_grad * up_slope).astype(BF16)], 1)
    down_partial = dot(active, cotangent_all, TN).astype(BF16).reshape(groups, 1, batch, hidden_rows, width)
    feed_partial = dot(normed_two, feed_grads, TN).astype(BF16).reshape(groups, GROUP, batch, rows, -1)
    hidden_grad, down_weight_grad, rows_grad, feed_grad, out_lines = back(
        groups, hops, dot(feed_grads, feed, NT).astype(BF16), hidden, cotangent[0], gain_two, attended_low, out_full, query, value,
        within, maps, doc_query, doc_key, attended, stats, values, moved, projected, inverse, down_partial, feed_partial,
    )
    first_partial = dot(normed, rows_grad, TN).astype(BF16).reshape(groups, GROUP, batch, rows, -1)
    beta_parts = jnp.pad(columns(beta_weight), ((0, 0), (0, 0), (0, EXTRA - OWN)))
    weights = (query_weight, key_weight, value_weight, house_weight) + feed_weights
    first_grad, out_grad, tokens_grad, output = finish(
        groups, first_partial, first, down_full, rows_grad, active, out_lines, tokens[0], hidden, hidden_grad, gain_one
    )
    gains = jnp.stack([norm_gain, ffn_gain], 1).astype(BF16).astype(F32)
    results = layout(groups, batch, whole_tiles, first_grad, feed_grad, out_grad, beta_parts, gains, weights)
    query_weight_grad, key_weight_grad, value_weight_grad, house_weight_grad, out_weight_grad, norm_gain_grad = results[:6]
    output, tokens_grad = output[None], tokens_grad[None]
    down_weight_grad = down_weight_grad[0]
    beta_weight_grad = jnp.transpose(first_grad[:, :, 4 * WIDE : 4 * WIDE + OWN].astype(F32), (1, 0, 2)).reshape(rows, -1)

    def unit_whole(parts):
        parts = parts.astype(F32).reshape(GROUP, rows, groups, batch, hidden_rows)
        return jnp.transpose(parts, (1, 2, 0, 3, 4)).reshape(rows, -1)

    if whole_tiles:
        gate_weight_grad, up_weight_grad, ffn_gain_grad = results[6:]
        ffn_gain_grad = ffn_gain_grad[:, 0]
    else:
        gate_weight_grad, up_weight_grad = unit_whole(feed_grad[:, :, :hidden_own]), unit_whole(feed_grad[:, :, hidden_own:])
        feed_sum = jnp.sum(gate_weight_grad * gate_weight.astype(BF16).astype(F32), axis=1) + jnp.sum(
            up_weight_grad * up_weight.astype(BF16).astype(F32), axis=1
        )
        ffn_gain_grad = feed_sum / gains[:, 1]
    return (
        output,
        tokens_grad,
        norm_gain_grad[:, 0],
        query_weight_grad,
        key_weight_grad,
        value_weight_grad,
        house_weight_grad,
        beta_weight_grad,
        out_weight_grad,
        ffn_gain_grad,
        gate_weight_grad,
        up_weight_grad,
        down_weight_grad,
    )


def solution(mesh):
    groups = mesh.shape["seq"] // GROUP
    inner = Mesh(mesh.devices.reshape(groups, GROUP, mesh.shape["batch"]), ("g", "m", "b"))
    line = P("b", ("g", "m"), None)
    vector = P(("g", "m", "b"))
    matrix = P(("g", "m", "b"), None)
    in_specs = (line, P("b", ("g", "m")), vector) + (matrix,) * 6 + (vector,) + (matrix,) * 3 + (line,)
    out_specs = (line, line, vector) + (matrix,) * 6 + (vector,) + (matrix,) * 3
    return jax.shard_map(on_device, mesh=inner, in_specs=in_specs, out_specs=out_specs, check_vma=False)
```

```python
import functools

import jax
import jax.numpy as jnp
from jax import lax
from jax.experimental import pallas as pl
from jax.experimental.pallas import tpu as pltpu
from jax.sharding import Mesh
from jax.sharding import PartitionSpec as P

HEADS = 12
HEAD_DIM = 128
GROUP = 4
OWN = HEADS // GROUP
WIDE = OWN * HEAD_DIM
BLOCK = 128
EXTRA = 128
EPSILON = 1e-06
NEGATIVE = -1e30
SCALE = HEAD_DIM ** (-0.5)
MESH = pl.DeviceIdType.MESH
F32 = jnp.float32
BF16 = jnp.bfloat16
NN = (((1,), (0,)), ((), ()))
NT = (((1,), (1,)), ((), ()))
TN = (((0,), (0,)), ((), ()))


def dot(left, right, dims=NN):
    return lax.dot_general(left, right, dims, preferred_element_type=F32)


def split(value):
    high = value.astype(BF16)
    return high, (value - high.astype(F32)).astype(BF16)


def dot3(left, right, dims=NN):
    left_high, left_low = split(left)
    right_high, right_low = split(right)
    return dot(left_high, right_high, dims) + (
        dot(left_high, right_low, dims) + dot(left_low, right_high, dims)
    )


def dot2(left, right, dims=NN):
    high, low = split(right)
    return dot(left, high, dims) + dot(left, low, dims)


def tile(index, count=1):
    return pl.ds(index * BLOCK, count * BLOCK)


def iota(axis, shape=(BLOCK, BLOCK)):
    return lax.broadcasted_iota(jnp.int32, shape, axis)


def invert(strict):
    row, col = iota(0), iota(1)
    eye = jnp.where(row == col, 1.0, 0.0)

    def part(size):
        return (row // (2 * size) == col // (2 * size)) & (row // size > col // size)

    totals = [eye - jnp.where(part(1), value, 0.0) for value in strict]
    size = 2
    while size < BLOCK:
        mask = part(size)
        pieces = [jnp.where(mask, value, 0.0) for value in strict]
        inner = [dot3(piece, total) for piece, total in zip(pieces, totals)]
        outer = [dot3(total, value) for total, value in zip(totals, inner)]
        totals = [total - value for total, value in zip(totals, outer)]
        size *= 2
    return totals


def unit_of(house):
    scale = lax.rsqrt(jnp.sum(house * house, axis=-1, keepdims=True) + EPSILON)
    return house * scale, scale


def products(query, key, unit):
    both = dot3(jnp.concatenate([unit, query], 0), jnp.concatenate([unit, key], 0), NT)
    return both[:BLOCK, :BLOCK], both[:BLOCK, BLOCK:], both[BLOCK:, :BLOCK], both[BLOCK:, BLOCK:]


def prepare_blocks(first, last, rows_ref, query_ref, key_ref, value_ref, within_ref, map_ref, inverse_ref):
    row, col = iota(0), iota(1)

    def one_block(block, carry):
        at = tile(block)
        kept, strict = [], []
        for head in range(OWN):
            query, key, value, house = [
                rows_ref[at, pl.ds(part * WIDE + head * BLOCK, BLOCK)] for part in range(4)
            ]
            rate = rows_ref[at, pl.ds(4 * WIDE, EXTRA)][:, head : head + 1]
            value_ref[at, tile(head)] = value.astype(BF16)
            unit, _ = unit_of(house)
            strength = 2.0 * jax.nn.sigmoid(rate)
            unit_unit, unit_key, query_unit, query_key = products(query, key, unit)
            strict.append(jnp.where(row > col, strength * unit_unit, 0.0))
            reach = jnp.where(row > col, strength * unit_key, 0.0)
            project = jnp.where(row >= col, query_unit, 0.0)
            kept.append((query, key, unit, strength, reach, project, query_key))
        inverses = invert(strict)
        for head in range(OWN):
            query, key, unit, strength, reach, project, query_key = kept[head]
            inverse = inverses[head]
            solved = dot3(inverse, jnp.concatenate([strength * unit, reach], 1))
            from_query = dot3(project, solved)
            from_unit = dot3(solved, unit, TN)
            query_ref[at, tile(head)] = (query - from_query[:, :BLOCK]).astype(BF16)
            within_ref[at, tile(head)] = query_key - from_query[:, BLOCK:]
            map_ref[at, tile(head)] = jnp.where(row == col, 1.0, 0.0) - from_unit[:BLOCK]
            key_ref[at, tile(head)] = (key - from_unit[BLOCK:]).astype(BF16)
            inverse_ref[at, tile(head)] = inverse
        return carry

    lax.fori_loop(first, last, one_block, 0)


def prepare_back_blocks(first, last, panels_ref, extra_ref, query_grad_ref, key_grad_ref, within_grad_ref, map_grad_ref, value_grad_ref, out_ref):
    row, col = iota(0), iota(1)

    def one_block(block, carry):
        at = tile(block)
        rates = jnp.zeros((BLOCK, EXTRA), F32)
        for head in range(OWN):
            query, key, house, inverse = [panels_ref[part, at, tile(head)] for part in range(4)]
            rate = extra_ref[at, :][:, head : head + 1]
            query_grad = query_grad_ref[at, tile(head)]
            key_grad = key_grad_ref[at, tile(head)]
            within_grad = within_grad_ref[at, tile(head)]
            map_grad = map_grad_ref[at, tile(head)]
            unit, scale = unit_of(house)
            strength = 2.0 * jax.nn.sigmoid(rate)
            unit_unit, unit_key, query_unit, query_key = products(query, key, unit)
            reach = jnp.where(row > col, strength * unit_key, 0.0)
            project = jnp.where(row >= col, query_unit, 0.0)
            solved = dot3(inverse, jnp.concatenate([strength * unit, reach], 1))
            both_grad = jnp.concatenate([query_grad, within_grad], 1)
            project_grad = jnp.where(row >= col, -dot3(both_grad, solved, NT), 0.0)
            solved_grad = -(
                dot3(project, both_grad, TN)
                + dot3(unit, jnp.concatenate([map_grad, key_grad], 0), NT)
            )
            given_grad = dot3(inverse, solved_grad, TN)
            strict_grad = jnp.where(row > col, -dot3(given_grad, solved, NT), 0.0)
            scaled_grad = given_grad[:, :BLOCK]
            reach_grad = jnp.where(row > col, given_grad[:, BLOCK:], 0.0)
            strength_grad = jnp.sum(
                scaled_grad * unit + reach_grad * unit_key + strict_grad * unit_unit, axis=1, keepdims=True
            )
            reach_part = strength * reach_grad
            inner_part = strength * strict_grad
            unit_grad = (
                strength * scaled_grad
                + dot3(reach_part, key)
                + dot3(inner_part + inner_part.T, unit)
                + dot3(project_grad, query, TN)
                - dot3(solved[:, :BLOCK], map_grad)
                - dot3(solved[:, BLOCK:], key_grad)
            )
            query_out = query_grad + dot3(within_grad, key) + dot3(project_grad, unit)
            key_out = key_grad + dot3(within_grad, query, TN) + dot3(reach_part, unit, TN)
            house_out = scale * (unit_grad - unit * jnp.sum(unit * unit_grad, axis=1, keepdims=True))
            rate_out = strength_grad * strength * (1.0 - 0.5 * strength)
            rates = jnp.where(iota(1, (BLOCK, EXTRA)) == head, rate_out, rates)
            out_ref[at, pl.ds(head * BLOCK, BLOCK)] = query_out.astype(BF16)
            out_ref[at, pl.ds(WIDE + head * BLOCK, BLOCK)] = key_out.astype(BF16)
            out_ref[at, pl.ds(2 * WIDE + head * BLOCK, BLOCK)] = value_grad_ref[at, tile(head)].astype(BF16)
            out_ref[at, pl.ds(3 * WIDE + head * BLOCK, BLOCK)] = house_out.astype(BF16)
        out_ref[at, pl.ds(4 * WIDE, EXTRA)] = rates.astype(BF16)
        return carry

    lax.fori_loop(first, last, one_block, 0)


def remote(source, target, send, recv, device):
    return pltpu.make_async_remote_copy(
        src_ref=source, dst_ref=target, send_sem=send, recv_sem=recv, device_id=device, device_id_type=MESH
    )


class Place:
    def __init__(self, groups, lines):
        self.groups, self.lines = groups, lines
        self.g, self.m, self.b = lax.axis_index("g"), lax.axis_index("m"), lax.axis_index("b")
        self.below, self.above = self.g > 0, self.g < groups - 1

    def other(self, offset):
        return {1: self.m + 1 - 2 * (self.m % 2), 2: (self.m + 2) % GROUP, 3: GROUP - 1 - self.m}[offset]

    def member(self, offset):
        return {"g": self.g, "m": self.other(offset), "b": self.b}

    def up(self):
        return {"g": self.g + 1, "m": self.m, "b": self.b}

    def down(self):
        return {"g": self.g - 1, "m": self.m, "b": self.b}

    def across(self):
        return {"g": self.g, "m": self.m, "b": 1 - self.b}

    def column(self, group):
        return {"g": group, "m": self.m, "b": self.b}

    def meet(self, column=False):
        barrier = pltpu.get_barrier_semaphore()

        def greet(device):
            pl.semaphore_signal(barrier, 1, device_id=device, device_id_type=MESH)

        for offset in range(1, GROUP):
            greet(self.member(offset))
        greet(self.across())
        if column:
            for step in range(1, self.groups):
                greet(self.column((self.g + step) % self.groups))
            count = GROUP + self.groups - 1
        else:
            pl.when(self.above)(lambda: greet(self.up()))
            pl.when(self.below)(lambda: greet(self.down()))
            count = GROUP + self.above.astype(jnp.int32) + self.below.astype(jnp.int32)
        pl.semaphore_wait(barrier, count)


class Gather:
    def __init__(self, place, parts, full, sems, mixed=True):
        self.place, self.parts, self.full, self.mixed = place, parts, full, mixed
        sems = list(sems)
        if parts is not None:
            self.part_send, self.part_recv, self.own_sem = sems[:3]
            sems = sems[3:]
        if sems:
            self.up_send, self.down_send, self.chain_recv, self.line_send, self.line_recv = sems

    @staticmethod
    def inside():
        dma = pltpu.SemaphoreType.DMA
        return [dma((GROUP,)), dma((GROUP,)), dma((1,))]

    @staticmethod
    def outside(groups):
        return [pltpu.SemaphoreType.DMA((groups,))] * 5

    def unit(self, group, line):
        return self.full.at[group, :, line] if self.mixed else self.full.at[group, line]

    def own(self):
        p = self.place
        if self.mixed:
            return pltpu.make_async_copy(self.parts.at[p.m], self.full.at[p.g, p.m, p.b], self.own_sem.at[0])
        return pltpu.make_async_copy(self.parts, self.full.at[p.g, p.b], self.own_sem.at[0])

    def part(self, offset):
        p = self.place
        other = p.other(offset)
        return remote(
            self.parts.at[other], self.full.at[p.g, p.m, p.b], self.part_send.at[offset], self.part_recv.at[offset], p.member(offset)
        )

    def start(self):
        if self.mixed:
            for offset in (2, 3, 1):
                self.part(offset).start()
        self.own().start()

    def chain(self, source, up):
        p = self.place
        unit = self.unit(source, p.b)
        sems = self.up_send if up else self.down_send
        return remote(unit, unit, sems.at[source], self.chain_recv.at[source], p.up() if up else p.down())

    def across(self, source):
        p = self.place
        unit = self.unit(source, p.b)
        return remote(unit, unit, self.line_send.at[source], self.line_recv.at[source], p.across())

    def settle(self):
        self.own().wait()
        if self.mixed:
            for offset in (2, 3, 1):
                self.part(offset).wait()

    def spread(self):
        p = self.place
        pl.when(p.above)(lambda: self.chain(p.g, True).start())
        pl.when(p.below)(lambda: self.chain(p.g, False).start())
        self.across(p.g).start()

    def step(self, distance):
        p = self.place

        @pl.when(p.g >= distance)
        def _():
            source = p.g - distance
            self.chain(source, True).wait_recv()
            pl.when(p.above)(lambda: self.chain(source, True).start())
            self.across(source).start()

        @pl.when(p.g + distance < p.groups)
        def _():
            source = p.g + distance
            self.chain(source, False).wait_recv()
            pl.when(p.below)(lambda: self.chain(source, False).start())
            self.across(source).start()

    def finish(self):
        p = self.place

        def settle(source, carry):
            self.across(source).wait()
            pl.when(p.above & (source <= p.g))(lambda: self.chain(source, True).wait_send())
            pl.when(p.below & (source >= p.g))(lambda: self.chain(source, False).wait_send())
            return carry

        lax.fori_loop(0, p.groups, settle, 0)


class HomeGather:
    def __init__(self, place, part, full, sems):
        self.place, self.part_ref, self.full = place, part, full
        self.home = place.groups // GROUP
        self.part_send, self.part_recv, self.up_send, self.down_send, self.chain_recv = sems

    @staticmethod
    def scratch(groups):
        dma = pltpu.SemaphoreType.DMA
        return [dma((1,)), dma((GROUP,))] + [dma((groups // GROUP,))] * 3

    def at_home(self):
        return self.place.m == self.place.g // self.home

    def slot(self):
        p = self.place
        return self.full.at[p.g % self.home, p.m, p.b]

    def hand(self):
        p = self.place
        keeper = p.g // self.home
        device = {"g": p.g, "m": keeper, "b": p.b}
        return remote(self.part_ref, self.slot(), self.part_send.at[0], self.part_recv.at[p.m], device)

    def taken(self, source):
        p = self.place
        target = self.full.at[p.g % self.home, source, p.b]
        return remote(self.part_ref, target, self.part_send.at[0], self.part_recv.at[source], p.member(1))

    def own(self):
        return pltpu.make_async_copy(self.part_ref, self.slot(), self.part_send.at[0])

    def start(self):
        pl.when(self.at_home())(lambda: self.own().start())
        pl.when(jnp.logical_not(self.at_home()))(lambda: self.hand().start())

    def chain(self, slot, up):
        p = self.place
        unit = self.full.at[slot, :, p.b]
        sems = self.up_send if up else self.down_send
        return remote(unit, unit, sems.at[slot], self.chain_recv.at[slot], p.up() if up else p.down())

    def spread(self):
        p = self.place

        @pl.when(self.at_home())
        def _():
            self.own().wait()
            for offset in range(1, GROUP):
                self.taken(p.other(offset)).wait_recv()
            slot = p.g % self.home
            pl.when(p.above)(lambda: self.chain(slot, True).start())
            pl.when(p.below)(lambda: self.chain(slot, False).start())

    def step(self, distance):
        p = self.place
        for slot in range(self.home):
            source = p.m * self.home + slot

            @pl.when(p.g - source == distance)
            def _():
                self.chain(slot, True).wait_recv()
                pl.when(p.above)(lambda: self.chain(slot, True).start())

            @pl.when(source - p.g == distance)
            def _():
                self.chain(slot, False).wait_recv()
                pl.when(p.below)(lambda: self.chain(slot, False).start())

    def finish(self):
        p = self.place
        pl.when(jnp.logical_not(self.at_home()))(lambda: self.hand().wait_send())
        for slot in range(self.home):
            source = p.m * self.home + slot
            pl.when(p.above & (p.g >= source))(lambda: self.chain(slot, True).wait_send())
            pl.when(p.below & (p.g <= source))(lambda: self.chain(slot, False).wait_send())


def home_lines(place, full, send, recv):
    copies = []
    for slot in range(place.groups // GROUP):
        unit = full.at[slot, :, place.b]
        copies.append(remote(unit, unit, send.at[slot], recv.at[slot], place.across()))
    return copies


class Scatter:
    def __init__(self, place, partial, result, refs, make=None):
        self.place, self.partial, self.result, self.make = place, partial, result, make
        (self.land, self.chain_land, self.leave, self.mine_sem, self.line_send, self.line_recv, self.chain_send,
         self.chain_recv, self.part_send, self.part_recv) = refs
        self.parts = partial.shape[1]

    @staticmethod
    def scratch(groups, shape):
        dma = pltpu.SemaphoreType.DMA
        unit = (shape[1],) + tuple(shape[3:])
        return [
            pltpu.VMEM((groups,) + unit, BF16),
            pltpu.VMEM((groups + 1,) + unit, BF16),
            pltpu.VMEM((groups,) + unit, BF16),
            dma((groups,)),
            dma((groups,)),
            dma((groups,)),
            dma((groups,)),
            dma((groups + 1,)),
            dma((GROUP,)),
            dma((GROUP,)),
        ]

    def load(self, target):
        return pltpu.make_async_copy(self.partial.at[target, :, self.place.b], self.leave.at[target], self.mine_sem.at[target])

    def line(self, target):
        p = self.place
        return remote(
            self.partial.at[target, :, 1 - p.b], self.land.at[target], self.line_send.at[target], self.line_recv.at[target], p.across()
        )

    def up(self, target):
        p = self.place
        return remote(
            self.leave.at[target], self.chain_land.at[target], self.chain_send.at[target], self.chain_recv.at[target], p.up()
        )

    def down(self, target, slot):
        p = self.place
        return remote(
            self.leave.at[target], self.chain_land.at[slot], self.chain_send.at[target], self.chain_recv.at[slot], p.down()
        )

    def send_up(self, target):
        self.up(target).start()

    def send_down(self, target):
        p = self.place
        pl.when(p.g - 1 == target)(lambda: self.down(target, p.groups).start())
        pl.when(p.g - 1 != target)(lambda: self.down(target, target).start())

    def arrived(self, slot):
        p = self.place
        return remote(self.leave.at[0], self.chain_land.at[slot], self.chain_send.at[0], self.chain_recv.at[slot], p.across())

    def wave(self, wave, act_up, act_down):
        p = self.place
        pl.when(wave > p.g)(lambda: act_up(p.groups - wave + p.g))
        pl.when(wave >= p.groups - p.g)(lambda: act_down(wave - p.groups + p.g))

    def act(self, target):
        if self.make is not None:
            self.make(target)
        self.line(target).start()
        self.load(target).start()

    def start(self):
        self.start_far()
        self.act(self.place.g)

    def start_far(self, first=1, last=None):
        p = self.place
        if self.make is None:
            for wave in range(first, p.groups if last is None else last + 1):
                self.wave(wave, self.act, self.act)
        else:

            def one(wave, carry):
                self.wave(wave, self.act, self.act)
                return carry

            lax.fori_loop(1, p.groups, one, 0)
        if first > 1:
            return

        @pl.when(jnp.logical_not(p.below))
        def _():
            self.chain_land[p.g] = jnp.zeros(self.chain_land.shape[1:], BF16)

        @pl.when(jnp.logical_not(p.above))
        def _():
            self.chain_land[p.groups] = jnp.zeros(self.chain_land.shape[1:], BF16)

    def both(self, target, part):
        return self.leave[target, part].astype(F32) + self.land[target, part].astype(F32)

    def step(self, wave):
        p = self.place

        def send(target, inner, copy):
            self.load(target).wait()
            self.line(target).wait_recv()

            @pl.when(inner)
            def _():
                self.arrived(target).wait_recv()
                for part in range(self.parts):
                    self.leave[target, part] = (self.both(target, part) + self.chain_land[target, part].astype(F32)).astype(BF16)

            @pl.when(jnp.logical_not(inner))
            def _():
                for part in range(self.parts):
                    self.leave[target, part] = self.both(target, part).astype(BF16)

            copy(target)

        self.wave(
            wave,
            lambda target: send(target, p.below, self.send_up),
            lambda target: send(target, p.above, self.send_down),
        )

    def hand(self, offset):
        p = self.place
        return remote(
            self.leave.at[p.g, p.other(offset)], self.result.at[p.m], self.part_send.at[offset], self.part_recv.at[offset], p.member(offset)
        )

    def last(self):
        p = self.place
        self.load(p.g).wait()
        self.line(p.g).wait_recv()
        pl.when(p.below)(lambda: self.arrived(p.g).wait_recv())
        pl.when(p.above)(lambda: self.arrived(p.groups).wait_recv())
        for part in range(self.parts):
            total = self.both(p.g, part) + self.chain_land[p.g, part].astype(F32) + self.chain_land[p.groups, part].astype(F32)
            if self.parts == 1:
                self.result[part] = total.astype(self.result.dtype)
            else:
                self.leave[p.g, part] = total.astype(BF16)
        if self.parts > 1:
            for offset in (2, 3, 1):
                self.hand(offset).start()
            self.result[p.m] = self.leave[p.g, p.m]

    def finish(self):
        p = self.place
        for target in range(p.groups):
            self.line(target).wait_send()
            pl.when(p.g != target)(lambda: self.up(target).wait_send())
        if self.parts > 1:
            for offset in (2, 3, 1):
                self.hand(offset).wait()


class LineSum:
    def __init__(self, place, partial, result, refs):
        self.place, self.partial, self.result = place, partial, result
        self.land, self.mine_sem, self.send, self.recv = refs

    @staticmethod
    def scratch(groups, shape):
        home = groups // GROUP
        return [pltpu.VMEM((home, GROUP) + tuple(shape[3:]), BF16)] + [pltpu.SemaphoreType.DMA((home,))] * 3

    def load(self, slot):
        return pltpu.make_async_copy(self.partial.at[slot, :, self.place.b], self.result.at[slot], self.mine_sem.at[slot])

    def line(self, slot):
        p = self.place
        return remote(self.partial.at[slot, :, 1 - p.b], self.land.at[slot], self.send.at[slot], self.recv.at[slot], p.across())

    def start(self):
        for slot in range(self.partial.shape[0]):
            self.line(slot).start()
            self.load(slot).start()

    def finish(self):
        for slot in range(self.partial.shape[0]):
            self.load(slot).wait()
            self.line(slot).wait()
            for part in range(GROUP):
                total = self.result[slot, part].astype(F32) + self.land[slot, part].astype(F32)
                self.result[slot, part] = total.astype(BF16)


class HomeScatter:
    def __init__(self, place, partial, result, refs):
        self.place, self.partial, self.result = place, partial, result
        self.home_land, self.leave, self.home_send, self.home_recv, self.part_send, self.part_recv = refs
        self.home = place.groups // GROUP

    @staticmethod
    def scratch(groups, shape):
        dma = pltpu.SemaphoreType.DMA
        unit = tuple(shape[1:])
        return [
            pltpu.VMEM((groups - 1,) + unit, BF16),
            pltpu.VMEM(unit, BF16),
            dma((shape[0],)),
            dma((groups - 1,)),
            dma((GROUP,)),
            dma((1,)),
        ]

    def home_copy(self, slot):
        p = self.place
        target = p.m * self.home + slot
        index = (p.g - target + p.groups - 1) % p.groups
        return remote(
            self.partial.at[slot], self.home_land.at[index], self.home_send.at[slot], self.home_recv.at[index], p.column(target)
        )

    def landed(self, index):
        p = self.place
        return remote(self.leave, self.home_land.at[index], self.home_send.at[0], self.home_recv.at[index], p.across())

    def start(self):
        p = self.place
        for slot in range(self.home):
            pl.when(p.g != p.m * self.home + slot)(lambda: self.home_copy(slot).start())

    def hand(self, other):
        p = self.place
        return remote(
            self.leave.at[other], self.result, self.part_send.at[other], self.part_recv.at[0], {"g": p.g, "m": other, "b": p.b}
        )

    def last(self):
        p = self.place

        @pl.when(p.m == p.g // self.home)
        def _():
            for index in range(p.groups - 1):
                self.landed(index).wait_recv()
            for part in range(GROUP):
                total = self.partial[p.g % self.home, part].astype(F32)
                for index in range(p.groups - 1):
                    total = total + self.home_land[index, part].astype(F32)
                self.leave[part] = total.astype(BF16)
            for offset in range(1, GROUP):
                self.hand(p.other(offset)).start()
            self.result[...] = self.leave[p.m]

    def finish(self):
        p = self.place
        keeper = p.m == p.g // self.home

        @pl.when(keeper)
        def _():
            for offset in range(1, GROUP):
                self.hand(p.other(offset)).wait_send()

        pl.when(jnp.logical_not(keeper))(lambda: self.hand(p.other(1)).wait_recv())
        for slot in range(self.home):
            pl.when(p.g != p.m * self.home + slot)(lambda: self.home_copy(slot).wait_send())


CHUNKS = 4


class GroupSum:
    def __init__(self, place, partial, refs):
        self.place, self.partial = place, partial
        self.pair_land, self.leave, self.land, self.pair_send, self.pair_recv, self.send, self.recv = refs
        self.size = partial.shape[0] // GROUP
        self.rows = self.size // CHUNKS

    @staticmethod
    def scratch(size, width):
        dma = pltpu.SemaphoreType.DMA
        return [
            pltpu.VMEM((2, size, width), BF16),
            pltpu.VMEM((size, width), BF16),
            pltpu.VMEM((size, width), BF16),
            dma((2, CHUNKS)),
            dma((2, CHUNKS)),
            dma((CHUNKS,)),
            dma((CHUNKS,)),
        ]

    def at(self, chunk, member=0):
        return pl.ds(pl.multiple_of(member * self.size + chunk * self.rows, self.rows), self.rows)

    def pair(self, chunk, far):
        p = self.place
        member = p.other(3 if far else 1)
        slot = 1 if far else 0
        return remote(
            self.partial.at[self.at(chunk, member)], self.pair_land.at[slot, self.at(chunk)], self.pair_send.at[slot, chunk],
            self.pair_recv.at[slot, chunk], p.member(1),
        )

    def cross(self, chunk):
        return remote(
            self.leave.at[self.at(chunk)], self.land.at[self.at(chunk)], self.send.at[chunk], self.recv.at[chunk], self.place.member(2)
        )

    def start(self):
        for chunk in range(CHUNKS):
            self.pair(chunk, True).start()
        for chunk in range(CHUNKS):
            self.pair(chunk, False).start()

    def pass_on(self, chunk):
        self.pair(chunk, True).wait_recv()
        own = self.partial[self.at(chunk, self.place.other(2)), :].astype(F32)
        self.leave[self.at(chunk), :] = (own + self.pair_land[1, self.at(chunk), :].astype(F32)).astype(BF16)
        self.cross(chunk).start()

    def take(self, chunk):
        self.pair(chunk, False).wait_recv()
        self.cross(chunk).wait_recv()
        own = self.partial[self.at(chunk, self.place.m), :].astype(F32)
        return own + self.pair_land[0, self.at(chunk), :].astype(F32) + self.land[self.at(chunk), :].astype(F32)

    def finish(self):
        for chunk in range(CHUNKS):
            self.pair(chunk, True).wait_send()
            self.pair(chunk, False).wait_send()
            self.cross(chunk).wait_send()


class GroupGather:
    def __init__(self, place, whole, refs):
        self.place, self.whole = place, whole
        self.send, self.recv = refs
        self.size = whole.shape[0] // GROUP
        self.rows = self.size // CHUNKS

    @staticmethod
    def scratch():
        dma = pltpu.SemaphoreType.DMA
        return [dma((3, CHUNKS)), dma((3, CHUNKS))]

    def at(self, chunk, member):
        return pl.ds(pl.multiple_of(member * self.size + chunk * self.rows, self.rows), self.rows)

    def copy(self, chunk, way):
        p = self.place
        rows = self.whole.at[self.at(chunk, p.other(2) if way == 2 else p.m)]
        return remote(rows, rows, self.send.at[way, chunk], self.recv.at[way, chunk], p.member(2 if way == 0 else 1))

    def give(self, chunk):
        self.copy(chunk, 0).start()
        self.copy(chunk, 1).start()

    def pass_on(self, chunk):
        self.copy(chunk, 0).wait_recv()
        self.copy(chunk, 2).start()

    def finish(self):
        for chunk in range(CHUNKS):
            self.copy(chunk, 1).wait_recv()
            self.copy(chunk, 2).wait_recv()
            for way in range(3):
                self.copy(chunk, way).wait_send()


def masked(scores, counts):
    return jnp.where(counts, scores * SCALE, NEGATIVE)


class Pauses:
    def __init__(self, *steps):
        self.steps = list(steps)

    def __call__(self):
        if self.steps:
            for act in self.steps.pop(0):
                act()

    def rest(self):
        while self.steps:
            self()


def several(refs, *counts):
    refs = list(refs)
    taken = []
    for count in counts:
        taken.append(refs[:count])
        refs = refs[count:]
    return taken


def attend_kernel(
    groups,
    hops,
    rows_ref,
    doc_query_ref,
    doc_key_ref,
    out_home_ref,
    feed_unit_ref,
    query_ref,
    value_ref,
    within_ref,
    map_ref,
    inverse_ref,
    attended_ref,
    low_ref,
    stats_ref,
    moved_ref,
    values_ref,
    out_full_ref,
    feed_full_ref,
    key_ref,
    leave_ref,
    top_ref,
    total_ref,
    accum_ref,
    key_send,
    key_recv,
    value_send,
    value_recv,
    *sems,
):
    here = Place(groups, feed_full_ref.shape[2])
    here.meet()
    place, has_next, following = here.g, here.above, here.up()
    home_sems, feed_sems = several(sems, 2, 5)
    out_copies = home_lines(here, out_full_ref, *home_sems)
    feed_gather = Gather(here, None, feed_full_ref, feed_sems)
    feed_gather.spread()
    for copy in out_copies:
        copy.start()
    pauses = Pauses(
        *[
            (functools.partial(feed_gather.step, distance),)
            for distance in range(1, groups)
        ]
    )
    prepared = (rows_ref, query_ref, key_ref, value_ref, within_ref, map_ref, inverse_ref)
    prepare_blocks(0, GROUP, *prepared)

    def value_copy(source, slot):
        return remote(source, values_ref.at[slot], value_send.at[slot], value_recv.at[slot], following)

    def key_copy(slot):
        return remote(leave_ref.at[slot], moved_ref.at[slot + 1, 0], key_send.at[slot], key_recv.at[slot], following)

    def move(keys, block, head):
        return dot2(keys, map_ref[tile(block), tile(head)]).astype(BF16)

    for head in range(OWN):
        keys = key_ref[tile(0), tile(head)]
        for block in range(1, GROUP):
            moved_ref[0, block, tile(0, block), tile(head)] = keys
            keys = jnp.concatenate([move(keys, block, head), key_ref[tile(block), tile(head)]], 0)
        leave_ref[0, :, tile(head)] = keys

    @pl.when(has_next)
    def _():
        key_copy(0).start()
        value_copy(value_ref, 0).start()

    pauses()

    def row_counts(block, hop, first, count):
        return doc_query_ref[tile(block), :] == doc_key_ref[hop, :, tile(first, count)]

    for block in range(GROUP):
        counts = row_counts(block, 0, 0, block + 1)
        wide = (BLOCK, (block + 1) * BLOCK)
        counts = counts & (iota(0, wide) + block * BLOCK >= iota(1, wide))
        for head in range(OWN):
            scores = within_ref[tile(block), tile(head)]
            if block:
                before = dot(query_ref[tile(block), tile(head)], moved_ref[0, block, tile(0, block), tile(head)], NT)
                scores = jnp.concatenate([before, scores], 1)
            scores = masked(scores, counts)
            top = jnp.max(scores, axis=1, keepdims=True)
            weights = jnp.exp(scores - top)
            top_ref[head, tile(block), :] = jnp.broadcast_to(top, (BLOCK, BLOCK))
            total_ref[head, tile(block), :] = jnp.broadcast_to(jnp.sum(weights, axis=1, keepdims=True), (BLOCK, BLOCK))
            accum_ref[tile(block), tile(head)] = dot(weights.astype(BF16), value_ref[tile(0, block + 1), tile(head)])

    def hop_step(hop, last):
        @pl.when(place >= hop)
        def _():
            key_copy(hop - 1).wait_recv()
            for head in range(OWN):
                keys = moved_ref[hop, 0, :, tile(head)]
                for block in range(GROUP):
                    if last:
                        if block == GROUP - 1:
                            break
                        keys = move(keys[BLOCK:], block, head)
                        moved_ref[hop, block + 1, tile(block + 1, GROUP - 1 - block), tile(head)] = keys
                    else:
                        keys = move(keys, block, head)
                        if block < GROUP - 1:
                            moved_ref[hop, block + 1, :, tile(head)] = keys
                        else:
                            leave_ref[hop, :, tile(head)] = keys
            value_copy(value_ref, hop - 1).wait_recv()
            if not last:

                @pl.when(has_next)
                def _():
                    key_copy(hop).start()
                    value_copy(values_ref.at[hop - 1], hop).start()

            for block in range(GROUP):
                first = block if last else 0
                count = GROUP - first
                counts = row_counts(block, hop, first, count)
                for head in range(OWN):
                    scores = masked(
                        dot(query_ref[tile(block), tile(head)], moved_ref[hop, block, tile(first, count), tile(head)], NT),
                        counts,
                    )
                    old = top_ref[head, tile(block), :]
                    top = jnp.maximum(old, jnp.broadcast_to(jnp.max(scores, axis=1, keepdims=True), (BLOCK, BLOCK)))
                    factor = jnp.exp(old - top)
                    weights = jnp.exp(scores - jnp.concatenate([top] * count, 1))
                    top_ref[head, tile(block), :] = top
                    total_ref[head, tile(block), :] = total_ref[head, tile(block), :] * factor + jnp.sum(
                        weights, axis=1, keepdims=True
                    )
                    accum_ref[tile(block), tile(head)] = accum_ref[tile(block), tile(head)] * factor + dot(
                        weights.astype(BF16), values_ref[hop - 1, tile(first, count), tile(head)]
                    )

    if hops > 2:

        def between(hop, carry):
            hop_step(hop, False)
            return carry

        lax.fori_loop(1, hops, between, 0)
    else:
        for hop in range(1, hops):
            pauses()
            hop_step(hop, False)
    pauses()
    hop_step(hops, True)

    for block in range(GROUP):
        stats = jnp.zeros((BLOCK, BLOCK), F32)
        for head in range(OWN):
            total = total_ref[head, tile(block), :]
            result = accum_ref[tile(block), tile(head)] / total
            attended_ref[tile(block), tile(head)] = result
            low_ref[tile(block), tile(head)] = result.astype(BF16)
            stats = jnp.where(iota(1) == head, top_ref[head, tile(block), :], stats)
            stats = jnp.where(iota(1) == OWN + head, total, stats)
        stats_ref[tile(block), :] = stats

    def settle(slot, carry):
        @pl.when(has_next & (place >= slot))
        def _():
            key_copy(slot).wait_send()
            value_copy(value_ref, slot).wait_send()

        return carry

    lax.fori_loop(0, hops, settle, 0)
    pauses.rest()
    for copy in out_copies:
        copy.wait()
    feed_gather.finish()


def in_vmem(count):
    return [pl.BlockSpec(memory_space=pltpu.VMEM)] * count


def anywhere(count):
    return [pl.BlockSpec(memory_space=pl.ANY)] * count


def shape(kind, *dims):
    return jax.ShapeDtypeStruct(dims, kind)


def communicating(number, name, vmem=58):
    return {
        "compiler_params": pltpu.CompilerParams(collective_id=number, has_side_effects=True, vmem_limit_bytes=vmem << 20),
        "name": name,
    }


def attend(groups, hops, projected, doc_query, doc_key, out_full, feed_full):
    length = projected.shape[0]
    dma = pltpu.SemaphoreType.DMA
    return pl.pallas_call(
        functools.partial(attend_kernel, groups, hops),
        out_shape=[
            shape(BF16, length, WIDE),
            shape(BF16, length, WIDE),
            shape(F32, length, WIDE),
            shape(F32, length, WIDE),
            shape(F32, length, WIDE),
            shape(F32, length, WIDE),
            shape(BF16, length, WIDE),
            shape(F32, length, BLOCK),
            shape(BF16, hops + 1, GROUP, length, WIDE),
            shape(BF16, hops, length, WIDE),
            shape(BF16, *out_full.shape),
            shape(BF16, *feed_full.shape),
        ],
        in_specs=in_vmem(3) + anywhere(2),
        out_specs=in_vmem(10) + anywhere(2),
        scratch_shapes=[
            pltpu.VMEM((length, WIDE), BF16),
            pltpu.VMEM((hops, length, WIDE), BF16),
            pltpu.VMEM((OWN, length, BLOCK), F32),
            pltpu.VMEM((OWN, length, BLOCK), F32),
            pltpu.VMEM((length, WIDE), F32),
            dma((hops,)),
            dma((hops,)),
            dma((hops,)),
            dma((hops,)),
        ]
        + [dma((groups // GROUP,))] * 2
        + Gather.outside(groups),
        input_output_aliases={3: 10, 4: 11},
        **communicating(1, "attend"),
    )(projected, doc_query, doc_key, out_full, feed_full)


def back_kernel(
    groups,
    hops,
    partial_ref,
    hidden_ref,
    cotangent_ref,
    gain_ref,
    low_ref,
    out_ref,
    query_ref,
    value_ref,
    within_ref,
    map_ref,
    doc_query_ref,
    doc_key_ref,
    attended_ref,
    stats_ref,
    values_hbm,
    moved_hbm,
    rows_hbm,
    inverse_hbm,
    down_partial_ref,
    feed_partial_ref,
    grad_ref,
    down_result_ref,
    rows_grad_ref,
    feed_result_ref,
    out_result_ref,
    grad_low_ref,
    att_grad_ref,
    out_partial_ref,
    moved_ref,
    values_ref,
    extra_ref,
    load_sem,
    query_grad_ref,
    key_grad_ref,
    within_grad_ref,
    map_grad_ref,
    value_grad_ref,
    scaled_ref,
    dots_ref,
    direct_ref,
    panels_ref,
    key_slots_ref,
    value_slots_ref,
    key_send,
    key_recv,
    value_send,
    value_recv,
    *refs,
):
    lines = feed_partial_ref.shape[2]
    here = Place(groups, lines)
    here.meet()
    place, has_next, previous = here.g, here.above, here.down()
    sum_refs, gather_refs, down_refs, feed_refs, out_refs = several(
        refs,
        7,
        2,
        len(Scatter.scratch(groups, down_partial_ref.shape)),
        len(Scatter.scratch(groups, feed_partial_ref.shape)),
        len(LineSum.scratch(groups, out_partial_ref.shape)),
    )
    sums = GroupSum(here, partial_ref, sum_refs)
    whole = GroupGather(here, grad_low_ref, gather_refs)
    down = Scatter(here, down_partial_ref, down_result_ref, down_refs)
    feed_scatter = Scatter(here, feed_partial_ref, feed_result_ref, feed_refs)
    out_lines = LineSum(here, out_partial_ref, out_result_ref, out_refs)
    pauses = Pauses(*[(functools.partial(feed_scatter.step, wave),) for wave in range(1, groups)])

    def load(hop):
        return pltpu.make_async_copy(moved_hbm.at[hop], moved_ref.at[hop % 2], load_sem.at[hop % 2])

    def load_values(hop):
        return pltpu.make_async_copy(values_hbm.at[hop - 1], values_ref.at[hop % 2], load_sem.at[2 + hop % 2])

    short = hops > 2
    loads = [pltpu.make_async_copy(rows_hbm.at[:, pl.ds(4 * WIDE, EXTRA)], extra_ref, load_sem.at[4])]
    panels = direct_ref if short else panels_ref
    for index, panel in enumerate((0, 1, 3)):
        loads.append(pltpu.make_async_copy(rows_hbm.at[:, pl.ds(panel * WIDE, WIDE)], panels.at[index], load_sem.at[5 + index]))
    loads.append(pltpu.make_async_copy(inverse_hbm, panels.at[3], load_sem.at[8]))
    sums.start()
    down.start()
    load(hops).start()
    load_values(hops).start()
    if not short:
        for copy in loads:
            copy.start()
    feed_scatter.start_far(1, 1)
    for chunk in range(CHUNKS):
        sums.pass_on(chunk)
    for chunk in range(CHUNKS):
        back = rms_back(hidden_ref[sums.at(chunk), :], gain_ref[...], sums.take(chunk))
        grad = cotangent_ref[sums.at(chunk), :].astype(F32) + back
        grad_ref[sums.at(chunk), :] = grad
        grad_low_ref[whole.at(chunk, here.m), :] = grad.astype(BF16)
        whole.give(chunk)
    down.step(1)
    for chunk in range(CHUNKS):
        whole.pass_on(chunk)
    if groups > 2:
        down.step(2)
    whole.finish()
    att_grad_ref[...] = dot(grad_low_ref[...], out_ref[...], NT).astype(BF16)
    turned = low_ref[...].T
    units = out_partial_ref.shape[3]

    def out_tile(at):
        value = dot(turned, grad_low_ref[:, at])
        for index in range(WIDE // units):
            slot, member, line = index // (GROUP * lines), index // lines % GROUP, index % lines
            out_partial_ref[slot, member, line, :, at] = value[index * units : (index + 1) * units].astype(BF16)

    in_tiles(out_partial_ref.shape[4], out_tile)
    out_lines.start()
    feed_scatter.start_far(2)
    feed_scatter.act(here.g)
    for wave in range(3, groups):
        down.step(wave)

    def key_copy(hop):
        slot = hop - 1
        return remote(key_slots_ref.at[hop], key_slots_ref.at[slot], key_send.at[slot], key_recv.at[slot], previous)

    def value_copy(hop):
        slot = hop - 1
        return remote(value_slots_ref.at[hop], value_slots_ref.at[slot], value_send.at[slot], value_recv.at[slot], previous)

    map_grad_ref[...] = jnp.zeros_like(map_grad_ref)
    query_grad_ref[...] = jnp.zeros_like(query_grad_ref)
    for block in range(GROUP):
        for head in range(OWN):
            at = (tile(block), tile(head))
            grad = att_grad_ref[at].astype(F32)
            total = stats_ref[tile(block), OWN + head : OWN + head + 1]
            scaled_ref[at] = (grad / total).astype(BF16)
            dots = -jnp.sum(grad * attended_ref[at], axis=1, keepdims=True) / total
            dots_ref[head, tile(block), :] = jnp.broadcast_to(dots, (BLOCK, BLOCK))

    def pair(block, head, scores, counts, values):
        count = scores.shape[1] // BLOCK
        top = stats_ref[tile(block), head : head + 1]
        weights = jnp.exp(masked(scores, counts) - top)
        weight_grad = dot(scaled_ref[tile(block), tile(head)], values, NT)
        dots = jnp.concatenate([dots_ref[head, tile(block), :]] * count, 1)
        return weights, weights * (weight_grad + dots) * SCALE

    def row_counts(block, hop, first, count):
        return doc_query_ref[tile(block), :] == doc_key_ref[hop, :, tile(first, count)]

    def hop_direct(hop, last):
        for head in range(OWN):
            value_grad_ref[:, tile(head)] = jnp.zeros((GROUP * BLOCK, BLOCK), F32)
        for block in range(GROUP):
            first = block if last else 0
            count = GROUP - first
            counts = row_counts(block, hop, first, count)
            for head in range(OWN):
                query = query_ref[tile(block), tile(head)]
                keys = moved_ref[hop % 2, block, tile(first, count), tile(head)]
                weights, grad = pair(
                    block, head, dot(query, keys, NT), counts, values_ref[hop % 2, tile(first, count), tile(head)]
                )
                raw = grad.astype(BF16)
                query_grad_ref[tile(block), tile(head)] += dot(raw, keys)
                direct_ref[block, tile(first, count), tile(head)] = dot(raw, query, TN)
                value_grad_ref[tile(first, count), tile(head)] += dot(
                    weights.astype(BF16), scaled_ref[tile(block), tile(head)], TN
                )

    def collect_map(block, head, keys, grads):
        map_grad_ref[tile(block), tile(head)] += dot2(keys, grads, TN)

    def hop_chain(hop, last):
        for head in range(OWN):
            if last:
                grads = direct_ref[GROUP - 1, tile(GROUP - 1), tile(head)]
                for block in range(GROUP - 2, -1, -1):
                    rows = tile(block + 1, GROUP - 1 - block)
                    collect_map(block, head, moved_ref[hop % 2, block, rows, tile(head)], grads)
                    back = dot3(grads, map_ref[tile(block), tile(head)], NT)
                    direct = direct_ref[block, tile(block, GROUP - block), tile(head)]
                    grads = jnp.concatenate([direct[:BLOCK], direct[BLOCK:] + back], 0)
                key_slots_ref[hop, :, tile(head)] = grads.astype(BF16)
                value_slots_ref[hop, :, tile(head)] = value_grad_ref[:, tile(head)].astype(BF16)
            else:
                grads = key_grad_ref[:, tile(head)]
                for block in range(GROUP - 1, -1, -1):
                    collect_map(block, head, moved_ref[hop % 2, block, :, tile(head)], grads)
                    grads = direct_ref[block, :, tile(head)] + dot3(grads, map_ref[tile(block), tile(head)], NT)
                key_slots_ref[hop, :, tile(head)] = grads.astype(BF16)

    def take(hop):
        @pl.when(has_next)
        def _():
            key_copy(hop).wait_recv()
            key_grad_ref[...] = key_slots_ref[hop - 1].astype(F32)

        @pl.when(jnp.logical_not(has_next))
        def _():
            key_grad_ref[...] = jnp.zeros_like(key_grad_ref)

    load(hops - 1).start()
    load_values(hops - 1).start()
    load(hops).wait()
    load_values(hops).wait()

    @pl.when(place >= hops)
    def _():
        hop_direct(hops, True)
        hop_chain(hops, True)
        key_copy(hops).start()
        value_copy(hops).start()

    down.last()

    def between(hop, pause=None):
        load(hop - 1).start()
        pl.when(jnp.asarray(hop) > 1)(lambda: load_values(hop - 1).start())
        load(hop).wait()
        load_values(hop).wait()
        pl.when(place >= hop)(lambda: hop_direct(hop, False))
        if pause is not None:
            pause()

        @pl.when(place >= hop)
        def _():
            take(hop + 1)
            hop_chain(hop, False)
            key_copy(hop).start()

            @pl.when(has_next)
            def _():
                value_copy(hop + 1).wait_recv()
                for head in range(OWN):
                    value_slots_ref[hop, :, tile(head)] = (
                        value_grad_ref[:, tile(head)] + value_slots_ref[hop, :, tile(head)].astype(F32)
                    ).astype(BF16)

            @pl.when(jnp.logical_not(has_next))
            def _():
                for head in range(OWN):
                    value_slots_ref[hop, :, tile(head)] = value_grad_ref[:, tile(head)].astype(BF16)

            value_copy(hop).start()

    if hops > 2:

        def step(counter, carry):
            between(hops - 1 - counter)
            return carry

        lax.fori_loop(0, hops - 1, step, 0)
    else:
        for hop in range(hops - 1, 0, -1):
            between(hop, pauses)

    load(0).wait()
    for head in range(OWN):
        value_grad_ref[:, tile(head)] = jnp.zeros((GROUP * BLOCK, BLOCK), F32)
    for block in range(GROUP):
        wide = (BLOCK, (block + 1) * BLOCK)
        counts = row_counts(block, 0, 0, block + 1) & (iota(0, wide) + block * BLOCK >= iota(1, wide))
        for head in range(OWN):
            query = query_ref[tile(block), tile(head)]
            scores = within_ref[tile(block), tile(head)]
            if block:
                keys = moved_ref[0, block, tile(0, block), tile(head)]
                scores = jnp.concatenate([dot(query, keys, NT), scores], 1)
            weights, grad = pair(block, head, scores, counts, value_ref[tile(0, block + 1), tile(head)])
            within_grad_ref[tile(block), tile(head)] = grad[:, block * BLOCK :]
            value_grad_ref[tile(0, block + 1), tile(head)] += dot(
                weights.astype(BF16), scaled_ref[tile(block), tile(head)], TN
            )
            if block:
                raw = grad[:, : block * BLOCK].astype(BF16)
                query_grad_ref[tile(block), tile(head)] += dot(raw, keys)
                direct_ref[block, tile(0, block), tile(head)] = dot(raw, query, TN)
    take(1)
    for head in range(OWN):
        grads = key_grad_ref[:, tile(head)]
        for block in range(GROUP - 1, 0, -1):
            key_grad_ref[tile(block), tile(head)] = grads[block * BLOCK :]
            grads = grads[: block * BLOCK]
            collect_map(block, head, moved_ref[0, block, tile(0, block), tile(head)], grads)
            grads = direct_ref[block, tile(0, block), tile(head)] + dot3(grads, map_ref[tile(block), tile(head)], NT)
        key_grad_ref[tile(0), tile(head)] = grads

    @pl.when(has_next)
    def _():
        value_copy(1).wait_recv()
        value_grad_ref[...] += value_slots_ref[0].astype(F32)

    def settle(hop, carry):
        @pl.when(place >= hop)
        def _():
            key_copy(hop).wait_send()
            value_copy(hop).wait_send()

        return carry

    lax.fori_loop(1, hops + 1, settle, 0)
    if short:
        for copy in loads:
            copy.start()
    for copy in loads:
        copy.wait()
    pauses()
    pieces = (panels, extra_ref, query_grad_ref, key_grad_ref, within_grad_ref, map_grad_ref, value_grad_ref, rows_grad_ref)
    prepare_back_blocks(0, GROUP // 2, *pieces)
    pauses.rest()
    prepare_back_blocks(GROUP // 2, GROUP, *pieces)
    out_lines.finish()
    feed_scatter.last()
    sums.finish()
    down.finish()
    feed_scatter.finish()


def back(groups, hops, partial, hidden, cotangent, gain, low, out, *args):
    values, moved, rows, inverse, down, feed = args[-6:]
    size, width = hidden.shape
    length = partial.shape[0]
    lines, units = feed.shape[2:4]
    out_shape = (groups // GROUP, GROUP, lines, units, width)
    dma = pltpu.SemaphoreType.DMA
    inputs = (partial, hidden, cotangent, gain, low, out) + args
    return pl.pallas_call(
        functools.partial(back_kernel, groups, hops),
        out_shape=[
            shape(F32, size, width),
            shape(F32, 1, *down.shape[3:]),
            shape(BF16, *rows.shape),
            shape(BF16, GROUP, *feed.shape[3:]),
            shape(BF16, groups // GROUP, GROUP, units, width),
        ],
        in_specs=in_vmem(len(inputs) - 6) + anywhere(6),
        out_specs=in_vmem(5),
        scratch_shapes=[
            pltpu.VMEM((length, width), BF16),
            pltpu.VMEM((length, WIDE), BF16),
            pltpu.VMEM(out_shape, BF16),
            pltpu.VMEM((2,) + moved.shape[1:], BF16),
            pltpu.VMEM((2,) + values.shape[1:], BF16),
            pltpu.VMEM((length, EXTRA), F32),
            dma((9,)),
        ]
        + [pltpu.VMEM((length, WIDE), F32)] * 5
        + [
            pltpu.VMEM((length, WIDE), BF16),
            pltpu.VMEM((OWN, length, BLOCK), F32),
            pltpu.VMEM((GROUP, length, WIDE), F32),
            pltpu.VMEM((1 if hops > 2 else GROUP, BLOCK if hops > 2 else length, WIDE), F32),
            pltpu.VMEM((hops + 1, length, WIDE), BF16),
            pltpu.VMEM((hops + 1, length, WIDE), BF16),
            dma((hops,)),
            dma((hops,)),
            dma((hops,)),
            dma((hops,)),
        ]
        + GroupSum.scratch(size, width)
        + GroupGather.scratch()
        + Scatter.scratch(groups, down.shape)
        + Scatter.scratch(groups, feed.shape)
        + LineSum.scratch(groups, out_shape),
        **communicating(2, "back", 60),
    )(*inputs)


def gather_kernel(
    groups, query_ref, key_ref, value_ref, house_ref, extra_ref, gate_hbm, up_hbm, out_hbm, down_hbm, tokens_ref, cotangent_ref,
    full_ref, feed_full_ref, out_full_ref, down_low_ref, tokens_all_ref, cotangent_all_ref, first_ref, feed_parts_ref, out_low_ref,
    gate_ref, up_ref, out_ref, down_ref, load_sem, send, recv, local, *sems
):
    lines = full_ref.shape[2]
    here = Place(groups, lines)
    loads = [
        pltpu.make_async_copy(source, target, load_sem.at[index])
        for index, (source, target) in enumerate(
            ((out_hbm, out_ref), (gate_hbm, gate_ref), (up_hbm, up_ref), (down_hbm, down_ref))
        )
    ]
    for copy in loads:
        copy.start()
    for member in range(GROUP):
        for part, weight_ref in enumerate((query_ref, key_ref, value_ref, house_ref)):
            first_ref[member, :, pl.ds(part * WIDE, WIDE)] = weight_ref[:, pl.ds(member * WIDE, WIDE)].astype(BF16)
        first_ref[member, :, pl.ds(4 * WIDE, EXTRA)] = extra_ref[member]
    here.meet()
    first_sems, feed_sems, out_sems = several(sems, 8, 3, 5)
    first = Gather(here, first_ref, full_ref, first_sems)
    feed = Gather(here, feed_parts_ref, feed_full_ref, feed_sems)
    out = HomeGather(here, out_low_ref, out_full_ref, out_sems)
    first.start()
    loads[0].wait()
    out_low_ref[...] = out_ref[...].astype(BF16)
    out.start()
    size = tokens_ref.shape[0]
    own = pl.ds(pl.multiple_of(here.m * size, size), size)
    copies = []
    for index, (source, target) in enumerate(((tokens_ref, tokens_all_ref), (cotangent_ref, cotangent_all_ref))):
        copies.append(pltpu.make_async_copy(source, target.at[own], local.at[index]))
        for offset in (2, 3, 1):
            copies.append(
                remote(source, target.at[own], send.at[index, offset], recv.at[index, offset], here.member(offset))
            )
    for copy in copies:
        copy.start()
    for copy in loads[1:]:
        copy.wait()
    down_low_ref[...] = down_ref[...].astype(BF16)
    own_units = feed_parts_ref.shape[2] // 2
    for at, weight_ref in ((0, gate_ref), (own_units, up_ref)):
        if len(weight_ref.shape) == 3:
            feed_parts_ref[:, :, at : at + own_units] = weight_ref[...]
        else:
            for member in range(GROUP):
                for index in range(groups * lines):
                    block = (index // lines * GROUP + member) * lines + index % lines
                    feed_parts_ref[member, :, pl.ds(at + index * BLOCK, BLOCK)] = weight_ref[:, tile(block)].astype(BF16)
    feed.start()
    first.settle()
    first.spread()
    out.spread()
    for distance in range(1, groups):
        first.step(distance)
        out.step(distance)
    feed.settle()
    out.finish()
    for copy in copies:
        copy.wait()
    first.finish()


def gather_first(groups, lines, first, extra, gate, up, out, down, tokens, cotangent):
    dma = pltpu.SemaphoreType.DMA
    size, width = tokens.shape
    rows = out.shape[0]
    units = 2 * down.shape[0] * groups * lines
    return pl.pallas_call(
        functools.partial(gather_kernel, groups),
        out_shape=[
            shape(BF16, groups, GROUP, lines, rows, 4 * WIDE + EXTRA),
            shape(BF16, groups, GROUP, lines, rows, units),
            shape(BF16, groups // GROUP, GROUP, lines, rows, width),
            shape(BF16, *down.shape),
            shape(BF16, GROUP * size, width),
            shape(BF16, GROUP * size, width),
        ],
        in_specs=in_vmem(5) + anywhere(6),
        out_specs=anywhere(3) + in_vmem(1) + anywhere(2),
        scratch_shapes=[
            pltpu.VMEM((GROUP, rows, 4 * WIDE + EXTRA), BF16),
            pltpu.VMEM((GROUP, rows, units), BF16),
            pltpu.VMEM((rows, width), BF16),
            pltpu.VMEM(gate.shape, gate.dtype),
            pltpu.VMEM(up.shape, up.dtype),
            pltpu.VMEM(out.shape, F32),
            pltpu.VMEM(down.shape, F32),
            dma((4,)),
            dma((2, GROUP)),
            dma((2, GROUP)),
            dma((2,)),
        ]
        + Gather.inside()
        + Gather.outside(groups)
        + Gather.inside()
        + HomeGather.scratch(groups),
        **communicating(0, "gather_first", 60),
    )(*first, extra, gate, up, out, down, tokens, cotangent)


def rms_norm(values, gain):
    return values * lax.rsqrt(jnp.mean(values * values, axis=-1, keepdims=True) + EPSILON) * gain


def rms_back(values, gain, grad):
    scale = lax.rsqrt(jnp.mean(values * values, axis=-1, keepdims=True) + EPSILON)
    straight = values * scale
    lifted = grad * gain
    return scale * (lifted - straight * jnp.mean(lifted * straight, axis=-1, keepdims=True))


def in_tiles(size, act, step=2 * BLOCK):
    def one(index, carry):
        act(pl.ds(pl.multiple_of(index * step, step), step))
        return carry

    lax.fori_loop(0, size // step, one, 0)


def branch_kernel(
    groups, partial_ref, tokens_ref, gain_ref, down_ref, feed_hbm, hidden_ref, normed_ref, active_ref, gate_slope_ref, up_slope_ref,
    down_full_ref, feed_ref, feed_sem, *refs
):
    here = Place(groups, down_full_ref.shape[1])
    here.meet()
    sum_refs, gather_refs, down_refs = several(refs, 7, 2, 8)
    total = GroupSum(here, partial_ref, sum_refs)
    whole = GroupGather(here, normed_ref, gather_refs)
    down = Gather(here, down_ref, down_full_ref, down_refs, mixed=False)
    pauses = Pauses(*[(functools.partial(down.step, distance),) for distance in range(1, groups)])
    total.start()
    down.start()
    down.settle()
    down.spread()
    feed_copy = pltpu.make_async_copy(feed_hbm, feed_ref, feed_sem.at[0])
    feed_copy.start()
    for chunk in range(CHUNKS):
        total.pass_on(chunk)
    pauses()
    for chunk in range(CHUNKS):
        hidden = tokens_ref[total.at(chunk), :].astype(F32) + total.take(chunk)
        hidden_ref[total.at(chunk), :] = hidden
        normed_ref[whole.at(chunk, here.m), :] = rms_norm(hidden, gain_ref[...]).astype(BF16)
        whole.give(chunk)
    pauses()
    for chunk in range(CHUNKS):
        whole.pass_on(chunk)
    pauses.rest()
    feed_copy.wait()
    whole.finish()
    units = active_ref.shape[1]

    def act(at):
        normed = normed_ref[...]
        gate = dot(normed, feed_ref[:, at])
        up = dot(normed, feed_ref[:, pl.ds(pl.multiple_of(at.start + units, BLOCK), at.size)])
        sigmoid = jax.nn.sigmoid(gate)
        silu = gate * sigmoid
        active_ref[:, at] = (silu * up).astype(BF16)
        gate_slope_ref[:, at] = up * (sigmoid * (1.0 + gate * (1.0 - sigmoid)))
        up_slope_ref[:, at] = silu

    in_tiles(units, act)
    total.finish()
    down.finish()


def branch(groups, lines, partial, tokens, gain, down, feed):
    size, width = tokens.shape
    length, units = partial.shape[0], feed.shape[1] // 2
    dma = pltpu.SemaphoreType.DMA
    return pl.pallas_call(
        functools.partial(branch_kernel, groups),
        out_shape=[
            shape(F32, size, width),
            shape(BF16, length, width),
            shape(BF16, length, units),
            shape(F32, length, units),
            shape(F32, length, units),
            shape(BF16, groups, lines, *down.shape),
        ],
        in_specs=in_vmem(3) + anywhere(2),
        out_specs=in_vmem(5) + anywhere(1),
        scratch_shapes=[pltpu.VMEM(feed.shape, BF16), dma((1,))]
        + GroupSum.scratch(size, width)
        + GroupGather.scratch()
        + Gather.inside()
        + Gather.outside(groups),
        **communicating(3, "branch", 48),
    )(partial, tokens, gain, down, feed)


def finish_kernel(
    groups, first_partial_ref, wide_hbm, first_hbm, down_hbm, rows_grad_ref, active_ref, out_lines_ref, tokens_ref, hidden_ref, grad_ref, gain_ref,
    first_result_ref, out_result_ref, tokens_grad_ref, output_ref, first_full_ref, down_full_ref, normed_partial_ref,
    output_partial_ref, wide_ref, normed_ref, made_ref, load_sem, *refs
):
    lines, rows = first_partial_ref.shape[2:4]
    here = Place(groups, lines)
    made = rows % 16 == 0
    if made:
        first_partial_ref = made_ref
    wide_copy = pltpu.make_async_copy(wide_hbm, wide_ref, load_sem.at[2])
    wide_copy.start()
    here.meet(column=True)

    def make(target):
        span = GROUP * lines * rows
        left = normed_ref[:, pl.ds(pl.multiple_of(target * span, BLOCK), span)].T
        for at, size in [(part * WIDE, WIDE) for part in range(4)] + [(4 * WIDE, EXTRA)]:
            value = dot(left, rows_grad_ref[:, pl.ds(at, size)])
            for index in range(GROUP * lines):
                made_ref[target, index // lines, index % lines, :, pl.ds(at, size)] = value[index * rows : (index + 1) * rows].astype(BF16)

    first_refs, out_refs, normed_refs, output_refs = several(
        refs, len(Scatter.scratch(groups, first_partial_ref.shape)), len(HomeScatter.scratch(groups, out_lines_ref.shape)), 7, 7
    )
    first = Scatter(here, first_partial_ref, first_result_ref, first_refs, make if made else None)
    out = HomeScatter(here, out_lines_ref, out_result_ref, out_refs)
    normed = GroupSum(here, normed_partial_ref, normed_refs)
    output = GroupSum(here, output_partial_ref, output_refs)
    first_copy = pltpu.make_async_copy(first_hbm, first_full_ref, load_sem.at[0])
    down_copy = pltpu.make_async_copy(down_hbm, down_full_ref, load_sem.at[1])
    first_copy.start()
    down_copy.start()
    wide_copy.wait()
    out.start()
    if made:
        for block in range(GROUP):
            normed_ref[tile(block), :] = rms_norm(wide_ref[tile(block), :].astype(F32), gain_ref[...]).astype(BF16)
    first.start()
    first_copy.wait()

    def normed_tile(at):
        normed_partial_ref[:, at] = dot(rows_grad_ref[...], first_full_ref[at, :], NT).astype(BF16)

    in_tiles(normed_partial_ref.shape[1], normed_tile)
    normed.start()
    down_copy.wait()
    for chunk in range(CHUNKS):
        normed.pass_on(chunk)

    def output_tile(at):
        output_partial_ref[:, at] = dot(active_ref[...], down_full_ref[:, at]).astype(BF16)

    in_tiles(output_partial_ref.shape[1], output_tile)
    output.start()
    first.step(1)
    for chunk in range(CHUNKS):
        output.pass_on(chunk)
    for chunk in range(CHUNKS):
        back = rms_back(tokens_ref[normed.at(chunk), :].astype(F32), gain_ref[...], normed.take(chunk))
        tokens_grad_ref[normed.at(chunk), :] = (grad_ref[normed.at(chunk), :] + back).astype(BF16)
    if groups > 2:
        first.step(2)
    for chunk in range(CHUNKS):
        output_ref[output.at(chunk), :] = (hidden_ref[output.at(chunk), :] + output.take(chunk)).astype(BF16)
    for wave in range(3, groups):
        first.step(wave)
    out.last()
    normed.finish()
    output.finish()
    first.last()
    out.finish()
    first.finish()


def finish(groups, first_partial, wide, first, down, rows_grad, active, out_lines, tokens, hidden, grad, gain):
    size, width = tokens.shape
    length = rows_grad.shape[0]
    made = first_partial.shape if first_partial.shape[3] % 16 == 0 else (1, 1, 1, 16, BLOCK)
    return pl.pallas_call(
        functools.partial(finish_kernel, groups),
        out_shape=[
            shape(BF16, GROUP, *first_partial.shape[3:]),
            shape(BF16, *out_lines.shape[2:]),
            shape(BF16, size, width),
            shape(BF16, size, width),
        ],
        in_specs=anywhere(4) + in_vmem(7),
        out_specs=in_vmem(4),
        scratch_shapes=[
            pltpu.VMEM(first.shape, BF16),
            pltpu.VMEM(down.shape, BF16),
            pltpu.VMEM((length, width), BF16),
            pltpu.VMEM((length, width), BF16),
            pltpu.VMEM(wide.shape, BF16),
            pltpu.VMEM(wide.shape, BF16),
            pltpu.VMEM(made, BF16),
            pltpu.SemaphoreType.DMA((3,)),
        ]
        + Scatter.scratch(groups, first_partial.shape)
        + HomeScatter.scratch(groups, out_lines.shape)
        + GroupSum.scratch(size, width)
        + GroupSum.scratch(size, width),
        **communicating(5, "finish"),
    )(first_partial, wide, first, down, rows_grad, active, out_lines, tokens, hidden, grad, gain)


def layout_kernel(groups, lines, first_ref, feed_ref, out_ref, beta_ref, gains_ref, down_ref, tokens_ref, result_ref, *refs):
    weights, targets = refs[:6], refs[6:]
    query_out, key_out, value_out, house_out, out_out, down_out, tokens_out, result_out, norm_gain_out, beta_out = targets[:10]
    rows = gains_ref.shape[1]
    down_out[...] = down_ref[0]
    tokens_out[...] = tokens_ref[...]
    result_out[...] = result_ref[...]

    def as_row(column):
        return jnp.broadcast_to(column, (rows, BLOCK)).T[0:1, :]

    first_sum = jnp.zeros((rows, WIDE), F32)
    extra_sum = jnp.zeros((rows, EXTRA), F32)
    for member in range(GROUP):
        for part, target_ref in enumerate((query_out, key_out, value_out, house_out)):
            value = first_ref[member, :, pl.ds(part * WIDE, WIDE)].astype(F32)
            at = pl.ds(member * WIDE, WIDE)
            target_ref[:, at] = value
            first_sum = first_sum + value * weights[part][:, at].astype(BF16).astype(F32)
        extra = first_ref[member, :, pl.ds(4 * WIDE, EXTRA)].astype(F32)
        extra_sum = extra_sum + extra * beta_ref[member].astype(F32)
        beta_out[member] = extra.T[0:OWN, :]
    total = jnp.sum(first_sum, axis=1, keepdims=True) + jnp.sum(extra_sum, axis=1, keepdims=True)
    norm_gain_out[...] = as_row(total) / gains_ref[0:1, :]
    out_out[...] = out_ref[...].astype(F32)
    if len(targets) > 10:
        gate_out, up_out, ffn_gain_out = targets[10:]
        units = feed_ref.shape[2] // 2
        feed_sum = jnp.zeros((rows, BLOCK), F32)
        for at, weight_ref, target_ref in ((0, weights[4], gate_out), (units, weights[5], up_out)):
            for member in range(GROUP):
                for index in range(groups * lines):
                    block = (index // lines * GROUP + member) * lines + index % lines
                    value = feed_ref[member, :, pl.ds(at + index * BLOCK, BLOCK)].astype(F32)
                    target_ref[:, tile(block)] = value
                    feed_sum = feed_sum + value * weight_ref[:, tile(block)].astype(BF16).astype(F32)
        ffn_gain_out[...] = as_row(jnp.sum(feed_sum, axis=1, keepdims=True)) / gains_ref[1:2, :]


def layout(groups, lines, whole_tiles, first, feed, out, beta, gains, down, tokens, result, weights):
    rows, width = out.shape
    outs = [shape(F32, rows, width)] * 5 + [
        shape(F32, *down.shape[1:]),
        shape(BF16, *tokens.shape),
        shape(BF16, *tokens.shape),
        shape(F32, 1, rows),
        shape(F32, GROUP, OWN, rows),
    ]
    if whole_tiles:
        outs = outs + [shape(F32, *weights[4].shape)] * 2 + [shape(F32, 1, rows)]
    return pl.pallas_call(
        functools.partial(layout_kernel, groups, lines),
        out_shape=outs,
        in_specs=in_vmem(8 + len(weights)),
        out_specs=in_vmem(len(outs)),
        compiler_params=pltpu.CompilerParams(vmem_limit_bytes=60 << 20),
        name="layout",
    )(first, feed, out, beta, gains, down, tokens, result, *weights)


def on_device(
    tokens,
    doc_ids,
    norm_gain,
    query_weight,
    key_weight,
    value_weight,
    house_weight,
    beta_weight,
    out_weight,
    ffn_gain,
    gate_weight,
    up_weight,
    down_weight,
    cotangent,
):
    groups, batch = lax.axis_size("g"), lax.axis_size("b")
    devices = groups * GROUP * batch
    rows, width = query_weight.shape
    hidden_rows = down_weight.shape[0]
    hidden_own = gate_weight.shape[1] // GROUP
    block_rows = tokens.shape[1]
    hops = groups // 2
    doc_columns = -(-block_rows // rows)
    place, line = lax.axis_index("g"), lax.axis_index("b")

    def columns(weight):
        return jnp.transpose(weight.astype(BF16).reshape(rows, GROUP, -1), (1, 0, 2))

    docs = jnp.pad(doc_ids[0].astype(BF16), (0, rows * doc_columns - block_rows)).reshape(rows, doc_columns)
    same = jnp.concatenate([norm_gain.astype(BF16)[:, None], ffn_gain.astype(BF16)[:, None], docs], 1)
    same = jnp.broadcast_to(same[None], (GROUP,) + same.shape)
    same = jnp.pad(same, ((0, 0), (0, 0), (0, EXTRA - OWN - same.shape[2])))
    extra = jnp.concatenate([columns(beta_weight), same], 2)

    def unit_columns(weight):
        parts = weight.astype(BF16).reshape(rows, groups, GROUP, batch, hidden_rows)
        return jnp.transpose(parts, (2, 0, 1, 3, 4)).reshape(GROUP, rows, hidden_own)

    whole_tiles = hidden_rows == BLOCK
    feed_weights = (gate_weight, up_weight) if whole_tiles else (unit_columns(gate_weight), unit_columns(up_weight))
    first, feed, out_full, down_low, tokens_all, cotangent_all = gather_first(
        groups, batch, (query_weight, key_weight, value_weight, house_weight), extra, *feed_weights, out_weight, down_weight, tokens[0], cotangent[0]
    )
    first = first.reshape(width, -1)

    extra = first[:, 4 * WIDE :]
    gain_one = extra[:, OWN].astype(F32)[None]
    gain_two = extra[:, OWN + 1].astype(F32)[None]
    docs = extra[:, OWN + 2 : OWN + 2 + doc_columns].astype(jnp.int32)
    docs = docs.reshape(devices, -1)[:, :block_rows].reshape(groups, GROUP, batch, block_rows)
    docs = lax.dynamic_index_in_dim(docs, line, 2, keepdims=False).reshape(groups, GROUP * block_rows)
    doc_key = jnp.stack(
        [
            jnp.where(place >= hop, lax.dynamic_index_in_dim(docs, jnp.maximum(place - hop, 0), 0, keepdims=False), -1)
            for hop in range(hops + 1)
        ]
    )[:, None, :]
    doc_query = lax.dynamic_index_in_dim(docs, place, 0, keepdims=False)[:, None]

    normed = rms_norm(tokens_all.astype(F32), gain_one).astype(BF16)
    projected = dot(normed, first)
    (query, value, within, maps, inverse, attended, attended_low, stats, moved, values, out_full, feed) = attend(
        groups, hops, projected, doc_query, doc_key, out_full, feed
    )
    out_full = out_full.reshape(WIDE, width)
    feed = feed.reshape(width, -1)
    hidden, normed_two, active, gate_slope, up_slope, down_full = branch(
        groups, batch, dot(attended_low, out_full).astype(BF16), tokens[0], gain_two, down_low, feed
    )
    down_full = down_full.reshape(hidden_own, width)
    active_grad = dot(cotangent_all, down_full, NT)
    feed_grads = jnp.concatenate([(active_grad * gate_slope).astype(BF16), (active_grad * up_slope).astype(BF16)], 1)
    down_partial = dot(active, cotangent_all, TN).astype(BF16).reshape(groups, 1, batch, hidden_rows, width)
    feed_partial = dot(normed_two, feed_grads, TN).astype(BF16).reshape(groups, GROUP, batch, rows, -1)
    hidden_grad, down_weight_grad, rows_grad, feed_grad, out_lines = back(
        groups, hops, dot(feed_grads, feed, NT).astype(BF16), hidden, cotangent[0], gain_two, attended_low, out_full, query, value,
        within, maps, doc_query, doc_key, attended, stats, values, moved, projected, inverse, down_partial, feed_partial,
    )
    partial_shape = (groups, GROUP, batch, rows, rows_grad.shape[1])
    if rows % 16 == 0:
        first_partial = first.reshape(partial_shape)
    else:
        first_partial = dot(normed, rows_grad, TN).astype(BF16).reshape(partial_shape)
    beta_parts = jnp.pad(columns(beta_weight), ((0, 0), (0, 0), (0, EXTRA - OWN)))
    weights = (query_weight, key_weight, value_weight, house_weight) + feed_weights
    first_grad, out_grad, tokens_grad, output = finish(
        groups, first_partial, tokens_all, first, down_full, rows_grad, active, out_lines, tokens[0], hidden, hidden_grad, gain_one
    )
    gains = jnp.stack([norm_gain, ffn_gain]).astype(BF16).astype(F32)
    results = layout(
        groups, batch, whole_tiles, first_grad, feed_grad, out_grad, beta_parts, gains, down_weight_grad, tokens_grad, output, weights
    )
    query_weight_grad, key_weight_grad, value_weight_grad, house_weight_grad, out_weight_grad, down_weight_grad = results[:6]
    tokens_grad, output, norm_gain_grad, beta_weight_grad = results[6:10]
    output, tokens_grad = output[None], tokens_grad[None]
    beta_weight_grad = beta_weight_grad.reshape(-1, rows).T
    def unit_whole(parts):
        parts = parts.astype(F32).reshape(GROUP, rows, groups, batch, hidden_rows)
        return jnp.transpose(parts, (1, 2, 0, 3, 4)).reshape(rows, -1)

    if whole_tiles:
        gate_weight_grad, up_weight_grad, ffn_gain_grad = results[10:]
        ffn_gain_grad = ffn_gain_grad[0]
    else:
        gate_weight_grad, up_weight_grad = unit_whole(feed_grad[:, :, :hidden_own]), unit_whole(feed_grad[:, :, hidden_own:])
        feed_sum = jnp.sum(gate_weight_grad * gate_weight.astype(BF16).astype(F32), axis=1) + jnp.sum(
            up_weight_grad * up_weight.astype(BF16).astype(F32), axis=1
        )
        ffn_gain_grad = feed_sum / gains[1]
    return (
        output,
        tokens_grad,
        norm_gain_grad[0],
        query_weight_grad,
        key_weight_grad,
        value_weight_grad,
        house_weight_grad,
        beta_weight_grad,
        out_weight_grad,
        ffn_gain_grad,
        gate_weight_grad,
        up_weight_grad,
        down_weight_grad,
    )


def solution(mesh):
    groups = mesh.shape["seq"] // GROUP
    inner = Mesh(mesh.devices.reshape(groups, GROUP, mesh.shape["batch"]), ("g", "m", "b"))
    line = P("b", ("g", "m"), None)
    vector = P(("g", "m", "b"))
    matrix = P(("g", "m", "b"), None)
    in_specs = (line, P("b", ("g", "m")), vector) + (matrix,) * 6 + (vector,) + (matrix,) * 3 + (line,)
    out_specs = (line, line, vector) + (matrix,) * 6 + (vector,) + (matrix,) * 3
    return jax.shard_map(on_device, mesh=inner, in_specs=in_specs, out_specs=out_specs, check_vma=False)
```

```python
import functools

import jax
import jax.numpy as jnp
from jax import lax
from jax.experimental import pallas as pl
from jax.experimental.pallas import tpu as pltpu
from jax.sharding import Mesh
from jax.sharding import PartitionSpec as P

HEADS = 12
HEAD_DIM = 128
GROUP = 4
OWN = HEADS // GROUP
WIDE = OWN * HEAD_DIM
BLOCK = 128
EXTRA = 128
EPSILON = 1e-06
NEGATIVE = -1e30
SCALE = HEAD_DIM ** (-0.5)
MESH = pl.DeviceIdType.MESH
F32 = jnp.float32
BF16 = jnp.bfloat16
NN = (((1,), (0,)), ((), ()))
NT = (((1,), (1,)), ((), ()))
TN = (((0,), (0,)), ((), ()))


def dot(left, right, dims=NN):
    return lax.dot_general(left, right, dims, preferred_element_type=F32)


def split(value):
    high = value.astype(BF16)
    return high, (value - high.astype(F32)).astype(BF16)


def dot3(left, right, dims=NN):
    left_high, left_low = split(left)
    right_high, right_low = split(right)
    return dot(left_high, right_high, dims) + (
        dot(left_high, right_low, dims) + dot(left_low, right_high, dims)
    )


def dot2(left, right, dims=NN):
    high, low = split(right)
    return dot(left, high, dims) + dot(left, low, dims)


def tile(index, count=1):
    return pl.ds(index * BLOCK, count * BLOCK)


def iota(axis, shape=(BLOCK, BLOCK)):
    return lax.broadcasted_iota(jnp.int32, shape, axis)


def invert(strict):
    row, col = iota(0), iota(1)
    eye = jnp.where(row == col, 1.0, 0.0)

    def part(size):
        return (row // (2 * size) == col // (2 * size)) & (row // size > col // size)

    totals = [eye - jnp.where(part(1), value, 0.0) for value in strict]
    size = 2
    while size < BLOCK:
        mask = part(size)
        pieces = [jnp.where(mask, value, 0.0) for value in strict]
        inner = [dot3(piece, total) for piece, total in zip(pieces, totals)]
        outer = [dot3(total, value) for total, value in zip(totals, inner)]
        totals = [total - value for total, value in zip(totals, outer)]
        size *= 2
    return totals


def unit_of(house):
    scale = lax.rsqrt(jnp.sum(house * house, axis=-1, keepdims=True) + EPSILON)
    return house * scale, scale


def products(query, key, unit):
    both = dot3(jnp.concatenate([unit, query], 0), jnp.concatenate([unit, key], 0), NT)
    return both[:BLOCK, :BLOCK], both[:BLOCK, BLOCK:], both[BLOCK:, :BLOCK], both[BLOCK:, BLOCK:]


def prepare_blocks(first, last, rows_ref, query_ref, key_ref, value_ref, within_ref, map_ref, inverse_ref):
    row, col = iota(0), iota(1)

    def one_block(block, carry):
        at = tile(block)
        kept, strict = [], []
        for head in range(OWN):
            query, key, value, house = [
                rows_ref[at, pl.ds(part * WIDE + head * BLOCK, BLOCK)] for part in range(4)
            ]
            rate = rows_ref[at, pl.ds(4 * WIDE, EXTRA)][:, head : head + 1]
            value_ref[at, tile(head)] = value.astype(BF16)
            unit, _ = unit_of(house)
            strength = 2.0 * jax.nn.sigmoid(rate)
            unit_unit, unit_key, query_unit, query_key = products(query, key, unit)
            strict.append(jnp.where(row > col, strength * unit_unit, 0.0))
            reach = jnp.where(row > col, strength * unit_key, 0.0)
            project = jnp.where(row >= col, query_unit, 0.0)
            kept.append((query, key, unit, strength, reach, project, query_key))
        inverses = invert(strict)
        for head in range(OWN):
            query, key, unit, strength, reach, project, query_key = kept[head]
            inverse = inverses[head]
            solved = dot3(inverse, jnp.concatenate([strength * unit, reach], 1))
            from_query = dot3(project, solved)
            from_unit = dot3(solved, unit, TN)
            query_ref[at, tile(head)] = (query - from_query[:, :BLOCK]).astype(BF16)
            within_ref[at, tile(head)] = query_key - from_query[:, BLOCK:]
            map_ref[at, tile(head)] = jnp.where(row == col, 1.0, 0.0) - from_unit[:BLOCK]
            key_ref[at, tile(head)] = (key - from_unit[BLOCK:]).astype(BF16)
            inverse_ref[at, tile(head)] = inverse
        return carry

    lax.fori_loop(first, last, one_block, 0)


def prepare_back_blocks(first, last, panels_ref, extra_ref, query_grad_ref, key_grad_ref, within_grad_ref, map_grad_ref, value_grad_ref, out_ref):
    row, col = iota(0), iota(1)

    def one_block(block, carry):
        at = tile(block)
        rates = jnp.zeros((BLOCK, EXTRA), F32)
        for head in range(OWN):
            query, key, house, inverse = [panels_ref[part, at, tile(head)] for part in range(4)]
            rate = extra_ref[at, :][:, head : head + 1]
            query_grad = query_grad_ref[at, tile(head)]
            key_grad = key_grad_ref[at, tile(head)]
            within_grad = within_grad_ref[at, tile(head)]
            map_grad = map_grad_ref[at, tile(head)]
            unit, scale = unit_of(house)
            strength = 2.0 * jax.nn.sigmoid(rate)
            unit_unit, unit_key, query_unit, query_key = products(query, key, unit)
            reach = jnp.where(row > col, strength * unit_key, 0.0)
            project = jnp.where(row >= col, query_unit, 0.0)
            solved = dot3(inverse, jnp.concatenate([strength * unit, reach], 1))
            both_grad = jnp.concatenate([query_grad, within_grad], 1)
            project_grad = jnp.where(row >= col, -dot3(both_grad, solved, NT), 0.0)
            solved_grad = -(
                dot3(project, both_grad, TN)
                + dot3(unit, jnp.concatenate([map_grad, key_grad], 0), NT)
            )
            given_grad = dot3(inverse, solved_grad, TN)
            strict_grad = jnp.where(row > col, -dot3(given_grad, solved, NT), 0.0)
            scaled_grad = given_grad[:, :BLOCK]
            reach_grad = jnp.where(row > col, given_grad[:, BLOCK:], 0.0)
            strength_grad = jnp.sum(
                scaled_grad * unit + reach_grad * unit_key + strict_grad * unit_unit, axis=1, keepdims=True
            )
            reach_part = strength * reach_grad
            inner_part = strength * strict_grad
            unit_grad = (
                strength * scaled_grad
                + dot3(reach_part, key)
                + dot3(inner_part + inner_part.T, unit)
                + dot3(project_grad, query, TN)
                - dot3(solved[:, :BLOCK], map_grad)
                - dot3(solved[:, BLOCK:], key_grad)
            )
            query_out = query_grad + dot3(within_grad, key) + dot3(project_grad, unit)
            key_out = key_grad + dot3(within_grad, query, TN) + dot3(reach_part, unit, TN)
            house_out = scale * (unit_grad - unit * jnp.sum(unit * unit_grad, axis=1, keepdims=True))
            rate_out = strength_grad * strength * (1.0 - 0.5 * strength)
            rates = jnp.where(iota(1, (BLOCK, EXTRA)) == head, rate_out, rates)
            out_ref[at, pl.ds(head * BLOCK, BLOCK)] = query_out.astype(BF16)
            out_ref[at, pl.ds(WIDE + head * BLOCK, BLOCK)] = key_out.astype(BF16)
            out_ref[at, pl.ds(2 * WIDE + head * BLOCK, BLOCK)] = value_grad_ref[at, tile(head)].astype(BF16)
            out_ref[at, pl.ds(3 * WIDE + head * BLOCK, BLOCK)] = house_out.astype(BF16)
        out_ref[at, pl.ds(4 * WIDE, EXTRA)] = rates.astype(BF16)
        return carry

    lax.fori_loop(first, last, one_block, 0)


def remote(source, target, send, recv, device):
    return pltpu.make_async_remote_copy(
        src_ref=source, dst_ref=target, send_sem=send, recv_sem=recv, device_id=device, device_id_type=MESH
    )


class Place:
    def __init__(self, groups, lines):
        self.groups, self.lines = groups, lines
        self.g, self.m, self.b = lax.axis_index("g"), lax.axis_index("m"), lax.axis_index("b")
        self.below, self.above = self.g > 0, self.g < groups - 1

    def other(self, offset):
        return {1: self.m + 1 - 2 * (self.m % 2), 2: (self.m + 2) % GROUP, 3: GROUP - 1 - self.m}[offset]

    def member(self, offset):
        return {"g": self.g, "m": self.other(offset), "b": self.b}

    def up(self):
        return {"g": self.g + 1, "m": self.m, "b": self.b}

    def down(self):
        return {"g": self.g - 1, "m": self.m, "b": self.b}

    def across(self):
        return {"g": self.g, "m": self.m, "b": 1 - self.b}

    def column(self, group):
        return {"g": group, "m": self.m, "b": self.b}

    def meet(self, column=False):
        barrier = pltpu.get_barrier_semaphore()

        def greet(device):
            pl.semaphore_signal(barrier, 1, device_id=device, device_id_type=MESH)

        for offset in range(1, GROUP):
            greet(self.member(offset))
        greet(self.across())
        if column:
            for step in range(1, self.groups):
                greet(self.column((self.g + step) % self.groups))
            count = GROUP + self.groups - 1
        else:
            pl.when(self.above)(lambda: greet(self.up()))
            pl.when(self.below)(lambda: greet(self.down()))
            count = GROUP + self.above.astype(jnp.int32) + self.below.astype(jnp.int32)
        pl.semaphore_wait(barrier, count)


class Gather:
    def __init__(self, place, parts, full, sems, mixed=True):
        self.place, self.parts, self.full, self.mixed = place, parts, full, mixed
        sems = list(sems)
        if parts is not None:
            self.part_send, self.part_recv, self.own_sem = sems[:3]
            sems = sems[3:]
        if sems:
            self.up_send, self.down_send, self.chain_recv, self.line_send, self.line_recv = sems

    @staticmethod
    def inside():
        dma = pltpu.SemaphoreType.DMA
        return [dma((GROUP,)), dma((GROUP,)), dma((1,))]

    @staticmethod
    def outside(groups):
        return [pltpu.SemaphoreType.DMA((groups,))] * 5

    def unit(self, group, line):
        return self.full.at[group, :, line] if self.mixed else self.full.at[group, line]

    def own(self):
        p = self.place
        if self.mixed:
            return pltpu.make_async_copy(self.parts.at[p.m], self.full.at[p.g, p.m, p.b], self.own_sem.at[0])
        return pltpu.make_async_copy(self.parts, self.full.at[p.g, p.b], self.own_sem.at[0])

    def part(self, offset):
        p = self.place
        other = p.other(offset)
        return remote(
            self.parts.at[other], self.full.at[p.g, p.m, p.b], self.part_send.at[offset], self.part_recv.at[offset], p.member(offset)
        )

    def start(self):
        if self.mixed:
            for offset in (2, 3, 1):
                self.part(offset).start()
        self.own().start()

    def chain(self, source, up):
        p = self.place
        unit = self.unit(source, p.b)
        sems = self.up_send if up else self.down_send
        return remote(unit, unit, sems.at[source], self.chain_recv.at[source], p.up() if up else p.down())

    def across(self, source):
        p = self.place
        unit = self.unit(source, p.b)
        return remote(unit, unit, self.line_send.at[source], self.line_recv.at[source], p.across())

    def settle(self):
        self.own().wait()
        if self.mixed:
            for offset in (2, 3, 1):
                self.part(offset).wait()

    def spread(self):
        p = self.place
        pl.when(p.above)(lambda: self.chain(p.g, True).start())
        pl.when(p.below)(lambda: self.chain(p.g, False).start())
        self.across(p.g).start()

    def step(self, distance):
        p = self.place

        @pl.when(p.g >= distance)
        def _():
            source = p.g - distance
            self.chain(source, True).wait_recv()
            pl.when(p.above)(lambda: self.chain(source, True).start())
            self.across(source).start()

        @pl.when(p.g + distance < p.groups)
        def _():
            source = p.g + distance
            self.chain(source, False).wait_recv()
            pl.when(p.below)(lambda: self.chain(source, False).start())
            self.across(source).start()

    def finish(self):
        p = self.place

        def settle(source, carry):
            self.across(source).wait()
            pl.when(p.above & (source <= p.g))(lambda: self.chain(source, True).wait_send())
            pl.when(p.below & (source >= p.g))(lambda: self.chain(source, False).wait_send())
            return carry

        lax.fori_loop(0, p.groups, settle, 0)


class HomeGather:
    def __init__(self, place, part, full, sems):
        self.place, self.part_ref, self.full = place, part, full
        self.home = place.groups // GROUP
        self.part_send, self.part_recv, self.up_send, self.down_send, self.chain_recv = sems

    @staticmethod
    def scratch(groups):
        dma = pltpu.SemaphoreType.DMA
        return [dma((1,)), dma((GROUP,))] + [dma((groups // GROUP,))] * 3

    def at_home(self):
        return self.place.m == self.place.g // self.home

    def slot(self):
        p = self.place
        return self.full.at[p.g % self.home, p.m, p.b]

    def hand(self):
        p = self.place
        keeper = p.g // self.home
        device = {"g": p.g, "m": keeper, "b": p.b}
        return remote(self.part_ref, self.slot(), self.part_send.at[0], self.part_recv.at[p.m], device)

    def taken(self, source):
        p = self.place
        target = self.full.at[p.g % self.home, source, p.b]
        return remote(self.part_ref, target, self.part_send.at[0], self.part_recv.at[source], p.member(1))

    def own(self):
        return pltpu.make_async_copy(self.part_ref, self.slot(), self.part_send.at[0])

    def start(self):
        pl.when(self.at_home())(lambda: self.own().start())
        pl.when(jnp.logical_not(self.at_home()))(lambda: self.hand().start())

    def chain(self, slot, up):
        p = self.place
        unit = self.full.at[slot, :, p.b]
        sems = self.up_send if up else self.down_send
        return remote(unit, unit, sems.at[slot], self.chain_recv.at[slot], p.up() if up else p.down())

    def spread(self):
        p = self.place

        @pl.when(self.at_home())
        def _():
            self.own().wait()
            for offset in range(1, GROUP):
                self.taken(p.other(offset)).wait_recv()
            slot = p.g % self.home
            pl.when(p.above)(lambda: self.chain(slot, True).start())
            pl.when(p.below)(lambda: self.chain(slot, False).start())

    def step(self, distance):
        p = self.place
        for slot in range(self.home):
            source = p.m * self.home + slot

            @pl.when(p.g - source == distance)
            def _():
                self.chain(slot, True).wait_recv()
                pl.when(p.above)(lambda: self.chain(slot, True).start())

            @pl.when(source - p.g == distance)
            def _():
                self.chain(slot, False).wait_recv()
                pl.when(p.below)(lambda: self.chain(slot, False).start())

    def finish(self):
        p = self.place
        pl.when(jnp.logical_not(self.at_home()))(lambda: self.hand().wait_send())
        for slot in range(self.home):
            source = p.m * self.home + slot
            pl.when(p.above & (p.g >= source))(lambda: self.chain(slot, True).wait_send())
            pl.when(p.below & (p.g <= source))(lambda: self.chain(slot, False).wait_send())


def home_lines(place, full, send, recv):
    copies = []
    for slot in range(place.groups // GROUP):
        unit = full.at[slot, :, place.b]
        copies.append(remote(unit, unit, send.at[slot], recv.at[slot], place.across()))
    return copies


class Scatter:
    def __init__(self, place, partial, result, refs, make=None):
        self.place, self.partial, self.result, self.make = place, partial, result, make
        (self.land, self.chain_land, self.leave, self.mine_sem, self.line_send, self.line_recv, self.chain_send,
         self.chain_recv, self.part_send, self.part_recv) = refs
        self.parts = partial.shape[1]

    @staticmethod
    def scratch(groups, shape):
        dma = pltpu.SemaphoreType.DMA
        unit = (shape[1],) + tuple(shape[3:])
        return [
            pltpu.VMEM((groups,) + unit, BF16),
            pltpu.VMEM((groups + 1,) + unit, BF16),
            pltpu.VMEM((groups,) + unit, BF16),
            dma((groups,)),
            dma((groups,)),
            dma((groups,)),
            dma((groups,)),
            dma((groups + 1,)),
            dma((GROUP,)),
            dma((GROUP,)),
        ]

    def load(self, target):
        return pltpu.make_async_copy(self.partial.at[target, :, self.place.b], self.leave.at[target], self.mine_sem.at[target])

    def line(self, target):
        p = self.place
        return remote(
            self.partial.at[target, :, 1 - p.b], self.land.at[target], self.line_send.at[target], self.line_recv.at[target], p.across()
        )

    def up(self, target):
        p = self.place
        return remote(
            self.leave.at[target], self.chain_land.at[target], self.chain_send.at[target], self.chain_recv.at[target], p.up()
        )

    def down(self, target, slot):
        p = self.place
        return remote(
            self.leave.at[target], self.chain_land.at[slot], self.chain_send.at[target], self.chain_recv.at[slot], p.down()
        )

    def send_up(self, target):
        self.up(target).start()

    def send_down(self, target):
        p = self.place
        pl.when(p.g - 1 == target)(lambda: self.down(target, p.groups).start())
        pl.when(p.g - 1 != target)(lambda: self.down(target, target).start())

    def arrived(self, slot):
        p = self.place
        return remote(self.leave.at[0], self.chain_land.at[slot], self.chain_send.at[0], self.chain_recv.at[slot], p.across())

    def wave(self, wave, act_up, act_down):
        p = self.place
        pl.when(wave > p.g)(lambda: act_up(p.groups - wave + p.g))
        pl.when(wave >= p.groups - p.g)(lambda: act_down(wave - p.groups + p.g))

    def act(self, target):
        if self.make is not None:
            self.make(target)
        self.line(target).start()
        self.load(target).start()

    def start(self):
        self.start_far()
        self.act(self.place.g)

    def start_far(self, first=1, last=None):
        p = self.place
        if self.make is None:
            for wave in range(first, p.groups if last is None else last + 1):
                self.wave(wave, self.act, self.act)
        else:

            def one(wave, carry):
                self.wave(wave, self.act, self.act)
                return carry

            lax.fori_loop(first, p.groups if last is None else last + 1, one, 0)
        if first > 1:
            return

        @pl.when(jnp.logical_not(p.below))
        def _():
            self.chain_land[p.g] = jnp.zeros(self.chain_land.shape[1:], BF16)

        @pl.when(jnp.logical_not(p.above))
        def _():
            self.chain_land[p.groups] = jnp.zeros(self.chain_land.shape[1:], BF16)

    def both(self, target, part):
        return self.leave[target, part].astype(F32) + self.land[target, part].astype(F32)

    def step(self, wave):
        p = self.place

        def send(target, inner, copy):
            self.load(target).wait()
            self.line(target).wait_recv()

            @pl.when(inner)
            def _():
                self.arrived(target).wait_recv()
                for part in range(self.parts):
                    self.leave[target, part] = (self.both(target, part) + self.chain_land[target, part].astype(F32)).astype(BF16)

            @pl.when(jnp.logical_not(inner))
            def _():
                for part in range(self.parts):
                    self.leave[target, part] = self.both(target, part).astype(BF16)

            copy(target)

        self.wave(
            wave,
            lambda target: send(target, p.below, self.send_up),
            lambda target: send(target, p.above, self.send_down),
        )

    def hand(self, offset):
        p = self.place
        return remote(
            self.leave.at[p.g, p.other(offset)], self.result.at[p.m], self.part_send.at[offset], self.part_recv.at[offset], p.member(offset)
        )

    def last(self):
        p = self.place
        self.load(p.g).wait()
        self.line(p.g).wait_recv()
        pl.when(p.below)(lambda: self.arrived(p.g).wait_recv())
        pl.when(p.above)(lambda: self.arrived(p.groups).wait_recv())
        for part in range(self.parts):
            total = self.both(p.g, part) + self.chain_land[p.g, part].astype(F32) + self.chain_land[p.groups, part].astype(F32)
            if self.parts == 1:
                self.result[part] = total.astype(self.result.dtype)
            else:
                self.leave[p.g, part] = total.astype(BF16)
        if self.parts > 1:
            for offset in (2, 3, 1):
                self.hand(offset).start()
            self.result[p.m] = self.leave[p.g, p.m]

    def finish(self):
        p = self.place
        for target in range(p.groups):
            self.line(target).wait_send()
            pl.when(p.g != target)(lambda: self.up(target).wait_send())
        if self.parts > 1:
            for offset in (2, 3, 1):
                self.hand(offset).wait()


class LineSum:
    def __init__(self, place, partial, result, refs):
        self.place, self.partial, self.result = place, partial, result
        self.land, self.mine_sem, self.send, self.recv = refs

    @staticmethod
    def scratch(groups, shape):
        home = groups // GROUP
        return [pltpu.VMEM((home, GROUP) + tuple(shape[3:]), BF16)] + [pltpu.SemaphoreType.DMA((home,))] * 3

    def load(self, slot):
        return pltpu.make_async_copy(self.partial.at[slot, :, self.place.b], self.result.at[slot], self.mine_sem.at[slot])

    def line(self, slot):
        p = self.place
        return remote(self.partial.at[slot, :, 1 - p.b], self.land.at[slot], self.send.at[slot], self.recv.at[slot], p.across())

    def start(self):
        for slot in range(self.partial.shape[0]):
            self.line(slot).start()
            self.load(slot).start()

    def finish(self):
        for slot in range(self.partial.shape[0]):
            self.load(slot).wait()
            self.line(slot).wait()
            for part in range(GROUP):
                total = self.result[slot, part].astype(F32) + self.land[slot, part].astype(F32)
                self.result[slot, part] = total.astype(BF16)


class HomeScatter:
    def __init__(self, place, partial, result, refs):
        self.place, self.partial, self.result = place, partial, result
        self.home_land, self.leave, self.home_send, self.home_recv, self.part_send, self.part_recv = refs
        self.home = place.groups // GROUP

    @staticmethod
    def scratch(groups, shape):
        dma = pltpu.SemaphoreType.DMA
        unit = tuple(shape[1:])
        return [
            pltpu.VMEM((groups - 1,) + unit, BF16),
            pltpu.VMEM(unit, BF16),
            dma((shape[0],)),
            dma((groups - 1,)),
            dma((GROUP,)),
            dma((1,)),
        ]

    def home_copy(self, slot):
        p = self.place
        target = p.m * self.home + slot
        index = (p.g - target + p.groups - 1) % p.groups
        return remote(
            self.partial.at[slot], self.home_land.at[index], self.home_send.at[slot], self.home_recv.at[index], p.column(target)
        )

    def landed(self, index):
        p = self.place
        return remote(self.leave, self.home_land.at[index], self.home_send.at[0], self.home_recv.at[index], p.across())

    def start(self):
        p = self.place
        for slot in range(self.home):
            pl.when(p.g != p.m * self.home + slot)(lambda: self.home_copy(slot).start())

    def hand(self, other):
        p = self.place
        return remote(
            self.leave.at[other], self.result, self.part_send.at[other], self.part_recv.at[0], {"g": p.g, "m": other, "b": p.b}
        )

    def last(self):
        p = self.place

        @pl.when(p.m == p.g // self.home)
        def _():
            for index in range(p.groups - 1):
                self.landed(index).wait_recv()
            for part in range(GROUP):
                total = self.partial[p.g % self.home, part].astype(F32)
                for index in range(p.groups - 1):
                    total = total + self.home_land[index, part].astype(F32)
                self.leave[part] = total.astype(BF16)
            for offset in range(1, GROUP):
                self.hand(p.other(offset)).start()
            self.result[...] = self.leave[p.m]

    def finish(self):
        p = self.place
        keeper = p.m == p.g // self.home

        @pl.when(keeper)
        def _():
            for offset in range(1, GROUP):
                self.hand(p.other(offset)).wait_send()

        pl.when(jnp.logical_not(keeper))(lambda: self.hand(p.other(1)).wait_recv())
        for slot in range(self.home):
            pl.when(p.g != p.m * self.home + slot)(lambda: self.home_copy(slot).wait_send())


CHUNKS = 4


class GroupSum:
    def __init__(self, place, partial, refs):
        self.place, self.partial = place, partial
        self.pair_land, self.leave, self.land, self.pair_send, self.pair_recv, self.send, self.recv = refs
        self.size = partial.shape[0] // GROUP
        self.rows = self.size // CHUNKS

    @staticmethod
    def scratch(size, width):
        dma = pltpu.SemaphoreType.DMA
        return [
            pltpu.VMEM((2, size, width), BF16),
            pltpu.VMEM((size, width), BF16),
            pltpu.VMEM((size, width), BF16),
            dma((2, CHUNKS)),
            dma((2, CHUNKS)),
            dma((CHUNKS,)),
            dma((CHUNKS,)),
        ]

    def at(self, chunk, member=0):
        return pl.ds(pl.multiple_of(member * self.size + chunk * self.rows, self.rows), self.rows)

    def pair(self, chunk, far):
        p = self.place
        member = p.other(3 if far else 1)
        slot = 1 if far else 0
        return remote(
            self.partial.at[self.at(chunk, member)], self.pair_land.at[slot, self.at(chunk)], self.pair_send.at[slot, chunk],
            self.pair_recv.at[slot, chunk], p.member(1),
        )

    def cross(self, chunk):
        return remote(
            self.leave.at[self.at(chunk)], self.land.at[self.at(chunk)], self.send.at[chunk], self.recv.at[chunk], self.place.member(2)
        )

    def start(self):
        for chunk in range(CHUNKS):
            self.pair(chunk, True).start()
        for chunk in range(CHUNKS):
            self.pair(chunk, False).start()

    def pass_on(self, chunk):
        self.pair(chunk, True).wait_recv()
        own = self.partial[self.at(chunk, self.place.other(2)), :].astype(F32)
        self.leave[self.at(chunk), :] = (own + self.pair_land[1, self.at(chunk), :].astype(F32)).astype(BF16)
        self.cross(chunk).start()

    def take(self, chunk):
        self.pair(chunk, False).wait_recv()
        self.cross(chunk).wait_recv()
        own = self.partial[self.at(chunk, self.place.m), :].astype(F32)
        return own + self.pair_land[0, self.at(chunk), :].astype(F32) + self.land[self.at(chunk), :].astype(F32)

    def finish(self):
        for chunk in range(CHUNKS):
            self.pair(chunk, True).wait_send()
            self.pair(chunk, False).wait_send()
            self.cross(chunk).wait_send()


class GroupGather:
    def __init__(self, place, whole, refs):
        self.place, self.whole = place, whole
        self.send, self.recv = refs
        self.size = whole.shape[0] // GROUP
        self.rows = self.size // CHUNKS

    @staticmethod
    def scratch():
        dma = pltpu.SemaphoreType.DMA
        return [dma((3, CHUNKS)), dma((3, CHUNKS))]

    def at(self, chunk, member):
        return pl.ds(pl.multiple_of(member * self.size + chunk * self.rows, self.rows), self.rows)

    def copy(self, chunk, way):
        p = self.place
        rows = self.whole.at[self.at(chunk, p.other(2) if way == 2 else p.m)]
        return remote(rows, rows, self.send.at[way, chunk], self.recv.at[way, chunk], p.member(2 if way == 0 else 1))

    def give(self, chunk):
        self.copy(chunk, 0).start()
        self.copy(chunk, 1).start()

    def pass_on(self, chunk):
        self.copy(chunk, 0).wait_recv()
        self.copy(chunk, 2).start()

    def finish(self):
        for chunk in range(CHUNKS):
            self.copy(chunk, 1).wait_recv()
            self.copy(chunk, 2).wait_recv()
            for way in range(3):
                self.copy(chunk, way).wait_send()


def masked(scores, counts):
    return jnp.where(counts, scores * SCALE, NEGATIVE)


class Pauses:
    def __init__(self, *steps):
        self.steps = list(steps)

    def __call__(self):
        if self.steps:
            for act in self.steps.pop(0):
                act()

    def rest(self):
        while self.steps:
            self()


def several(refs, *counts):
    refs = list(refs)
    taken = []
    for count in counts:
        taken.append(refs[:count])
        refs = refs[count:]
    return taken


def attend_kernel(
    groups,
    hops,
    tokens_hbm,
    first_hbm,
    gain_ref,
    doc_query_ref,
    doc_key_ref,
    out_home_ref,
    feed_unit_ref,
    rows_ref,
    query_ref,
    value_ref,
    within_ref,
    map_ref,
    inverse_ref,
    attended_ref,
    low_ref,
    stats_ref,
    moved_ref,
    values_ref,
    out_full_ref,
    feed_full_ref,
    tokens_ref,
    first_ref,
    normed_ref,
    load_sem,
    key_ref,
    leave_ref,
    top_ref,
    total_ref,
    accum_ref,
    key_send,
    key_recv,
    value_send,
    value_recv,
    *sems,
):
    here = Place(groups, feed_full_ref.shape[2])
    tokens_load = pltpu.make_async_copy(tokens_hbm, tokens_ref, load_sem.at[0])
    first_load = pltpu.make_async_copy(first_hbm, first_ref, load_sem.at[1])
    tokens_load.start()
    first_load.start()
    here.meet()
    place, has_next, following = here.g, here.above, here.up()
    home_sems, feed_sems = several(sems, 2, 5)
    out_copies = home_lines(here, out_full_ref, *home_sems)
    feed_gather = Gather(here, None, feed_full_ref, feed_sems)
    feed_gather.spread()
    for copy in out_copies:
        copy.start()
    pauses = Pauses(
        *[
            (functools.partial(feed_gather.step, distance),)
            for distance in range(1, groups)
        ]
    )
    prepared = (rows_ref, query_ref, key_ref, value_ref, within_ref, map_ref, inverse_ref)
    tokens_load.wait()
    for block in range(GROUP):
        normed_ref[tile(block), :] = rms_norm(tokens_ref[tile(block), :].astype(F32), gain_ref[...]).astype(BF16)
    first_load.wait()
    for at, size in [(part * WIDE, WIDE) for part in range(4)] + [(4 * WIDE, EXTRA)]:
        rows_ref[:, pl.ds(at, size)] = dot(normed_ref[...], first_ref[:, pl.ds(at, size)])
    prepare_blocks(0, GROUP // 2, *prepared)
    pauses()
    prepare_blocks(GROUP // 2, GROUP, *prepared)

    def value_copy(source, slot):
        return remote(source, values_ref.at[slot], value_send.at[slot], value_recv.at[slot], following)

    def key_copy(slot):
        return remote(leave_ref.at[slot], moved_ref.at[slot + 1, 0], key_send.at[slot], key_recv.at[slot], following)

    def move(keys, block, head):
        return dot2(keys, map_ref[tile(block), tile(head)]).astype(BF16)

    for head in range(OWN):
        keys = key_ref[tile(0), tile(head)]
        for block in range(1, GROUP):
            moved_ref[0, block, tile(0, block), tile(head)] = keys
            keys = jnp.concatenate([move(keys, block, head), key_ref[tile(block), tile(head)]], 0)
        leave_ref[0, :, tile(head)] = keys

    @pl.when(has_next)
    def _():
        key_copy(0).start()
        value_copy(value_ref, 0).start()


    def row_counts(block, hop, first, count):
        return doc_query_ref[tile(block), :] == doc_key_ref[hop, :, tile(first, count)]

    for block in range(GROUP):
        counts = row_counts(block, 0, 0, block + 1)
        wide = (BLOCK, (block + 1) * BLOCK)
        counts = counts & (iota(0, wide) + block * BLOCK >= iota(1, wide))
        for head in range(OWN):
            scores = within_ref[tile(block), tile(head)]
            if block:
                before = dot(query_ref[tile(block), tile(head)], moved_ref[0, block, tile(0, block), tile(head)], NT)
                scores = jnp.concatenate([before, scores], 1)
            scores = masked(scores, counts)
            top = jnp.max(scores, axis=1, keepdims=True)
            weights = jnp.exp(scores - top)
            top_ref[head, tile(block), :] = jnp.broadcast_to(top, (BLOCK, BLOCK))
            total_ref[head, tile(block), :] = jnp.broadcast_to(jnp.sum(weights, axis=1, keepdims=True), (BLOCK, BLOCK))
            accum_ref[tile(block), tile(head)] = dot(weights.astype(BF16), value_ref[tile(0, block + 1), tile(head)])

    def hop_step(hop, last):
        @pl.when(place >= hop)
        def _():
            key_copy(hop - 1).wait_recv()
            for head in range(OWN):
                keys = moved_ref[hop, 0, :, tile(head)]
                for block in range(GROUP):
                    if last:
                        if block == GROUP - 1:
                            break
                        keys = move(keys[BLOCK:], block, head)
                        moved_ref[hop, block + 1, tile(block + 1, GROUP - 1 - block), tile(head)] = keys
                    else:
                        keys = move(keys, block, head)
                        if block < GROUP - 1:
                            moved_ref[hop, block + 1, :, tile(head)] = keys
                        else:
                            leave_ref[hop, :, tile(head)] = keys
            value_copy(value_ref, hop - 1).wait_recv()
            if not last:

                @pl.when(has_next)
                def _():
                    key_copy(hop).start()
                    value_copy(values_ref.at[hop - 1], hop).start()

            for block in range(GROUP):
                first = block if last else 0
                count = GROUP - first
                counts = row_counts(block, hop, first, count)
                for head in range(OWN):
                    scores = masked(
                        dot(query_ref[tile(block), tile(head)], moved_ref[hop, block, tile(first, count), tile(head)], NT),
                        counts,
                    )
                    old = top_ref[head, tile(block), :]
                    top = jnp.maximum(old, jnp.broadcast_to(jnp.max(scores, axis=1, keepdims=True), (BLOCK, BLOCK)))
                    factor = jnp.exp(old - top)
                    weights = jnp.exp(scores - jnp.concatenate([top] * count, 1))
                    top_ref[head, tile(block), :] = top
                    total_ref[head, tile(block), :] = total_ref[head, tile(block), :] * factor + jnp.sum(
                        weights, axis=1, keepdims=True
                    )
                    accum_ref[tile(block), tile(head)] = accum_ref[tile(block), tile(head)] * factor + dot(
                        weights.astype(BF16), values_ref[hop - 1, tile(first, count), tile(head)]
                    )

    if hops > 2:

        def between(hop, carry):
            hop_step(hop, False)
            return carry

        lax.fori_loop(1, hops, between, 0)
    else:
        for hop in range(1, hops):
            pauses()
            hop_step(hop, False)
    pauses()
    hop_step(hops, True)

    for block in range(GROUP):
        stats = jnp.zeros((BLOCK, BLOCK), F32)
        for head in range(OWN):
            total = total_ref[head, tile(block), :]
            result = accum_ref[tile(block), tile(head)] / total
            attended_ref[tile(block), tile(head)] = result
            low_ref[tile(block), tile(head)] = result.astype(BF16)
            stats = jnp.where(iota(1) == head, top_ref[head, tile(block), :], stats)
            stats = jnp.where(iota(1) == OWN + head, total, stats)
        stats_ref[tile(block), :] = stats

    def settle(slot, carry):
        @pl.when(has_next & (place >= slot))
        def _():
            key_copy(slot).wait_send()
            value_copy(value_ref, slot).wait_send()

        return carry

    lax.fori_loop(0, hops, settle, 0)
    pauses.rest()
    for copy in out_copies:
        copy.wait()
    feed_gather.finish()


def in_vmem(count):
    return [pl.BlockSpec(memory_space=pltpu.VMEM)] * count


def anywhere(count):
    return [pl.BlockSpec(memory_space=pl.ANY)] * count


def shape(kind, *dims):
    return jax.ShapeDtypeStruct(dims, kind)


def communicating(number, name, vmem=58):
    return {
        "compiler_params": pltpu.CompilerParams(collective_id=number, has_side_effects=True, vmem_limit_bytes=vmem << 20),
        "name": name,
    }


def attend(groups, hops, tokens, first, gain, doc_query, doc_key, out_full, feed_full):
    length = tokens.shape[0]
    dma = pltpu.SemaphoreType.DMA
    return pl.pallas_call(
        functools.partial(attend_kernel, groups, hops),
        out_shape=[
            shape(F32, length, first.shape[1]),
            shape(BF16, length, WIDE),
            shape(BF16, length, WIDE),
            shape(F32, length, WIDE),
            shape(F32, length, WIDE),
            shape(F32, length, WIDE),
            shape(F32, length, WIDE),
            shape(BF16, length, WIDE),
            shape(F32, length, BLOCK),
            shape(BF16, hops + 1, GROUP, length, WIDE),
            shape(BF16, hops, length, WIDE),
            shape(BF16, *out_full.shape),
            shape(BF16, *feed_full.shape),
        ],
        in_specs=anywhere(2) + in_vmem(3) + anywhere(2),
        out_specs=in_vmem(11) + anywhere(2),
        scratch_shapes=[
            pltpu.VMEM(tokens.shape, BF16),
            pltpu.VMEM(first.shape, BF16),
            pltpu.VMEM(tokens.shape, BF16),
            dma((2,)),
            pltpu.VMEM((length, WIDE), BF16),
            pltpu.VMEM((hops, length, WIDE), BF16),
            pltpu.VMEM((OWN, length, BLOCK), F32),
            pltpu.VMEM((OWN, length, BLOCK), F32),
            pltpu.VMEM((length, WIDE), F32),
            dma((hops,)),
            dma((hops,)),
            dma((hops,)),
            dma((hops,)),
        ]
        + [dma((groups // GROUP,))] * 2
        + Gather.outside(groups),
        input_output_aliases={5: 11, 6: 12},
        **communicating(1, "attend"),
    )(tokens, first, gain, doc_query, doc_key, out_full, feed_full)


def made_feed(groups, rows):
    return groups == GROUP and rows % 16 == 0


def back_kernel(
    groups,
    hops,
    partial_ref,
    hidden_ref,
    cotangent_ref,
    gain_ref,
    low_ref,
    out_ref,
    query_ref,
    value_ref,
    within_ref,
    map_ref,
    doc_query_ref,
    doc_key_ref,
    attended_ref,
    stats_ref,
    values_hbm,
    moved_hbm,
    rows_hbm,
    inverse_hbm,
    down_partial_ref,
    feed_partial_ref,
    normed_hbm,
    feed_grads_hbm,
    grad_ref,
    down_result_ref,
    rows_grad_ref,
    feed_result_ref,
    out_result_ref,
    grad_low_ref,
    att_grad_ref,
    out_partial_ref,
    moved_ref,
    values_ref,
    extra_ref,
    normed_ref,
    feed_grads_ref,
    made_ref,
    load_sem,
    query_grad_ref,
    key_grad_ref,
    within_grad_ref,
    map_grad_ref,
    value_grad_ref,
    scaled_ref,
    dots_ref,
    direct_ref,
    key_slots_ref,
    value_slots_ref,
    key_send,
    key_recv,
    value_send,
    value_recv,
    *refs,
):
    lines, rows = feed_partial_ref.shape[2:4]
    here = Place(groups, lines)
    make = None
    if made_feed(groups, rows):
        normed_load = pltpu.make_async_copy(normed_hbm, normed_ref, load_sem.at[9])
        feed_load = pltpu.make_async_copy(feed_grads_hbm, feed_grads_ref, load_sem.at[10])
        feed_partial_ref = made_ref
        normed_load.start()
        feed_load.start()

        def make(target):
            span = GROUP * lines * rows
            left = normed_ref[:, pl.ds(pl.multiple_of(target * span, BLOCK), span)].T

            def one(at):
                value = dot(left, feed_grads_ref[:, at])
                for index in range(GROUP * lines):
                    made_ref[target, index // lines, index % lines, :, at] = value[index * rows : (index + 1) * rows].astype(BF16)

            in_tiles(feed_grads_ref.shape[1], one, 4 * BLOCK)

    here.meet()
    place, has_next, previous = here.g, here.above, here.down()
    sum_refs, gather_refs, down_refs, feed_refs, out_refs = several(
        refs,
        7,
        2,
        len(Scatter.scratch(groups, down_partial_ref.shape)),
        len(Scatter.scratch(groups, feed_partial_ref.shape)),
        len(LineSum.scratch(groups, out_partial_ref.shape)),
    )
    sums = GroupSum(here, partial_ref, sum_refs)
    whole = GroupGather(here, grad_low_ref, gather_refs)
    down = Scatter(here, down_partial_ref, down_result_ref, down_refs)
    feed_scatter = Scatter(here, feed_partial_ref, feed_result_ref, feed_refs, make)
    out_lines = LineSum(here, out_partial_ref, out_result_ref, out_refs)
    pauses = Pauses(*[(functools.partial(feed_scatter.step, wave),) for wave in range(1, groups)])

    def load(hop):
        return pltpu.make_async_copy(moved_hbm.at[hop], moved_ref.at[hop % 2], load_sem.at[hop % 2])

    def load_values(hop):
        return pltpu.make_async_copy(values_hbm.at[hop - 1], values_ref.at[hop % 2], load_sem.at[2 + hop % 2])

    loads = [pltpu.make_async_copy(rows_hbm.at[:, pl.ds(4 * WIDE, EXTRA)], extra_ref, load_sem.at[4])]
    for index, panel in enumerate((0, 1, 3)):
        loads.append(pltpu.make_async_copy(rows_hbm.at[:, pl.ds(panel * WIDE, WIDE)], direct_ref.at[index], load_sem.at[5 + index]))
    loads.append(pltpu.make_async_copy(inverse_hbm, direct_ref.at[3], load_sem.at[8]))
    sums.start()
    down.start()
    load(hops).start()
    load_values(hops).start()
    if make is not None:
        normed_load.wait()
        feed_load.wait()
    feed_scatter.start_far(1, 1)
    for chunk in range(CHUNKS):
        sums.pass_on(chunk)
    for chunk in range(CHUNKS):
        back = rms_back(hidden_ref[sums.at(chunk), :], gain_ref[...], sums.take(chunk))
        grad = cotangent_ref[sums.at(chunk), :].astype(F32) + back
        grad_ref[sums.at(chunk), :] = grad
        grad_low_ref[whole.at(chunk, here.m), :] = grad.astype(BF16)
        whole.give(chunk)
    down.step(1)
    for chunk in range(CHUNKS):
        whole.pass_on(chunk)
    if groups > 2:
        down.step(2)
    whole.finish()
    att_grad_ref[...] = dot(grad_low_ref[...], out_ref[...], NT).astype(BF16)
    turned = low_ref[...].T
    units = out_partial_ref.shape[3]

    def out_tile(at):
        value = dot(turned, grad_low_ref[:, at])
        for index in range(WIDE // units):
            slot, member, line = index // (GROUP * lines), index // lines % GROUP, index % lines
            out_partial_ref[slot, member, line, :, at] = value[index * units : (index + 1) * units].astype(BF16)

    in_tiles(out_partial_ref.shape[4], out_tile)
    out_lines.start()
    feed_scatter.start_far(2)
    feed_scatter.act(here.g)
    for wave in range(3, groups):
        down.step(wave)

    def key_copy(hop):
        slot = hop - 1
        return remote(key_slots_ref.at[hop], key_slots_ref.at[slot], key_send.at[slot], key_recv.at[slot], previous)

    def value_copy(hop):
        slot = hop - 1
        return remote(value_slots_ref.at[hop], value_slots_ref.at[slot], value_send.at[slot], value_recv.at[slot], previous)

    map_grad_ref[...] = jnp.zeros_like(map_grad_ref)
    query_grad_ref[...] = jnp.zeros_like(query_grad_ref)
    for block in range(GROUP):
        for head in range(OWN):
            at = (tile(block), tile(head))
            grad = att_grad_ref[at].astype(F32)
            total = stats_ref[tile(block), OWN + head : OWN + head + 1]
            scaled_ref[at] = (grad / total).astype(BF16)
            dots = -jnp.sum(grad * attended_ref[at], axis=1, keepdims=True) / total
            dots_ref[head, tile(block), :] = jnp.broadcast_to(dots, (BLOCK, BLOCK))

    def pair(block, head, scores, counts, values):
        count = scores.shape[1] // BLOCK
        top = stats_ref[tile(block), head : head + 1]
        weights = jnp.exp(masked(scores, counts) - top)
        weight_grad = dot(scaled_ref[tile(block), tile(head)], values, NT)
        dots = jnp.concatenate([dots_ref[head, tile(block), :]] * count, 1)
        return weights, weights * (weight_grad + dots) * SCALE

    def row_counts(block, hop, first, count):
        return doc_query_ref[tile(block), :] == doc_key_ref[hop, :, tile(first, count)]

    def hop_direct(hop, last):
        for head in range(OWN):
            value_grad_ref[:, tile(head)] = jnp.zeros((GROUP * BLOCK, BLOCK), F32)
        for block in range(GROUP):
            first = block if last else 0
            count = GROUP - first
            counts = row_counts(block, hop, first, count)
            for head in range(OWN):
                query = query_ref[tile(block), tile(head)]
                keys = moved_ref[hop % 2, block, tile(first, count), tile(head)]
                weights, grad = pair(
                    block, head, dot(query, keys, NT), counts, values_ref[hop % 2, tile(first, count), tile(head)]
                )
                raw = grad.astype(BF16)
                query_grad_ref[tile(block), tile(head)] += dot(raw, keys)
                direct_ref[block, tile(first, count), tile(head)] = dot(raw, query, TN)
                value_grad_ref[tile(first, count), tile(head)] += dot(
                    weights.astype(BF16), scaled_ref[tile(block), tile(head)], TN
                )

    def collect_map(block, head, keys, grads):
        map_grad_ref[tile(block), tile(head)] += dot2(keys, grads, TN)

    def hop_chain(hop, last):
        for head in range(OWN):
            if last:
                grads = direct_ref[GROUP - 1, tile(GROUP - 1), tile(head)]
                for block in range(GROUP - 2, -1, -1):
                    rows = tile(block + 1, GROUP - 1 - block)
                    collect_map(block, head, moved_ref[hop % 2, block, rows, tile(head)], grads)
                    back = dot3(grads, map_ref[tile(block), tile(head)], NT)
                    direct = direct_ref[block, tile(block, GROUP - block), tile(head)]
                    grads = jnp.concatenate([direct[:BLOCK], direct[BLOCK:] + back], 0)
                key_slots_ref[hop, :, tile(head)] = grads.astype(BF16)
                value_slots_ref[hop, :, tile(head)] = value_grad_ref[:, tile(head)].astype(BF16)
            else:
                grads = key_grad_ref[:, tile(head)]
                for block in range(GROUP - 1, -1, -1):
                    collect_map(block, head, moved_ref[hop % 2, block, :, tile(head)], grads)
                    grads = direct_ref[block, :, tile(head)] + dot3(grads, map_ref[tile(block), tile(head)], NT)
                key_slots_ref[hop, :, tile(head)] = grads.astype(BF16)

    def take(hop):
        @pl.when(has_next)
        def _():
            key_copy(hop).wait_recv()
            key_grad_ref[...] = key_slots_ref[hop - 1].astype(F32)

        @pl.when(jnp.logical_not(has_next))
        def _():
            key_grad_ref[...] = jnp.zeros_like(key_grad_ref)

    load(hops - 1).start()
    load_values(hops - 1).start()
    load(hops).wait()
    load_values(hops).wait()

    @pl.when(place >= hops)
    def _():
        hop_direct(hops, True)
        hop_chain(hops, True)
        key_copy(hops).start()
        value_copy(hops).start()

    down.last()

    def between(hop, pause=None):
        load(hop - 1).start()
        pl.when(jnp.asarray(hop) > 1)(lambda: load_values(hop - 1).start())
        load(hop).wait()
        load_values(hop).wait()
        pl.when(place >= hop)(lambda: hop_direct(hop, False))
        if pause is not None:
            pause()

        @pl.when(place >= hop)
        def _():
            take(hop + 1)
            hop_chain(hop, False)
            key_copy(hop).start()

            @pl.when(has_next)
            def _():
                value_copy(hop + 1).wait_recv()
                for head in range(OWN):
                    value_slots_ref[hop, :, tile(head)] = (
                        value_grad_ref[:, tile(head)] + value_slots_ref[hop, :, tile(head)].astype(F32)
                    ).astype(BF16)

            @pl.when(jnp.logical_not(has_next))
            def _():
                for head in range(OWN):
                    value_slots_ref[hop, :, tile(head)] = value_grad_ref[:, tile(head)].astype(BF16)

            value_copy(hop).start()

    if hops > 2:

        def step(counter, carry):
            between(hops - 1 - counter)
            return carry

        lax.fori_loop(0, hops - 1, step, 0)
    else:
        for hop in range(hops - 1, 0, -1):
            between(hop, pauses)

    load(0).wait()
    for head in range(OWN):
        value_grad_ref[:, tile(head)] = jnp.zeros((GROUP * BLOCK, BLOCK), F32)
    for block in range(GROUP):
        wide = (BLOCK, (block + 1) * BLOCK)
        counts = row_counts(block, 0, 0, block + 1) & (iota(0, wide) + block * BLOCK >= iota(1, wide))
        for head in range(OWN):
            query = query_ref[tile(block), tile(head)]
            scores = within_ref[tile(block), tile(head)]
            if block:
                keys = moved_ref[0, block, tile(0, block), tile(head)]
                scores = jnp.concatenate([dot(query, keys, NT), scores], 1)
            weights, grad = pair(block, head, scores, counts, value_ref[tile(0, block + 1), tile(head)])
            within_grad_ref[tile(block), tile(head)] = grad[:, block * BLOCK :]
            value_grad_ref[tile(0, block + 1), tile(head)] += dot(
                weights.astype(BF16), scaled_ref[tile(block), tile(head)], TN
            )
            if block:
                raw = grad[:, : block * BLOCK].astype(BF16)
                query_grad_ref[tile(block), tile(head)] += dot(raw, keys)
                direct_ref[block, tile(0, block), tile(head)] = dot(raw, query, TN)
    take(1)
    for head in range(OWN):
        grads = key_grad_ref[:, tile(head)]
        for block in range(GROUP - 1, 0, -1):
            key_grad_ref[tile(block), tile(head)] = grads[block * BLOCK :]
            grads = grads[: block * BLOCK]
            collect_map(block, head, moved_ref[0, block, tile(0, block), tile(head)], grads)
            grads = direct_ref[block, tile(0, block), tile(head)] + dot3(grads, map_ref[tile(block), tile(head)], NT)
        key_grad_ref[tile(0), tile(head)] = grads

    @pl.when(has_next)
    def _():
        value_copy(1).wait_recv()
        value_grad_ref[...] += value_slots_ref[0].astype(F32)

    def settle(hop, carry):
        @pl.when(place >= hop)
        def _():
            key_copy(hop).wait_send()
            value_copy(hop).wait_send()

        return carry

    lax.fori_loop(1, hops + 1, settle, 0)
    for copy in loads:
        copy.start()
    for copy in loads:
        copy.wait()
    pauses()
    pieces = (direct_ref, extra_ref, query_grad_ref, key_grad_ref, within_grad_ref, map_grad_ref, value_grad_ref, rows_grad_ref)
    prepare_back_blocks(0, GROUP // 2, *pieces)
    pauses.rest()
    prepare_back_blocks(GROUP // 2, GROUP, *pieces)
    out_lines.finish()
    feed_scatter.last()
    sums.finish()
    down.finish()
    feed_scatter.finish()


def back(groups, hops, partial, hidden, cotangent, gain, low, out, *args):
    values, moved, rows, inverse, down, feed, normed, feed_grads = args[-8:]
    size, width = hidden.shape
    length = partial.shape[0]
    lines, units = feed.shape[2:4]
    out_shape = (groups // GROUP, GROUP, lines, units, width)
    dma = pltpu.SemaphoreType.DMA
    inputs = (partial, hidden, cotangent, gain, low, out) + args
    return pl.pallas_call(
        functools.partial(back_kernel, groups, hops),
        out_shape=[
            shape(F32, size, width),
            shape(F32, 1, *down.shape[3:]),
            shape(BF16, *rows.shape),
            shape(BF16, GROUP, *feed.shape[3:]),
            shape(BF16, groups // GROUP, GROUP, units, width),
        ],
        in_specs=in_vmem(len(inputs) - 8) + anywhere(8),
        out_specs=in_vmem(5),
        scratch_shapes=[
            pltpu.VMEM((length, width), BF16),
            pltpu.VMEM((length, WIDE), BF16),
            pltpu.VMEM(out_shape, BF16),
            pltpu.VMEM((2,) + moved.shape[1:], BF16),
            pltpu.VMEM((2,) + values.shape[1:], BF16),
            pltpu.VMEM((length, EXTRA), F32),
            pltpu.VMEM(normed.shape if made_feed(groups, units) else (16, BLOCK), BF16),
            pltpu.VMEM(feed_grads.shape if made_feed(groups, units) else (16, BLOCK), BF16),
            pltpu.VMEM(feed.shape if made_feed(groups, units) else (1, 1, 1, 16, BLOCK), BF16),
            dma((11,)),
        ]
        + [pltpu.VMEM((length, WIDE), F32)] * 5
        + [
            pltpu.VMEM((length, WIDE), BF16),
            pltpu.VMEM((OWN, length, BLOCK), F32),
            pltpu.VMEM((GROUP, length, WIDE), F32),
            pltpu.VMEM((hops + 1, length, WIDE), BF16),
            pltpu.VMEM((hops + 1, length, WIDE), BF16),
            dma((hops,)),
            dma((hops,)),
            dma((hops,)),
            dma((hops,)),
        ]
        + GroupSum.scratch(size, width)
        + GroupGather.scratch()
        + Scatter.scratch(groups, down.shape)
        + Scatter.scratch(groups, feed.shape)
        + LineSum.scratch(groups, out_shape),
        **communicating(2, "back", 60),
    )(*inputs)


def gather_kernel(
    groups, query_ref, key_ref, value_ref, house_ref, extra_ref, gate_hbm, up_hbm, out_hbm, down_hbm, tokens_ref, cotangent_ref,
    full_ref, feed_full_ref, out_full_ref, down_low_ref, tokens_all_ref, cotangent_all_ref, first_ref, feed_parts_ref, out_low_ref,
    gate_ref, up_ref, out_ref, down_ref, load_sem, send, recv, local, *sems
):
    lines = full_ref.shape[2]
    here = Place(groups, lines)
    loads = [
        pltpu.make_async_copy(source, target, load_sem.at[index])
        for index, (source, target) in enumerate(
            ((out_hbm, out_ref), (gate_hbm, gate_ref), (up_hbm, up_ref), (down_hbm, down_ref))
        )
    ]
    for copy in loads:
        copy.start()
    for member in range(GROUP):
        for part, weight_ref in enumerate((query_ref, key_ref, value_ref, house_ref)):
            first_ref[member, :, pl.ds(part * WIDE, WIDE)] = weight_ref[:, pl.ds(member * WIDE, WIDE)].astype(BF16)
        first_ref[member, :, pl.ds(4 * WIDE, EXTRA)] = extra_ref[member]
    here.meet()
    first_sems, feed_sems, out_sems = several(sems, 8, 3, 5)
    first = Gather(here, first_ref, full_ref, first_sems)
    feed = Gather(here, feed_parts_ref, feed_full_ref, feed_sems)
    out = HomeGather(here, out_low_ref, out_full_ref, out_sems)
    first.start()
    loads[0].wait()
    out_low_ref[...] = out_ref[...].astype(BF16)
    out.start()
    size = tokens_ref.shape[0]
    own = pl.ds(pl.multiple_of(here.m * size, size), size)
    copies = []
    for index, (source, target) in enumerate(((tokens_ref, tokens_all_ref), (cotangent_ref, cotangent_all_ref))):
        copies.append(pltpu.make_async_copy(source, target.at[own], local.at[index]))
        for offset in (2, 3, 1):
            copies.append(
                remote(source, target.at[own], send.at[index, offset], recv.at[index, offset], here.member(offset))
            )
    for copy in copies:
        copy.start()
    for copy in loads[1:]:
        copy.wait()
    down_low_ref[...] = down_ref[...].astype(BF16)
    own_units = feed_parts_ref.shape[2] // 2
    for at, weight_ref in ((0, gate_ref), (own_units, up_ref)):
        if len(weight_ref.shape) == 3:
            feed_parts_ref[:, :, at : at + own_units] = weight_ref[...]
        else:
            for member in range(GROUP):
                for index in range(groups * lines):
                    block = (index // lines * GROUP + member) * lines + index % lines
                    feed_parts_ref[member, :, pl.ds(at + index * BLOCK, BLOCK)] = weight_ref[:, tile(block)].astype(BF16)
    feed.start()
    first.settle()
    first.spread()
    out.spread()
    for distance in range(1, groups):
        first.step(distance)
        out.step(distance)
    feed.settle()
    out.finish()
    for copy in copies:
        copy.wait()
    first.finish()


def gather_first(groups, lines, first, extra, gate, up, out, down, tokens, cotangent):
    dma = pltpu.SemaphoreType.DMA
    size, width = tokens.shape
    rows = out.shape[0]
    units = 2 * down.shape[0] * groups * lines
    return pl.pallas_call(
        functools.partial(gather_kernel, groups),
        out_shape=[
            shape(BF16, groups, GROUP, lines, rows, 4 * WIDE + EXTRA),
            shape(BF16, groups, GROUP, lines, rows, units),
            shape(BF16, groups // GROUP, GROUP, lines, rows, width),
            shape(BF16, *down.shape),
            shape(BF16, GROUP * size, width),
            shape(BF16, GROUP * size, width),
        ],
        in_specs=in_vmem(5) + anywhere(6),
        out_specs=anywhere(3) + in_vmem(1) + anywhere(2),
        scratch_shapes=[
            pltpu.VMEM((GROUP, rows, 4 * WIDE + EXTRA), BF16),
            pltpu.VMEM((GROUP, rows, units), BF16),
            pltpu.VMEM((rows, width), BF16),
            pltpu.VMEM(gate.shape, gate.dtype),
            pltpu.VMEM(up.shape, up.dtype),
            pltpu.VMEM(out.shape, F32),
            pltpu.VMEM(down.shape, F32),
            dma((4,)),
            dma((2, GROUP)),
            dma((2, GROUP)),
            dma((2,)),
        ]
        + Gather.inside()
        + Gather.outside(groups)
        + Gather.inside()
        + HomeGather.scratch(groups),
        **communicating(0, "gather_first", 60),
    )(*first, extra, gate, up, out, down, tokens, cotangent)


def rms_norm(values, gain):
    return values * lax.rsqrt(jnp.mean(values * values, axis=-1, keepdims=True) + EPSILON) * gain


def rms_back(values, gain, grad):
    scale = lax.rsqrt(jnp.mean(values * values, axis=-1, keepdims=True) + EPSILON)
    straight = values * scale
    lifted = grad * gain
    return scale * (lifted - straight * jnp.mean(lifted * straight, axis=-1, keepdims=True))


def in_tiles(size, act, step=2 * BLOCK):
    def one(index, carry):
        act(pl.ds(pl.multiple_of(index * step, step), step))
        return carry

    lax.fori_loop(0, size // step, one, 0)


def branch_kernel(
    groups, partial_ref, tokens_ref, gain_ref, down_ref, feed_hbm, hidden_ref, normed_ref, active_ref, gate_slope_ref, up_slope_ref,
    down_full_ref, feed_ref, feed_sem, *refs
):
    here = Place(groups, down_full_ref.shape[1])
    here.meet()
    sum_refs, gather_refs, down_refs = several(refs, 7, 2, 8)
    total = GroupSum(here, partial_ref, sum_refs)
    whole = GroupGather(here, normed_ref, gather_refs)
    down = Gather(here, down_ref, down_full_ref, down_refs, mixed=False)
    pauses = Pauses(*[(functools.partial(down.step, distance),) for distance in range(1, groups)])
    total.start()
    down.start()
    down.settle()
    down.spread()
    feed_copy = pltpu.make_async_copy(feed_hbm, feed_ref, feed_sem.at[0])
    feed_copy.start()
    for chunk in range(CHUNKS):
        total.pass_on(chunk)
    pauses()
    for chunk in range(CHUNKS):
        hidden = tokens_ref[total.at(chunk), :].astype(F32) + total.take(chunk)
        hidden_ref[total.at(chunk), :] = hidden
        normed_ref[whole.at(chunk, here.m), :] = rms_norm(hidden, gain_ref[...]).astype(BF16)
        whole.give(chunk)
    pauses()
    for chunk in range(CHUNKS):
        whole.pass_on(chunk)
    pauses.rest()
    feed_copy.wait()
    whole.finish()
    units = active_ref.shape[1]

    def act(at):
        normed = normed_ref[...]
        gate = dot(normed, feed_ref[:, at])
        up = dot(normed, feed_ref[:, pl.ds(pl.multiple_of(at.start + units, BLOCK), at.size)])
        sigmoid = jax.nn.sigmoid(gate)
        silu = gate * sigmoid
        active_ref[:, at] = (silu * up).astype(BF16)
        gate_slope_ref[:, at] = up * (sigmoid * (1.0 + gate * (1.0 - sigmoid)))
        up_slope_ref[:, at] = silu

    in_tiles(units, act)
    total.finish()
    down.finish()


def branch(groups, lines, partial, tokens, gain, down, feed):
    size, width = tokens.shape
    length, units = partial.shape[0], feed.shape[1] // 2
    dma = pltpu.SemaphoreType.DMA
    return pl.pallas_call(
        functools.partial(branch_kernel, groups),
        out_shape=[
            shape(F32, size, width),
            shape(BF16, length, width),
            shape(BF16, length, units),
            shape(F32, length, units),
            shape(F32, length, units),
            shape(BF16, groups, lines, *down.shape),
        ],
        in_specs=in_vmem(3) + anywhere(2),
        out_specs=in_vmem(5) + anywhere(1),
        scratch_shapes=[pltpu.VMEM(feed.shape, BF16), dma((1,))]
        + GroupSum.scratch(size, width)
        + GroupGather.scratch()
        + Gather.inside()
        + Gather.outside(groups),
        **communicating(3, "branch", 48),
    )(partial, tokens, gain, down, feed)


def finish_kernel(
    groups, first_partial_ref, wide_hbm, first_hbm, down_hbm, rows_grad_ref, active_ref, out_lines_ref, tokens_ref, hidden_ref, grad_ref, gain_ref,
    first_result_ref, out_result_ref, tokens_grad_ref, output_ref, first_full_ref, down_full_ref, normed_partial_ref,
    output_partial_ref, wide_ref, normed_ref, made_ref, load_sem, *refs
):
    lines, rows = first_partial_ref.shape[2:4]
    here = Place(groups, lines)
    made = rows % 16 == 0
    if made:
        first_partial_ref = made_ref
    wide_copy = pltpu.make_async_copy(wide_hbm, wide_ref, load_sem.at[2])
    wide_copy.start()
    here.meet(column=True)

    def make(target):
        span = GROUP * lines * rows
        left = normed_ref[:, pl.ds(pl.multiple_of(target * span, BLOCK), span)].T
        for at, size in [(part * WIDE, WIDE) for part in range(4)] + [(4 * WIDE, EXTRA)]:
            value = dot(left, rows_grad_ref[:, pl.ds(at, size)])
            for index in range(GROUP * lines):
                made_ref[target, index // lines, index % lines, :, pl.ds(at, size)] = value[index * rows : (index + 1) * rows].astype(BF16)

    first_refs, out_refs, normed_refs, output_refs = several(
        refs, len(Scatter.scratch(groups, first_partial_ref.shape)), len(HomeScatter.scratch(groups, out_lines_ref.shape)), 7, 7
    )
    first = Scatter(here, first_partial_ref, first_result_ref, first_refs, make if made else None)
    out = HomeScatter(here, out_lines_ref, out_result_ref, out_refs)
    normed = GroupSum(here, normed_partial_ref, normed_refs)
    output = GroupSum(here, output_partial_ref, output_refs)
    first_copy = pltpu.make_async_copy(first_hbm, first_full_ref, load_sem.at[0])
    down_copy = pltpu.make_async_copy(down_hbm, down_full_ref, load_sem.at[1])
    first_copy.start()
    down_copy.start()
    wide_copy.wait()
    out.start()
    if made:
        for block in range(GROUP):
            normed_ref[tile(block), :] = rms_norm(wide_ref[tile(block), :].astype(F32), gain_ref[...]).astype(BF16)
    first.start()
    first_copy.wait()

    def normed_tile(at):
        normed_partial_ref[:, at] = dot(rows_grad_ref[...], first_full_ref[at, :], NT).astype(BF16)

    in_tiles(normed_partial_ref.shape[1], normed_tile)
    normed.start()
    down_copy.wait()
    for chunk in range(CHUNKS):
        normed.pass_on(chunk)

    def output_tile(at):
        output_partial_ref[:, at] = dot(active_ref[...], down_full_ref[:, at]).astype(BF16)

    in_tiles(output_partial_ref.shape[1], output_tile)
    output.start()
    first.step(1)
    for chunk in range(CHUNKS):
        output.pass_on(chunk)
    for chunk in range(CHUNKS):
        back = rms_back(tokens_ref[normed.at(chunk), :].astype(F32), gain_ref[...], normed.take(chunk))
        tokens_grad_ref[normed.at(chunk), :] = (grad_ref[normed.at(chunk), :] + back).astype(BF16)
    if groups > 2:
        first.step(2)
    for chunk in range(CHUNKS):
        output_ref[output.at(chunk), :] = (hidden_ref[output.at(chunk), :] + output.take(chunk)).astype(BF16)
    for wave in range(3, groups):
        first.step(wave)
    out.last()
    normed.finish()
    output.finish()
    first.last()
    out.finish()
    first.finish()


def finish(groups, first_partial, wide, first, down, rows_grad, active, out_lines, tokens, hidden, grad, gain):
    size, width = tokens.shape
    length = rows_grad.shape[0]
    made = first_partial.shape if first_partial.shape[3] % 16 == 0 else (1, 1, 1, 16, BLOCK)
    return pl.pallas_call(
        functools.partial(finish_kernel, groups),
        out_shape=[
            shape(BF16, GROUP, *first_partial.shape[3:]),
            shape(BF16, *out_lines.shape[2:]),
            shape(BF16, size, width),
            shape(BF16, size, width),
        ],
        in_specs=anywhere(4) + in_vmem(7),
        out_specs=in_vmem(4),
        scratch_shapes=[
            pltpu.VMEM(first.shape, BF16),
            pltpu.VMEM(down.shape, BF16),
            pltpu.VMEM((length, width), BF16),
            pltpu.VMEM((length, width), BF16),
            pltpu.VMEM(wide.shape, BF16),
            pltpu.VMEM(wide.shape, BF16),
            pltpu.VMEM(made, BF16),
            pltpu.SemaphoreType.DMA((3,)),
        ]
        + Scatter.scratch(groups, first_partial.shape)
        + HomeScatter.scratch(groups, out_lines.shape)
        + GroupSum.scratch(size, width)
        + GroupSum.scratch(size, width),
        **communicating(5, "finish"),
    )(first_partial, wide, first, down, rows_grad, active, out_lines, tokens, hidden, grad, gain)


def layout_kernel(groups, lines, first_ref, feed_ref, out_ref, beta_ref, gains_ref, down_ref, tokens_ref, result_ref, *refs):
    weights, targets = refs[:6], refs[6:]
    query_out, key_out, value_out, house_out, out_out, down_out, tokens_out, result_out, norm_gain_out, beta_out = targets[:10]
    rows = gains_ref.shape[1]
    down_out[...] = down_ref[0]
    tokens_out[...] = tokens_ref[...]
    result_out[...] = result_ref[...]

    def as_row(column):
        return jnp.broadcast_to(column, (rows, BLOCK)).T[0:1, :]

    first_sum = jnp.zeros((rows, WIDE), F32)
    extra_sum = jnp.zeros((rows, EXTRA), F32)
    for member in range(GROUP):
        for part, target_ref in enumerate((query_out, key_out, value_out, house_out)):
            value = first_ref[member, :, pl.ds(part * WIDE, WIDE)].astype(F32)
            at = pl.ds(member * WIDE, WIDE)
            target_ref[:, at] = value
            first_sum = first_sum + value * weights[part][:, at].astype(BF16).astype(F32)
        extra = first_ref[member, :, pl.ds(4 * WIDE, EXTRA)].astype(F32)
        extra_sum = extra_sum + extra * beta_ref[member].astype(F32)
        beta_out[member] = extra.T[0:OWN, :]
    total = jnp.sum(first_sum, axis=1, keepdims=True) + jnp.sum(extra_sum, axis=1, keepdims=True)
    norm_gain_out[...] = as_row(total) / gains_ref[0:1, :]
    out_out[...] = out_ref[...].astype(F32)
    if len(targets) > 10:
        gate_out, up_out, ffn_gain_out = targets[10:]
        units = feed_ref.shape[2] // 2
        feed_sum = jnp.zeros((rows, BLOCK), F32)
        for at, weight_ref, target_ref in ((0, weights[4], gate_out), (units, weights[5], up_out)):
            for member in range(GROUP):
                for index in range(groups * lines):
                    block = (index // lines * GROUP + member) * lines + index % lines
                    value = feed_ref[member, :, pl.ds(at + index * BLOCK, BLOCK)].astype(F32)
                    target_ref[:, tile(block)] = value
                    feed_sum = feed_sum + value * weight_ref[:, tile(block)].astype(BF16).astype(F32)
        ffn_gain_out[...] = as_row(jnp.sum(feed_sum, axis=1, keepdims=True)) / gains_ref[1:2, :]


def layout(groups, lines, whole_tiles, first, feed, out, beta, gains, down, tokens, result, weights):
    rows, width = out.shape
    outs = [shape(F32, rows, width)] * 5 + [
        shape(F32, *down.shape[1:]),
        shape(BF16, *tokens.shape),
        shape(BF16, *tokens.shape),
        shape(F32, 1, rows),
        shape(F32, GROUP, OWN, rows),
    ]
    if whole_tiles:
        outs = outs + [shape(F32, *weights[4].shape)] * 2 + [shape(F32, 1, rows)]
    return pl.pallas_call(
        functools.partial(layout_kernel, groups, lines),
        out_shape=outs,
        in_specs=in_vmem(8 + len(weights)),
        out_specs=in_vmem(len(outs)),
        compiler_params=pltpu.CompilerParams(vmem_limit_bytes=60 << 20),
        name="layout",
    )(first, feed, out, beta, gains, down, tokens, result, *weights)


def on_device(
    tokens,
    doc_ids,
    norm_gain,
    query_weight,
    key_weight,
    value_weight,
    house_weight,
    beta_weight,
    out_weight,
    ffn_gain,
    gate_weight,
    up_weight,
    down_weight,
    cotangent,
):
    groups, batch = lax.axis_size("g"), lax.axis_size("b")
    devices = groups * GROUP * batch
    rows, width = query_weight.shape
    hidden_rows = down_weight.shape[0]
    hidden_own = gate_weight.shape[1] // GROUP
    block_rows = tokens.shape[1]
    hops = groups // 2
    doc_columns = -(-block_rows // rows)
    place, line = lax.axis_index("g"), lax.axis_index("b")

    def columns(weight):
        return jnp.transpose(weight.astype(BF16).reshape(rows, GROUP, -1), (1, 0, 2))

    docs = jnp.pad(doc_ids[0].astype(BF16), (0, rows * doc_columns - block_rows)).reshape(rows, doc_columns)
    same = jnp.concatenate([norm_gain.astype(BF16)[:, None], ffn_gain.astype(BF16)[:, None], docs], 1)
    same = jnp.broadcast_to(same[None], (GROUP,) + same.shape)
    same = jnp.pad(same, ((0, 0), (0, 0), (0, EXTRA - OWN - same.shape[2])))
    extra = jnp.concatenate([columns(beta_weight), same], 2)

    def unit_columns(weight):
        parts = weight.astype(BF16).reshape(rows, groups, GROUP, batch, hidden_rows)
        return jnp.transpose(parts, (2, 0, 1, 3, 4)).reshape(GROUP, rows, hidden_own)

    whole_tiles = hidden_rows == BLOCK
    feed_weights = (gate_weight, up_weight) if whole_tiles else (unit_columns(gate_weight), unit_columns(up_weight))
    first, feed, out_full, down_low, tokens_all, cotangent_all = gather_first(
        groups, batch, (query_weight, key_weight, value_weight, house_weight), extra, *feed_weights, out_weight, down_weight, tokens[0], cotangent[0]
    )
    first = first.reshape(width, -1)

    extra = first[:, 4 * WIDE :]
    gain_one = extra[:, OWN].astype(F32)[None]
    gain_two = extra[:, OWN + 1].astype(F32)[None]
    docs = extra[:, OWN + 2 : OWN + 2 + doc_columns].astype(jnp.int32)
    docs = docs.reshape(devices, -1)[:, :block_rows].reshape(groups, GROUP, batch, block_rows)
    docs = lax.dynamic_index_in_dim(docs, line, 2, keepdims=False).reshape(groups, GROUP * block_rows)
    doc_key = jnp.stack(
        [
            jnp.where(place >= hop, lax.dynamic_index_in_dim(docs, jnp.maximum(place - hop, 0), 0, keepdims=False), -1)
            for hop in range(hops + 1)
        ]
    )[:, None, :]
    doc_query = lax.dynamic_index_in_dim(docs, place, 0, keepdims=False)[:, None]

    (projected, query, value, within, maps, inverse, attended, attended_low, stats, moved, values, out_full, feed) = attend(
        groups, hops, tokens_all, first, gain_one, doc_query, doc_key, out_full, feed
    )
    out_full = out_full.reshape(WIDE, width)
    feed = feed.reshape(width, -1)
    hidden, normed_two, active, gate_slope, up_slope, down_full = branch(
        groups, batch, dot(attended_low, out_full).astype(BF16), tokens[0], gain_two, down_low, feed
    )
    down_full = down_full.reshape(hidden_own, width)
    active_grad = dot(cotangent_all, down_full, NT)
    feed_grads = jnp.concatenate([(active_grad * gate_slope).astype(BF16), (active_grad * up_slope).astype(BF16)], 1)
    down_partial = dot(active, cotangent_all, TN).astype(BF16).reshape(groups, 1, batch, hidden_rows, width)
    if made_feed(groups, rows):
        feed_partial = feed.reshape(groups, GROUP, batch, rows, -1)
    else:
        feed_partial = dot(normed_two, feed_grads, TN).astype(BF16).reshape(groups, GROUP, batch, rows, -1)
    hidden_grad, down_weight_grad, rows_grad, feed_grad, out_lines = back(
        groups, hops, dot(feed_grads, feed, NT).astype(BF16), hidden, cotangent[0], gain_two, attended_low, out_full, query, value,
        within, maps, doc_query, doc_key, attended, stats, values, moved, projected, inverse, down_partial, feed_partial,
        normed_two, feed_grads,
    )
    partial_shape = (groups, GROUP, batch, rows, rows_grad.shape[1])
    if rows % 16 == 0:
        first_partial = first.reshape(partial_shape)
    else:
        normed = rms_norm(tokens_all.astype(F32), gain_one).astype(BF16)
        first_partial = dot(normed, rows_grad, TN).astype(BF16).reshape(partial_shape)
    beta_parts = jnp.pad(columns(beta_weight), ((0, 0), (0, 0), (0, EXTRA - OWN)))
    weights = (query_weight, key_weight, value_weight, house_weight) + feed_weights
    first_grad, out_grad, tokens_grad, output = finish(
        groups, first_partial, tokens_all, first, down_full, rows_grad, active, out_lines, tokens[0], hidden, hidden_grad, gain_one
    )
    gains = jnp.stack([norm_gain, ffn_gain]).astype(BF16).astype(F32)
    results = layout(
        groups, batch, whole_tiles, first_grad, feed_grad, out_grad, beta_parts, gains, down_weight_grad, tokens_grad, output, weights
    )
    query_weight_grad, key_weight_grad, value_weight_grad, house_weight_grad, out_weight_grad, down_weight_grad = results[:6]
    tokens_grad, output, norm_gain_grad, beta_weight_grad = results[6:10]
    output, tokens_grad = output[None], tokens_grad[None]
    beta_weight_grad = beta_weight_grad.reshape(-1, rows).T
    def unit_whole(parts):
        parts = parts.astype(F32).reshape(GROUP, rows, groups, batch, hidden_rows)
        return jnp.transpose(parts, (1, 2, 0, 3, 4)).reshape(rows, -1)

    if whole_tiles:
        gate_weight_grad, up_weight_grad, ffn_gain_grad = results[10:]
        ffn_gain_grad = ffn_gain_grad[0]
    else:
        gate_weight_grad, up_weight_grad = unit_whole(feed_grad[:, :, :hidden_own]), unit_whole(feed_grad[:, :, hidden_own:])
        feed_sum = jnp.sum(gate_weight_grad * gate_weight.astype(BF16).astype(F32), axis=1) + jnp.sum(
            up_weight_grad * up_weight.astype(BF16).astype(F32), axis=1
        )
        ffn_gain_grad = feed_sum / gains[1]
    return (
        output,
        tokens_grad,
        norm_gain_grad[0],
        query_weight_grad,
        key_weight_grad,
        value_weight_grad,
        house_weight_grad,
        beta_weight_grad,
        out_weight_grad,
        ffn_gain_grad,
        gate_weight_grad,
        up_weight_grad,
        down_weight_grad,
    )


def solution(mesh):
    groups = mesh.shape["seq"] // GROUP
    inner = Mesh(mesh.devices.reshape(groups, GROUP, mesh.shape["batch"]), ("g", "m", "b"))
    line = P("b", ("g", "m"), None)
    vector = P(("g", "m", "b"))
    matrix = P(("g", "m", "b"), None)
    in_specs = (line, P("b", ("g", "m")), vector) + (matrix,) * 6 + (vector,) + (matrix,) * 3 + (line,)
    out_specs = (line, line, vector) + (matrix,) * 6 + (vector,) + (matrix,) * 3
    return jax.shard_map(on_device, mesh=inner, in_specs=in_specs, out_specs=out_specs, check_vma=False)
```

```python
import functools

import jax
import jax.numpy as jnp
from jax import lax
from jax.experimental import pallas as pl
from jax.experimental.pallas import tpu as pltpu
from jax.sharding import Mesh
from jax.sharding import PartitionSpec as P

HEADS = 12
HEAD_DIM = 128
GROUP = 4
OWN = HEADS // GROUP
WIDE = OWN * HEAD_DIM
BLOCK = 128
EXTRA = 128
EPSILON = 1e-06
NEGATIVE = -1e30
SCALE = HEAD_DIM ** (-0.5)
MESH = pl.DeviceIdType.MESH
F32 = jnp.float32
BF16 = jnp.bfloat16
NN = (((1,), (0,)), ((), ()))
NT = (((1,), (1,)), ((), ()))
TN = (((0,), (0,)), ((), ()))


def dot(left, right, dims=NN):
    return lax.dot_general(left, right, dims, preferred_element_type=F32)


def split(value):
    high = value.astype(BF16)
    return high, (value - high.astype(F32)).astype(BF16)


def dot3(left, right, dims=NN):
    left_high, left_low = split(left)
    right_high, right_low = split(right)
    return dot(left_high, right_high, dims) + (
        dot(left_high, right_low, dims) + dot(left_low, right_high, dims)
    )


def dot2(left, right, dims=NN):
    high, low = split(right)
    return dot(left, high, dims) + dot(left, low, dims)


def tile(index, count=1):
    return pl.ds(index * BLOCK, count * BLOCK)


def iota(axis, shape=(BLOCK, BLOCK)):
    return lax.broadcasted_iota(jnp.int32, shape, axis)


def invert(strict):
    row, col = iota(0), iota(1)
    eye = jnp.where(row == col, 1.0, 0.0)

    def part(size):
        return (row // (2 * size) == col // (2 * size)) & (row // size > col // size)

    totals = [eye - jnp.where(part(1), value, 0.0) for value in strict]
    size = 2
    while size < BLOCK:
        mask = part(size)
        pieces = [jnp.where(mask, value, 0.0) for value in strict]
        inner = [dot3(piece, total) for piece, total in zip(pieces, totals)]
        outer = [dot3(total, value) for total, value in zip(totals, inner)]
        totals = [total - value for total, value in zip(totals, outer)]
        size *= 2
    return totals


def unit_of(house):
    scale = lax.rsqrt(jnp.sum(house * house, axis=-1, keepdims=True) + EPSILON)
    return house * scale, scale


def products(query, key, unit):
    both = dot3(jnp.concatenate([unit, query], 0), jnp.concatenate([unit, key], 0), NT)
    return both[:BLOCK, :BLOCK], both[:BLOCK, BLOCK:], both[BLOCK:, :BLOCK], both[BLOCK:, BLOCK:]


def prepare_blocks(first, last, rows_ref, query_ref, key_ref, value_ref, within_ref, map_ref, inverse_ref):
    row, col = iota(0), iota(1)

    def one_block(block, carry):
        at = tile(block)
        kept, strict = [], []
        for head in range(OWN):
            query, key, value, house = [
                rows_ref[at, pl.ds(part * WIDE + head * BLOCK, BLOCK)] for part in range(4)
            ]
            rate = rows_ref[at, pl.ds(4 * WIDE, EXTRA)][:, head : head + 1]
            value_ref[at, tile(head)] = value.astype(BF16)
            unit, _ = unit_of(house)
            strength = 2.0 * jax.nn.sigmoid(rate)
            unit_unit, unit_key, query_unit, query_key = products(query, key, unit)
            strict.append(jnp.where(row > col, strength * unit_unit, 0.0))
            reach = jnp.where(row > col, strength * unit_key, 0.0)
            project = jnp.where(row >= col, query_unit, 0.0)
            kept.append((query, key, unit, strength, reach, project, query_key))
        inverses = invert(strict)
        for head in range(OWN):
            query, key, unit, strength, reach, project, query_key = kept[head]
            inverse = inverses[head]
            solved = dot3(inverse, jnp.concatenate([strength * unit, reach], 1))
            from_query = dot3(project, solved)
            from_unit = dot3(solved, unit, TN)
            query_ref[at, tile(head)] = (query - from_query[:, :BLOCK]).astype(BF16)
            within_ref[at, tile(head)] = query_key - from_query[:, BLOCK:]
            map_ref[at, tile(head)] = jnp.where(row == col, 1.0, 0.0) - from_unit[:BLOCK]
            key_ref[at, tile(head)] = (key - from_unit[BLOCK:]).astype(BF16)
            inverse_ref[at, tile(head)] = inverse
        return carry

    lax.fori_loop(first, last, one_block, 0)


def prepare_back_blocks(first, last, panels_ref, extra_ref, query_grad_ref, key_grad_ref, within_grad_ref, map_grad_ref, value_grad_ref, out_ref):
    row, col = iota(0), iota(1)

    def one_block(block, carry):
        at = tile(block)
        rates = jnp.zeros((BLOCK, EXTRA), F32)
        for head in range(OWN):
            query, key, house, inverse = [panels_ref[part, at, tile(head)] for part in range(4)]
            rate = extra_ref[at, :][:, head : head + 1]
            query_grad = query_grad_ref[at, tile(head)]
            key_grad = key_grad_ref[at, tile(head)]
            within_grad = within_grad_ref[at, tile(head)]
            map_grad = map_grad_ref[at, tile(head)]
            unit, scale = unit_of(house)
            strength = 2.0 * jax.nn.sigmoid(rate)
            unit_unit, unit_key, query_unit, query_key = products(query, key, unit)
            reach = jnp.where(row > col, strength * unit_key, 0.0)
            project = jnp.where(row >= col, query_unit, 0.0)
            solved = dot3(inverse, jnp.concatenate([strength * unit, reach], 1))
            both_grad = jnp.concatenate([query_grad, within_grad], 1)
            project_grad = jnp.where(row >= col, -dot3(both_grad, solved, NT), 0.0)
            solved_grad = -(
                dot3(project, both_grad, TN)
                + dot3(unit, jnp.concatenate([map_grad, key_grad], 0), NT)
            )
            given_grad = dot3(inverse, solved_grad, TN)
            strict_grad = jnp.where(row > col, -dot3(given_grad, solved, NT), 0.0)
            scaled_grad = given_grad[:, :BLOCK]
            reach_grad = jnp.where(row > col, given_grad[:, BLOCK:], 0.0)
            strength_grad = jnp.sum(
                scaled_grad * unit + reach_grad * unit_key + strict_grad * unit_unit, axis=1, keepdims=True
            )
            reach_part = strength * reach_grad
            inner_part = strength * strict_grad
            unit_grad = (
                strength * scaled_grad
                + dot3(reach_part, key)
                + dot3(inner_part + inner_part.T, unit)
                + dot3(project_grad, query, TN)
                - dot3(solved[:, :BLOCK], map_grad)
                - dot3(solved[:, BLOCK:], key_grad)
            )
            query_out = query_grad + dot3(within_grad, key) + dot3(project_grad, unit)
            key_out = key_grad + dot3(within_grad, query, TN) + dot3(reach_part, unit, TN)
            house_out = scale * (unit_grad - unit * jnp.sum(unit * unit_grad, axis=1, keepdims=True))
            rate_out = strength_grad * strength * (1.0 - 0.5 * strength)
            rates = jnp.where(iota(1, (BLOCK, EXTRA)) == head, rate_out, rates)
            out_ref[at, pl.ds(head * BLOCK, BLOCK)] = query_out.astype(BF16)
            out_ref[at, pl.ds(WIDE + head * BLOCK, BLOCK)] = key_out.astype(BF16)
            out_ref[at, pl.ds(2 * WIDE + head * BLOCK, BLOCK)] = value_grad_ref[at, tile(head)].astype(BF16)
            out_ref[at, pl.ds(3 * WIDE + head * BLOCK, BLOCK)] = house_out.astype(BF16)
        out_ref[at, pl.ds(4 * WIDE, EXTRA)] = rates.astype(BF16)
        return carry

    lax.fori_loop(first, last, one_block, 0)


def remote(source, target, send, recv, device):
    return pltpu.make_async_remote_copy(
        src_ref=source, dst_ref=target, send_sem=send, recv_sem=recv, device_id=device, device_id_type=MESH
    )


class Place:
    def __init__(self, groups, lines):
        self.groups, self.lines = groups, lines
        self.g, self.m, self.b = lax.axis_index("g"), lax.axis_index("m"), lax.axis_index("b")
        self.below, self.above = self.g > 0, self.g < groups - 1

    def other(self, offset):
        return {1: self.m + 1 - 2 * (self.m % 2), 2: (self.m + 2) % GROUP, 3: GROUP - 1 - self.m}[offset]

    def member(self, offset):
        return {"g": self.g, "m": self.other(offset), "b": self.b}

    def up(self):
        return {"g": self.g + 1, "m": self.m, "b": self.b}

    def down(self):
        return {"g": self.g - 1, "m": self.m, "b": self.b}

    def across(self):
        return {"g": self.g, "m": self.m, "b": 1 - self.b}

    def column(self, group):
        return {"g": group, "m": self.m, "b": self.b}

    def meet(self, column=False):
        barrier = pltpu.get_barrier_semaphore()

        def greet(device):
            pl.semaphore_signal(barrier, 1, device_id=device, device_id_type=MESH)

        for offset in range(1, GROUP):
            greet(self.member(offset))
        greet(self.across())
        if column:
            for step in range(1, self.groups):
                greet(self.column((self.g + step) % self.groups))
            count = GROUP + self.groups - 1
        else:
            pl.when(self.above)(lambda: greet(self.up()))
            pl.when(self.below)(lambda: greet(self.down()))
            count = GROUP + self.above.astype(jnp.int32) + self.below.astype(jnp.int32)
        pl.semaphore_wait(barrier, count)


class Gather:
    def __init__(self, place, parts, full, sems, mixed=True):
        self.place, self.parts, self.full, self.mixed = place, parts, full, mixed
        sems = list(sems)
        if parts is not None:
            self.part_send, self.part_recv, self.own_sem = sems[:3]
            sems = sems[3:]
        if sems:
            self.up_send, self.down_send, self.chain_recv, self.line_send, self.line_recv = sems

    @staticmethod
    def inside():
        dma = pltpu.SemaphoreType.DMA
        return [dma((GROUP,)), dma((GROUP,)), dma((1,))]

    @staticmethod
    def outside(groups):
        return [pltpu.SemaphoreType.DMA((groups,))] * 5

    def unit(self, group, line):
        return self.full.at[group, :, line] if self.mixed else self.full.at[group, line]

    def own(self):
        p = self.place
        if self.mixed:
            return pltpu.make_async_copy(self.parts.at[p.m], self.full.at[p.g, p.m, p.b], self.own_sem.at[0])
        return pltpu.make_async_copy(self.parts, self.full.at[p.g, p.b], self.own_sem.at[0])

    def part(self, offset):
        p = self.place
        other = p.other(offset)
        return remote(
            self.parts.at[other], self.full.at[p.g, p.m, p.b], self.part_send.at[offset], self.part_recv.at[offset], p.member(offset)
        )

    def start(self):
        if self.mixed:
            for offset in (2, 3, 1):
                self.part(offset).start()
        self.own().start()

    def chain(self, source, up):
        p = self.place
        unit = self.unit(source, p.b)
        sems = self.up_send if up else self.down_send
        return remote(unit, unit, sems.at[source], self.chain_recv.at[source], p.up() if up else p.down())

    def across(self, source):
        p = self.place
        unit = self.unit(source, p.b)
        return remote(unit, unit, self.line_send.at[source], self.line_recv.at[source], p.across())

    def settle(self):
        self.own().wait()
        if self.mixed:
            for offset in (2, 3, 1):
                self.part(offset).wait()

    def spread(self):
        p = self.place
        pl.when(p.above)(lambda: self.chain(p.g, True).start())
        pl.when(p.below)(lambda: self.chain(p.g, False).start())
        self.across(p.g).start()

    def step(self, distance):
        p = self.place

        @pl.when(p.g >= distance)
        def _():
            source = p.g - distance
            self.chain(source, True).wait_recv()
            pl.when(p.above)(lambda: self.chain(source, True).start())
            self.across(source).start()

        @pl.when(p.g + distance < p.groups)
        def _():
            source = p.g + distance
            self.chain(source, False).wait_recv()
            pl.when(p.below)(lambda: self.chain(source, False).start())
            self.across(source).start()

    def finish(self):
        p = self.place

        def settle(source, carry):
            self.across(source).wait()
            pl.when(p.above & (source <= p.g))(lambda: self.chain(source, True).wait_send())
            pl.when(p.below & (source >= p.g))(lambda: self.chain(source, False).wait_send())
            return carry

        lax.fori_loop(0, p.groups, settle, 0)


class HomeGather:
    def __init__(self, place, part, full, sems):
        self.place, self.part_ref, self.full = place, part, full
        self.home = place.groups // GROUP
        self.part_send, self.part_recv, self.up_send, self.down_send, self.chain_recv = sems

    @staticmethod
    def scratch(groups):
        dma = pltpu.SemaphoreType.DMA
        return [dma((1,)), dma((GROUP,))] + [dma((groups // GROUP,))] * 3

    def at_home(self):
        return self.place.m == self.place.g // self.home

    def slot(self):
        p = self.place
        return self.full.at[p.g % self.home, p.m, p.b]

    def hand(self):
        p = self.place
        keeper = p.g // self.home
        device = {"g": p.g, "m": keeper, "b": p.b}
        return remote(self.part_ref, self.slot(), self.part_send.at[0], self.part_recv.at[p.m], device)

    def taken(self, source):
        p = self.place
        target = self.full.at[p.g % self.home, source, p.b]
        return remote(self.part_ref, target, self.part_send.at[0], self.part_recv.at[source], p.member(1))

    def own(self):
        return pltpu.make_async_copy(self.part_ref, self.slot(), self.part_send.at[0])

    def start(self):
        pl.when(self.at_home())(lambda: self.own().start())
        pl.when(jnp.logical_not(self.at_home()))(lambda: self.hand().start())

    def chain(self, slot, up):
        p = self.place
        unit = self.full.at[slot, :, p.b]
        sems = self.up_send if up else self.down_send
        return remote(unit, unit, sems.at[slot], self.chain_recv.at[slot], p.up() if up else p.down())

    def spread(self):
        p = self.place

        @pl.when(self.at_home())
        def _():
            self.own().wait()
            for offset in range(1, GROUP):
                self.taken(p.other(offset)).wait_recv()
            slot = p.g % self.home
            pl.when(p.above)(lambda: self.chain(slot, True).start())
            pl.when(p.below)(lambda: self.chain(slot, False).start())

    def step(self, distance):
        p = self.place
        for slot in range(self.home):
            source = p.m * self.home + slot

            @pl.when(p.g - source == distance)
            def _():
                self.chain(slot, True).wait_recv()
                pl.when(p.above)(lambda: self.chain(slot, True).start())

            @pl.when(source - p.g == distance)
            def _():
                self.chain(slot, False).wait_recv()
                pl.when(p.below)(lambda: self.chain(slot, False).start())

    def finish(self):
        p = self.place
        pl.when(jnp.logical_not(self.at_home()))(lambda: self.hand().wait_send())
        for slot in range(self.home):
            source = p.m * self.home + slot
            pl.when(p.above & (p.g >= source))(lambda: self.chain(slot, True).wait_send())
            pl.when(p.below & (p.g <= source))(lambda: self.chain(slot, False).wait_send())


def home_lines(place, full, send, recv):
    copies = []
    for slot in range(place.groups // GROUP):
        unit = full.at[slot, :, place.b]
        copies.append(remote(unit, unit, send.at[slot], recv.at[slot], place.across()))
    return copies


class Scatter:
    def __init__(self, place, partial, result, refs, make=None):
        self.place, self.partial, self.result, self.make = place, partial, result, make
        (self.land, self.chain_land, self.leave, self.mine_sem, self.line_send, self.line_recv, self.chain_send,
         self.chain_recv, self.part_send, self.part_recv) = refs
        self.parts = partial.shape[1]

    @staticmethod
    def scratch(groups, shape):
        dma = pltpu.SemaphoreType.DMA
        unit = (shape[1],) + tuple(shape[3:])
        return [
            pltpu.VMEM((groups,) + unit, BF16),
            pltpu.VMEM((groups + 1,) + unit, BF16),
            pltpu.VMEM((groups,) + unit, BF16),
            dma((groups,)),
            dma((groups,)),
            dma((groups,)),
            dma((groups,)),
            dma((groups + 1,)),
            dma((GROUP,)),
            dma((GROUP,)),
        ]

    def load(self, target):
        return pltpu.make_async_copy(self.partial.at[target, :, self.place.b], self.leave.at[target], self.mine_sem.at[target])

    def line(self, target):
        p = self.place
        return remote(
            self.partial.at[target, :, 1 - p.b], self.land.at[target], self.line_send.at[target], self.line_recv.at[target], p.across()
        )

    def up(self, target):
        p = self.place
        return remote(
            self.leave.at[target], self.chain_land.at[target], self.chain_send.at[target], self.chain_recv.at[target], p.up()
        )

    def down(self, target, slot):
        p = self.place
        return remote(
            self.leave.at[target], self.chain_land.at[slot], self.chain_send.at[target], self.chain_recv.at[slot], p.down()
        )

    def send_up(self, target):
        self.up(target).start()

    def send_down(self, target):
        p = self.place
        pl.when(p.g - 1 == target)(lambda: self.down(target, p.groups).start())
        pl.when(p.g - 1 != target)(lambda: self.down(target, target).start())

    def arrived(self, slot):
        p = self.place
        return remote(self.leave.at[0], self.chain_land.at[slot], self.chain_send.at[0], self.chain_recv.at[slot], p.across())

    def wave(self, wave, act_up, act_down):
        p = self.place
        pl.when(wave > p.g)(lambda: act_up(p.groups - wave + p.g))
        pl.when(wave >= p.groups - p.g)(lambda: act_down(wave - p.groups + p.g))

    def act(self, target):
        if self.make is not None:
            self.make(target)
        self.line(target).start()
        self.load(target).start()

    def start(self):
        self.start_far()
        self.act(self.place.g)

    def start_far(self, first=1, last=None):
        p = self.place
        if self.make is None:
            for wave in range(first, p.groups if last is None else last + 1):
                self.wave(wave, self.act, self.act)
        else:

            def one(wave, carry):
                self.wave(wave, self.act, self.act)
                return carry

            lax.fori_loop(first, p.groups if last is None else last + 1, one, 0)
        if first > 1:
            return

        @pl.when(jnp.logical_not(p.below))
        def _():
            self.chain_land[p.g] = jnp.zeros(self.chain_land.shape[1:], BF16)

        @pl.when(jnp.logical_not(p.above))
        def _():
            self.chain_land[p.groups] = jnp.zeros(self.chain_land.shape[1:], BF16)

    def both(self, target, part):
        return self.leave[target, part].astype(F32) + self.land[target, part].astype(F32)

    def step(self, wave):
        p = self.place

        def send(target, inner, copy):
            self.load(target).wait()
            self.line(target).wait_recv()

            @pl.when(inner)
            def _():
                self.arrived(target).wait_recv()
                for part in range(self.parts):
                    self.leave[target, part] = (self.both(target, part) + self.chain_land[target, part].astype(F32)).astype(BF16)

            @pl.when(jnp.logical_not(inner))
            def _():
                for part in range(self.parts):
                    self.leave[target, part] = self.both(target, part).astype(BF16)

            copy(target)

        self.wave(
            wave,
            lambda target: send(target, p.below, self.send_up),
            lambda target: send(target, p.above, self.send_down),
        )

    def hand(self, offset):
        p = self.place
        return remote(
            self.leave.at[p.g, p.other(offset)], self.result.at[p.m], self.part_send.at[offset], self.part_recv.at[offset], p.member(offset)
        )

    def last(self):
        p = self.place
        self.load(p.g).wait()
        self.line(p.g).wait_recv()
        pl.when(p.below)(lambda: self.arrived(p.g).wait_recv())
        pl.when(p.above)(lambda: self.arrived(p.groups).wait_recv())
        for part in range(self.parts):
            total = self.both(p.g, part) + self.chain_land[p.g, part].astype(F32) + self.chain_land[p.groups, part].astype(F32)
            if self.parts == 1:
                self.result[part] = total.astype(self.result.dtype)
            else:
                self.leave[p.g, part] = total.astype(BF16)
        if self.parts > 1:
            for offset in (2, 3, 1):
                self.hand(offset).start()
            self.result[p.m] = self.leave[p.g, p.m]

    def finish(self):
        p = self.place
        for target in range(p.groups):
            self.line(target).wait_send()
            pl.when(p.g != target)(lambda: self.up(target).wait_send())
        if self.parts > 1:
            for offset in (2, 3, 1):
                self.hand(offset).wait()


class LineSum:
    def __init__(self, place, partial, result, refs):
        self.place, self.partial, self.result = place, partial, result
        self.land, self.mine_sem, self.send, self.recv = refs

    @staticmethod
    def scratch(groups, shape):
        home = groups // GROUP
        return [pltpu.VMEM((home, GROUP) + tuple(shape[3:]), BF16)] + [pltpu.SemaphoreType.DMA((home,))] * 3

    def load(self, slot):
        return pltpu.make_async_copy(self.partial.at[slot, :, self.place.b], self.result.at[slot], self.mine_sem.at[slot])

    def line(self, slot):
        p = self.place
        return remote(self.partial.at[slot, :, 1 - p.b], self.land.at[slot], self.send.at[slot], self.recv.at[slot], p.across())

    def start(self):
        for slot in range(self.partial.shape[0]):
            self.line(slot).start()
            self.load(slot).start()

    def finish(self):
        for slot in range(self.partial.shape[0]):
            self.load(slot).wait()
            self.line(slot).wait()
            for part in range(GROUP):
                total = self.result[slot, part].astype(F32) + self.land[slot, part].astype(F32)
                self.result[slot, part] = total.astype(BF16)


class HomeScatter:
    def __init__(self, place, partial, result, refs):
        self.place, self.partial, self.result = place, partial, result
        self.home_land, self.leave, self.home_send, self.home_recv, self.part_send, self.part_recv = refs
        self.home = place.groups // GROUP

    @staticmethod
    def scratch(groups, shape):
        dma = pltpu.SemaphoreType.DMA
        unit = tuple(shape[1:])
        return [
            pltpu.VMEM((groups - 1,) + unit, BF16),
            pltpu.VMEM(unit, BF16),
            dma((shape[0],)),
            dma((groups - 1,)),
            dma((GROUP,)),
            dma((1,)),
        ]

    def home_copy(self, slot):
        p = self.place
        target = p.m * self.home + slot
        index = (p.g - target + p.groups - 1) % p.groups
        return remote(
            self.partial.at[slot], self.home_land.at[index], self.home_send.at[slot], self.home_recv.at[index], p.column(target)
        )

    def landed(self, index):
        p = self.place
        return remote(self.leave, self.home_land.at[index], self.home_send.at[0], self.home_recv.at[index], p.across())

    def start(self):
        p = self.place
        for slot in range(self.home):
            pl.when(p.g != p.m * self.home + slot)(lambda: self.home_copy(slot).start())

    def hand(self, other):
        p = self.place
        return remote(
            self.leave.at[other], self.result, self.part_send.at[other], self.part_recv.at[0], {"g": p.g, "m": other, "b": p.b}
        )

    def last(self):
        p = self.place

        @pl.when(p.m == p.g // self.home)
        def _():
            for index in range(p.groups - 1):
                self.landed(index).wait_recv()
            for part in range(GROUP):
                total = self.partial[p.g % self.home, part].astype(F32)
                for index in range(p.groups - 1):
                    total = total + self.home_land[index, part].astype(F32)
                self.leave[part] = total.astype(BF16)
            for offset in range(1, GROUP):
                self.hand(p.other(offset)).start()
            self.result[...] = self.leave[p.m]

    def finish(self):
        p = self.place
        keeper = p.m == p.g // self.home

        @pl.when(keeper)
        def _():
            for offset in range(1, GROUP):
                self.hand(p.other(offset)).wait_send()

        pl.when(jnp.logical_not(keeper))(lambda: self.hand(p.other(1)).wait_recv())
        for slot in range(self.home):
            pl.when(p.g != p.m * self.home + slot)(lambda: self.home_copy(slot).wait_send())


CHUNKS = 4


class GroupSum:
    def __init__(self, place, partial, refs):
        self.place, self.partial = place, partial
        self.pair_land, self.leave, self.land, self.pair_send, self.pair_recv, self.send, self.recv = refs
        self.size = partial.shape[0] // GROUP
        self.rows = self.size // CHUNKS

    @staticmethod
    def scratch(size, width):
        dma = pltpu.SemaphoreType.DMA
        return [
            pltpu.VMEM((2, size, width), BF16),
            pltpu.VMEM((size, width), BF16),
            pltpu.VMEM((size, width), BF16),
            dma((2, CHUNKS)),
            dma((2, CHUNKS)),
            dma((CHUNKS,)),
            dma((CHUNKS,)),
        ]

    def at(self, chunk, member=0):
        return pl.ds(pl.multiple_of(member * self.size + chunk * self.rows, self.rows), self.rows)

    def pair(self, chunk, far):
        p = self.place
        member = p.other(3 if far else 1)
        slot = 1 if far else 0
        return remote(
            self.partial.at[self.at(chunk, member)], self.pair_land.at[slot, self.at(chunk)], self.pair_send.at[slot, chunk],
            self.pair_recv.at[slot, chunk], p.member(1),
        )

    def cross(self, chunk):
        return remote(
            self.leave.at[self.at(chunk)], self.land.at[self.at(chunk)], self.send.at[chunk], self.recv.at[chunk], self.place.member(2)
        )

    def start(self):
        for chunk in range(CHUNKS):
            self.pair(chunk, True).start()
        for chunk in range(CHUNKS):
            self.pair(chunk, False).start()

    def pass_on(self, chunk):
        self.pair(chunk, True).wait_recv()
        own = self.partial[self.at(chunk, self.place.other(2)), :].astype(F32)
        self.leave[self.at(chunk), :] = (own + self.pair_land[1, self.at(chunk), :].astype(F32)).astype(BF16)
        self.cross(chunk).start()

    def take(self, chunk):
        self.pair(chunk, False).wait_recv()
        self.cross(chunk).wait_recv()
        own = self.partial[self.at(chunk, self.place.m), :].astype(F32)
        return own + self.pair_land[0, self.at(chunk), :].astype(F32) + self.land[self.at(chunk), :].astype(F32)

    def finish(self):
        for chunk in range(CHUNKS):
            self.pair(chunk, True).wait_send()
            self.pair(chunk, False).wait_send()
            self.cross(chunk).wait_send()


class GroupGather:
    def __init__(self, place, whole, refs):
        self.place, self.whole = place, whole
        self.send, self.recv = refs
        self.size = whole.shape[0] // GROUP
        self.rows = self.size // CHUNKS

    @staticmethod
    def scratch():
        dma = pltpu.SemaphoreType.DMA
        return [dma((3, CHUNKS)), dma((3, CHUNKS))]

    def at(self, chunk, member):
        return pl.ds(pl.multiple_of(member * self.size + chunk * self.rows, self.rows), self.rows)

    def copy(self, chunk, way):
        p = self.place
        rows = self.whole.at[self.at(chunk, p.other(2) if way == 2 else p.m)]
        return remote(rows, rows, self.send.at[way, chunk], self.recv.at[way, chunk], p.member(2 if way == 0 else 1))

    def give(self, chunk):
        self.copy(chunk, 0).start()
        self.copy(chunk, 1).start()

    def pass_on(self, chunk):
        self.copy(chunk, 0).wait_recv()
        self.copy(chunk, 2).start()

    def finish(self):
        for chunk in range(CHUNKS):
            self.copy(chunk, 1).wait_recv()
            self.copy(chunk, 2).wait_recv()
            for way in range(3):
                self.copy(chunk, way).wait_send()


def masked(scores, counts):
    return jnp.where(counts, scores * SCALE, NEGATIVE)


class Pauses:
    def __init__(self, *steps):
        self.steps = list(steps)

    def __call__(self):
        if self.steps:
            for act in self.steps.pop(0):
                act()

    def rest(self):
        while self.steps:
            self()


def several(refs, *counts):
    refs = list(refs)
    taken = []
    for count in counts:
        taken.append(refs[:count])
        refs = refs[count:]
    return taken


def attend_kernel(
    groups,
    hops,
    tokens_hbm,
    first_hbm,
    gain_ref,
    doc_query_ref,
    doc_key_ref,
    out_home_ref,
    feed_unit_ref,
    rows_ref,
    query_ref,
    value_ref,
    within_ref,
    map_ref,
    inverse_ref,
    attended_ref,
    low_ref,
    stats_ref,
    moved_ref,
    values_ref,
    out_full_ref,
    feed_full_ref,
    tokens_ref,
    first_ref,
    normed_ref,
    load_sem,
    key_ref,
    leave_ref,
    top_ref,
    total_ref,
    accum_ref,
    key_send,
    key_recv,
    value_send,
    value_recv,
    *sems,
):
    here = Place(groups, feed_full_ref.shape[2])
    tokens_load = pltpu.make_async_copy(tokens_hbm, tokens_ref, load_sem.at[0])
    first_load = pltpu.make_async_copy(first_hbm, first_ref, load_sem.at[1])
    tokens_load.start()
    first_load.start()
    here.meet()
    place, has_next, following = here.g, here.above, here.up()
    home_sems, feed_sems = several(sems, 2, 5)
    out_copies = home_lines(here, out_full_ref, *home_sems)
    feed_gather = Gather(here, None, feed_full_ref, feed_sems)
    feed_gather.spread()
    for copy in out_copies:
        copy.start()
    pauses = Pauses(
        *[
            (functools.partial(feed_gather.step, distance),)
            for distance in range(1, groups)
        ]
    )
    prepared = (rows_ref, query_ref, key_ref, value_ref, within_ref, map_ref, inverse_ref)
    tokens_load.wait()
    for block in range(GROUP):
        normed_ref[tile(block), :] = rms_norm(tokens_ref[tile(block), :].astype(F32), gain_ref[...]).astype(BF16)
    first_load.wait()
    for at, size in [(part * WIDE, WIDE) for part in range(4)] + [(4 * WIDE, EXTRA)]:
        rows_ref[:, pl.ds(at, size)] = dot(normed_ref[...], first_ref[:, pl.ds(at, size)])
    prepare_blocks(0, GROUP // 2, *prepared)
    pauses()
    prepare_blocks(GROUP // 2, GROUP, *prepared)

    def value_copy(source, slot):
        return remote(source, values_ref.at[slot], value_send.at[slot], value_recv.at[slot], following)

    def key_copy(slot):
        return remote(leave_ref.at[slot], moved_ref.at[slot + 1, 0], key_send.at[slot], key_recv.at[slot], following)

    def move(keys, block, head):
        return dot2(keys, map_ref[tile(block), tile(head)]).astype(BF16)

    for head in range(OWN):
        keys = key_ref[tile(0), tile(head)]
        for block in range(1, GROUP):
            moved_ref[0, block, tile(0, block), tile(head)] = keys
            keys = jnp.concatenate([move(keys, block, head), key_ref[tile(block), tile(head)]], 0)
        leave_ref[0, :, tile(head)] = keys

    @pl.when(has_next)
    def _():
        key_copy(0).start()
        value_copy(value_ref, 0).start()


    def row_counts(block, hop, first, count):
        return doc_query_ref[tile(block), :] == doc_key_ref[hop, :, tile(first, count)]

    for block in range(GROUP):
        counts = row_counts(block, 0, 0, block + 1)
        wide = (BLOCK, (block + 1) * BLOCK)
        counts = counts & (iota(0, wide) + block * BLOCK >= iota(1, wide))
        for head in range(OWN):
            scores = within_ref[tile(block), tile(head)]
            if block:
                before = dot(query_ref[tile(block), tile(head)], moved_ref[0, block, tile(0, block), tile(head)], NT)
                scores = jnp.concatenate([before, scores], 1)
            scores = masked(scores, counts)
            top = jnp.max(scores, axis=1, keepdims=True)
            weights = jnp.exp(scores - top)
            top_ref[head, tile(block), :] = jnp.broadcast_to(top, (BLOCK, BLOCK))
            total_ref[head, tile(block), :] = jnp.broadcast_to(jnp.sum(weights, axis=1, keepdims=True), (BLOCK, BLOCK))
            accum_ref[tile(block), tile(head)] = dot(weights.astype(BF16), value_ref[tile(0, block + 1), tile(head)])

    def hop_step(hop, last):
        @pl.when(place >= hop)
        def _():
            key_copy(hop - 1).wait_recv()
            for head in range(OWN):
                keys = moved_ref[hop, 0, :, tile(head)]
                for block in range(GROUP):
                    if last:
                        if block == GROUP - 1:
                            break
                        keys = move(keys[BLOCK:], block, head)
                        moved_ref[hop, block + 1, tile(block + 1, GROUP - 1 - block), tile(head)] = keys
                    else:
                        keys = move(keys, block, head)
                        if block < GROUP - 1:
                            moved_ref[hop, block + 1, :, tile(head)] = keys
                        else:
                            leave_ref[hop, :, tile(head)] = keys
            value_copy(value_ref, hop - 1).wait_recv()
            if not last:

                @pl.when(has_next)
                def _():
                    key_copy(hop).start()
                    value_copy(values_ref.at[hop - 1], hop).start()

            for block in range(GROUP):
                first = block if last else 0
                count = GROUP - first
                counts = row_counts(block, hop, first, count)
                for head in range(OWN):
                    scores = masked(
                        dot(query_ref[tile(block), tile(head)], moved_ref[hop, block, tile(first, count), tile(head)], NT),
                        counts,
                    )
                    old = top_ref[head, tile(block), :]
                    top = jnp.maximum(old, jnp.broadcast_to(jnp.max(scores, axis=1, keepdims=True), (BLOCK, BLOCK)))
                    factor = jnp.exp(old - top)
                    weights = jnp.exp(scores - jnp.concatenate([top] * count, 1))
                    top_ref[head, tile(block), :] = top
                    total_ref[head, tile(block), :] = total_ref[head, tile(block), :] * factor + jnp.sum(
                        weights, axis=1, keepdims=True
                    )
                    accum_ref[tile(block), tile(head)] = accum_ref[tile(block), tile(head)] * factor + dot(
                        weights.astype(BF16), values_ref[hop - 1, tile(first, count), tile(head)]
                    )

    if hops > 2:

        def between(hop, carry):
            hop_step(hop, False)
            return carry

        lax.fori_loop(1, hops, between, 0)
    else:
        for hop in range(1, hops):
            pauses()
            hop_step(hop, False)
    pauses()
    hop_step(hops, True)

    for block in range(GROUP):
        stats = jnp.zeros((BLOCK, BLOCK), F32)
        for head in range(OWN):
            total = total_ref[head, tile(block), :]
            result = accum_ref[tile(block), tile(head)] / total
            attended_ref[tile(block), tile(head)] = result
            low_ref[tile(block), tile(head)] = result.astype(BF16)
            stats = jnp.where(iota(1) == head, top_ref[head, tile(block), :], stats)
            stats = jnp.where(iota(1) == OWN + head, total, stats)
        stats_ref[tile(block), :] = stats

    def settle(slot, carry):
        @pl.when(has_next & (place >= slot))
        def _():
            key_copy(slot).wait_send()
            value_copy(value_ref, slot).wait_send()

        return carry

    lax.fori_loop(0, hops, settle, 0)
    pauses.rest()
    for copy in out_copies:
        copy.wait()
    feed_gather.finish()


def in_vmem(count):
    return [pl.BlockSpec(memory_space=pltpu.VMEM)] * count


def anywhere(count):
    return [pl.BlockSpec(memory_space=pl.ANY)] * count


def shape(kind, *dims):
    return jax.ShapeDtypeStruct(dims, kind)


def communicating(number, name, vmem=58):
    return {
        "compiler_params": pltpu.CompilerParams(collective_id=number, has_side_effects=True, vmem_limit_bytes=vmem << 20),
        "name": name,
    }


def attend(groups, hops, tokens, first, gain, doc_query, doc_key, out_full, feed_full):
    length = tokens.shape[0]
    dma = pltpu.SemaphoreType.DMA
    return pl.pallas_call(
        functools.partial(attend_kernel, groups, hops),
        out_shape=[
            shape(F32, length, first.shape[1]),
            shape(BF16, length, WIDE),
            shape(BF16, length, WIDE),
            shape(F32, length, WIDE),
            shape(F32, length, WIDE),
            shape(F32, length, WIDE),
            shape(F32, length, WIDE),
            shape(BF16, length, WIDE),
            shape(F32, length, BLOCK),
            shape(BF16, hops + 1, GROUP, length, WIDE),
            shape(BF16, hops, length, WIDE),
            shape(BF16, *out_full.shape),
            shape(BF16, *feed_full.shape),
        ],
        in_specs=anywhere(2) + in_vmem(3) + anywhere(2),
        out_specs=in_vmem(11) + anywhere(2),
        scratch_shapes=[
            pltpu.VMEM(tokens.shape, BF16),
            pltpu.VMEM(first.shape, BF16),
            pltpu.VMEM(tokens.shape, BF16),
            dma((2,)),
            pltpu.VMEM((length, WIDE), BF16),
            pltpu.VMEM((hops, length, WIDE), BF16),
            pltpu.VMEM((OWN, length, BLOCK), F32),
            pltpu.VMEM((OWN, length, BLOCK), F32),
            pltpu.VMEM((length, WIDE), F32),
            dma((hops,)),
            dma((hops,)),
            dma((hops,)),
            dma((hops,)),
        ]
        + [dma((groups // GROUP,))] * 2
        + Gather.outside(groups),
        input_output_aliases={5: 11, 6: 12},
        **communicating(1, "attend"),
    )(tokens, first, gain, doc_query, doc_key, out_full, feed_full)


def made_feed(groups, rows):
    return groups == GROUP and rows % 16 == 0


def back_kernel(
    groups,
    hops,
    partial_ref,
    hidden_ref,
    cotangent_ref,
    gain_ref,
    low_ref,
    out_ref,
    query_ref,
    value_ref,
    within_ref,
    map_ref,
    doc_query_ref,
    doc_key_ref,
    attended_ref,
    stats_ref,
    values_hbm,
    moved_hbm,
    rows_hbm,
    inverse_hbm,
    down_partial_ref,
    feed_partial_ref,
    normed_hbm,
    feed_grads_hbm,
    grad_ref,
    down_result_ref,
    rows_grad_ref,
    feed_result_ref,
    out_result_ref,
    grad_low_ref,
    att_grad_ref,
    out_partial_ref,
    moved_ref,
    values_ref,
    extra_ref,
    normed_ref,
    feed_grads_ref,
    made_ref,
    load_sem,
    query_grad_ref,
    key_grad_ref,
    within_grad_ref,
    map_grad_ref,
    value_grad_ref,
    scaled_ref,
    dots_ref,
    direct_ref,
    key_slots_ref,
    value_slots_ref,
    key_send,
    key_recv,
    value_send,
    value_recv,
    *refs,
):
    lines, rows = feed_partial_ref.shape[2:4]
    here = Place(groups, lines)
    make = None
    if made_feed(groups, rows):
        normed_load = pltpu.make_async_copy(normed_hbm, normed_ref, load_sem.at[9])
        feed_load = pltpu.make_async_copy(feed_grads_hbm, feed_grads_ref, load_sem.at[10])
        feed_partial_ref = made_ref
        normed_load.start()
        feed_load.start()

        def make(target):
            span = GROUP * lines * rows
            left = normed_ref[:, pl.ds(pl.multiple_of(target * span, BLOCK), span)].T

            def one(at):
                value = dot(left, feed_grads_ref[:, at])
                for index in range(GROUP * lines):
                    made_ref[target, index // lines, index % lines, :, at] = value[index * rows : (index + 1) * rows].astype(BF16)

            in_tiles(feed_grads_ref.shape[1], one, 4 * BLOCK)

    here.meet()
    place, has_next, previous = here.g, here.above, here.down()
    sum_refs, gather_refs, down_refs, feed_refs, out_refs = several(
        refs,
        7,
        2,
        len(Scatter.scratch(groups, down_partial_ref.shape)),
        len(Scatter.scratch(groups, feed_partial_ref.shape)),
        len(LineSum.scratch(groups, out_partial_ref.shape)),
    )
    sums = GroupSum(here, partial_ref, sum_refs)
    whole = GroupGather(here, grad_low_ref, gather_refs)
    down = Scatter(here, down_partial_ref, down_result_ref, down_refs)
    feed_scatter = Scatter(here, feed_partial_ref, feed_result_ref, feed_refs, make)
    out_lines = LineSum(here, out_partial_ref, out_result_ref, out_refs)
    pauses = Pauses(*[(functools.partial(feed_scatter.step, wave),) for wave in range(1, groups)])

    def load(hop):
        return pltpu.make_async_copy(moved_hbm.at[hop], moved_ref.at[hop % 2], load_sem.at[hop % 2])

    def load_values(hop):
        return pltpu.make_async_copy(values_hbm.at[hop - 1], values_ref.at[hop % 2], load_sem.at[2 + hop % 2])

    loads = [pltpu.make_async_copy(rows_hbm.at[:, pl.ds(4 * WIDE, EXTRA)], extra_ref, load_sem.at[4])]
    for index, panel in enumerate((0, 1, 3)):
        loads.append(pltpu.make_async_copy(rows_hbm.at[:, pl.ds(panel * WIDE, WIDE)], direct_ref.at[index], load_sem.at[5 + index]))
    loads.append(pltpu.make_async_copy(inverse_hbm, direct_ref.at[3], load_sem.at[8]))
    sums.start()
    down.start()
    load(hops).start()
    load_values(hops).start()
    if make is not None:
        normed_load.wait()
        feed_load.wait()
    feed_scatter.start_far(1, 1)
    for chunk in range(CHUNKS):
        sums.pass_on(chunk)
    for chunk in range(CHUNKS):
        back = rms_back(hidden_ref[sums.at(chunk), :], gain_ref[...], sums.take(chunk))
        grad = cotangent_ref[sums.at(chunk), :].astype(F32) + back
        grad_ref[sums.at(chunk), :] = grad
        grad_low_ref[whole.at(chunk, here.m), :] = grad.astype(BF16)
        whole.give(chunk)
    down.step(1)
    for chunk in range(CHUNKS):
        whole.pass_on(chunk)
    if groups > 2:
        down.step(2)
    whole.finish()
    att_grad_ref[...] = dot(grad_low_ref[...], out_ref[...], NT).astype(BF16)
    turned = low_ref[...].T
    units = out_partial_ref.shape[3]

    def out_tile(at):
        value = dot(turned, grad_low_ref[:, at])
        for index in range(WIDE // units):
            slot, member, line = index // (GROUP * lines), index // lines % GROUP, index % lines
            out_partial_ref[slot, member, line, :, at] = value[index * units : (index + 1) * units].astype(BF16)

    in_tiles(out_partial_ref.shape[4], out_tile)
    out_lines.start()
    feed_scatter.start_far(2)
    feed_scatter.act(here.g)
    for wave in range(3, groups):
        down.step(wave)

    def key_copy(hop):
        slot = hop - 1
        return remote(key_slots_ref.at[hop], key_slots_ref.at[slot], key_send.at[slot], key_recv.at[slot], previous)

    def value_copy(hop):
        slot = hop - 1
        return remote(value_slots_ref.at[hop], value_slots_ref.at[slot], value_send.at[slot], value_recv.at[slot], previous)

    map_grad_ref[...] = jnp.zeros_like(map_grad_ref)
    query_grad_ref[...] = jnp.zeros_like(query_grad_ref)
    for block in range(GROUP):
        for head in range(OWN):
            at = (tile(block), tile(head))
            grad = att_grad_ref[at].astype(F32)
            total = stats_ref[tile(block), OWN + head : OWN + head + 1]
            scaled_ref[at] = (grad / total).astype(BF16)
            dots = -jnp.sum(grad * attended_ref[at], axis=1, keepdims=True) / total
            dots_ref[head, tile(block), :] = jnp.broadcast_to(dots, (BLOCK, BLOCK))

    def pair(block, head, scores, counts, values):
        count = scores.shape[1] // BLOCK
        top = stats_ref[tile(block), head : head + 1]
        weights = jnp.exp(masked(scores, counts) - top)
        weight_grad = dot(scaled_ref[tile(block), tile(head)], values, NT)
        dots = jnp.concatenate([dots_ref[head, tile(block), :]] * count, 1)
        return weights, weights * (weight_grad + dots) * SCALE

    def row_counts(block, hop, first, count):
        return doc_query_ref[tile(block), :] == doc_key_ref[hop, :, tile(first, count)]

    def hop_direct(hop, last):
        for head in range(OWN):
            value_grad_ref[:, tile(head)] = jnp.zeros((GROUP * BLOCK, BLOCK), F32)
        for block in range(GROUP):
            first = block if last else 0
            count = GROUP - first
            counts = row_counts(block, hop, first, count)
            for head in range(OWN):
                query = query_ref[tile(block), tile(head)]
                keys = moved_ref[hop % 2, block, tile(first, count), tile(head)]
                weights, grad = pair(
                    block, head, dot(query, keys, NT), counts, values_ref[hop % 2, tile(first, count), tile(head)]
                )
                raw = grad.astype(BF16)
                query_grad_ref[tile(block), tile(head)] += dot(raw, keys)
                direct_ref[block, tile(first, count), tile(head)] = dot(raw, query, TN)
                value_grad_ref[tile(first, count), tile(head)] += dot(
                    weights.astype(BF16), scaled_ref[tile(block), tile(head)], TN
                )

    def collect_map(block, head, keys, grads):
        map_grad_ref[tile(block), tile(head)] += dot2(keys, grads, TN)

    def hop_chain(hop, last):
        for head in range(OWN):
            if last:
                grads = direct_ref[GROUP - 1, tile(GROUP - 1), tile(head)]
                for block in range(GROUP - 2, -1, -1):
                    rows = tile(block + 1, GROUP - 1 - block)
                    collect_map(block, head, moved_ref[hop % 2, block, rows, tile(head)], grads)
                    back = dot3(grads, map_ref[tile(block), tile(head)], NT)
                    direct = direct_ref[block, tile(block, GROUP - block), tile(head)]
                    grads = jnp.concatenate([direct[:BLOCK], direct[BLOCK:] + back], 0)
                key_slots_ref[hop, :, tile(head)] = grads.astype(BF16)
                value_slots_ref[hop, :, tile(head)] = value_grad_ref[:, tile(head)].astype(BF16)
            else:
                grads = key_grad_ref[:, tile(head)]
                for block in range(GROUP - 1, -1, -1):
                    collect_map(block, head, moved_ref[hop % 2, block, :, tile(head)], grads)
                    grads = direct_ref[block, :, tile(head)] + dot3(grads, map_ref[tile(block), tile(head)], NT)
                key_slots_ref[hop, :, tile(head)] = grads.astype(BF16)

    def take(hop):
        @pl.when(has_next)
        def _():
            key_copy(hop).wait_recv()
            key_grad_ref[...] = key_slots_ref[hop - 1].astype(F32)

        @pl.when(jnp.logical_not(has_next))
        def _():
            key_grad_ref[...] = jnp.zeros_like(key_grad_ref)

    load(hops - 1).start()
    load_values(hops - 1).start()
    load(hops).wait()
    load_values(hops).wait()

    @pl.when(place >= hops)
    def _():
        hop_direct(hops, True)
        hop_chain(hops, True)
        key_copy(hops).start()
        value_copy(hops).start()

    down.last()

    def between(hop, pause=None):
        load(hop - 1).start()
        pl.when(jnp.asarray(hop) > 1)(lambda: load_values(hop - 1).start())
        load(hop).wait()
        load_values(hop).wait()
        pl.when(place >= hop)(lambda: hop_direct(hop, False))
        if pause is not None:
            pause()

        @pl.when(place >= hop)
        def _():
            take(hop + 1)
            hop_chain(hop, False)
            key_copy(hop).start()

            @pl.when(has_next)
            def _():
                value_copy(hop + 1).wait_recv()
                for head in range(OWN):
                    value_slots_ref[hop, :, tile(head)] = (
                        value_grad_ref[:, tile(head)] + value_slots_ref[hop, :, tile(head)].astype(F32)
                    ).astype(BF16)

            @pl.when(jnp.logical_not(has_next))
            def _():
                for head in range(OWN):
                    value_slots_ref[hop, :, tile(head)] = value_grad_ref[:, tile(head)].astype(BF16)

            value_copy(hop).start()

    if hops > 2:

        def step(counter, carry):
            between(hops - 1 - counter)
            return carry

        lax.fori_loop(0, hops - 1, step, 0)
    else:
        for hop in range(hops - 1, 0, -1):
            between(hop, pauses)

    load(0).wait()
    for head in range(OWN):
        value_grad_ref[:, tile(head)] = jnp.zeros((GROUP * BLOCK, BLOCK), F32)
    for block in range(GROUP):
        wide = (BLOCK, (block + 1) * BLOCK)
        counts = row_counts(block, 0, 0, block + 1) & (iota(0, wide) + block * BLOCK >= iota(1, wide))
        for head in range(OWN):
            query = query_ref[tile(block), tile(head)]
            scores = within_ref[tile(block), tile(head)]
            if block:
                keys = moved_ref[0, block, tile(0, block), tile(head)]
                scores = jnp.concatenate([dot(query, keys, NT), scores], 1)
            weights, grad = pair(block, head, scores, counts, value_ref[tile(0, block + 1), tile(head)])
            within_grad_ref[tile(block), tile(head)] = grad[:, block * BLOCK :]
            value_grad_ref[tile(0, block + 1), tile(head)] += dot(
                weights.astype(BF16), scaled_ref[tile(block), tile(head)], TN
            )
            if block:
                raw = grad[:, : block * BLOCK].astype(BF16)
                query_grad_ref[tile(block), tile(head)] += dot(raw, keys)
                direct_ref[block, tile(0, block), tile(head)] = dot(raw, query, TN)
    take(1)
    for head in range(OWN):
        grads = key_grad_ref[:, tile(head)]
        for block in range(GROUP - 1, 0, -1):
            key_grad_ref[tile(block), tile(head)] = grads[block * BLOCK :]
            grads = grads[: block * BLOCK]
            collect_map(block, head, moved_ref[0, block, tile(0, block), tile(head)], grads)
            grads = direct_ref[block, tile(0, block), tile(head)] + dot3(grads, map_ref[tile(block), tile(head)], NT)
        key_grad_ref[tile(0), tile(head)] = grads

    @pl.when(has_next)
    def _():
        value_copy(1).wait_recv()
        value_grad_ref[...] += value_slots_ref[0].astype(F32)

    def settle(hop, carry):
        @pl.when(place >= hop)
        def _():
            key_copy(hop).wait_send()
            value_copy(hop).wait_send()

        return carry

    lax.fori_loop(1, hops + 1, settle, 0)
    for copy in loads:
        copy.start()
    for copy in loads:
        copy.wait()
    pauses()
    pieces = (direct_ref, extra_ref, query_grad_ref, key_grad_ref, within_grad_ref, map_grad_ref, value_grad_ref, rows_grad_ref)
    prepare_back_blocks(0, GROUP // 2, *pieces)
    pauses.rest()
    prepare_back_blocks(GROUP // 2, GROUP, *pieces)
    out_lines.finish()
    feed_scatter.last()
    sums.finish()
    down.finish()
    feed_scatter.finish()


def back(groups, hops, partial, hidden, cotangent, gain, low, out, *args):
    values, moved, rows, inverse, down, feed, normed, feed_grads = args[-8:]
    size, width = hidden.shape
    length = partial.shape[0]
    lines, units = feed.shape[2:4]
    out_shape = (groups // GROUP, GROUP, lines, units, width)
    dma = pltpu.SemaphoreType.DMA
    inputs = (partial, hidden, cotangent, gain, low, out) + args
    return pl.pallas_call(
        functools.partial(back_kernel, groups, hops),
        out_shape=[
            shape(F32, size, width),
            shape(F32, 1, *down.shape[3:]),
            shape(BF16, *rows.shape),
            shape(BF16, GROUP, *feed.shape[3:]),
            shape(BF16, groups // GROUP, GROUP, units, width),
        ],
        in_specs=in_vmem(len(inputs) - 8) + anywhere(8),
        out_specs=in_vmem(5),
        scratch_shapes=[
            pltpu.VMEM((length, width), BF16),
            pltpu.VMEM((length, WIDE), BF16),
            pltpu.VMEM(out_shape, BF16),
            pltpu.VMEM((2,) + moved.shape[1:], BF16),
            pltpu.VMEM((2,) + values.shape[1:], BF16),
            pltpu.VMEM((length, EXTRA), F32),
            pltpu.VMEM(normed.shape if made_feed(groups, units) else (16, BLOCK), BF16),
            pltpu.VMEM(feed_grads.shape if made_feed(groups, units) else (16, BLOCK), BF16),
            pltpu.VMEM(feed.shape if made_feed(groups, units) else (1, 1, 1, 16, BLOCK), BF16),
            dma((11,)),
        ]
        + [pltpu.VMEM((length, WIDE), F32)] * 5
        + [
            pltpu.VMEM((length, WIDE), BF16),
            pltpu.VMEM((OWN, length, BLOCK), F32),
            pltpu.VMEM((GROUP, length, WIDE), F32),
            pltpu.VMEM((hops + 1, length, WIDE), BF16),
            pltpu.VMEM((hops + 1, length, WIDE), BF16),
            dma((hops,)),
            dma((hops,)),
            dma((hops,)),
            dma((hops,)),
        ]
        + GroupSum.scratch(size, width)
        + GroupGather.scratch()
        + Scatter.scratch(groups, down.shape)
        + Scatter.scratch(groups, feed.shape)
        + LineSum.scratch(groups, out_shape),
        **communicating(2, "back", 60),
    )(*inputs)


def gather_kernel(
    groups, query_ref, key_ref, value_ref, house_ref, extra_ref, gate_hbm, up_hbm, out_hbm, down_hbm, tokens_ref, cotangent_ref,
    full_ref, feed_full_ref, out_full_ref, down_low_ref, tokens_all_ref, cotangent_all_ref, first_ref, feed_parts_ref, out_low_ref,
    gate_ref, up_ref, out_ref, down_ref, load_sem, send, recv, local, *sems
):
    lines = full_ref.shape[2]
    here = Place(groups, lines)
    loads = [
        pltpu.make_async_copy(source, target, load_sem.at[index])
        for index, (source, target) in enumerate(
            ((out_hbm, out_ref), (gate_hbm, gate_ref), (up_hbm, up_ref), (down_hbm, down_ref))
        )
    ]
    for copy in loads:
        copy.start()
    for member in range(GROUP):
        for part, weight_ref in enumerate((query_ref, key_ref, value_ref, house_ref)):
            first_ref[member, :, pl.ds(part * WIDE, WIDE)] = weight_ref[:, pl.ds(member * WIDE, WIDE)].astype(BF16)
        first_ref[member, :, pl.ds(4 * WIDE, EXTRA)] = extra_ref[member]
    here.meet()
    first_sems, feed_sems, out_sems = several(sems, 8, 3, 5)
    first = Gather(here, first_ref, full_ref, first_sems)
    feed = Gather(here, feed_parts_ref, feed_full_ref, feed_sems)
    out = HomeGather(here, out_low_ref, out_full_ref, out_sems)
    first.start()
    loads[0].wait()
    out_low_ref[...] = out_ref[...].astype(BF16)
    out.start()
    size = tokens_ref.shape[0]
    own = pl.ds(pl.multiple_of(here.m * size, size), size)
    copies = []
    for index, (source, target) in enumerate(((tokens_ref, tokens_all_ref), (cotangent_ref, cotangent_all_ref))):
        copies.append(pltpu.make_async_copy(source, target.at[own], local.at[index]))
        for offset in (2, 3, 1):
            copies.append(
                remote(source, target.at[own], send.at[index, offset], recv.at[index, offset], here.member(offset))
            )
    for copy in copies:
        copy.start()
    for copy in loads[1:]:
        copy.wait()
    down_low_ref[...] = down_ref[...].astype(BF16)
    own_units = feed_parts_ref.shape[2] // 2
    for at, weight_ref in ((0, gate_ref), (own_units, up_ref)):
        if len(weight_ref.shape) == 3:
            feed_parts_ref[:, :, at : at + own_units] = weight_ref[...]
        else:
            for member in range(GROUP):
                for index in range(groups * lines):
                    block = (index // lines * GROUP + member) * lines + index % lines
                    feed_parts_ref[member, :, pl.ds(at + index * BLOCK, BLOCK)] = weight_ref[:, tile(block)].astype(BF16)
    feed.start()
    first.settle()
    first.spread()
    out.spread()
    for distance in range(1, groups):
        first.step(distance)
        out.step(distance)
    feed.settle()
    out.finish()
    for copy in copies:
        copy.wait()
    first.finish()


def gather_first(groups, lines, first, extra, gate, up, out, down, tokens, cotangent):
    dma = pltpu.SemaphoreType.DMA
    size, width = tokens.shape
    rows = out.shape[0]
    units = 2 * down.shape[0] * groups * lines
    return pl.pallas_call(
        functools.partial(gather_kernel, groups),
        out_shape=[
            shape(BF16, groups, GROUP, lines, rows, 4 * WIDE + EXTRA),
            shape(BF16, groups, GROUP, lines, rows, units),
            shape(BF16, groups // GROUP, GROUP, lines, rows, width),
            shape(BF16, *down.shape),
            shape(BF16, GROUP * size, width),
            shape(BF16, GROUP * size, width),
        ],
        in_specs=in_vmem(5) + anywhere(6),
        out_specs=anywhere(3) + in_vmem(1) + anywhere(2),
        scratch_shapes=[
            pltpu.VMEM((GROUP, rows, 4 * WIDE + EXTRA), BF16),
            pltpu.VMEM((GROUP, rows, units), BF16),
            pltpu.VMEM((rows, width), BF16),
            pltpu.VMEM(gate.shape, gate.dtype),
            pltpu.VMEM(up.shape, up.dtype),
            pltpu.VMEM(out.shape, F32),
            pltpu.VMEM(down.shape, F32),
            dma((4,)),
            dma((2, GROUP)),
            dma((2, GROUP)),
            dma((2,)),
        ]
        + Gather.inside()
        + Gather.outside(groups)
        + Gather.inside()
        + HomeGather.scratch(groups),
        **communicating(0, "gather_first", 60),
    )(*first, extra, gate, up, out, down, tokens, cotangent)


def rms_norm(values, gain):
    return values * lax.rsqrt(jnp.mean(values * values, axis=-1, keepdims=True) + EPSILON) * gain


def rms_back(values, gain, grad):
    scale = lax.rsqrt(jnp.mean(values * values, axis=-1, keepdims=True) + EPSILON)
    straight = values * scale
    lifted = grad * gain
    return scale * (lifted - straight * jnp.mean(lifted * straight, axis=-1, keepdims=True))


def in_tiles(size, act, step=2 * BLOCK):
    def one(index, carry):
        act(pl.ds(pl.multiple_of(index * step, step), step))
        return carry

    lax.fori_loop(0, size // step, one, 0)


def branch_kernel(
    groups, partial_ref, tokens_ref, gain_ref, down_ref, feed_hbm, cotangent_hbm, hidden_ref, normed_ref, active_ref, feed_grads_ref,
    down_full_ref, gate_slope_ref, up_slope_ref, cotangent_ref, down_rows_ref, feed_ref, feed_sem, *refs
):
    here = Place(groups, down_full_ref.shape[1])
    here.meet()
    sum_refs, gather_refs, down_refs = several(refs, 7, 2, 8)
    total = GroupSum(here, partial_ref, sum_refs)
    whole = GroupGather(here, normed_ref, gather_refs)
    down = Gather(here, down_ref, down_full_ref, down_refs, mixed=False)
    pauses = Pauses(*[(functools.partial(down.step, distance),) for distance in range(1, groups)])
    total.start()
    down.start()
    down.settle()
    down.spread()
    feed_copy = pltpu.make_async_copy(feed_hbm, feed_ref, feed_sem.at[0])
    feed_copy.start()
    cotangent_copy = pltpu.make_async_copy(cotangent_hbm, cotangent_ref, feed_sem.at[1])
    cotangent_copy.start()
    for chunk in range(CHUNKS):
        total.pass_on(chunk)
    pauses()
    for chunk in range(CHUNKS):
        hidden = tokens_ref[total.at(chunk), :].astype(F32) + total.take(chunk)
        hidden_ref[total.at(chunk), :] = hidden
        normed_ref[whole.at(chunk, here.m), :] = rms_norm(hidden, gain_ref[...]).astype(BF16)
        whole.give(chunk)
    pauses()
    for chunk in range(CHUNKS):
        whole.pass_on(chunk)
    pauses.rest()
    feed_copy.wait()
    whole.finish()
    units = active_ref.shape[1]

    def act(at):
        normed = normed_ref[...]
        gate = dot(normed, feed_ref[:, at])
        up = dot(normed, feed_ref[:, pl.ds(pl.multiple_of(at.start + units, BLOCK), at.size)])
        sigmoid = jax.nn.sigmoid(gate)
        silu = gate * sigmoid
        active_ref[:, at] = (silu * up).astype(BF16)
        gate_slope_ref[:, at] = up * (sigmoid * (1.0 + gate * (1.0 - sigmoid)))
        up_slope_ref[:, at] = silu

    in_tiles(units, act)
    total.finish()
    cotangent_copy.wait()
    down.finish()
    down_copy = pltpu.make_async_copy(down_full_ref, down_rows_ref, feed_sem.at[2])
    down_copy.start()
    down_copy.wait()
    down_rows = down_rows_ref[...].reshape(units, down_rows_ref.shape[3])
    step = 2 * BLOCK
    for index in range(units // step):
        at = pl.ds(index * step, step)
        grad = dot(cotangent_ref[...], down_rows[index * step : (index + 1) * step], NT)
        feed_grads_ref[:, at] = (grad * gate_slope_ref[:, at]).astype(BF16)
        feed_grads_ref[:, pl.ds(units + index * step, step)] = (grad * up_slope_ref[:, at]).astype(BF16)


def branch(groups, lines, partial, tokens, gain, down, feed, cotangent):
    size, width = tokens.shape
    length, units = partial.shape[0], feed.shape[1] // 2
    dma = pltpu.SemaphoreType.DMA
    return pl.pallas_call(
        functools.partial(branch_kernel, groups),
        out_shape=[
            shape(F32, size, width),
            shape(BF16, length, width),
            shape(BF16, length, units),
            shape(BF16, length, 2 * units),
            shape(BF16, groups, lines, *down.shape),
        ],
        in_specs=in_vmem(3) + anywhere(3),
        out_specs=in_vmem(4) + anywhere(1),
        scratch_shapes=[
            pltpu.VMEM((length, units), F32),
            pltpu.VMEM((length, units), F32),
            pltpu.VMEM(cotangent.shape, BF16),
            pltpu.VMEM((groups, lines) + down.shape, BF16),
            pltpu.VMEM(feed.shape, BF16),
            dma((3,)),
        ]
        + GroupSum.scratch(size, width)
        + GroupGather.scratch()
        + Gather.inside()
        + Gather.outside(groups),
        **communicating(3, "branch", 48),
    )(partial, tokens, gain, down, feed, cotangent)


def finish_kernel(
    groups, first_partial_ref, wide_hbm, first_hbm, down_hbm, rows_grad_ref, active_ref, out_lines_ref, tokens_ref, hidden_ref, grad_ref, gain_ref,
    first_result_ref, out_result_ref, tokens_grad_ref, output_ref, first_full_ref, down_full_ref, normed_partial_ref,
    output_partial_ref, wide_ref, normed_ref, made_ref, load_sem, *refs
):
    lines, rows = first_partial_ref.shape[2:4]
    here = Place(groups, lines)
    made = rows % 16 == 0
    if made:
        first_partial_ref = made_ref
    wide_copy = pltpu.make_async_copy(wide_hbm, wide_ref, load_sem.at[2])
    wide_copy.start()
    here.meet(column=True)

    def make(target):
        span = GROUP * lines * rows
        left = normed_ref[:, pl.ds(pl.multiple_of(target * span, BLOCK), span)].T
        for at, size in [(part * WIDE, WIDE) for part in range(4)] + [(4 * WIDE, EXTRA)]:
            value = dot(left, rows_grad_ref[:, pl.ds(at, size)])
            for index in range(GROUP * lines):
                made_ref[target, index // lines, index % lines, :, pl.ds(at, size)] = value[index * rows : (index + 1) * rows].astype(BF16)

    first_refs, out_refs, normed_refs, output_refs = several(
        refs, len(Scatter.scratch(groups, first_partial_ref.shape)), len(HomeScatter.scratch(groups, out_lines_ref.shape)), 7, 7
    )
    first = Scatter(here, first_partial_ref, first_result_ref, first_refs, make if made else None)
    out = HomeScatter(here, out_lines_ref, out_result_ref, out_refs)
    normed = GroupSum(here, normed_partial_ref, normed_refs)
    output = GroupSum(here, output_partial_ref, output_refs)
    first_copy = pltpu.make_async_copy(first_hbm, first_full_ref, load_sem.at[0])
    down_copy = pltpu.make_async_copy(down_hbm, down_full_ref, load_sem.at[1])
    first_copy.start()
    down_copy.start()
    wide_copy.wait()
    out.start()
    if made:
        for block in range(GROUP):
            normed_ref[tile(block), :] = rms_norm(wide_ref[tile(block), :].astype(F32), gain_ref[...]).astype(BF16)
    first.start()
    first_copy.wait()

    def normed_tile(at):
        normed_partial_ref[:, at] = dot(rows_grad_ref[...], first_full_ref[at, :], NT).astype(BF16)

    in_tiles(normed_partial_ref.shape[1], normed_tile)
    normed.start()
    down_copy.wait()
    for chunk in range(CHUNKS):
        normed.pass_on(chunk)

    def output_tile(at):
        output_partial_ref[:, at] = dot(active_ref[...], down_full_ref[:, at]).astype(BF16)

    in_tiles(output_partial_ref.shape[1], output_tile)
    output.start()
    first.step(1)
    for chunk in range(CHUNKS):
        output.pass_on(chunk)
    for chunk in range(CHUNKS):
        back = rms_back(tokens_ref[normed.at(chunk), :].astype(F32), gain_ref[...], normed.take(chunk))
        tokens_grad_ref[normed.at(chunk), :] = (grad_ref[normed.at(chunk), :] + back).astype(BF16)
    if groups > 2:
        first.step(2)
    for chunk in range(CHUNKS):
        output_ref[output.at(chunk), :] = (hidden_ref[output.at(chunk), :] + output.take(chunk)).astype(BF16)
    for wave in range(3, groups):
        first.step(wave)
    out.last()
    normed.finish()
    output.finish()
    first.last()
    out.finish()
    first.finish()


def finish(groups, first_partial, wide, first, down, rows_grad, active, out_lines, tokens, hidden, grad, gain):
    size, width = tokens.shape
    length = rows_grad.shape[0]
    made = first_partial.shape if first_partial.shape[3] % 16 == 0 else (1, 1, 1, 16, BLOCK)
    return pl.pallas_call(
        functools.partial(finish_kernel, groups),
        out_shape=[
            shape(BF16, GROUP, *first_partial.shape[3:]),
            shape(BF16, *out_lines.shape[2:]),
            shape(BF16, size, width),
            shape(BF16, size, width),
        ],
        in_specs=anywhere(4) + in_vmem(7),
        out_specs=in_vmem(4),
        scratch_shapes=[
            pltpu.VMEM(first.shape, BF16),
            pltpu.VMEM(down.shape, BF16),
            pltpu.VMEM((length, width), BF16),
            pltpu.VMEM((length, width), BF16),
            pltpu.VMEM(wide.shape, BF16),
            pltpu.VMEM(wide.shape, BF16),
            pltpu.VMEM(made, BF16),
            pltpu.SemaphoreType.DMA((3,)),
        ]
        + Scatter.scratch(groups, first_partial.shape)
        + HomeScatter.scratch(groups, out_lines.shape)
        + GroupSum.scratch(size, width)
        + GroupSum.scratch(size, width),
        **communicating(5, "finish"),
    )(first_partial, wide, first, down, rows_grad, active, out_lines, tokens, hidden, grad, gain)


def layout_kernel(groups, lines, first_ref, feed_ref, out_ref, beta_ref, gains_ref, down_ref, tokens_ref, result_ref, *refs):
    weights, targets = refs[:6], refs[6:]
    query_out, key_out, value_out, house_out, out_out, down_out, tokens_out, result_out, norm_gain_out, beta_out = targets[:10]
    rows = gains_ref.shape[1]
    down_out[...] = down_ref[0]
    tokens_out[...] = tokens_ref[...]
    result_out[...] = result_ref[...]

    def as_row(column):
        return jnp.broadcast_to(column, (rows, BLOCK)).T[0:1, :]

    first_sum = jnp.zeros((rows, WIDE), F32)
    extra_sum = jnp.zeros((rows, EXTRA), F32)
    for member in range(GROUP):
        for part, target_ref in enumerate((query_out, key_out, value_out, house_out)):
            value = first_ref[member, :, pl.ds(part * WIDE, WIDE)].astype(F32)
            at = pl.ds(member * WIDE, WIDE)
            target_ref[:, at] = value
            first_sum = first_sum + value * weights[part][:, at].astype(BF16).astype(F32)
        extra = first_ref[member, :, pl.ds(4 * WIDE, EXTRA)].astype(F32)
        extra_sum = extra_sum + extra * beta_ref[member].astype(F32)
        beta_out[member] = extra.T[0:OWN, :]
    total = jnp.sum(first_sum, axis=1, keepdims=True) + jnp.sum(extra_sum, axis=1, keepdims=True)
    norm_gain_out[...] = as_row(total) / gains_ref[0:1, :]
    out_out[...] = out_ref[...].astype(F32)
    if len(targets) > 10:
        gate_out, up_out, ffn_gain_out = targets[10:]
        units = feed_ref.shape[2] // 2
        feed_sum = jnp.zeros((rows, BLOCK), F32)
        for at, weight_ref, target_ref in ((0, weights[4], gate_out), (units, weights[5], up_out)):
            for member in range(GROUP):
                for index in range(groups * lines):
                    block = (index // lines * GROUP + member) * lines + index % lines
                    value = feed_ref[member, :, pl.ds(at + index * BLOCK, BLOCK)].astype(F32)
                    target_ref[:, tile(block)] = value
                    feed_sum = feed_sum + value * weight_ref[:, tile(block)].astype(BF16).astype(F32)
        ffn_gain_out[...] = as_row(jnp.sum(feed_sum, axis=1, keepdims=True)) / gains_ref[1:2, :]


def layout(groups, lines, whole_tiles, first, feed, out, beta, gains, down, tokens, result, weights):
    rows, width = out.shape
    outs = [shape(F32, rows, width)] * 5 + [
        shape(F32, *down.shape[1:]),
        shape(BF16, *tokens.shape),
        shape(BF16, *tokens.shape),
        shape(F32, 1, rows),
        shape(F32, GROUP, OWN, rows),
    ]
    if whole_tiles:
        outs = outs + [shape(F32, *weights[4].shape)] * 2 + [shape(F32, 1, rows)]
    return pl.pallas_call(
        functools.partial(layout_kernel, groups, lines),
        out_shape=outs,
        in_specs=in_vmem(8 + len(weights)),
        out_specs=in_vmem(len(outs)),
        compiler_params=pltpu.CompilerParams(vmem_limit_bytes=60 << 20),
        name="layout",
    )(first, feed, out, beta, gains, down, tokens, result, *weights)


def on_device(
    tokens,
    doc_ids,
    norm_gain,
    query_weight,
    key_weight,
    value_weight,
    house_weight,
    beta_weight,
    out_weight,
    ffn_gain,
    gate_weight,
    up_weight,
    down_weight,
    cotangent,
):
    groups, batch = lax.axis_size("g"), lax.axis_size("b")
    devices = groups * GROUP * batch
    rows, width = query_weight.shape
    hidden_rows = down_weight.shape[0]
    hidden_own = gate_weight.shape[1] // GROUP
    block_rows = tokens.shape[1]
    hops = groups // 2
    doc_columns = -(-block_rows // rows)
    place, line = lax.axis_index("g"), lax.axis_index("b")

    def columns(weight):
        return jnp.transpose(weight.astype(BF16).reshape(rows, GROUP, -1), (1, 0, 2))

    docs = jnp.pad(doc_ids[0].astype(BF16), (0, rows * doc_columns - block_rows)).reshape(rows, doc_columns)
    same = jnp.concatenate([norm_gain.astype(BF16)[:, None], ffn_gain.astype(BF16)[:, None], docs], 1)
    same = jnp.broadcast_to(same[None], (GROUP,) + same.shape)
    same = jnp.pad(same, ((0, 0), (0, 0), (0, EXTRA - OWN - same.shape[2])))
    extra = jnp.concatenate([columns(beta_weight), same], 2)

    def unit_columns(weight):
        parts = weight.astype(BF16).reshape(rows, groups, GROUP, batch, hidden_rows)
        return jnp.transpose(parts, (2, 0, 1, 3, 4)).reshape(GROUP, rows, hidden_own)

    whole_tiles = hidden_rows == BLOCK
    feed_weights = (gate_weight, up_weight) if whole_tiles else (unit_columns(gate_weight), unit_columns(up_weight))
    first, feed, out_full, down_low, tokens_all, cotangent_all = gather_first(
        groups, batch, (query_weight, key_weight, value_weight, house_weight), extra, *feed_weights, out_weight, down_weight, tokens[0], cotangent[0]
    )
    first = first.reshape(width, -1)

    extra = first[:, 4 * WIDE :]
    gain_one = extra[:, OWN].astype(F32)[None]
    gain_two = extra[:, OWN + 1].astype(F32)[None]
    docs = extra[:, OWN + 2 : OWN + 2 + doc_columns].astype(jnp.int32)
    docs = docs.reshape(devices, -1)[:, :block_rows].reshape(groups, GROUP, batch, block_rows)
    docs = lax.dynamic_index_in_dim(docs, line, 2, keepdims=False).reshape(groups, GROUP * block_rows)
    doc_key = jnp.stack(
        [
            jnp.where(place >= hop, lax.dynamic_index_in_dim(docs, jnp.maximum(place - hop, 0), 0, keepdims=False), -1)
            for hop in range(hops + 1)
        ]
    )[:, None, :]
    doc_query = lax.dynamic_index_in_dim(docs, place, 0, keepdims=False)[:, None]

    (projected, query, value, within, maps, inverse, attended, attended_low, stats, moved, values, out_full, feed) = attend(
        groups, hops, tokens_all, first, gain_one, doc_query, doc_key, out_full, feed
    )
    out_full = out_full.reshape(WIDE, width)
    feed = feed.reshape(width, -1)
    hidden, normed_two, active, feed_grads, down_full = branch(
        groups, batch, dot(attended_low, out_full).astype(BF16), tokens[0], gain_two, down_low, feed, cotangent_all
    )
    down_full = down_full.reshape(hidden_own, width)
    down_partial = dot(active, cotangent_all, TN).astype(BF16).reshape(groups, 1, batch, hidden_rows, width)
    if made_feed(groups, rows):
        feed_partial = feed.reshape(groups, GROUP, batch, rows, -1)
    else:
        feed_partial = dot(normed_two, feed_grads, TN).astype(BF16).reshape(groups, GROUP, batch, rows, -1)
    hidden_grad, down_weight_grad, rows_grad, feed_grad, out_lines = back(
        groups, hops, dot(feed_grads, feed, NT).astype(BF16), hidden, cotangent[0], gain_two, attended_low, out_full, query, value,
        within, maps, doc_query, doc_key, attended, stats, values, moved, projected, inverse, down_partial, feed_partial,
        normed_two, feed_grads,
    )
    partial_shape = (groups, GROUP, batch, rows, rows_grad.shape[1])
    if rows % 16 == 0:
        first_partial = first.reshape(partial_shape)
    else:
        normed = rms_norm(tokens_all.astype(F32), gain_one).astype(BF16)
        first_partial = dot(normed, rows_grad, TN).astype(BF16).reshape(partial_shape)
    beta_parts = jnp.pad(columns(beta_weight), ((0, 0), (0, 0), (0, EXTRA - OWN)))
    weights = (query_weight, key_weight, value_weight, house_weight) + feed_weights
    first_grad, out_grad, tokens_grad, output = finish(
        groups, first_partial, tokens_all, first, down_full, rows_grad, active, out_lines, tokens[0], hidden, hidden_grad, gain_one
    )
    gains = jnp.stack([norm_gain, ffn_gain]).astype(BF16).astype(F32)
    results = layout(
        groups, batch, whole_tiles, first_grad, feed_grad, out_grad, beta_parts, gains, down_weight_grad, tokens_grad, output, weights
    )
    query_weight_grad, key_weight_grad, value_weight_grad, house_weight_grad, out_weight_grad, down_weight_grad = results[:6]
    tokens_grad, output, norm_gain_grad, beta_weight_grad = results[6:10]
    output, tokens_grad = output[None], tokens_grad[None]
    beta_weight_grad = beta_weight_grad.reshape(-1, rows).T
    def unit_whole(parts):
        parts = parts.astype(F32).reshape(GROUP, rows, groups, batch, hidden_rows)
        return jnp.transpose(parts, (1, 2, 0, 3, 4)).reshape(rows, -1)

    if whole_tiles:
        gate_weight_grad, up_weight_grad, ffn_gain_grad = results[10:]
        ffn_gain_grad = ffn_gain_grad[0]
    else:
        gate_weight_grad, up_weight_grad = unit_whole(feed_grad[:, :, :hidden_own]), unit_whole(feed_grad[:, :, hidden_own:])
        feed_sum = jnp.sum(gate_weight_grad * gate_weight.astype(BF16).astype(F32), axis=1) + jnp.sum(
            up_weight_grad * up_weight.astype(BF16).astype(F32), axis=1
        )
        ffn_gain_grad = feed_sum / gains[1]
    return (
        output,
        tokens_grad,
        norm_gain_grad[0],
        query_weight_grad,
        key_weight_grad,
        value_weight_grad,
        house_weight_grad,
        beta_weight_grad,
        out_weight_grad,
        ffn_gain_grad,
        gate_weight_grad,
        up_weight_grad,
        down_weight_grad,
    )


def solution(mesh):
    groups = mesh.shape["seq"] // GROUP
    inner = Mesh(mesh.devices.reshape(groups, GROUP, mesh.shape["batch"]), ("g", "m", "b"))
    line = P("b", ("g", "m"), None)
    vector = P(("g", "m", "b"))
    matrix = P(("g", "m", "b"), None)
    in_specs = (line, P("b", ("g", "m")), vector) + (matrix,) * 6 + (vector,) + (matrix,) * 3 + (line,)
    out_specs = (line, line, vector) + (matrix,) * 6 + (vector,) + (matrix,) * 3
    return jax.shard_map(on_device, mesh=inner, in_specs=in_specs, out_specs=out_specs, check_vma=False)
```

```python
import functools

import jax
import jax.numpy as jnp
from jax import lax
from jax.experimental import pallas as pl
from jax.experimental.pallas import tpu as pltpu
from jax.sharding import Mesh
from jax.sharding import PartitionSpec as P

HEADS = 12
HEAD_DIM = 128
GROUP = 4
OWN = HEADS // GROUP
WIDE = OWN * HEAD_DIM
BLOCK = 128
EXTRA = 128
EPSILON = 1e-06
NEGATIVE = -1e30
SCALE = HEAD_DIM ** (-0.5)
MESH = pl.DeviceIdType.MESH
F32 = jnp.float32
BF16 = jnp.bfloat16
NN = (((1,), (0,)), ((), ()))
NT = (((1,), (1,)), ((), ()))
TN = (((0,), (0,)), ((), ()))


def dot(left, right, dims=NN):
    return lax.dot_general(left, right, dims, preferred_element_type=F32)


def split(value):
    high = value.astype(BF16)
    return high, (value - high.astype(F32)).astype(BF16)


def dot3(left, right, dims=NN):
    left_high, left_low = split(left)
    right_high, right_low = split(right)
    return dot(left_high, right_high, dims) + (
        dot(left_high, right_low, dims) + dot(left_low, right_high, dims)
    )


def dot2(left, right, dims=NN):
    high, low = split(right)
    return dot(left, high, dims) + dot(left, low, dims)


def tile(index, count=1):
    return pl.ds(index * BLOCK, count * BLOCK)


def iota(axis, shape=(BLOCK, BLOCK)):
    return lax.broadcasted_iota(jnp.int32, shape, axis)


def invert(strict):
    row, col = iota(0), iota(1)
    eye = jnp.where(row == col, 1.0, 0.0)

    def part(size):
        return (row // (2 * size) == col // (2 * size)) & (row // size > col // size)

    totals = [eye - jnp.where(part(1), value, 0.0) for value in strict]
    size = 2
    while size < BLOCK:
        mask = part(size)
        pieces = [jnp.where(mask, value, 0.0) for value in strict]
        inner = [dot3(piece, total) for piece, total in zip(pieces, totals)]
        outer = [dot3(total, value) for total, value in zip(totals, inner)]
        totals = [total - value for total, value in zip(totals, outer)]
        size *= 2
    return totals


def unit_of(house):
    scale = lax.rsqrt(jnp.sum(house * house, axis=-1, keepdims=True) + EPSILON)
    return house * scale, scale


def products(query, key, unit):
    both = dot3(jnp.concatenate([unit, query], 0), jnp.concatenate([unit, key], 0), NT)
    return both[:BLOCK, :BLOCK], both[:BLOCK, BLOCK:], both[BLOCK:, :BLOCK], both[BLOCK:, BLOCK:]


def prepare_blocks(first, last, rows_ref, query_ref, key_ref, value_ref, within_ref, map_ref, inverse_ref):
    row, col = iota(0), iota(1)

    def one_block(block, carry):
        at = tile(block)
        kept, strict = [], []
        for head in range(OWN):
            query, key, value, house = [
                rows_ref[at, pl.ds(part * WIDE + head * BLOCK, BLOCK)] for part in range(4)
            ]
            rate = rows_ref[at, pl.ds(4 * WIDE, EXTRA)][:, head : head + 1]
            value_ref[at, tile(head)] = value.astype(BF16)
            unit, _ = unit_of(house)
            strength = 2.0 * jax.nn.sigmoid(rate)
            unit_unit, unit_key, query_unit, query_key = products(query, key, unit)
            strict.append(jnp.where(row > col, strength * unit_unit, 0.0))
            reach = jnp.where(row > col, strength * unit_key, 0.0)
            project = jnp.where(row >= col, query_unit, 0.0)
            kept.append((query, key, unit, strength, reach, project, query_key))
        inverses = invert(strict)
        for head in range(OWN):
            query, key, unit, strength, reach, project, query_key = kept[head]
            inverse = inverses[head]
            solved = dot3(inverse, jnp.concatenate([strength * unit, reach], 1))
            from_query = dot3(project, solved)
            from_unit = dot3(solved, unit, TN)
            query_ref[at, tile(head)] = (query - from_query[:, :BLOCK]).astype(BF16)
            within_ref[at, tile(head)] = query_key - from_query[:, BLOCK:]
            map_ref[at, tile(head)] = jnp.where(row == col, 1.0, 0.0) - from_unit[:BLOCK]
            key_ref[at, tile(head)] = (key - from_unit[BLOCK:]).astype(BF16)
            inverse_ref[at, tile(head)] = inverse
        return carry

    lax.fori_loop(first, last, one_block, 0)


def prepare_back_blocks(first, last, panels_ref, extra_ref, query_grad_ref, key_grad_ref, within_grad_ref, map_grad_ref, value_grad_ref, out_ref):
    row, col = iota(0), iota(1)

    def one_block(block, carry):
        at = tile(block)
        rates = jnp.zeros((BLOCK, EXTRA), F32)
        for head in range(OWN):
            query, key, house, inverse = [panels_ref[part, at, tile(head)] for part in range(4)]
            rate = extra_ref[at, :][:, head : head + 1]
            query_grad = query_grad_ref[at, tile(head)]
            key_grad = key_grad_ref[at, tile(head)]
            within_grad = within_grad_ref[at, tile(head)]
            map_grad = map_grad_ref[at, tile(head)]
            unit, scale = unit_of(house)
            strength = 2.0 * jax.nn.sigmoid(rate)
            unit_unit, unit_key, query_unit, query_key = products(query, key, unit)
            reach = jnp.where(row > col, strength * unit_key, 0.0)
            project = jnp.where(row >= col, query_unit, 0.0)
            solved = dot3(inverse, jnp.concatenate([strength * unit, reach], 1))
            both_grad = jnp.concatenate([query_grad, within_grad], 1)
            project_grad = jnp.where(row >= col, -dot3(both_grad, solved, NT), 0.0)
            solved_grad = -(
                dot3(project, both_grad, TN)
                + dot3(unit, jnp.concatenate([map_grad, key_grad], 0), NT)
            )
            given_grad = dot3(inverse, solved_grad, TN)
            strict_grad = jnp.where(row > col, -dot3(given_grad, solved, NT), 0.0)
            scaled_grad = given_grad[:, :BLOCK]
            reach_grad = jnp.where(row > col, given_grad[:, BLOCK:], 0.0)
            strength_grad = jnp.sum(
                scaled_grad * unit + reach_grad * unit_key + strict_grad * unit_unit, axis=1, keepdims=True
            )
            reach_part = strength * reach_grad
            inner_part = strength * strict_grad
            unit_grad = (
                strength * scaled_grad
                + dot3(reach_part, key)
                + dot3(inner_part + inner_part.T, unit)
                + dot3(project_grad, query, TN)
                - dot3(solved[:, :BLOCK], map_grad)
                - dot3(solved[:, BLOCK:], key_grad)
            )
            query_out = query_grad + dot3(within_grad, key) + dot3(project_grad, unit)
            key_out = key_grad + dot3(within_grad, query, TN) + dot3(reach_part, unit, TN)
            house_out = scale * (unit_grad - unit * jnp.sum(unit * unit_grad, axis=1, keepdims=True))
            rate_out = strength_grad * strength * (1.0 - 0.5 * strength)
            rates = jnp.where(iota(1, (BLOCK, EXTRA)) == head, rate_out, rates)
            out_ref[at, pl.ds(head * BLOCK, BLOCK)] = query_out.astype(BF16)
            out_ref[at, pl.ds(WIDE + head * BLOCK, BLOCK)] = key_out.astype(BF16)
            out_ref[at, pl.ds(2 * WIDE + head * BLOCK, BLOCK)] = value_grad_ref[at, tile(head)].astype(BF16)
            out_ref[at, pl.ds(3 * WIDE + head * BLOCK, BLOCK)] = house_out.astype(BF16)
        out_ref[at, pl.ds(4 * WIDE, EXTRA)] = rates.astype(BF16)
        return carry

    lax.fori_loop(first, last, one_block, 0)


def remote(source, target, send, recv, device):
    return pltpu.make_async_remote_copy(
        src_ref=source, dst_ref=target, send_sem=send, recv_sem=recv, device_id=device, device_id_type=MESH
    )


class Place:
    def __init__(self, groups, lines):
        self.groups, self.lines = groups, lines
        self.g, self.m, self.b = lax.axis_index("g"), lax.axis_index("m"), lax.axis_index("b")
        self.below, self.above = self.g > 0, self.g < groups - 1

    def other(self, offset):
        return {1: self.m + 1 - 2 * (self.m % 2), 2: (self.m + 2) % GROUP, 3: GROUP - 1 - self.m}[offset]

    def member(self, offset):
        return {"g": self.g, "m": self.other(offset), "b": self.b}

    def up(self):
        return {"g": self.g + 1, "m": self.m, "b": self.b}

    def down(self):
        return {"g": self.g - 1, "m": self.m, "b": self.b}

    def across(self):
        return {"g": self.g, "m": self.m, "b": 1 - self.b}

    def column(self, group):
        return {"g": group, "m": self.m, "b": self.b}

    def meet(self, column=False):
        barrier = pltpu.get_barrier_semaphore()

        def greet(device):
            pl.semaphore_signal(barrier, 1, device_id=device, device_id_type=MESH)

        for offset in range(1, GROUP):
            greet(self.member(offset))
        greet(self.across())
        if column:
            for step in range(1, self.groups):
                greet(self.column((self.g + step) % self.groups))
            count = GROUP + self.groups - 1
        else:
            pl.when(self.above)(lambda: greet(self.up()))
            pl.when(self.below)(lambda: greet(self.down()))
            count = GROUP + self.above.astype(jnp.int32) + self.below.astype(jnp.int32)
        pl.semaphore_wait(barrier, count)


class Gather:
    def __init__(self, place, parts, full, sems, mixed=True):
        self.place, self.parts, self.full, self.mixed = place, parts, full, mixed
        sems = list(sems)
        if parts is not None:
            self.part_send, self.part_recv, self.own_sem = sems[:3]
            sems = sems[3:]
        if sems:
            self.up_send, self.down_send, self.chain_recv, self.line_send, self.line_recv = sems

    @staticmethod
    def inside():
        dma = pltpu.SemaphoreType.DMA
        return [dma((GROUP,)), dma((GROUP,)), dma((1,))]

    @staticmethod
    def outside(groups):
        return [pltpu.SemaphoreType.DMA((groups,))] * 5

    def unit(self, group, line):
        return self.full.at[group, :, line] if self.mixed else self.full.at[group, line]

    def own(self):
        p = self.place
        if self.mixed:
            return pltpu.make_async_copy(self.parts.at[p.m], self.full.at[p.g, p.m, p.b], self.own_sem.at[0])
        return pltpu.make_async_copy(self.parts, self.full.at[p.g, p.b], self.own_sem.at[0])

    def part(self, offset):
        p = self.place
        other = p.other(offset)
        return remote(
            self.parts.at[other], self.full.at[p.g, p.m, p.b], self.part_send.at[offset], self.part_recv.at[offset], p.member(offset)
        )

    def start(self):
        if self.mixed:
            for offset in (2, 3, 1):
                self.part(offset).start()
        self.own().start()

    def chain(self, source, up):
        p = self.place
        unit = self.unit(source, p.b)
        sems = self.up_send if up else self.down_send
        return remote(unit, unit, sems.at[source], self.chain_recv.at[source], p.up() if up else p.down())

    def across(self, source):
        p = self.place
        unit = self.unit(source, p.b)
        return remote(unit, unit, self.line_send.at[source], self.line_recv.at[source], p.across())

    def settle(self):
        self.own().wait()
        if self.mixed:
            for offset in (2, 3, 1):
                self.part(offset).wait()

    def spread(self):
        p = self.place
        pl.when(p.above)(lambda: self.chain(p.g, True).start())
        pl.when(p.below)(lambda: self.chain(p.g, False).start())
        self.across(p.g).start()

    def step(self, distance):
        p = self.place

        @pl.when(p.g >= distance)
        def _():
            source = p.g - distance
            self.chain(source, True).wait_recv()
            pl.when(p.above)(lambda: self.chain(source, True).start())
            self.across(source).start()

        @pl.when(p.g + distance < p.groups)
        def _():
            source = p.g + distance
            self.chain(source, False).wait_recv()
            pl.when(p.below)(lambda: self.chain(source, False).start())
            self.across(source).start()

    def finish(self):
        p = self.place

        def settle(source, carry):
            self.across(source).wait()
            pl.when(p.above & (source <= p.g))(lambda: self.chain(source, True).wait_send())
            pl.when(p.below & (source >= p.g))(lambda: self.chain(source, False).wait_send())
            return carry

        lax.fori_loop(0, p.groups, settle, 0)


class HomeGather:
    def __init__(self, place, part, full, sems):
        self.place, self.part_ref, self.full = place, part, full
        self.home = place.groups // GROUP
        self.part_send, self.part_recv, self.up_send, self.down_send, self.chain_recv = sems

    @staticmethod
    def scratch(groups):
        dma = pltpu.SemaphoreType.DMA
        return [dma((1,)), dma((GROUP,))] + [dma((groups // GROUP,))] * 3

    def at_home(self):
        return self.place.m == self.place.g // self.home

    def slot(self):
        p = self.place
        return self.full.at[p.g % self.home, p.m, p.b]

    def hand(self):
        p = self.place
        keeper = p.g // self.home
        device = {"g": p.g, "m": keeper, "b": p.b}
        return remote(self.part_ref, self.slot(), self.part_send.at[0], self.part_recv.at[p.m], device)

    def taken(self, source):
        p = self.place
        target = self.full.at[p.g % self.home, source, p.b]
        return remote(self.part_ref, target, self.part_send.at[0], self.part_recv.at[source], p.member(1))

    def own(self):
        return pltpu.make_async_copy(self.part_ref, self.slot(), self.part_send.at[0])

    def start(self):
        pl.when(self.at_home())(lambda: self.own().start())
        pl.when(jnp.logical_not(self.at_home()))(lambda: self.hand().start())

    def chain(self, slot, up):
        p = self.place
        unit = self.full.at[slot, :, p.b]
        sems = self.up_send if up else self.down_send
        return remote(unit, unit, sems.at[slot], self.chain_recv.at[slot], p.up() if up else p.down())

    def spread(self):
        p = self.place

        @pl.when(self.at_home())
        def _():
            self.own().wait()
            for offset in range(1, GROUP):
                self.taken(p.other(offset)).wait_recv()
            slot = p.g % self.home
            pl.when(p.above)(lambda: self.chain(slot, True).start())
            pl.when(p.below)(lambda: self.chain(slot, False).start())

    def step(self, distance):
        p = self.place
        for slot in range(self.home):
            source = p.m * self.home + slot

            @pl.when(p.g - source == distance)
            def _():
                self.chain(slot, True).wait_recv()
                pl.when(p.above)(lambda: self.chain(slot, True).start())

            @pl.when(source - p.g == distance)
            def _():
                self.chain(slot, False).wait_recv()
                pl.when(p.below)(lambda: self.chain(slot, False).start())

    def finish(self):
        p = self.place
        pl.when(jnp.logical_not(self.at_home()))(lambda: self.hand().wait_send())
        for slot in range(self.home):
            source = p.m * self.home + slot
            pl.when(p.above & (p.g >= source))(lambda: self.chain(slot, True).wait_send())
            pl.when(p.below & (p.g <= source))(lambda: self.chain(slot, False).wait_send())


def home_lines(place, full, send, recv):
    copies = []
    for slot in range(place.groups // GROUP):
        unit = full.at[slot, :, place.b]
        copies.append(remote(unit, unit, send.at[slot], recv.at[slot], place.across()))
    return copies


class Scatter:
    def __init__(self, place, partial, result, refs, make=None):
        self.place, self.partial, self.result, self.make = place, partial, result, make
        (self.land, self.chain_land, self.leave, self.mine_sem, self.line_send, self.line_recv, self.chain_send,
         self.chain_recv, self.part_send, self.part_recv) = refs
        self.parts = partial.shape[1]

    @staticmethod
    def scratch(groups, shape):
        dma = pltpu.SemaphoreType.DMA
        unit = (shape[1],) + tuple(shape[3:])
        return [
            pltpu.VMEM((groups,) + unit, BF16),
            pltpu.VMEM((groups + 1,) + unit, BF16),
            pltpu.VMEM((groups,) + unit, BF16),
            dma((groups,)),
            dma((groups,)),
            dma((groups,)),
            dma((groups,)),
            dma((groups + 1,)),
            dma((GROUP,)),
            dma((GROUP,)),
        ]

    def load(self, target):
        return pltpu.make_async_copy(self.partial.at[target, :, self.place.b], self.leave.at[target], self.mine_sem.at[target])

    def line(self, target):
        p = self.place
        return remote(
            self.partial.at[target, :, 1 - p.b], self.land.at[target], self.line_send.at[target], self.line_recv.at[target], p.across()
        )

    def up(self, target):
        p = self.place
        return remote(
            self.leave.at[target], self.chain_land.at[target], self.chain_send.at[target], self.chain_recv.at[target], p.up()
        )

    def down(self, target, slot):
        p = self.place
        return remote(
            self.leave.at[target], self.chain_land.at[slot], self.chain_send.at[target], self.chain_recv.at[slot], p.down()
        )

    def send_up(self, target):
        self.up(target).start()

    def send_down(self, target):
        p = self.place
        pl.when(p.g - 1 == target)(lambda: self.down(target, p.groups).start())
        pl.when(p.g - 1 != target)(lambda: self.down(target, target).start())

    def arrived(self, slot):
        p = self.place
        return remote(self.leave.at[0], self.chain_land.at[slot], self.chain_send.at[0], self.chain_recv.at[slot], p.across())

    def wave(self, wave, act_up, act_down):
        p = self.place
        pl.when(wave > p.g)(lambda: act_up(p.groups - wave + p.g))
        pl.when(wave >= p.groups - p.g)(lambda: act_down(wave - p.groups + p.g))

    def act(self, target):
        if self.make is not None:
            self.make(target)
        self.line(target).start()
        self.load(target).start()

    def start(self):
        self.start_far()
        self.act(self.place.g)

    def start_far(self, first=1, last=None):
        p = self.place
        if self.make is None:
            for wave in range(first, p.groups if last is None else last + 1):
                self.wave(wave, self.act, self.act)
        else:

            def one(wave, carry):
                self.wave(wave, self.act, self.act)
                return carry

            lax.fori_loop(first, p.groups if last is None else last + 1, one, 0)
        if first > 1:
            return

        @pl.when(jnp.logical_not(p.below))
        def _():
            self.chain_land[p.g] = jnp.zeros(self.chain_land.shape[1:], BF16)

        @pl.when(jnp.logical_not(p.above))
        def _():
            self.chain_land[p.groups] = jnp.zeros(self.chain_land.shape[1:], BF16)

    def both(self, target, part):
        return self.leave[target, part].astype(F32) + self.land[target, part].astype(F32)

    def step(self, wave):
        p = self.place

        def send(target, inner, copy):
            self.load(target).wait()
            self.line(target).wait_recv()

            @pl.when(inner)
            def _():
                self.arrived(target).wait_recv()
                for part in range(self.parts):
                    self.leave[target, part] = (self.both(target, part) + self.chain_land[target, part].astype(F32)).astype(BF16)

            @pl.when(jnp.logical_not(inner))
            def _():
                for part in range(self.parts):
                    self.leave[target, part] = self.both(target, part).astype(BF16)

            copy(target)

        self.wave(
            wave,
            lambda target: send(target, p.below, self.send_up),
            lambda target: send(target, p.above, self.send_down),
        )

    def hand(self, offset):
        p = self.place
        return remote(
            self.leave.at[p.g, p.other(offset)], self.result.at[p.m], self.part_send.at[offset], self.part_recv.at[offset], p.member(offset)
        )

    def last(self):
        p = self.place
        self.load(p.g).wait()
        self.line(p.g).wait_recv()
        pl.when(p.below)(lambda: self.arrived(p.g).wait_recv())
        pl.when(p.above)(lambda: self.arrived(p.groups).wait_recv())
        for part in range(self.parts):
            total = self.both(p.g, part) + self.chain_land[p.g, part].astype(F32) + self.chain_land[p.groups, part].astype(F32)
            if self.parts == 1:
                self.result[part] = total.astype(self.result.dtype)
            else:
                self.leave[p.g, part] = total.astype(BF16)
        if self.parts > 1:
            for offset in (2, 3, 1):
                self.hand(offset).start()
            self.result[p.m] = self.leave[p.g, p.m]

    def finish(self):
        p = self.place
        for target in range(p.groups):
            self.line(target).wait_send()
            pl.when(p.g != target)(lambda: self.up(target).wait_send())
        if self.parts > 1:
            for offset in (2, 3, 1):
                self.hand(offset).wait()


class LineSum:
    def __init__(self, place, partial, result, refs):
        self.place, self.partial, self.result = place, partial, result
        self.land, self.mine_sem, self.send, self.recv = refs

    @staticmethod
    def scratch(groups, shape):
        home = groups // GROUP
        return [pltpu.VMEM((home, GROUP) + tuple(shape[3:]), BF16)] + [pltpu.SemaphoreType.DMA((home,))] * 3

    def load(self, slot):
        return pltpu.make_async_copy(self.partial.at[slot, :, self.place.b], self.result.at[slot], self.mine_sem.at[slot])

    def line(self, slot):
        p = self.place
        return remote(self.partial.at[slot, :, 1 - p.b], self.land.at[slot], self.send.at[slot], self.recv.at[slot], p.across())

    def start(self):
        for slot in range(self.partial.shape[0]):
            self.line(slot).start()
            self.load(slot).start()

    def finish(self):
        for slot in range(self.partial.shape[0]):
            self.load(slot).wait()
            self.line(slot).wait()
            for part in range(GROUP):
                total = self.result[slot, part].astype(F32) + self.land[slot, part].astype(F32)
                self.result[slot, part] = total.astype(BF16)


class HomeScatter:
    def __init__(self, place, partial, result, refs):
        self.place, self.partial, self.result = place, partial, result
        self.home_land, self.leave, self.home_send, self.home_recv, self.part_send, self.part_recv = refs
        self.home = place.groups // GROUP

    @staticmethod
    def scratch(groups, shape):
        dma = pltpu.SemaphoreType.DMA
        unit = tuple(shape[1:])
        return [
            pltpu.VMEM((groups - 1,) + unit, BF16),
            pltpu.VMEM(unit, BF16),
            dma((shape[0],)),
            dma((groups - 1,)),
            dma((GROUP,)),
            dma((1,)),
        ]

    def home_copy(self, slot):
        p = self.place
        target = p.m * self.home + slot
        index = (p.g - target + p.groups - 1) % p.groups
        return remote(
            self.partial.at[slot], self.home_land.at[index], self.home_send.at[slot], self.home_recv.at[index], p.column(target)
        )

    def landed(self, index):
        p = self.place
        return remote(self.leave, self.home_land.at[index], self.home_send.at[0], self.home_recv.at[index], p.across())

    def start(self):
        p = self.place
        for slot in range(self.home):
            pl.when(p.g != p.m * self.home + slot)(lambda: self.home_copy(slot).start())

    def hand(self, other):
        p = self.place
        return remote(
            self.leave.at[other], self.result, self.part_send.at[other], self.part_recv.at[0], {"g": p.g, "m": other, "b": p.b}
        )

    def last(self):
        p = self.place

        @pl.when(p.m == p.g // self.home)
        def _():
            for index in range(p.groups - 1):
                self.landed(index).wait_recv()
            for part in range(GROUP):
                total = self.partial[p.g % self.home, part].astype(F32)
                for index in range(p.groups - 1):
                    total = total + self.home_land[index, part].astype(F32)
                self.leave[part] = total.astype(BF16)
            for offset in range(1, GROUP):
                self.hand(p.other(offset)).start()
            self.result[...] = self.leave[p.m]

    def finish(self):
        p = self.place
        keeper = p.m == p.g // self.home

        @pl.when(keeper)
        def _():
            for offset in range(1, GROUP):
                self.hand(p.other(offset)).wait_send()

        pl.when(jnp.logical_not(keeper))(lambda: self.hand(p.other(1)).wait_recv())
        for slot in range(self.home):
            pl.when(p.g != p.m * self.home + slot)(lambda: self.home_copy(slot).wait_send())


CHUNKS = 4


class GroupSum:
    def __init__(self, place, partial, refs):
        self.place, self.partial = place, partial
        self.pair_land, self.leave, self.land, self.pair_send, self.pair_recv, self.send, self.recv = refs
        self.size = partial.shape[0] // GROUP
        self.rows = self.size // CHUNKS

    @staticmethod
    def scratch(size, width):
        dma = pltpu.SemaphoreType.DMA
        return [
            pltpu.VMEM((2, size, width), BF16),
            pltpu.VMEM((size, width), BF16),
            pltpu.VMEM((size, width), BF16),
            dma((2, CHUNKS)),
            dma((2, CHUNKS)),
            dma((CHUNKS,)),
            dma((CHUNKS,)),
        ]

    def at(self, chunk, member=0):
        return pl.ds(pl.multiple_of(member * self.size + chunk * self.rows, self.rows), self.rows)

    def pair(self, chunk, far):
        p = self.place
        member = p.other(3 if far else 1)
        slot = 1 if far else 0
        return remote(
            self.partial.at[self.at(chunk, member)], self.pair_land.at[slot, self.at(chunk)], self.pair_send.at[slot, chunk],
            self.pair_recv.at[slot, chunk], p.member(1),
        )

    def cross(self, chunk):
        return remote(
            self.leave.at[self.at(chunk)], self.land.at[self.at(chunk)], self.send.at[chunk], self.recv.at[chunk], self.place.member(2)
        )

    def start(self):
        for chunk in range(CHUNKS):
            self.pair(chunk, True).start()
        for chunk in range(CHUNKS):
            self.pair(chunk, False).start()

    def pass_on(self, chunk):
        self.pair(chunk, True).wait_recv()
        own = self.partial[self.at(chunk, self.place.other(2)), :].astype(F32)
        self.leave[self.at(chunk), :] = (own + self.pair_land[1, self.at(chunk), :].astype(F32)).astype(BF16)
        self.cross(chunk).start()

    def take(self, chunk):
        self.pair(chunk, False).wait_recv()
        self.cross(chunk).wait_recv()
        own = self.partial[self.at(chunk, self.place.m), :].astype(F32)
        return own + self.pair_land[0, self.at(chunk), :].astype(F32) + self.land[self.at(chunk), :].astype(F32)

    def finish(self):
        for chunk in range(CHUNKS):
            self.pair(chunk, True).wait_send()
            self.pair(chunk, False).wait_send()
            self.cross(chunk).wait_send()


class GroupGather:
    def __init__(self, place, whole, refs):
        self.place, self.whole = place, whole
        self.send, self.recv = refs
        self.size = whole.shape[0] // GROUP
        self.rows = self.size // CHUNKS

    @staticmethod
    def scratch():
        dma = pltpu.SemaphoreType.DMA
        return [dma((3, CHUNKS)), dma((3, CHUNKS))]

    def at(self, chunk, member):
        return pl.ds(pl.multiple_of(member * self.size + chunk * self.rows, self.rows), self.rows)

    def copy(self, chunk, way):
        p = self.place
        rows = self.whole.at[self.at(chunk, p.other(2) if way == 2 else p.m)]
        return remote(rows, rows, self.send.at[way, chunk], self.recv.at[way, chunk], p.member(2 if way == 0 else 1))

    def give(self, chunk):
        self.copy(chunk, 0).start()
        self.copy(chunk, 1).start()

    def pass_on(self, chunk):
        self.copy(chunk, 0).wait_recv()
        self.copy(chunk, 2).start()

    def finish(self):
        for chunk in range(CHUNKS):
            self.copy(chunk, 1).wait_recv()
            self.copy(chunk, 2).wait_recv()
            for way in range(3):
                self.copy(chunk, way).wait_send()


def masked(scores, counts):
    return jnp.where(counts, scores * SCALE, NEGATIVE)


class Pauses:
    def __init__(self, *steps):
        self.steps = list(steps)

    def __call__(self):
        if self.steps:
            for act in self.steps.pop(0):
                act()

    def rest(self):
        while self.steps:
            self()


def several(refs, *counts):
    refs = list(refs)
    taken = []
    for count in counts:
        taken.append(refs[:count])
        refs = refs[count:]
    return taken


def attend_kernel(
    groups,
    hops,
    tokens_hbm,
    first_hbm,
    gain_ref,
    doc_query_ref,
    doc_key_ref,
    out_home_ref,
    feed_unit_ref,
    rows_out,
    query_ref,
    value_ref,
    within_out,
    map_out,
    inverse_out,
    attended_ref,
    low_ref,
    stats_ref,
    moved_ref,
    values_ref,
    out_full_ref,
    feed_full_ref,
    tokens_ref,
    first_ref,
    normed_ref,
    load_sem,
    rows_ref,
    within_ref,
    map_ref,
    inverse_ref,
    key_ref,
    leave_ref,
    top_ref,
    total_ref,
    accum_ref,
    key_send,
    key_recv,
    value_send,
    value_recv,
    *sems,
):
    here = Place(groups, feed_full_ref.shape[2])
    tokens_load = pltpu.make_async_copy(tokens_hbm, tokens_ref, load_sem.at[0])
    first_load = pltpu.make_async_copy(first_hbm, first_ref, load_sem.at[1])
    tokens_load.start()
    first_load.start()
    here.meet()
    place, has_next, following = here.g, here.above, here.up()
    home_sems, feed_sems = several(sems, 2, 5)
    out_copies = home_lines(here, out_full_ref, *home_sems)
    feed_gather = Gather(here, None, feed_full_ref, feed_sems)
    feed_gather.spread()
    for copy in out_copies:
        copy.start()
    pauses = Pauses(
        *[
            (functools.partial(feed_gather.step, distance),)
            for distance in range(1, groups)
        ]
    )
    prepared = (rows_ref, query_ref, key_ref, value_ref, within_ref, map_ref, inverse_ref)
    tokens_load.wait()
    for block in range(GROUP):
        normed_ref[tile(block), :] = rms_norm(tokens_ref[tile(block), :].astype(F32), gain_ref[...]).astype(BF16)
    first_load.wait()
    for at, size in [(part * WIDE, WIDE) for part in range(4)] + [(4 * WIDE, EXTRA)]:
        rows_ref[:, pl.ds(at, size)] = dot(normed_ref[...], first_ref[:, pl.ds(at, size)])
    prepare_blocks(0, GROUP // 2, *prepared)
    pauses()
    prepare_blocks(GROUP // 2, GROUP, *prepared)
    stores = [
        pltpu.make_async_copy(source, target, load_sem.at[2 + index])
        for index, (source, target) in enumerate(
            ((rows_ref, rows_out), (within_ref, within_out), (map_ref, map_out), (inverse_ref, inverse_out))
        )
    ]
    for copy in stores:
        copy.start()

    def value_copy(source, slot):
        return remote(source, values_ref.at[slot], value_send.at[slot], value_recv.at[slot], following)

    def key_copy(slot):
        return remote(leave_ref.at[slot], moved_ref.at[slot + 1, 0], key_send.at[slot], key_recv.at[slot], following)

    def move(keys, block, head):
        return dot2(keys, map_ref[tile(block), tile(head)]).astype(BF16)

    for head in range(OWN):
        keys = key_ref[tile(0), tile(head)]
        for block in range(1, GROUP):
            moved_ref[0, block, tile(0, block), tile(head)] = keys
            keys = jnp.concatenate([move(keys, block, head), key_ref[tile(block), tile(head)]], 0)
        leave_ref[0, :, tile(head)] = keys

    @pl.when(has_next)
    def _():
        key_copy(0).start()
        value_copy(value_ref, 0).start()


    def row_counts(block, hop, first, count):
        return doc_query_ref[tile(block), :] == doc_key_ref[hop, :, tile(first, count)]

    for block in range(GROUP):
        counts = row_counts(block, 0, 0, block + 1)
        wide = (BLOCK, (block + 1) * BLOCK)
        counts = counts & (iota(0, wide) + block * BLOCK >= iota(1, wide))
        for head in range(OWN):
            scores = within_ref[tile(block), tile(head)]
            if block:
                before = dot(query_ref[tile(block), tile(head)], moved_ref[0, block, tile(0, block), tile(head)], NT)
                scores = jnp.concatenate([before, scores], 1)
            scores = masked(scores, counts)
            top = jnp.max(scores, axis=1, keepdims=True)
            weights = jnp.exp(scores - top)
            top_ref[head, tile(block), :] = jnp.broadcast_to(top, (BLOCK, BLOCK))
            total_ref[head, tile(block), :] = jnp.broadcast_to(jnp.sum(weights, axis=1, keepdims=True), (BLOCK, BLOCK))
            accum_ref[tile(block), tile(head)] = dot(weights.astype(BF16), value_ref[tile(0, block + 1), tile(head)])

    def hop_step(hop, last):
        @pl.when(place >= hop)
        def _():
            key_copy(hop - 1).wait_recv()
            for head in range(OWN):
                keys = moved_ref[hop, 0, :, tile(head)]
                for block in range(GROUP):
                    if last:
                        if block == GROUP - 1:
                            break
                        keys = move(keys[BLOCK:], block, head)
                        moved_ref[hop, block + 1, tile(block + 1, GROUP - 1 - block), tile(head)] = keys
                    else:
                        keys = move(keys, block, head)
                        if block < GROUP - 1:
                            moved_ref[hop, block + 1, :, tile(head)] = keys
                        else:
                            leave_ref[hop, :, tile(head)] = keys
            value_copy(value_ref, hop - 1).wait_recv()
            if not last:

                @pl.when(has_next)
                def _():
                    key_copy(hop).start()
                    value_copy(values_ref.at[hop - 1], hop).start()

            for block in range(GROUP):
                first = block if last else 0
                count = GROUP - first
                counts = row_counts(block, hop, first, count)
                for head in range(OWN):
                    scores = masked(
                        dot(query_ref[tile(block), tile(head)], moved_ref[hop, block, tile(first, count), tile(head)], NT),
                        counts,
                    )
                    old = top_ref[head, tile(block), :]
                    top = jnp.maximum(old, jnp.broadcast_to(jnp.max(scores, axis=1, keepdims=True), (BLOCK, BLOCK)))
                    factor = jnp.exp(old - top)
                    weights = jnp.exp(scores - jnp.concatenate([top] * count, 1))
                    top_ref[head, tile(block), :] = top
                    total_ref[head, tile(block), :] = total_ref[head, tile(block), :] * factor + jnp.sum(
                        weights, axis=1, keepdims=True
                    )
                    accum_ref[tile(block), tile(head)] = accum_ref[tile(block), tile(head)] * factor + dot(
                        weights.astype(BF16), values_ref[hop - 1, tile(first, count), tile(head)]
                    )

    if hops > 2:

        def between(hop, carry):
            hop_step(hop, False)
            return carry

        lax.fori_loop(1, hops, between, 0)
    else:
        for hop in range(1, hops):
            pauses()
            hop_step(hop, False)
    pauses()
    hop_step(hops, True)

    for block in range(GROUP):
        stats = jnp.zeros((BLOCK, BLOCK), F32)
        for head in range(OWN):
            total = total_ref[head, tile(block), :]
            result = accum_ref[tile(block), tile(head)] / total
            attended_ref[tile(block), tile(head)] = result
            low_ref[tile(block), tile(head)] = result.astype(BF16)
            stats = jnp.where(iota(1) == head, top_ref[head, tile(block), :], stats)
            stats = jnp.where(iota(1) == OWN + head, total, stats)
        stats_ref[tile(block), :] = stats

    def settle(slot, carry):
        @pl.when(has_next & (place >= slot))
        def _():
            key_copy(slot).wait_send()
            value_copy(value_ref, slot).wait_send()

        return carry

    lax.fori_loop(0, hops, settle, 0)
    pauses.rest()
    for copy in out_copies + stores:
        copy.wait()
    feed_gather.finish()


def in_vmem(count):
    return [pl.BlockSpec(memory_space=pltpu.VMEM)] * count


def anywhere(count):
    return [pl.BlockSpec(memory_space=pl.ANY)] * count


def shape(kind, *dims):
    return jax.ShapeDtypeStruct(dims, kind)


def communicating(number, name, vmem=58):
    return {
        "compiler_params": pltpu.CompilerParams(collective_id=number, has_side_effects=True, vmem_limit_bytes=vmem << 20),
        "name": name,
    }


def attend(groups, hops, tokens, first, gain, doc_query, doc_key, out_full, feed_full):
    length = tokens.shape[0]
    dma = pltpu.SemaphoreType.DMA
    return pl.pallas_call(
        functools.partial(attend_kernel, groups, hops),
        out_shape=[
            shape(F32, length, first.shape[1]),
            shape(BF16, length, WIDE),
            shape(BF16, length, WIDE),
            shape(F32, length, WIDE),
            shape(F32, length, WIDE),
            shape(F32, length, WIDE),
            shape(F32, length, WIDE),
            shape(BF16, length, WIDE),
            shape(F32, length, BLOCK),
            shape(BF16, hops + 1, GROUP, length, WIDE),
            shape(BF16, hops, length, WIDE),
            shape(BF16, *out_full.shape),
            shape(BF16, *feed_full.shape),
        ],
        in_specs=anywhere(2) + in_vmem(3) + anywhere(2),
        out_specs=anywhere(1) + in_vmem(2) + anywhere(3) + in_vmem(5) + anywhere(2),
        scratch_shapes=[
            pltpu.VMEM(tokens.shape, BF16),
            pltpu.VMEM(first.shape, BF16),
            pltpu.VMEM(tokens.shape, BF16),
            dma((6,)),
            pltpu.VMEM((length, first.shape[1]), F32),
            pltpu.VMEM((length, WIDE), F32),
            pltpu.VMEM((length, WIDE), F32),
            pltpu.VMEM((length, WIDE), F32),
            pltpu.VMEM((length, WIDE), BF16),
            pltpu.VMEM((hops, length, WIDE), BF16),
            pltpu.VMEM((OWN, length, BLOCK), F32),
            pltpu.VMEM((OWN, length, BLOCK), F32),
            pltpu.VMEM((length, WIDE), F32),
            dma((hops,)),
            dma((hops,)),
            dma((hops,)),
            dma((hops,)),
        ]
        + [dma((groups // GROUP,))] * 2
        + Gather.outside(groups),
        input_output_aliases={5: 11, 6: 12},
        **communicating(1, "attend"),
    )(tokens, first, gain, doc_query, doc_key, out_full, feed_full)


def made_feed(groups, rows):
    return groups == GROUP and rows % 16 == 0


def back_kernel(
    groups,
    hops,
    partial_ref,
    hidden_ref,
    cotangent_ref,
    gain_ref,
    low_ref,
    out_ref,
    query_ref,
    value_ref,
    within_ref,
    map_ref,
    doc_query_ref,
    doc_key_ref,
    attended_ref,
    stats_ref,
    values_hbm,
    moved_hbm,
    rows_hbm,
    inverse_hbm,
    down_partial_ref,
    feed_partial_ref,
    normed_hbm,
    feed_grads_hbm,
    grad_ref,
    down_result_ref,
    rows_grad_ref,
    feed_result_ref,
    out_result_ref,
    grad_low_ref,
    att_grad_ref,
    out_partial_ref,
    moved_ref,
    values_ref,
    extra_ref,
    normed_ref,
    feed_grads_ref,
    made_ref,
    load_sem,
    query_grad_ref,
    key_grad_ref,
    within_grad_ref,
    map_grad_ref,
    value_grad_ref,
    scaled_ref,
    dots_ref,
    direct_ref,
    key_slots_ref,
    value_slots_ref,
    key_send,
    key_recv,
    value_send,
    value_recv,
    *refs,
):
    lines, rows = feed_partial_ref.shape[2:4]
    here = Place(groups, lines)
    make = None
    if made_feed(groups, rows):
        normed_load = pltpu.make_async_copy(normed_hbm, normed_ref, load_sem.at[9])
        feed_load = pltpu.make_async_copy(feed_grads_hbm, feed_grads_ref, load_sem.at[10])
        feed_partial_ref = made_ref
        normed_load.start()
        feed_load.start()

        def make(target):
            span = GROUP * lines * rows
            left = normed_ref[:, pl.ds(pl.multiple_of(target * span, BLOCK), span)].T

            def one(at):
                value = dot(left, feed_grads_ref[:, at])
                for index in range(GROUP * lines):
                    made_ref[target, index // lines, index % lines, :, at] = value[index * rows : (index + 1) * rows].astype(BF16)

            in_tiles(feed_grads_ref.shape[1], one, 4 * BLOCK)

    here.meet()
    place, has_next, previous = here.g, here.above, here.down()
    sum_refs, gather_refs, down_refs, feed_refs, out_refs = several(
        refs,
        7,
        2,
        len(Scatter.scratch(groups, down_partial_ref.shape)),
        len(Scatter.scratch(groups, feed_partial_ref.shape)),
        len(LineSum.scratch(groups, out_partial_ref.shape)),
    )
    sums = GroupSum(here, partial_ref, sum_refs)
    whole = GroupGather(here, grad_low_ref, gather_refs)
    down = Scatter(here, down_partial_ref, down_result_ref, down_refs)
    feed_scatter = Scatter(here, feed_partial_ref, feed_result_ref, feed_refs, make)
    out_lines = LineSum(here, out_partial_ref, out_result_ref, out_refs)
    pauses = Pauses(*[(functools.partial(feed_scatter.step, wave),) for wave in range(1, groups)])

    def load(hop):
        return pltpu.make_async_copy(moved_hbm.at[hop], moved_ref.at[hop % 2], load_sem.at[hop % 2])

    def load_values(hop):
        return pltpu.make_async_copy(values_hbm.at[hop - 1], values_ref.at[hop % 2], load_sem.at[2 + hop % 2])

    loads = [pltpu.make_async_copy(rows_hbm.at[:, pl.ds(4 * WIDE, EXTRA)], extra_ref, load_sem.at[4])]
    for index, panel in enumerate((0, 1, 3)):
        loads.append(pltpu.make_async_copy(rows_hbm.at[:, pl.ds(panel * WIDE, WIDE)], direct_ref.at[index], load_sem.at[5 + index]))
    loads.append(pltpu.make_async_copy(inverse_hbm, direct_ref.at[3], load_sem.at[8]))
    sums.start()
    down.start()
    load(hops).start()
    load_values(hops).start()
    if make is not None:
        normed_load.wait()
        feed_load.wait()
    feed_scatter.start_far(1, 1)
    for chunk in range(CHUNKS):
        sums.pass_on(chunk)
    for chunk in range(CHUNKS):
        back = rms_back(hidden_ref[sums.at(chunk), :], gain_ref[...], sums.take(chunk))
        grad = cotangent_ref[sums.at(chunk), :].astype(F32) + back
        grad_ref[sums.at(chunk), :] = grad
        grad_low_ref[whole.at(chunk, here.m), :] = grad.astype(BF16)
        whole.give(chunk)
    down.step(1)
    for chunk in range(CHUNKS):
        whole.pass_on(chunk)
    if groups > 2:
        down.step(2)
    whole.finish()
    att_grad_ref[...] = dot(grad_low_ref[...], out_ref[...], NT).astype(BF16)
    turned = low_ref[...].T
    units = out_partial_ref.shape[3]

    def out_tile(at):
        value = dot(turned, grad_low_ref[:, at])
        for index in range(WIDE // units):
            slot, member, line = index // (GROUP * lines), index // lines % GROUP, index % lines
            out_partial_ref[slot, member, line, :, at] = value[index * units : (index + 1) * units].astype(BF16)

    in_tiles(out_partial_ref.shape[4], out_tile)
    out_lines.start()
    feed_scatter.start_far(2)
    feed_scatter.act(here.g)
    for wave in range(3, groups):
        down.step(wave)

    def key_copy(hop):
        slot = hop - 1
        return remote(key_slots_ref.at[hop], key_slots_ref.at[slot], key_send.at[slot], key_recv.at[slot], previous)

    def value_copy(hop):
        slot = hop - 1
        return remote(value_slots_ref.at[hop], value_slots_ref.at[slot], value_send.at[slot], value_recv.at[slot], previous)

    map_grad_ref[...] = jnp.zeros_like(map_grad_ref)
    query_grad_ref[...] = jnp.zeros_like(query_grad_ref)
    for block in range(GROUP):
        for head in range(OWN):
            at = (tile(block), tile(head))
            grad = att_grad_ref[at].astype(F32)
            total = stats_ref[tile(block), OWN + head : OWN + head + 1]
            scaled_ref[at] = (grad / total).astype(BF16)
            dots = -jnp.sum(grad * attended_ref[at], axis=1, keepdims=True) / total
            dots_ref[head, tile(block), :] = jnp.broadcast_to(dots, (BLOCK, BLOCK))

    def pair(block, head, scores, counts, values):
        count = scores.shape[1] // BLOCK
        top = stats_ref[tile(block), head : head + 1]
        weights = jnp.exp(masked(scores, counts) - top)
        weight_grad = dot(scaled_ref[tile(block), tile(head)], values, NT)
        dots = jnp.concatenate([dots_ref[head, tile(block), :]] * count, 1)
        return weights, weights * (weight_grad + dots) * SCALE

    def row_counts(block, hop, first, count):
        return doc_query_ref[tile(block), :] == doc_key_ref[hop, :, tile(first, count)]

    def hop_direct(hop, last):
        for head in range(OWN):
            value_grad_ref[:, tile(head)] = jnp.zeros((GROUP * BLOCK, BLOCK), F32)
        for block in range(GROUP):
            first = block if last else 0
            count = GROUP - first
            counts = row_counts(block, hop, first, count)
            for head in range(OWN):
                query = query_ref[tile(block), tile(head)]
                keys = moved_ref[hop % 2, block, tile(first, count), tile(head)]
                weights, grad = pair(
                    block, head, dot(query, keys, NT), counts, values_ref[hop % 2, tile(first, count), tile(head)]
                )
                raw = grad.astype(BF16)
                query_grad_ref[tile(block), tile(head)] += dot(raw, keys)
                direct_ref[block, tile(first, count), tile(head)] = dot(raw, query, TN)
                value_grad_ref[tile(first, count), tile(head)] += dot(
                    weights.astype(BF16), scaled_ref[tile(block), tile(head)], TN
                )

    def collect_map(block, head, keys, grads):
        map_grad_ref[tile(block), tile(head)] += dot2(keys, grads, TN)

    def hop_chain(hop, last):
        for head in range(OWN):
            if last:
                grads = direct_ref[GROUP - 1, tile(GROUP - 1), tile(head)]
                for block in range(GROUP - 2, -1, -1):
                    rows = tile(block + 1, GROUP - 1 - block)
                    collect_map(block, head, moved_ref[hop % 2, block, rows, tile(head)], grads)
                    back = dot3(grads, map_ref[tile(block), tile(head)], NT)
                    direct = direct_ref[block, tile(block, GROUP - block), tile(head)]
                    grads = jnp.concatenate([direct[:BLOCK], direct[BLOCK:] + back], 0)
                key_slots_ref[hop, :, tile(head)] = grads.astype(BF16)
                value_slots_ref[hop, :, tile(head)] = value_grad_ref[:, tile(head)].astype(BF16)
            else:
                grads = key_grad_ref[:, tile(head)]
                for block in range(GROUP - 1, -1, -1):
                    collect_map(block, head, moved_ref[hop % 2, block, :, tile(head)], grads)
                    grads = direct_ref[block, :, tile(head)] + dot3(grads, map_ref[tile(block), tile(head)], NT)
                key_slots_ref[hop, :, tile(head)] = grads.astype(BF16)

    def take(hop):
        @pl.when(has_next)
        def _():
            key_copy(hop).wait_recv()
            key_grad_ref[...] = key_slots_ref[hop - 1].astype(F32)

        @pl.when(jnp.logical_not(has_next))
        def _():
            key_grad_ref[...] = jnp.zeros_like(key_grad_ref)

    load(hops - 1).start()
    load_values(hops - 1).start()
    load(hops).wait()
    load_values(hops).wait()

    @pl.when(place >= hops)
    def _():
        hop_direct(hops, True)
        hop_chain(hops, True)
        key_copy(hops).start()
        value_copy(hops).start()

    down.last()

    def between(hop, pause=None):
        load(hop - 1).start()
        pl.when(jnp.asarray(hop) > 1)(lambda: load_values(hop - 1).start())
        load(hop).wait()
        load_values(hop).wait()
        pl.when(place >= hop)(lambda: hop_direct(hop, False))
        if pause is not None:
            pause()

        @pl.when(place >= hop)
        def _():
            take(hop + 1)
            hop_chain(hop, False)
            key_copy(hop).start()

            @pl.when(has_next)
            def _():
                value_copy(hop + 1).wait_recv()
                for head in range(OWN):
                    value_slots_ref[hop, :, tile(head)] = (
                        value_grad_ref[:, tile(head)] + value_slots_ref[hop, :, tile(head)].astype(F32)
                    ).astype(BF16)

            @pl.when(jnp.logical_not(has_next))
            def _():
                for head in range(OWN):
                    value_slots_ref[hop, :, tile(head)] = value_grad_ref[:, tile(head)].astype(BF16)

            value_copy(hop).start()

    if hops > 2:

        def step(counter, carry):
            between(hops - 1 - counter)
            return carry

        lax.fori_loop(0, hops - 1, step, 0)
    else:
        for hop in range(hops - 1, 0, -1):
            between(hop, pauses)

    load(0).wait()
    for head in range(OWN):
        value_grad_ref[:, tile(head)] = jnp.zeros((GROUP * BLOCK, BLOCK), F32)
    for block in range(GROUP):
        wide = (BLOCK, (block + 1) * BLOCK)
        counts = row_counts(block, 0, 0, block + 1) & (iota(0, wide) + block * BLOCK >= iota(1, wide))
        for head in range(OWN):
            query = query_ref[tile(block), tile(head)]
            scores = within_ref[tile(block), tile(head)]
            if block:
                keys = moved_ref[0, block, tile(0, block), tile(head)]
                scores = jnp.concatenate([dot(query, keys, NT), scores], 1)
            weights, grad = pair(block, head, scores, counts, value_ref[tile(0, block + 1), tile(head)])
            within_grad_ref[tile(block), tile(head)] = grad[:, block * BLOCK :]
            value_grad_ref[tile(0, block + 1), tile(head)] += dot(
                weights.astype(BF16), scaled_ref[tile(block), tile(head)], TN
            )
            if block:
                raw = grad[:, : block * BLOCK].astype(BF16)
                query_grad_ref[tile(block), tile(head)] += dot(raw, keys)
                direct_ref[block, tile(0, block), tile(head)] = dot(raw, query, TN)
    take(1)
    for head in range(OWN):
        grads = key_grad_ref[:, tile(head)]
        for block in range(GROUP - 1, 0, -1):
            key_grad_ref[tile(block), tile(head)] = grads[block * BLOCK :]
            grads = grads[: block * BLOCK]
            collect_map(block, head, moved_ref[0, block, tile(0, block), tile(head)], grads)
            grads = direct_ref[block, tile(0, block), tile(head)] + dot3(grads, map_ref[tile(block), tile(head)], NT)
        key_grad_ref[tile(0), tile(head)] = grads

    @pl.when(has_next)
    def _():
        value_copy(1).wait_recv()
        value_grad_ref[...] += value_slots_ref[0].astype(F32)

    def settle(hop, carry):
        @pl.when(place >= hop)
        def _():
            key_copy(hop).wait_send()
            value_copy(hop).wait_send()

        return carry

    lax.fori_loop(1, hops + 1, settle, 0)
    for copy in loads:
        copy.start()
    for copy in loads:
        copy.wait()
    pauses()
    pieces = (direct_ref, extra_ref, query_grad_ref, key_grad_ref, within_grad_ref, map_grad_ref, value_grad_ref, rows_grad_ref)
    prepare_back_blocks(0, GROUP // 2, *pieces)
    pauses.rest()
    prepare_back_blocks(GROUP // 2, GROUP, *pieces)
    out_lines.finish()
    feed_scatter.last()
    sums.finish()
    down.finish()
    feed_scatter.finish()


def back(groups, hops, partial, hidden, cotangent, gain, low, out, *args):
    values, moved, rows, inverse, down, feed, normed, feed_grads = args[-8:]
    size, width = hidden.shape
    length = partial.shape[0]
    lines, units = feed.shape[2:4]
    out_shape = (groups // GROUP, GROUP, lines, units, width)
    dma = pltpu.SemaphoreType.DMA
    inputs = (partial, hidden, cotangent, gain, low, out) + args
    return pl.pallas_call(
        functools.partial(back_kernel, groups, hops),
        out_shape=[
            shape(F32, size, width),
            shape(F32, 1, *down.shape[3:]),
            shape(BF16, *rows.shape),
            shape(BF16, GROUP, *feed.shape[3:]),
            shape(BF16, groups // GROUP, GROUP, units, width),
        ],
        in_specs=in_vmem(len(inputs) - 8) + anywhere(8),
        out_specs=in_vmem(5),
        scratch_shapes=[
            pltpu.VMEM((length, width), BF16),
            pltpu.VMEM((length, WIDE), BF16),
            pltpu.VMEM(out_shape, BF16),
            pltpu.VMEM((2,) + moved.shape[1:], BF16),
            pltpu.VMEM((2,) + values.shape[1:], BF16),
            pltpu.VMEM((length, EXTRA), F32),
            pltpu.VMEM(normed.shape if made_feed(groups, units) else (16, BLOCK), BF16),
            pltpu.VMEM(feed_grads.shape if made_feed(groups, units) else (16, BLOCK), BF16),
            pltpu.VMEM(feed.shape if made_feed(groups, units) else (1, 1, 1, 16, BLOCK), BF16),
            dma((11,)),
        ]
        + [pltpu.VMEM((length, WIDE), F32)] * 5
        + [
            pltpu.VMEM((length, WIDE), BF16),
            pltpu.VMEM((OWN, length, BLOCK), F32),
            pltpu.VMEM((GROUP, length, WIDE), F32),
            pltpu.VMEM((hops + 1, length, WIDE), BF16),
            pltpu.VMEM((hops + 1, length, WIDE), BF16),
            dma((hops,)),
            dma((hops,)),
            dma((hops,)),
            dma((hops,)),
        ]
        + GroupSum.scratch(size, width)
        + GroupGather.scratch()
        + Scatter.scratch(groups, down.shape)
        + Scatter.scratch(groups, feed.shape)
        + LineSum.scratch(groups, out_shape),
        **communicating(2, "back", 60),
    )(*inputs)


def gather_kernel(
    groups, query_ref, key_ref, value_ref, house_ref, extra_ref, gate_hbm, up_hbm, out_hbm, down_hbm, tokens_ref, cotangent_ref,
    full_ref, feed_full_ref, out_full_ref, down_low_ref, tokens_all_ref, cotangent_all_ref, first_ref, feed_parts_ref, out_low_ref,
    gate_ref, up_ref, out_ref, down_ref, load_sem, send, recv, local, *sems
):
    lines = full_ref.shape[2]
    here = Place(groups, lines)
    loads = [
        pltpu.make_async_copy(source, target, load_sem.at[index])
        for index, (source, target) in enumerate(
            ((out_hbm, out_ref), (gate_hbm, gate_ref), (up_hbm, up_ref), (down_hbm, down_ref))
        )
    ]
    for copy in loads:
        copy.start()
    for member in range(GROUP):
        for part, weight_ref in enumerate((query_ref, key_ref, value_ref, house_ref)):
            first_ref[member, :, pl.ds(part * WIDE, WIDE)] = weight_ref[:, pl.ds(member * WIDE, WIDE)].astype(BF16)
        first_ref[member, :, pl.ds(4 * WIDE, EXTRA)] = extra_ref[member]
    here.meet()
    first_sems, feed_sems, out_sems = several(sems, 8, 3, 5)
    first = Gather(here, first_ref, full_ref, first_sems)
    feed = Gather(here, feed_parts_ref, feed_full_ref, feed_sems)
    out = HomeGather(here, out_low_ref, out_full_ref, out_sems)
    first.start()
    loads[0].wait()
    out_low_ref[...] = out_ref[...].astype(BF16)
    out.start()
    size = tokens_ref.shape[0]
    own = pl.ds(pl.multiple_of(here.m * size, size), size)
    copies = []
    for index, (source, target) in enumerate(((tokens_ref, tokens_all_ref), (cotangent_ref, cotangent_all_ref))):
        copies.append(pltpu.make_async_copy(source, target.at[own], local.at[index]))
        for offset in (2, 3, 1):
            copies.append(
                remote(source, target.at[own], send.at[index, offset], recv.at[index, offset], here.member(offset))
            )
    for copy in copies:
        copy.start()
    for copy in loads[1:]:
        copy.wait()
    down_low_ref[...] = down_ref[...].astype(BF16)
    own_units = feed_parts_ref.shape[2] // 2
    for at, weight_ref in ((0, gate_ref), (own_units, up_ref)):
        if len(weight_ref.shape) == 3:
            feed_parts_ref[:, :, at : at + own_units] = weight_ref[...]
        else:
            for member in range(GROUP):
                for index in range(groups * lines):
                    block = (index // lines * GROUP + member) * lines + index % lines
                    feed_parts_ref[member, :, pl.ds(at + index * BLOCK, BLOCK)] = weight_ref[:, tile(block)].astype(BF16)
    feed.start()
    first.settle()
    first.spread()
    out.spread()
    for distance in range(1, groups):
        first.step(distance)
        out.step(distance)
    feed.settle()
    out.finish()
    for copy in copies:
        copy.wait()
    first.finish()


def gather_first(groups, lines, first, extra, gate, up, out, down, tokens, cotangent):
    dma = pltpu.SemaphoreType.DMA
    size, width = tokens.shape
    rows = out.shape[0]
    units = 2 * down.shape[0] * groups * lines
    return pl.pallas_call(
        functools.partial(gather_kernel, groups),
        out_shape=[
            shape(BF16, groups, GROUP, lines, rows, 4 * WIDE + EXTRA),
            shape(BF16, groups, GROUP, lines, rows, units),
            shape(BF16, groups // GROUP, GROUP, lines, rows, width),
            shape(BF16, *down.shape),
            shape(BF16, GROUP * size, width),
            shape(BF16, GROUP * size, width),
        ],
        in_specs=in_vmem(5) + anywhere(6),
        out_specs=anywhere(3) + in_vmem(1) + anywhere(2),
        scratch_shapes=[
            pltpu.VMEM((GROUP, rows, 4 * WIDE + EXTRA), BF16),
            pltpu.VMEM((GROUP, rows, units), BF16),
            pltpu.VMEM((rows, width), BF16),
            pltpu.VMEM(gate.shape, gate.dtype),
            pltpu.VMEM(up.shape, up.dtype),
            pltpu.VMEM(out.shape, F32),
            pltpu.VMEM(down.shape, F32),
            dma((4,)),
            dma((2, GROUP)),
            dma((2, GROUP)),
            dma((2,)),
        ]
        + Gather.inside()
        + Gather.outside(groups)
        + Gather.inside()
        + HomeGather.scratch(groups),
        **communicating(0, "gather_first", 60),
    )(*first, extra, gate, up, out, down, tokens, cotangent)


def rms_norm(values, gain):
    return values * lax.rsqrt(jnp.mean(values * values, axis=-1, keepdims=True) + EPSILON) * gain


def rms_back(values, gain, grad):
    scale = lax.rsqrt(jnp.mean(values * values, axis=-1, keepdims=True) + EPSILON)
    straight = values * scale
    lifted = grad * gain
    return scale * (lifted - straight * jnp.mean(lifted * straight, axis=-1, keepdims=True))


def in_tiles(size, act, step=2 * BLOCK):
    def one(index, carry):
        act(pl.ds(pl.multiple_of(index * step, step), step))
        return carry

    lax.fori_loop(0, size // step, one, 0)


def branch_kernel(
    groups, partial_ref, tokens_ref, gain_ref, down_ref, feed_hbm, cotangent_hbm, hidden_ref, normed_ref, active_ref, feed_grads_ref,
    down_full_ref, gate_slope_ref, up_slope_ref, cotangent_ref, down_rows_ref, feed_ref, feed_sem, *refs
):
    here = Place(groups, down_full_ref.shape[1])
    here.meet()
    sum_refs, gather_refs, down_refs = several(refs, 7, 2, 8)
    total = GroupSum(here, partial_ref, sum_refs)
    whole = GroupGather(here, normed_ref, gather_refs)
    down = Gather(here, down_ref, down_full_ref, down_refs, mixed=False)
    pauses = Pauses(*[(functools.partial(down.step, distance),) for distance in range(1, groups)])
    total.start()
    down.start()
    down.settle()
    down.spread()
    feed_copy = pltpu.make_async_copy(feed_hbm, feed_ref, feed_sem.at[0])
    feed_copy.start()
    cotangent_copy = pltpu.make_async_copy(cotangent_hbm, cotangent_ref, feed_sem.at[1])
    cotangent_copy.start()
    for chunk in range(CHUNKS):
        total.pass_on(chunk)
    pauses()
    for chunk in range(CHUNKS):
        hidden = tokens_ref[total.at(chunk), :].astype(F32) + total.take(chunk)
        hidden_ref[total.at(chunk), :] = hidden
        normed_ref[whole.at(chunk, here.m), :] = rms_norm(hidden, gain_ref[...]).astype(BF16)
        whole.give(chunk)
    pauses()
    for chunk in range(CHUNKS):
        whole.pass_on(chunk)
    pauses.rest()
    feed_copy.wait()
    whole.finish()
    units = active_ref.shape[1]

    def act(at):
        normed = normed_ref[...]
        gate = dot(normed, feed_ref[:, at])
        up = dot(normed, feed_ref[:, pl.ds(pl.multiple_of(at.start + units, BLOCK), at.size)])
        sigmoid = jax.nn.sigmoid(gate)
        silu = gate * sigmoid
        active_ref[:, at] = (silu * up).astype(BF16)
        gate_slope_ref[:, at] = up * (sigmoid * (1.0 + gate * (1.0 - sigmoid)))
        up_slope_ref[:, at] = silu

    in_tiles(units, act)
    total.finish()
    cotangent_copy.wait()
    down.finish()
    down_copy = pltpu.make_async_copy(down_full_ref, down_rows_ref, feed_sem.at[2])
    down_copy.start()
    down_copy.wait()
    down_rows = down_rows_ref[...].reshape(units, down_rows_ref.shape[3])
    step = 2 * BLOCK
    for index in range(units // step):
        at = pl.ds(index * step, step)
        grad = dot(cotangent_ref[...], down_rows[index * step : (index + 1) * step], NT)
        feed_grads_ref[:, at] = (grad * gate_slope_ref[:, at]).astype(BF16)
        feed_grads_ref[:, pl.ds(units + index * step, step)] = (grad * up_slope_ref[:, at]).astype(BF16)


def branch(groups, lines, partial, tokens, gain, down, feed, cotangent):
    size, width = tokens.shape
    length, units = partial.shape[0], feed.shape[1] // 2
    dma = pltpu.SemaphoreType.DMA
    return pl.pallas_call(
        functools.partial(branch_kernel, groups),
        out_shape=[
            shape(F32, size, width),
            shape(BF16, length, width),
            shape(BF16, length, units),
            shape(BF16, length, 2 * units),
            shape(BF16, groups, lines, *down.shape),
        ],
        in_specs=in_vmem(3) + anywhere(3),
        out_specs=in_vmem(4) + anywhere(1),
        scratch_shapes=[
            pltpu.VMEM((length, units), F32),
            pltpu.VMEM((length, units), F32),
            pltpu.VMEM(cotangent.shape, BF16),
            pltpu.VMEM((groups, lines) + down.shape, BF16),
            pltpu.VMEM(feed.shape, BF16),
            dma((3,)),
        ]
        + GroupSum.scratch(size, width)
        + GroupGather.scratch()
        + Gather.inside()
        + Gather.outside(groups),
        **communicating(3, "branch", 48),
    )(partial, tokens, gain, down, feed, cotangent)


def finish_kernel(
    groups, first_partial_ref, wide_hbm, first_hbm, down_hbm, rows_grad_ref, active_ref, out_lines_ref, tokens_ref, hidden_ref, grad_ref, gain_ref,
    first_result_ref, out_result_ref, tokens_grad_ref, output_ref, first_full_ref, down_full_ref, normed_partial_ref,
    output_partial_ref, wide_ref, normed_ref, made_ref, load_sem, *refs
):
    lines, rows = first_partial_ref.shape[2:4]
    here = Place(groups, lines)
    made = rows % 16 == 0
    if made:
        first_partial_ref = made_ref
    wide_copy = pltpu.make_async_copy(wide_hbm, wide_ref, load_sem.at[2])
    wide_copy.start()
    here.meet(column=True)

    def make(target):
        span = GROUP * lines * rows
        left = normed_ref[:, pl.ds(pl.multiple_of(target * span, BLOCK), span)].T
        for at, size in [(part * WIDE, WIDE) for part in range(4)] + [(4 * WIDE, EXTRA)]:
            value = dot(left, rows_grad_ref[:, pl.ds(at, size)])
            for index in range(GROUP * lines):
                made_ref[target, index // lines, index % lines, :, pl.ds(at, size)] = value[index * rows : (index + 1) * rows].astype(BF16)

    first_refs, out_refs, normed_refs, output_refs = several(
        refs, len(Scatter.scratch(groups, first_partial_ref.shape)), len(HomeScatter.scratch(groups, out_lines_ref.shape)), 7, 7
    )
    first = Scatter(here, first_partial_ref, first_result_ref, first_refs, make if made else None)
    out = HomeScatter(here, out_lines_ref, out_result_ref, out_refs)
    normed = GroupSum(here, normed_partial_ref, normed_refs)
    output = GroupSum(here, output_partial_ref, output_refs)
    first_copy = pltpu.make_async_copy(first_hbm, first_full_ref, load_sem.at[0])
    down_copy = pltpu.make_async_copy(down_hbm, down_full_ref, load_sem.at[1])
    first_copy.start()
    down_copy.start()
    wide_copy.wait()
    out.start()
    if made:
        for block in range(GROUP):
            normed_ref[tile(block), :] = rms_norm(wide_ref[tile(block), :].astype(F32), gain_ref[...]).astype(BF16)
    first.start()
    first_copy.wait()

    def normed_tile(at):
        normed_partial_ref[:, at] = dot(rows_grad_ref[...], first_full_ref[at, :], NT).astype(BF16)

    in_tiles(normed_partial_ref.shape[1], normed_tile)
    normed.start()
    down_copy.wait()
    for chunk in range(CHUNKS):
        normed.pass_on(chunk)

    def output_tile(at):
        output_partial_ref[:, at] = dot(active_ref[...], down_full_ref[:, at]).astype(BF16)

    in_tiles(output_partial_ref.shape[1], output_tile)
    output.start()
    first.step(1)
    for chunk in range(CHUNKS):
        output.pass_on(chunk)
    for chunk in range(CHUNKS):
        back = rms_back(tokens_ref[normed.at(chunk), :].astype(F32), gain_ref[...], normed.take(chunk))
        tokens_grad_ref[normed.at(chunk), :] = (grad_ref[normed.at(chunk), :] + back).astype(BF16)
    if groups > 2:
        first.step(2)
    for chunk in range(CHUNKS):
        output_ref[output.at(chunk), :] = (hidden_ref[output.at(chunk), :] + output.take(chunk)).astype(BF16)
    for wave in range(3, groups):
        first.step(wave)
    out.last()
    normed.finish()
    output.finish()
    first.last()
    out.finish()
    first.finish()


def finish(groups, first_partial, wide, first, down, rows_grad, active, out_lines, tokens, hidden, grad, gain):
    size, width = tokens.shape
    length = rows_grad.shape[0]
    made = first_partial.shape if first_partial.shape[3] % 16 == 0 else (1, 1, 1, 16, BLOCK)
    return pl.pallas_call(
        functools.partial(finish_kernel, groups),
        out_shape=[
            shape(BF16, GROUP, *first_partial.shape[3:]),
            shape(BF16, *out_lines.shape[2:]),
            shape(BF16, size, width),
            shape(BF16, size, width),
        ],
        in_specs=anywhere(4) + in_vmem(7),
        out_specs=in_vmem(4),
        scratch_shapes=[
            pltpu.VMEM(first.shape, BF16),
            pltpu.VMEM(down.shape, BF16),
            pltpu.VMEM((length, width), BF16),
            pltpu.VMEM((length, width), BF16),
            pltpu.VMEM(wide.shape, BF16),
            pltpu.VMEM(wide.shape, BF16),
            pltpu.VMEM(made, BF16),
            pltpu.SemaphoreType.DMA((3,)),
        ]
        + Scatter.scratch(groups, first_partial.shape)
        + HomeScatter.scratch(groups, out_lines.shape)
        + GroupSum.scratch(size, width)
        + GroupSum.scratch(size, width),
        **communicating(5, "finish"),
    )(first_partial, wide, first, down, rows_grad, active, out_lines, tokens, hidden, grad, gain)


def layout_kernel(groups, lines, first_ref, feed_ref, out_ref, beta_ref, gains_ref, down_ref, tokens_ref, result_ref, *refs):
    weights, targets = refs[:6], refs[6:]
    query_out, key_out, value_out, house_out, out_out, down_out, tokens_out, result_out, norm_gain_out, beta_out = targets[:10]
    rows = gains_ref.shape[1]
    down_out[...] = down_ref[0]
    tokens_out[...] = tokens_ref[...]
    result_out[...] = result_ref[...]

    def as_row(column):
        return jnp.broadcast_to(column, (rows, BLOCK)).T[0:1, :]

    first_sum = jnp.zeros((rows, WIDE), F32)
    extra_sum = jnp.zeros((rows, EXTRA), F32)
    for member in range(GROUP):
        for part, target_ref in enumerate((query_out, key_out, value_out, house_out)):
            value = first_ref[member, :, pl.ds(part * WIDE, WIDE)].astype(F32)
            at = pl.ds(member * WIDE, WIDE)
            target_ref[:, at] = value
            first_sum = first_sum + value * weights[part][:, at].astype(BF16).astype(F32)
        extra = first_ref[member, :, pl.ds(4 * WIDE, EXTRA)].astype(F32)
        extra_sum = extra_sum + extra * beta_ref[member].astype(F32)
        beta_out[member] = extra.T[0:OWN, :]
    total = jnp.sum(first_sum, axis=1, keepdims=True) + jnp.sum(extra_sum, axis=1, keepdims=True)
    norm_gain_out[...] = as_row(total) / gains_ref[0:1, :]
    out_out[...] = out_ref[...].astype(F32)
    if len(targets) > 10:
        gate_out, up_out, ffn_gain_out = targets[10:]
        units = feed_ref.shape[2] // 2
        feed_sum = jnp.zeros((rows, BLOCK), F32)
        for at, weight_ref, target_ref in ((0, weights[4], gate_out), (units, weights[5], up_out)):
            for member in range(GROUP):
                for index in range(groups * lines):
                    block = (index // lines * GROUP + member) * lines + index % lines
                    value = feed_ref[member, :, pl.ds(at + index * BLOCK, BLOCK)].astype(F32)
                    target_ref[:, tile(block)] = value
                    feed_sum = feed_sum + value * weight_ref[:, tile(block)].astype(BF16).astype(F32)
        ffn_gain_out[...] = as_row(jnp.sum(feed_sum, axis=1, keepdims=True)) / gains_ref[1:2, :]


def layout(groups, lines, whole_tiles, first, feed, out, beta, gains, down, tokens, result, weights):
    rows, width = out.shape
    outs = [shape(F32, rows, width)] * 5 + [
        shape(F32, *down.shape[1:]),
        shape(BF16, *tokens.shape),
        shape(BF16, *tokens.shape),
        shape(F32, 1, rows),
        shape(F32, GROUP, OWN, rows),
    ]
    if whole_tiles:
        outs = outs + [shape(F32, *weights[4].shape)] * 2 + [shape(F32, 1, rows)]
    return pl.pallas_call(
        functools.partial(layout_kernel, groups, lines),
        out_shape=outs,
        in_specs=in_vmem(8 + len(weights)),
        out_specs=in_vmem(len(outs)),
        compiler_params=pltpu.CompilerParams(vmem_limit_bytes=60 << 20),
        name="layout",
    )(first, feed, out, beta, gains, down, tokens, result, *weights)


def on_device(
    tokens,
    doc_ids,
    norm_gain,
    query_weight,
    key_weight,
    value_weight,
    house_weight,
    beta_weight,
    out_weight,
    ffn_gain,
    gate_weight,
    up_weight,
    down_weight,
    cotangent,
):
    groups, batch = lax.axis_size("g"), lax.axis_size("b")
    devices = groups * GROUP * batch
    rows, width = query_weight.shape
    hidden_rows = down_weight.shape[0]
    hidden_own = gate_weight.shape[1] // GROUP
    block_rows = tokens.shape[1]
    hops = groups // 2
    doc_columns = -(-block_rows // rows)
    place, line = lax.axis_index("g"), lax.axis_index("b")

    def columns(weight):
        return jnp.transpose(weight.astype(BF16).reshape(rows, GROUP, -1), (1, 0, 2))

    docs = jnp.pad(doc_ids[0].astype(BF16), (0, rows * doc_columns - block_rows)).reshape(rows, doc_columns)
    same = jnp.concatenate([norm_gain.astype(BF16)[:, None], ffn_gain.astype(BF16)[:, None], docs], 1)
    same = jnp.broadcast_to(same[None], (GROUP,) + same.shape)
    same = jnp.pad(same, ((0, 0), (0, 0), (0, EXTRA - OWN - same.shape[2])))
    extra = jnp.concatenate([columns(beta_weight), same], 2)

    def unit_columns(weight):
        parts = weight.astype(BF16).reshape(rows, groups, GROUP, batch, hidden_rows)
        return jnp.transpose(parts, (2, 0, 1, 3, 4)).reshape(GROUP, rows, hidden_own)

    whole_tiles = hidden_rows == BLOCK
    feed_weights = (gate_weight, up_weight) if whole_tiles else (unit_columns(gate_weight), unit_columns(up_weight))
    first, feed, out_full, down_low, tokens_all, cotangent_all = gather_first(
        groups, batch, (query_weight, key_weight, value_weight, house_weight), extra, *feed_weights, out_weight, down_weight, tokens[0], cotangent[0]
    )
    first = first.reshape(width, -1)

    extra = first[:, 4 * WIDE :]
    gain_one = extra[:, OWN].astype(F32)[None]
    gain_two = extra[:, OWN + 1].astype(F32)[None]
    docs = extra[:, OWN + 2 : OWN + 2 + doc_columns].astype(jnp.int32)
    docs = docs.reshape(devices, -1)[:, :block_rows].reshape(groups, GROUP, batch, block_rows)
    docs = lax.dynamic_index_in_dim(docs, line, 2, keepdims=False).reshape(groups, GROUP * block_rows)
    doc_key = jnp.stack(
        [
            jnp.where(place >= hop, lax.dynamic_index_in_dim(docs, jnp.maximum(place - hop, 0), 0, keepdims=False), -1)
            for hop in range(hops + 1)
        ]
    )[:, None, :]
    doc_query = lax.dynamic_index_in_dim(docs, place, 0, keepdims=False)[:, None]

    (projected, query, value, within, maps, inverse, attended, attended_low, stats, moved, values, out_full, feed) = attend(
        groups, hops, tokens_all, first, gain_one, doc_query, doc_key, out_full, feed
    )
    out_full = out_full.reshape(WIDE, width)
    feed = feed.reshape(width, -1)
    hidden, normed_two, active, feed_grads, down_full = branch(
        groups, batch, dot(attended_low, out_full).astype(BF16), tokens[0], gain_two, down_low, feed, cotangent_all
    )
    down_full = down_full.reshape(hidden_own, width)
    down_partial = dot(active, cotangent_all, TN).astype(BF16).reshape(groups, 1, batch, hidden_rows, width)
    if made_feed(groups, rows):
        feed_partial = feed.reshape(groups, GROUP, batch, rows, -1)
    else:
        feed_partial = dot(normed_two, feed_grads, TN).astype(BF16).reshape(groups, GROUP, batch, rows, -1)
    hidden_grad, down_weight_grad, rows_grad, feed_grad, out_lines = back(
        groups, hops, dot(feed_grads, feed, NT).astype(BF16), hidden, cotangent[0], gain_two, attended_low, out_full, query, value,
        within, maps, doc_query, doc_key, attended, stats, values, moved, projected, inverse, down_partial, feed_partial,
        normed_two, feed_grads,
    )
    partial_shape = (groups, GROUP, batch, rows, rows_grad.shape[1])
    if rows % 16 == 0:
        first_partial = first.reshape(partial_shape)
    else:
        normed = rms_norm(tokens_all.astype(F32), gain_one).astype(BF16)
        first_partial = dot(normed, rows_grad, TN).astype(BF16).reshape(partial_shape)
    beta_parts = jnp.pad(columns(beta_weight), ((0, 0), (0, 0), (0, EXTRA - OWN)))
    weights = (query_weight, key_weight, value_weight, house_weight) + feed_weights
    first_grad, out_grad, tokens_grad, output = finish(
        groups, first_partial, tokens_all, first, down_full, rows_grad, active, out_lines, tokens[0], hidden, hidden_grad, gain_one
    )
    gains = jnp.stack([norm_gain, ffn_gain]).astype(BF16).astype(F32)
    results = layout(
        groups, batch, whole_tiles, first_grad, feed_grad, out_grad, beta_parts, gains, down_weight_grad, tokens_grad, output, weights
    )
    query_weight_grad, key_weight_grad, value_weight_grad, house_weight_grad, out_weight_grad, down_weight_grad = results[:6]
    tokens_grad, output, norm_gain_grad, beta_weight_grad = results[6:10]
    output, tokens_grad = output[None], tokens_grad[None]
    beta_weight_grad = beta_weight_grad.reshape(-1, rows).T
    def unit_whole(parts):
        parts = parts.astype(F32).reshape(GROUP, rows, groups, batch, hidden_rows)
        return jnp.transpose(parts, (1, 2, 0, 3, 4)).reshape(rows, -1)

    if whole_tiles:
        gate_weight_grad, up_weight_grad, ffn_gain_grad = results[10:]
        ffn_gain_grad = ffn_gain_grad[0]
    else:
        gate_weight_grad, up_weight_grad = unit_whole(feed_grad[:, :, :hidden_own]), unit_whole(feed_grad[:, :, hidden_own:])
        feed_sum = jnp.sum(gate_weight_grad * gate_weight.astype(BF16).astype(F32), axis=1) + jnp.sum(
            up_weight_grad * up_weight.astype(BF16).astype(F32), axis=1
        )
        ffn_gain_grad = feed_sum / gains[1]
    return (
        output,
        tokens_grad,
        norm_gain_grad[0],
        query_weight_grad,
        key_weight_grad,
        value_weight_grad,
        house_weight_grad,
        beta_weight_grad,
        out_weight_grad,
        ffn_gain_grad,
        gate_weight_grad,
        up_weight_grad,
        down_weight_grad,
    )


def solution(mesh):
    groups = mesh.shape["seq"] // GROUP
    inner = Mesh(mesh.devices.reshape(groups, GROUP, mesh.shape["batch"]), ("g", "m", "b"))
    line = P("b", ("g", "m"), None)
    vector = P(("g", "m", "b"))
    matrix = P(("g", "m", "b"), None)
    in_specs = (line, P("b", ("g", "m")), vector) + (matrix,) * 6 + (vector,) + (matrix,) * 3 + (line,)
    out_specs = (line, line, vector) + (matrix,) * 6 + (vector,) + (matrix,) * 3
    return jax.shard_map(on_device, mesh=inner, in_specs=in_specs, out_specs=out_specs, check_vma=False)
```
